32 devices in a mesh: seg: 4 (over z), grp: 8 (over y, x, core).
Axes of the slice: x: 2, y: 2, z: 4, core: 2. Of those that a mesh axis runs over, the one named last changes fastest.
Arguments:
- frames_in: bfloat16 [32, 32, 120, 128], P(('seg', 'grp')), may hold values from -6 to 6
- spatial_weight: bfloat16 [9, 128, 128], replicated, may hold values from -0.1875 to 0.1875
- temporal_weight: bfloat16 [2, 5, 128, 128], replicated, may hold values from -0.25 to 0.25
- uniting_weight: bfloat16 [2, 128, 128], replicated, may hold values from -0.375 to 0.375
- key_index: int32 [4], replicated, may hold values from 0 to 7
- dilation: int32 [2], replicated, may hold values from 1 to 8, as said below
- cotangent: bfloat16 [32, 32, 120, 128], P(('seg', 'grp')), may hold values from -6 to 6
Outputs:
- united: bfloat16 [32, 32, 120, 128], P(('seg', 'grp'))
- grad_frames: bfloat16 [32, 32, 120, 128], P(('seg', 'grp'))
- grad_spatial: float32 [9, 128, 128], replicated
- grad_temporal: float32 [2, 5, 128, 128], replicated
- grad_uniting: float32 [2, 128, 128], replicated
The draws below stay inside these ranges and needn't reach their ends.
Inputs may be any that keep to these rules, and one draw needn't show every extreme that they name: `key_index`: position of a segment's keyframe within its 8 frames. Exactly one layer uses dilation 8; the others use less.
All inputs are finite; a program needn't handle non-finite values.
Results may differ from the reference program's by a relative error of at most 0.0095.
Values may be sent and summed in bfloat16 or wider, within the bound.
No kernel may reach another device: no remote copies, remote signals or barrier semaphores. Data moves between devices by JAX's collectives and lax.ppermute only.
A program may use at most 128 MiB of HBM per device.

```python
import jax
import jax.numpy as jnp
from jax import lax

C = 128
H = 32
W = 120
LAYERS = 2
DMAX = 8
FRAMES = 32
SEGLEN = 8
N_SEG = 4


def draw_dilation(key, part):
    first_key, second_key = jax.random.split(jax.random.fold_in(key, 17))
    values = jax.random.randint(first_key, (LAYERS,), 1, DMAX)
    chosen = jax.random.randint(second_key, (), 0, LAYERS)
    return jnp.where(jnp.arange(LAYERS) == chosen, DMAX, values).astype(jnp.int32)


def touch_ends(values, own_key, low, high):
    extent = values.shape
    index_at = [jax.random.randint(jax.random.fold_in(own_key, axis), (), 0, extent[axis]) for axis in range(len(extent))]
    values = values.at[tuple(index_at)].set(low)
    longest = extent.index(max(extent))
    index_at[longest] = (index_at[longest] + 1) % extent[longest]
    return values.at[tuple(index_at)].set(high)


def level_of(stream_key, dims, cuts, smallest, high):
    level = 1.0
    for position, blocks in cuts:
        heights = jax.random.uniform(jax.random.fold_in(jax.random.fold_in(stream_key, 6), position), (blocks,), jnp.float32, smallest / len(cuts), high / len(cuts))
        level = level * jnp.repeat(jnp.exp(heights), dims[position] // blocks).reshape((-1,) + (1,) * (len(dims) - 1 - position))
    return level


def normal_values(stream_key, dims, scale, limit, pieces=(), kind=jnp.bfloat16):
    drawn = scale * jax.random.normal(stream_key, dims, jnp.float32)
    if pieces:
        drawn = drawn * level_of(stream_key, dims, pieces, -0.22, 0.18)
    return jnp.clip(drawn, -limit, limit).astype(kind)


def setup_inputs(seed: int = 0) -> dict:
    streams_of = jax.random.split(jax.random.key(seed), 8)
    frames_in = normal_values(streams_of[0], (FRAMES, H, W, C), 1.0, 6.0, ((0, 32),))
    spatial_weight = normal_values(streams_of[1], (9, C, C), (9 * C) ** -0.5, 0.1875)
    temporal_weight = normal_values(streams_of[2], (LAYERS, 5, C, C), (5 * C) ** -0.5, 0.25)
    uniting_weight = normal_values(streams_of[3], (2, C, C), (2 * C) ** -0.5, 0.375)
    key_index = touch_ends(jax.random.randint(streams_of[4], (N_SEG,), 0, SEGLEN), jax.random.fold_in(streams_of[4], 1), 0, SEGLEN - 1).astype(jnp.int32)
    dilation = draw_dilation(jax.random.fold_in(streams_of[7], 71), 0)
    cotangent = normal_values(streams_of[6], (FRAMES, H, W, C), 1.0, 6.0, ((0, 32),))
    return {"frames_in": frames_in, "spatial_weight": spatial_weight, "temporal_weight": temporal_weight, "uniting_weight": uniting_weight, "key_index": key_index, "dilation": dilation, "cotangent": cotangent}


def silu_grad(value):
    sigma = jax.nn.sigmoid(value)
    return sigma * (1.0 + value * (1.0 - sigma))

def inner(left, right):
    return lax.dot_general(left, right, (((0,), (0,)), ((), ())), preferred_element_type=jnp.float32)

def spatial_forward(frames, kernel):
    count, rows, cols, chans = frames.shape
    padded = jnp.pad(frames, ((0, 0), (1, 1), (1, 1), (0, 0)))
    total = jnp.zeros((count * rows * cols, chans), jnp.float32)
    for row_tap in range(3):
        for col_tap in range(3):
            piece = padded[:, row_tap:row_tap + rows, col_tap:col_tap + cols, :].reshape(-1, chans)
            total = total + jnp.dot(piece, kernel[3 * row_tap + col_tap], preferred_element_type=jnp.float32)
    return total.reshape(frames.shape)

def spatial_back(grads, kernel):
    count, rows, cols, chans = grads.shape
    padded = jnp.pad(grads, ((0, 0), (1, 1), (1, 1), (0, 0)))
    total = jnp.zeros((count * rows * cols, chans), jnp.float32)
    for row_tap in range(3):
        for col_tap in range(3):
            piece = padded[:, 2 - row_tap:2 - row_tap + rows, 2 - col_tap:2 - col_tap + cols, :].reshape(-1, chans)
            total = total + jnp.dot(piece, kernel[3 * row_tap + col_tap].T, preferred_element_type=jnp.float32)
    return total.reshape(grads.shape)

def spatial_wgrad(frames, grads):
    count, rows, cols, chans = frames.shape
    padded = jnp.pad(frames, ((0, 0), (1, 1), (1, 1), (0, 0)))
    flat_grads = grads.reshape(-1, chans)
    result = []
    for row_tap in range(3):
        for col_tap in range(3):
            piece = padded[:, row_tap:row_tap + rows, col_tap:col_tap + cols, :].reshape(-1, chans)
            result.append(inner(piece, flat_grads))
    return jnp.stack(result)

def shifted(values, offset):
    padded = jnp.pad(values, ((2 * DMAX, 2 * DMAX), (0, 0), (0, 0)))
    start = (2 * DMAX + offset).astype(jnp.int32)
    return lax.dynamic_slice_in_dim(padded, start, values.shape[0], 0)

def temporal_forward(acts, kernel, step_size):
    chans = acts.shape[2]
    total = jnp.zeros((acts.shape[0] * acts.shape[1], chans), jnp.float32)
    for tap in range(5):
        piece = shifted(acts, (tap - 2) * step_size).reshape(-1, chans)
        total = total + jnp.dot(piece, kernel[tap], preferred_element_type=jnp.float32)
    return total.reshape(acts.shape)

def temporal_back(grads, kernel, step_size):
    chans = grads.shape[2]
    total = jnp.zeros((grads.shape[0] * grads.shape[1], chans), jnp.float32)
    for tap in range(5):
        piece = shifted(grads, (2 - tap) * step_size).reshape(-1, chans)
        total = total + jnp.dot(piece, kernel[tap].T, preferred_element_type=jnp.float32)
    return total.reshape(grads.shape)

def temporal_wgrad(acts, grads, step_size):
    chans = acts.shape[2]
    flat_grads = grads.reshape(-1, chans)
    return jnp.stack([inner(shifted(acts, (tap - 2) * step_size).reshape(-1, chans), flat_grads) for tap in range(5)])

def reference(frames_in, spatial_weight, temporal_weight, uniting_weight, key_index, dilation, cotangent):
    pixels = H * W
    pre_spatial = spatial_forward(frames_in, spatial_weight)
    act = jax.nn.silu(pre_spatial).astype(jnp.bfloat16).reshape(FRAMES, pixels, C)
    acts = [act]
    pres = []
    for layer in range(LAYERS):
        pre = temporal_forward(acts[-1], temporal_weight[layer], dilation[layer])
        pres.append(pre)
        acts.append(jax.nn.silu(pre).astype(jnp.bfloat16))
    feat = acts[-1]
    feat_seg = feat.reshape(N_SEG, SEGLEN, pixels, C)
    keys = feat_seg[jnp.arange(N_SEG), key_index]
    key_full = jnp.broadcast_to(keys[:, None], feat_seg.shape).reshape(-1, C)
    feat_flat = feat.reshape(-1, C)
    united = (jnp.dot(feat_flat, uniting_weight[0], preferred_element_type=jnp.float32) + jnp.dot(key_full, uniting_weight[1], preferred_element_type=jnp.float32)).astype(jnp.bfloat16)
    cot_flat = cotangent.reshape(-1, C)
    grad_feat = jnp.dot(cot_flat, uniting_weight[0].T, preferred_element_type=jnp.float32).reshape(FRAMES, pixels, C)
    seg_cot = lax.optimization_barrier(jnp.sum(cotangent.reshape(N_SEG, SEGLEN, pixels, C).astype(jnp.float32), axis=1))
    key_term = jnp.dot(seg_cot.reshape(-1, C), uniting_weight[1].T.astype(jnp.float32), precision=lax.Precision.HIGHEST).reshape(N_SEG, pixels, C)
    onehot = (jnp.arange(SEGLEN, dtype=jnp.int32)[None, :] == key_index[:, None]).astype(jnp.float32)
    grad_feat = grad_feat + (onehot[:, :, None, None] * key_term[:, None]).reshape(FRAMES, pixels, C)
    grad_uniting = jnp.stack([inner(feat_flat, cot_flat), inner(key_full, cot_flat)])
    grad_pre = (grad_feat * silu_grad(pres[-1])).astype(jnp.bfloat16)
    tgrads = [None] * LAYERS
    grad_act0 = None
    for layer in range(LAYERS - 1, -1, -1):
        tgrads[layer] = temporal_wgrad(acts[layer], grad_pre, dilation[layer])
        grad_act = temporal_back(grad_pre, temporal_weight[layer], dilation[layer])
        if layer > 0:
            grad_pre = (grad_act * silu_grad(pres[layer - 1])).astype(jnp.bfloat16)
        else:
            grad_act0 = grad_act.astype(jnp.bfloat16)
    grad_spre = (grad_act0.reshape(frames_in.shape).astype(jnp.float32) * silu_grad(pre_spatial)).astype(jnp.bfloat16)
    grad_frames = spatial_back(grad_spre, spatial_weight).astype(jnp.bfloat16)
    grad_spatial = spatial_wgrad(frames_in, grad_spre)
    scale = 1.0 / jnp.sqrt(jnp.float32(FRAMES * H * W))
    return (united.reshape(frames_in.shape), grad_frames, grad_spatial * scale, jnp.stack(tgrads) * scale, grad_uniting * scale)
```

```python
import functools

import jax
import jax.numpy as jnp
from jax import lax
from jax.experimental import pallas as pl
from jax.experimental.pallas import tpu as pltpu
from jax.sharding import PartitionSpec as P

LAYERS = 2
TAPS = 5
DMAX = 8
HALO = 2 * DMAX
AXES = ("seg", "grp")
BF16 = jnp.bfloat16
F32 = jnp.float32
VMEM_LIMIT = 48 * 1024 * 1024


def round_up(value, step):
    return -(-value // step) * step


def silu_parts(value):
    sigma = 0.5 * jnp.tanh(0.5 * value) + 0.5
    act = value * sigma
    return act, sigma + act * (1.0 - sigma)


def mm(left, right):
    return jnp.dot(left, right, preferred_element_type=F32)


def mm_nt(left, right):
    return lax.dot_general(left, right, (((1,), (1,)), ((), ())), preferred_element_type=F32)


def mm_tn(left, right):
    return lax.dot_general(left, right, (((0,), (0,)), ((), ())), preferred_element_type=F32)


def three_parts(value):
    high = value.astype(BF16)
    rest = value - high.astype(F32)
    middle = rest.astype(BF16)
    return high, middle, (rest - middle.astype(F32)).astype(BF16)


def call(kernel, outs, scratch, flops, moved, smem, args):
    specs = [pl.BlockSpec(memory_space=pltpu.SMEM)] * smem
    specs += [pl.BlockSpec(memory_space=pltpu.VMEM)] * (len(args) - smem)
    return pl.pallas_call(
        kernel,
        out_shape=[jax.ShapeDtypeStruct(shape, kind) for shape, kind in outs],
        in_specs=specs,
        out_specs=[pl.BlockSpec(memory_space=pltpu.VMEM)] * len(outs),
        scratch_shapes=scratch,
        compiler_params=pltpu.CompilerParams(vmem_limit_bytes=VMEM_LIMIT),
        cost_estimate=pl.CostEstimate(flops=flops, bytes_accessed=moved, transcendentals=0),
    )(*args)


def roll_rows(value, shift):
    return pltpu.roll(value, shift % value.shape[0], 0)


def spatial_fwd_kernel(rows_step, x_ref, w_ref, act_ref, slope_ref, xs):
    rows, cols, ch = x_ref.shape
    wide = xs.shape[1]
    xs[...] = jnp.zeros(xs.shape, xs.dtype)
    xs[1 : rows + 1, :cols, :] = x_ref[...]
    weight = jnp.concatenate(
        [jnp.concatenate([w_ref[3 * a + b] for b in range(3)], axis=1) for a in range(3)], axis=0
    )
    flat = rows_step * wide
    for step in range(rows // rows_step):
        at = step * rows_step
        left = jnp.concatenate(
            [xs[at + a : at + a + rows_step].reshape(flat, ch) for a in range(3)], axis=1
        )
        y = mm(left, weight)
        pre = y[:, ch : 2 * ch] + roll_rows(y[:, :ch], 1) + roll_rows(y[:, 2 * ch :], -1)
        act, slope = silu_parts(pre)
        act_ref[at : at + rows_step] = act.astype(BF16).reshape(rows_step, wide, ch)[:, :cols]
        slope_ref[at : at + rows_step] = slope.reshape(rows_step, wide, ch)


def spatial_bwd_kernel(rows_step, x_ref, w_ref, grad_ref, slope_ref, back_ref, wgrad_ref, gs):
    rows, cols, ch = x_ref.shape
    wide = gs.shape[1]
    gs[...] = jnp.zeros(gs.shape, gs.dtype)
    gs[1 : rows + 1, :cols, :] = (
        grad_ref[...].astype(F32) * slope_ref[:, :cols, :]
    ).astype(BF16)
    weight = jnp.concatenate(
        [
            jnp.concatenate([w_ref[3 * a + b].astype(F32).T.astype(BF16) for b in range(3)], axis=1)
            for a in range(3)
        ],
        axis=0,
    )
    flat = rows_step * wide
    pad = jnp.zeros((rows_step, wide - cols, ch), F32)
    total = jnp.zeros((3 * ch, 3 * ch), F32)
    for step in range(rows // rows_step):
        at = step * rows_step
        grads = jnp.concatenate(
            [gs[at + 2 - a : at + 2 - a + rows_step].reshape(flat, ch) for a in range(3)], axis=1
        )
        y = mm(grads, weight)
        back = y[:, ch : 2 * ch] + roll_rows(y[:, :ch], -1) + roll_rows(y[:, 2 * ch :], 1)
        back_ref[at : at + rows_step] = back.astype(BF16).reshape(rows_step, wide, ch)[:, :cols]
        x = jnp.concatenate([x_ref[at : at + rows_step].astype(F32), pad], axis=1).reshape(flat, ch)
        x_cat = jnp.concatenate([roll_rows(x, 1), x, roll_rows(x, -1)], axis=1).astype(BF16)
        total = total + mm_tn(x_cat, grads)
    for a in range(3):
        for b in range(3):
            wgrad_ref[3 * a + b] = total[b * ch : (b + 1) * ch, a * ch : (a + 1) * ch]


def fill_frames(pad_ref, value_ref):
    frames, block, ch = value_ref.shape
    pad_ref[...] = jnp.zeros(pad_ref.shape, pad_ref.dtype)
    pad_ref[HALO : HALO + frames, :block, :] = value_ref[...]


def clear_halo(pad_ref, frames):
    zeros = jnp.zeros((HALO,) + pad_ref.shape[1:], pad_ref.dtype)
    pad_ref[:HALO] = zeros
    pad_ref[HALO + frames :] = zeros


def taps_of(pad_ref, at, count, step_size, sign):
    high, ch = pad_ref.shape[1:]
    pieces = [
        pad_ref[pl.ds(HALO + at + sign * (k - 2) * step_size, count)].reshape(count * high, ch)
        for k in range(TAPS)
    ]
    return jnp.concatenate(pieces, axis=1)


def temporal_fwd_kernel(
    step_frames, dil_ref, key_ref, act_ref, tw_ref, uw_ref,
    united_ref, a0, a1, feat, slope0, slope1,
):
    frames, block, ch = act_ref.shape
    high = a0.shape[1]
    fill_frames(a0, act_ref)
    clear_halo(a1, frames)
    for layer, (source, target, slopes) in enumerate(((a0, a1, slope0), (a1, feat, slope1))):
        step_size = dil_ref[layer]
        weight = jnp.concatenate([tw_ref[layer, k] for k in range(TAPS)], axis=0)
        first = HALO if layer == 0 else 0
        for at in range(0, frames, step_frames):
            pre = mm(taps_of(source, at, step_frames, step_size, 1), weight)
            act, slope = silu_parts(pre)
            target[first + at : first + at + step_frames] = act.astype(BF16).reshape(
                step_frames, high, ch
            )
            slopes[at : at + step_frames] = slope.reshape(step_frames, high, ch)
    segs = key_ref.shape[0]
    seg_frames = frames // segs
    for seg in range(segs):
        key_part = mm(feat[seg * seg_frames + key_ref[seg]], uw_ref[1])
        main = mm(
            feat[seg * seg_frames : (seg + 1) * seg_frames].reshape(seg_frames * high, ch), uw_ref[0]
        ).reshape(seg_frames, high, ch)
        united_ref[seg * seg_frames : (seg + 1) * seg_frames] = (main + key_part[None]).astype(BF16)[
            :, :block
        ]


def temporal_bwd_kernel(
    step_frames, dil_ref, key_ref, cot_ref, tw_ref, uw_ref, slope0, slope1,
    grad_ref, cots, g0, g1, seg_cot, grad_feat,
):
    frames, block, ch = cot_ref.shape
    high = cots.shape[1]
    segs = key_ref.shape[0]
    seg_frames = frames // segs
    cots[...] = jnp.zeros(cots.shape, cots.dtype)
    cots[:, :block, :] = cot_ref[...]
    clear_halo(g0, frames)
    clear_halo(g1, frames)
    for seg in range(segs):
        low, top = seg * seg_frames, (seg + 1) * seg_frames
        mine = cots[low:top]
        total = jnp.sum(mine.astype(F32), axis=0)
        seg_cot[seg] = total
        grad_feat[low:top] = mm_nt(mine.reshape(seg_frames * high, ch), uw_ref[0]).reshape(
            seg_frames, high, ch
        )
        key_term = sum(mm_nt(part, uw_ref[1]) for part in three_parts(total))
        here = low + key_ref[seg]
        grad_feat[here] = grad_feat[here] + key_term
        g1[HALO + low : HALO + top] = (grad_feat[low:top] * slope1[low:top]).astype(BF16)
    for layer, source in ((1, g1), (0, g0)):
        step_size = dil_ref[layer]
        weight = jnp.concatenate([tw_ref[layer, k].astype(F32).T.astype(BF16) for k in range(TAPS)], axis=0)
        for at in range(0, frames, step_frames):
            grad = mm(taps_of(source, at, step_frames, step_size, -1), weight).reshape(
                step_frames, high, ch
            )
            if layer == 1:
                g0[HALO + at : HALO + at + step_frames] = (
                    grad * slope0[at : at + step_frames]
                ).astype(BF16)
            else:
                grad_ref[at : at + step_frames] = grad.astype(BF16)[:, :block]


def temporal_wgrad_kernel(
    step_frames, dil_ref, key_ref, a0, a1, feat, g0, g1, cots, seg_cot, out_ref
):
    frames, high, ch = feat.shape
    segs = key_ref.shape[0]
    seg_frames = frames // segs
    rows = step_frames * high
    for layer, acts, grads in ((0, a0, g0), (1, a1, g1)):
        total = jnp.zeros((TAPS * ch, ch), F32)
        for at in range(0, frames, step_frames):
            total = total + mm_tn(
                taps_of(acts, at, step_frames, dil_ref[layer], 1),
                grads[HALO + at : HALO + at + step_frames].reshape(rows, ch),
            )
        out_ref[layer * TAPS : (layer + 1) * TAPS] = total.reshape(TAPS, ch, ch).astype(out_ref.dtype)
    total = jnp.zeros((ch, ch), F32)
    for at in range(0, frames, step_frames):
        total = total + mm_tn(
            feat[at : at + step_frames].reshape(rows, ch),
            cots[at : at + step_frames].reshape(rows, ch),
        )
    out_ref[LAYERS * TAPS] = total.astype(out_ref.dtype)
    total = jnp.zeros((ch, ch), F32)
    for seg in range(segs):
        key = feat[seg * seg_frames + key_ref[seg]]
        total = total + sum(mm_tn(key, part) for part in three_parts(seg_cot[seg]))
    out_ref[LAYERS * TAPS + 1] = total.astype(out_ref.dtype)


def exchange(blocks):
    return lax.all_to_all(blocks, AXES, split_axis=0, concat_axis=0, tiled=True)


def reduce_everywhere(parts, devices):
    count, ch, _ = parts.shape
    pieces = exchange(parts.astype(BF16).reshape(devices, count * ch // devices, ch))
    mine = jnp.sum(pieces.astype(F32), axis=0)
    return lax.all_gather(mine, AXES, axis=0, tiled=True).reshape(count, ch, ch)


def local(
    frames_in, spatial_weight, temporal_weight, uniting_weight, key_index, dilation, cotangent
):
    held, rows, cols, ch = frames_in.shape
    pixels = rows * cols
    devices = lax.axis_size("seg") * lax.axis_size("grp")
    frames = held * devices
    block = pixels // devices
    wide = round_up(cols + 1, 16)
    high = round_up(block, 16)
    rows_step = next(n for n in (4, 2, 1) if rows % n == 0)
    step_frames = max(n for n in range(1, frames + 1) if frames % n == 0 and n * high <= 512)

    def to_pixels(values):
        split = values.reshape(held, devices, block, ch).swapaxes(0, 1)
        return exchange(split.reshape(devices * held, block, ch))

    def to_frames(blocks):
        got = exchange(blocks).reshape(devices, held, block, ch).swapaxes(0, 1)
        return got.reshape(held, rows, cols, ch)

    cot_blocks = to_pixels(cotangent)

    spatial = [
        call(
            functools.partial(spatial_fwd_kernel, rows_step),
            [((rows, cols, ch), BF16), ((rows, wide, ch), F32)],
            [pltpu.VMEM((rows + 2, wide, ch), BF16)],
            2 * 9 * pixels * ch * ch,
            pixels * ch * 8,
            0,
            (frames_in[i], spatial_weight),
        )
        for i in range(held)
    ]
    act_blocks = to_pixels(jnp.stack([act for act, _ in spatial]))

    padded = ((frames + 2 * HALO, high, ch), BF16)
    whole = (frames, high, ch)
    united_blocks, a0, a1, feat, slope0, slope1 = call(
        functools.partial(temporal_fwd_kernel, step_frames),
        [((frames, block, ch), BF16), padded, padded, (whole, BF16), (whole, F32), (whole, F32)],
        [],
        2 * 11 * frames * block * ch * ch,
        frames * block * ch * 18,
        2,
        (dilation, key_index, act_blocks, temporal_weight, uniting_weight),
    )
    grad_blocks, cots, g0, g1, seg_cot = call(
        functools.partial(temporal_bwd_kernel, step_frames),
        [
            ((frames, block, ch), BF16),
            (whole, BF16),
            padded,
            padded,
            ((key_index.shape[0], high, ch), F32),
        ],
        [pltpu.VMEM(whole, F32)],
        2 * 11 * frames * block * ch * ch,
        frames * block * ch * 18,
        2,
        (dilation, key_index, cot_blocks, temporal_weight, uniting_weight, slope0, slope1),
    )
    grad_time = to_frames(grad_blocks)
    united = to_frames(united_blocks)
    (tgrads,) = call(
        functools.partial(temporal_wgrad_kernel, step_frames),
        [((LAYERS * TAPS + 2, ch, ch), F32)],
        [],
        2 * 12 * frames * block * ch * ch,
        frames * block * ch * 14,
        2,
        (dilation, key_index, a0, a1, feat, g0, g1, cots, seg_cot),
    )
    back = [
        call(
            functools.partial(spatial_bwd_kernel, rows_step),
            [((rows, cols, ch), BF16), ((9, ch, ch), F32)],
            [pltpu.VMEM((rows + 2, wide, ch), BF16)],
            2 * 18 * pixels * ch * ch,
            pixels * ch * 10,
            0,
            (frames_in[i], spatial_weight, grad_time[i], spatial[i][1]),
        )
        for i in range(held)
    ]
    scale = 1.0 / jnp.sqrt(jnp.float32(frames * pixels))
    summed_time = reduce_everywhere(tgrads, devices) * scale
    summed_space = reduce_everywhere(sum(grad for _, grad in back), devices) * scale
    return (
        united,
        jnp.stack([grad for grad, _ in back]),
        summed_space,
        summed_time[: LAYERS * TAPS].reshape(LAYERS, TAPS, ch, ch),
        summed_time[LAYERS * TAPS :],
    )


def solution(mesh):
    frame_spec = P(AXES, None, None, None)
    return jax.shard_map(
        local,
        mesh=mesh,
        in_specs=(frame_spec, P(), P(), P(), P(), P(), frame_spec),
        out_specs=(frame_spec, frame_spec, P(), P(), P()),
        check_vma=False,
    )
```

```python
import functools

import jax
import jax.numpy as jnp
from jax import lax
from jax.experimental import pallas as pl
from jax.experimental.pallas import tpu as pltpu
from jax.sharding import PartitionSpec as P

LAYERS = 2
TAPS = 5
DMAX = 8
HALO = 2 * DMAX
AXES = ("seg", "grp")
BF16 = jnp.bfloat16
F32 = jnp.float32
VMEM_LIMIT = 48 * 1024 * 1024


def round_up(value, step):
    return -(-value // step) * step


def silu_parts(value):
    sigma = 0.5 * jnp.tanh(0.5 * value) + 0.5
    act = value * sigma
    return act, sigma + act * (1.0 - sigma)


def mm(left, right):
    return jnp.dot(left, right, preferred_element_type=F32)


def mm_nt(left, right):
    return lax.dot_general(left, right, (((1,), (1,)), ((), ())), preferred_element_type=F32)


def mm_tn(left, right):
    return lax.dot_general(left, right, (((0,), (0,)), ((), ())), preferred_element_type=F32)


def three_parts(value):
    high = value.astype(BF16)
    rest = value - high.astype(F32)
    middle = rest.astype(BF16)
    return high, middle, (rest - middle.astype(F32)).astype(BF16)


def call(kernel, outs, scratch, flops, moved, smem, args):
    specs = [pl.BlockSpec(memory_space=pltpu.SMEM)] * smem
    specs += [pl.BlockSpec(memory_space=pltpu.VMEM)] * (len(args) - smem)
    return pl.pallas_call(
        kernel,
        out_shape=[jax.ShapeDtypeStruct(shape, kind) for shape, kind in outs],
        in_specs=specs,
        out_specs=[pl.BlockSpec(memory_space=pltpu.VMEM)] * len(outs),
        scratch_shapes=scratch,
        compiler_params=pltpu.CompilerParams(vmem_limit_bytes=VMEM_LIMIT),
        cost_estimate=pl.CostEstimate(flops=flops, bytes_accessed=moved, transcendentals=0),
    )(*args)


def roll_rows(value, shift):
    return pltpu.roll(value, shift % value.shape[0], 0)


def spatial_fwd_kernel(rows_step, x_ref, w_ref, act_ref, slope_ref, xs):
    rows, cols, ch = x_ref.shape
    wide = xs.shape[1]
    xs[...] = jnp.zeros(xs.shape, xs.dtype)
    xs[1 : rows + 1, :cols, :] = x_ref[...]
    weight = jnp.concatenate(
        [jnp.concatenate([w_ref[3 * a + b] for b in range(3)], axis=1) for a in range(3)], axis=0
    )
    flat = rows_step * wide
    for step in range(rows // rows_step):
        at = step * rows_step
        left = jnp.concatenate(
            [xs[at + a : at + a + rows_step].reshape(flat, ch) for a in range(3)], axis=1
        )
        y = mm(left, weight)
        pre = y[:, ch : 2 * ch] + roll_rows(y[:, :ch], 1) + roll_rows(y[:, 2 * ch :], -1)
        act, slope = silu_parts(pre)
        act_ref[at : at + rows_step] = act.astype(BF16).reshape(rows_step, wide, ch)[:, :cols]
        slope_ref[at : at + rows_step] = slope.reshape(rows_step, wide, ch)


def spatial_bwd_kernel(rows_step, x_ref, w_ref, grad_ref, slope_ref, back_ref, wgrad_ref, gs):
    rows, cols, ch = x_ref.shape
    wide = gs.shape[1]
    gs[...] = jnp.zeros(gs.shape, gs.dtype)
    gs[1 : rows + 1, :cols, :] = (
        grad_ref[...].astype(F32) * slope_ref[:, :cols, :]
    ).astype(BF16)
    weight = jnp.concatenate(
        [
            jnp.concatenate([w_ref[3 * a + b].astype(F32).T.astype(BF16) for b in range(3)], axis=1)
            for a in range(3)
        ],
        axis=0,
    )
    flat = rows_step * wide
    pad = jnp.zeros((rows_step, wide - cols, ch), F32)
    total = jnp.zeros((3 * ch, 3 * ch), F32)
    for step in range(rows // rows_step):
        at = step * rows_step
        grads = jnp.concatenate(
            [gs[at + 2 - a : at + 2 - a + rows_step].reshape(flat, ch) for a in range(3)], axis=1
        )
        y = mm(grads, weight)
        back = y[:, ch : 2 * ch] + roll_rows(y[:, :ch], -1) + roll_rows(y[:, 2 * ch :], 1)
        back_ref[at : at + rows_step] = back.astype(BF16).reshape(rows_step, wide, ch)[:, :cols]
        x = jnp.concatenate([x_ref[at : at + rows_step].astype(F32), pad], axis=1).reshape(flat, ch)
        x_cat = jnp.concatenate([roll_rows(x, 1), x, roll_rows(x, -1)], axis=1).astype(BF16)
        total = total + mm_tn(x_cat, grads)
    for a in range(3):
        for b in range(3):
            wgrad_ref[3 * a + b] = total[b * ch : (b + 1) * ch, a * ch : (a + 1) * ch]


def fill_frames(pad_ref, value_ref):
    frames, block, ch = value_ref.shape
    pad_ref[...] = jnp.zeros(pad_ref.shape, pad_ref.dtype)
    pad_ref[HALO : HALO + frames, :block, :] = value_ref[...]


def place_of(here_ref, turns, peers, turn, peer):
    return lax.rem(here_ref[0] + (turns - turn), turns) * peers + jnp.bitwise_xor(here_ref[1], peer)


def order_kernel(here_ref, got_ref, out_ref):
    peers, turns = got_ref.shape[:2]
    for peer in range(peers):
        for turn in range(turns):
            out_ref[place_of(here_ref, turns, peers, turn, peer)] = got_ref[peer, turn]


def clear_halo(pad_ref, frames):
    zeros = jnp.zeros((HALO,) + pad_ref.shape[1:], pad_ref.dtype)
    pad_ref[:HALO] = zeros
    pad_ref[HALO + frames :] = zeros


def taps_of(pad_ref, at, count, step_size, sign):
    high, ch = pad_ref.shape[1:]
    pieces = [
        pad_ref[pl.ds(HALO + at + sign * (k - 2) * step_size, count)].reshape(count * high, ch)
        for k in range(TAPS)
    ]
    return jnp.concatenate(pieces, axis=1)


def temporal_fwd_kernel(
    step_frames, dil_ref, key_ref, act_ref, tw_ref, uw_ref,
    united_ref, a0, a1, feat, slope0, slope1,
):
    frames, block, ch = act_ref.shape
    high = a0.shape[1]
    fill_frames(a0, act_ref)
    clear_halo(a1, frames)
    for layer, (source, target, slopes) in enumerate(((a0, a1, slope0), (a1, feat, slope1))):
        step_size = dil_ref[layer]
        weight = jnp.concatenate([tw_ref[layer, k] for k in range(TAPS)], axis=0)
        first = HALO if layer == 0 else 0
        for at in range(0, frames, step_frames):
            pre = mm(taps_of(source, at, step_frames, step_size, 1), weight)
            act, slope = silu_parts(pre)
            target[first + at : first + at + step_frames] = act.astype(BF16).reshape(
                step_frames, high, ch
            )
            slopes[at : at + step_frames] = slope.reshape(step_frames, high, ch)
    segs = key_ref.shape[0]
    seg_frames = frames // segs
    for seg in range(segs):
        key_part = mm(feat[seg * seg_frames + key_ref[seg]], uw_ref[1])
        main = mm(
            feat[seg * seg_frames : (seg + 1) * seg_frames].reshape(seg_frames * high, ch), uw_ref[0]
        ).reshape(seg_frames, high, ch)
        united_ref[seg * seg_frames : (seg + 1) * seg_frames] = (main + key_part[None]).astype(BF16)[
            :, :block
        ]


def temporal_bwd_kernel(
    step_frames, here_ref, dil_ref, key_ref, cot_ref, tw_ref, uw_ref, slope0, slope1,
    grad_ref, cots, g0, g1, seg_cot, grad_feat,
):
    turns, peers, block, ch = cot_ref.shape
    frames, high, _ = cots.shape
    segs = key_ref.shape[0]
    seg_frames = frames // segs
    cots[...] = jnp.zeros(cots.shape, cots.dtype)
    for turn in range(turns):
        for peer in range(peers):
            cots[place_of(here_ref, turns, peers, turn, peer), :block, :] = cot_ref[turn, peer]
    clear_halo(g0, frames)
    clear_halo(g1, frames)
    for seg in range(segs):
        low, top = seg * seg_frames, (seg + 1) * seg_frames
        mine = cots[low:top]
        total = jnp.sum(mine.astype(F32), axis=0)
        seg_cot[seg] = total
        grad_feat[low:top] = mm_nt(mine.reshape(seg_frames * high, ch), uw_ref[0]).reshape(
            seg_frames, high, ch
        )
        key_term = sum(mm_nt(part, uw_ref[1]) for part in three_parts(total))
        here = low + key_ref[seg]
        grad_feat[here] = grad_feat[here] + key_term
        g1[HALO + low : HALO + top] = (grad_feat[low:top] * slope1[low:top]).astype(BF16)
    for layer, source in ((1, g1), (0, g0)):
        step_size = dil_ref[layer]
        weight = jnp.concatenate([tw_ref[layer, k].astype(F32).T.astype(BF16) for k in range(TAPS)], axis=0)
        for at in range(0, frames, step_frames):
            grad = mm(taps_of(source, at, step_frames, step_size, -1), weight).reshape(
                step_frames, high, ch
            )
            if layer == 1:
                g0[HALO + at : HALO + at + step_frames] = (
                    grad * slope0[at : at + step_frames]
                ).astype(BF16)
            else:
                grad_ref[at : at + step_frames] = grad.astype(BF16)[:, :block]


def temporal_wgrad_kernel(
    step_frames, dil_ref, key_ref, a0, a1, feat, g0, g1, cots, seg_cot, out_ref
):
    frames, high, ch = feat.shape
    segs = key_ref.shape[0]
    seg_frames = frames // segs
    rows = step_frames * high
    for layer, acts, grads in ((0, a0, g0), (1, a1, g1)):
        total = jnp.zeros((TAPS * ch, ch), F32)
        for at in range(0, frames, step_frames):
            total = total + mm_tn(
                taps_of(acts, at, step_frames, dil_ref[layer], 1),
                grads[HALO + at : HALO + at + step_frames].reshape(rows, ch),
            )
        out_ref[layer * TAPS : (layer + 1) * TAPS] = total.reshape(TAPS, ch, ch).astype(out_ref.dtype)
    total = jnp.zeros((ch, ch), F32)
    for at in range(0, frames, step_frames):
        total = total + mm_tn(
            feat[at : at + step_frames].reshape(rows, ch),
            cots[at : at + step_frames].reshape(rows, ch),
        )
    out_ref[LAYERS * TAPS] = total.astype(out_ref.dtype)
    total = jnp.zeros((ch, ch), F32)
    for seg in range(segs):
        key = feat[seg * seg_frames + key_ref[seg]]
        total = total + sum(mm_tn(key, part) for part in three_parts(seg_cot[seg]))
    out_ref[LAYERS * TAPS + 1] = total.astype(out_ref.dtype)


def exchange(blocks):
    return lax.all_to_all(blocks, AXES, split_axis=0, concat_axis=0, tiled=True)


def reduce_everywhere(parts, devices):
    count, ch, _ = parts.shape
    pieces = exchange(parts.astype(BF16).reshape(devices, count * ch // devices, ch))
    mine = jnp.sum(pieces.astype(F32), axis=0).astype(BF16)
    return exchange(jnp.broadcast_to(mine, pieces.shape)).reshape(count, ch, ch).astype(F32)


def flip(value, peer):
    size = lax.axis_size("grp")
    return lax.ppermute(value, "grp", [(i, i ^ peer) for i in range(size)])


def turn_by(value, turn):
    size = lax.axis_size("seg")
    return lax.ppermute(value, "seg", [(i, (i + turn) % size) for i in range(size)])


def pick(values, index):
    return lax.dynamic_index_in_dim(values, index, 0, keepdims=False)


def spread_grp_first(values):
    turns, peers = values.shape[:2]
    seg, grp = lax.axis_index("seg"), lax.axis_index("grp")
    near = []
    for peer in range(peers):
        mine = lax.dynamic_index_in_dim(values, grp ^ peer, 1, keepdims=False)
        near.append(flip(mine, peer) if peer else mine)
    far = []
    for turn in range(turns):
        mine = jnp.stack([pick(part, lax.rem(seg + turn, turns)) for part in near])
        far.append(turn_by(mine, turn) if turn else mine)
    return jnp.stack(far)


def spread_seg_first(values):
    turns, peers = values.shape[:2]
    seg, grp = lax.axis_index("seg"), lax.axis_index("grp")
    far = []
    for turn in range(turns):
        mine = pick(values, lax.rem(seg + turn, turns))
        far.append(turn_by(mine, turn) if turn else mine)
    near = []
    for peer in range(peers):
        mine = jnp.stack([pick(part, grp ^ peer) for part in far])
        near.append(flip(mine, peer) if peer else mine)
    return jnp.stack(near)


def local(
    frames_in, spatial_weight, temporal_weight, uniting_weight, key_index, dilation, cotangent
):
    held, rows, cols, ch = frames_in.shape
    pixels = rows * cols
    devices = lax.axis_size("seg") * lax.axis_size("grp")
    frames = held * devices
    block = pixels // devices
    wide = round_up(cols + 1, 16)
    high = round_up(block, 16)
    rows_step = next(n for n in (4, 2, 1) if rows % n == 0)
    step_frames = max(n for n in range(1, frames + 1) if frames % n == 0 and n * high <= 512)

    def to_pixels(values):
        split = values.reshape(held, devices, block, ch).swapaxes(0, 1)
        return exchange(split.reshape(devices * held, block, ch))

    def to_frames(blocks):
        got = exchange(blocks).reshape(devices, held, block, ch).swapaxes(0, 1)
        return got.reshape(held, rows, cols, ch)

    segs, peers = lax.axis_size("seg"), lax.axis_size("grp")
    here = jnp.stack([lax.axis_index("seg"), lax.axis_index("grp")]).astype(jnp.int32)
    cot_blocks = spread_grp_first(cotangent.reshape(segs, peers, block, ch))

    spatial = [
        call(
            functools.partial(spatial_fwd_kernel, rows_step),
            [((rows, cols, ch), BF16), ((rows, wide, ch), F32)],
            [pltpu.VMEM((rows + 2, wide, ch), BF16)],
            2 * 9 * pixels * ch * ch,
            pixels * ch * 8,
            0,
            (frames_in[i], spatial_weight),
        )
        for i in range(held)
    ]
    act_blocks = to_pixels(jnp.stack([act for act, _ in spatial]))

    padded = ((frames + 2 * HALO, high, ch), BF16)
    whole = (frames, high, ch)
    united_blocks, a0, a1, feat, slope0, slope1 = call(
        functools.partial(temporal_fwd_kernel, step_frames),
        [((frames, block, ch), BF16), padded, padded, (whole, BF16), (whole, F32), (whole, F32)],
        [],
        2 * 11 * frames * block * ch * ch,
        frames * block * ch * 18,
        2,
        (dilation, key_index, act_blocks, temporal_weight, uniting_weight),
    )
    grad_blocks, cots, g0, g1, seg_cot = call(
        functools.partial(temporal_bwd_kernel, step_frames),
        [
            ((frames, block, ch), BF16),
            (whole, BF16),
            padded,
            padded,
            ((key_index.shape[0], high, ch), F32),
        ],
        [pltpu.VMEM(whole, F32)],
        2 * 11 * frames * block * ch * ch,
        frames * block * ch * 18,
        3,
        (here, dilation, key_index, cot_blocks, temporal_weight, uniting_weight, slope0, slope1),
    )
    grad_time = to_frames(grad_blocks)
    (united,) = call(
        order_kernel,
        [((devices, block, ch), BF16)],
        [],
        0,
        pixels * ch * 4,
        1,
        (here, spread_seg_first(united_blocks.reshape(segs, peers, block, ch))),
    )
    (tgrads,) = call(
        functools.partial(temporal_wgrad_kernel, step_frames),
        [((LAYERS * TAPS + 2, ch, ch), F32)],
        [],
        2 * 12 * frames * block * ch * ch,
        frames * block * ch * 14,
        2,
        (dilation, key_index, a0, a1, feat, g0, g1, cots, seg_cot),
    )
    back = [
        call(
            functools.partial(spatial_bwd_kernel, rows_step),
            [((rows, cols, ch), BF16), ((9, ch, ch), F32)],
            [pltpu.VMEM((rows + 2, wide, ch), BF16)],
            2 * 18 * pixels * ch * ch,
            pixels * ch * 10,
            0,
            (frames_in[i], spatial_weight, grad_time[i], spatial[i][1]),
        )
        for i in range(held)
    ]
    scale = 1.0 / jnp.sqrt(jnp.float32(frames * pixels))
    space_grads = sum(grad for _, grad in back)
    summed = reduce_everywhere(jnp.concatenate([space_grads, tgrads]), devices) * scale
    return (
        united.reshape(frames_in.shape),
        jnp.stack([grad for grad, _ in back]),
        summed[:9],
        summed[9 : 9 + LAYERS * TAPS].reshape(LAYERS, TAPS, ch, ch),
        summed[9 + LAYERS * TAPS :],
    )


def solution(mesh):
    frame_spec = P(AXES, None, None, None)
    return jax.shard_map(
        local,
        mesh=mesh,
        in_specs=(frame_spec, P(), P(), P(), P(), P(), frame_spec),
        out_specs=(frame_spec, frame_spec, P(), P(), P()),
        check_vma=False,
    )
```

```python
import functools

import jax
import jax.numpy as jnp
from jax import lax
from jax.experimental import pallas as pl
from jax.experimental.pallas import tpu as pltpu
from jax.sharding import PartitionSpec as P

LAYERS = 2
TAPS = 5
DMAX = 8
HALO = 2 * DMAX
AXES = ("seg", "grp")
BF16 = jnp.bfloat16
F32 = jnp.float32
VMEM_LIMIT = 32 * 1024 * 1024


def round_up(value, step):
    return -(-value // step) * step


def silu_parts(value):
    sigma = 0.5 * jnp.tanh(0.5 * value) + 0.5
    act = value * sigma
    return act, sigma + act * (1.0 - sigma)


def mm(left, right):
    return jnp.dot(left, right, preferred_element_type=F32)


def mm_nt(left, right):
    return lax.dot_general(left, right, (((1,), (1,)), ((), ())), preferred_element_type=F32)


def mm_tn(left, right):
    return lax.dot_general(left, right, (((0,), (0,)), ((), ())), preferred_element_type=F32)


def three_parts(value):
    high = value.astype(BF16)
    rest = value - high.astype(F32)
    middle = rest.astype(BF16)
    return high, middle, (rest - middle.astype(F32)).astype(BF16)


def call(kernel, outs, scratch, flops, moved, smem, args):
    specs = [pl.BlockSpec(memory_space=pltpu.SMEM)] * smem
    specs += [pl.BlockSpec(memory_space=pltpu.VMEM)] * (len(args) - smem)
    return pl.pallas_call(
        kernel,
        out_shape=[jax.ShapeDtypeStruct(shape, kind) for shape, kind in outs],
        in_specs=specs,
        out_specs=[pl.BlockSpec(memory_space=pltpu.VMEM)] * len(outs),
        scratch_shapes=scratch,
        compiler_params=pltpu.CompilerParams(vmem_limit_bytes=VMEM_LIMIT),
        cost_estimate=pl.CostEstimate(flops=flops, bytes_accessed=moved, transcendentals=0),
    )(*args)


def roll_rows(value, shift):
    return pltpu.roll(value, shift % value.shape[0], 0)


def spatial_fwd_kernel(rows_step, x_ref, w_ref, cot_ref, send_ref, slope_ref, xs):
    rows, cols, ch = x_ref.shape
    wide = xs.shape[1]
    send_ref[:, 1] = cot_ref[...]
    xs[...] = jnp.zeros(xs.shape, xs.dtype)
    xs[1 : rows + 1, :cols, :] = x_ref[...]
    weight = jnp.concatenate(
        [jnp.concatenate([w_ref[3 * a + b] for b in range(3)], axis=1) for a in range(3)], axis=0
    )
    flat = rows_step * wide
    for step in range(rows // rows_step):
        at = step * rows_step
        left = jnp.concatenate(
            [xs[at + a : at + a + rows_step].reshape(flat, ch) for a in range(3)], axis=1
        )
        y = mm(left, weight)
        pre = y[:, ch : 2 * ch] + roll_rows(y[:, :ch], 1) + roll_rows(y[:, 2 * ch :], -1)
        act, slope = silu_parts(pre)
        send_ref[at : at + rows_step, 0] = act.astype(BF16).reshape(rows_step, wide, ch)[:, :cols]
        slope_ref[at : at + rows_step] = slope.reshape(rows_step, wide, ch)


def columns_kernel(rows_step, x_ref, cat_ref):
    rows, cols, ch = x_ref.shape
    wide = cat_ref.shape[0] // rows
    flat = rows_step * wide
    pad = jnp.zeros((rows_step, wide - cols, ch), F32)
    for at in range(0, rows, rows_step):
        x = jnp.concatenate([x_ref[at : at + rows_step].astype(F32), pad], axis=1).reshape(flat, ch)
        x_cat = jnp.concatenate([roll_rows(x, 1), x, roll_rows(x, -1)], axis=1)
        cat_ref[at * wide : at * wide + flat] = x_cat.astype(BF16)


def taps_up(gs, at, rows_step):
    wide, ch = gs.shape[1:]
    return jnp.concatenate(
        [gs[at + 2 - a : at + 2 - a + rows_step].reshape(rows_step * wide, ch) for a in range(3)],
        axis=1,
    )


def spatial_wgrad_kernel(rows_step, scale, got_ref, slope_ref, cat_ref, gs, united_ref, wgrad_ref):
    rows, _, cols, ch = got_ref.shape
    wide = gs.shape[1]
    gs[...] = jnp.zeros(gs.shape, gs.dtype)
    gs[1 : rows + 1, :cols, :] = (
        got_ref[:, 0].astype(F32) * slope_ref[:, :cols, :]
    ).astype(BF16)
    flat = rows_step * wide
    total = jnp.zeros((3 * ch, 3 * ch), F32)
    for at in range(0, rows, rows_step):
        total = total + mm_tn(cat_ref[at * wide : at * wide + flat], taps_up(gs, at, rows_step))
    for a in range(3):
        for b in range(3):
            piece = total[b * ch : (b + 1) * ch, a * ch : (a + 1) * ch] * scale
            wgrad_ref[3 * a + b] = piece.astype(wgrad_ref.dtype)
    united_ref[...] = got_ref[:, 1]


def spatial_back_kernel(rows_step, w_ref, gs, back_ref):
    rows, cols, ch = back_ref.shape
    wide = gs.shape[1]
    weight = jnp.concatenate(
        [
            jnp.concatenate([w_ref[3 * a + b].astype(F32).T.astype(BF16) for b in range(3)], axis=1)
            for a in range(3)
        ],
        axis=0,
    )
    for at in range(0, rows, rows_step):
        y = mm(taps_up(gs, at, rows_step), weight)
        back = y[:, ch : 2 * ch] + roll_rows(y[:, :ch], -1) + roll_rows(y[:, 2 * ch :], 1)
        back_ref[at : at + rows_step] = back.astype(BF16).reshape(rows_step, wide, ch)[:, :cols]


def clear_halo(pad_ref, frames):
    zeros = jnp.zeros((HALO,) + pad_ref.shape[1:], pad_ref.dtype)
    pad_ref[:HALO] = zeros
    pad_ref[HALO + frames :] = zeros


def taps_of(pad_ref, at, count, step_size, sign):
    high, ch = pad_ref.shape[1:]
    pieces = [
        pad_ref[pl.ds(HALO + at + sign * (k - 2) * step_size, count)].reshape(count * high, ch)
        for k in range(TAPS)
    ]
    return jnp.concatenate(pieces, axis=1)


def temporal_kernel(
    step_frames, dil_ref, key_ref, got_ref, tw_ref, uw_ref,
    send_ref, a0, a1, feat, cots, g0, g1, seg_cot, slope0, slope1, grad_feat,
):
    frames, _, block, ch = got_ref.shape
    high = feat.shape[1]
    segs = key_ref.shape[0]
    seg_frames = frames // segs
    for ref in (a0, a1, g0, g1):
        clear_halo(ref, frames)
    a0[HALO : HALO + frames] = jnp.zeros((frames, high, ch), BF16)
    a0[HALO : HALO + frames, :block, :] = got_ref[:, 0]
    cots[...] = jnp.zeros(cots.shape, cots.dtype)
    cots[:, :block, :] = got_ref[:, 1]
    for layer, (source, target, slopes) in enumerate(((a0, a1, slope0), (a1, feat, slope1))):
        step_size = dil_ref[layer]
        weight = jnp.concatenate([tw_ref[layer, k] for k in range(TAPS)], axis=0)
        first = HALO if layer == 0 else 0
        for at in range(0, frames, step_frames):
            pre = mm(taps_of(source, at, step_frames, step_size, 1), weight)
            act, slope = silu_parts(pre)
            target[first + at : first + at + step_frames] = act.astype(BF16).reshape(
                step_frames, high, ch
            )
            slopes[at : at + step_frames] = slope.reshape(step_frames, high, ch)
    for seg in range(segs):
        low, top = seg * seg_frames, (seg + 1) * seg_frames
        here = low + key_ref[seg]
        key_part = mm(feat[here], uw_ref[1])
        main = mm(feat[low:top].reshape(seg_frames * high, ch), uw_ref[0]).reshape(
            seg_frames, high, ch
        )
        send_ref[low:top, 1] = (main + key_part[None]).astype(BF16)[:, :block]
        mine = cots[low:top]
        total = jnp.sum(mine.astype(F32), axis=0)
        seg_cot[seg] = total
        grad_feat[low:top] = mm_nt(mine.reshape(seg_frames * high, ch), uw_ref[0]).reshape(
            seg_frames, high, ch
        )
        key_term = sum(mm_nt(part, uw_ref[1]) for part in three_parts(total))
        grad_feat[here] = grad_feat[here] + key_term
        g1[HALO + low : HALO + top] = (grad_feat[low:top] * slope1[low:top]).astype(BF16)
    for layer, source in ((1, g1), (0, g0)):
        step_size = dil_ref[layer]
        weight = jnp.concatenate(
            [tw_ref[layer, k].astype(F32).T.astype(BF16) for k in range(TAPS)], axis=0
        )
        for at in range(0, frames, step_frames):
            grad = mm(taps_of(source, at, step_frames, step_size, -1), weight).reshape(
                step_frames, high, ch
            )
            if layer == 1:
                g0[HALO + at : HALO + at + step_frames] = (
                    grad * slope0[at : at + step_frames]
                ).astype(BF16)
            else:
                send_ref[at : at + step_frames, 0] = grad.astype(BF16)[:, :block]


def temporal_wgrad_kernel(
    step_frames, scale, dil_ref, key_ref, a0, a1, feat, g0, g1, cots, seg_cot, out_ref
):
    frames, high, ch = feat.shape
    segs = key_ref.shape[0]
    seg_frames = frames // segs
    rows = step_frames * high
    for layer, acts, grads in ((0, a0, g0), (1, a1, g1)):
        total = jnp.zeros((TAPS * ch, ch), F32)
        for at in range(0, frames, step_frames):
            total = total + mm_tn(
                taps_of(acts, at, step_frames, dil_ref[layer], 1),
                grads[HALO + at : HALO + at + step_frames].reshape(rows, ch),
            )
        out_ref[layer * TAPS : (layer + 1) * TAPS] = total.reshape(TAPS, ch, ch) * scale
    total = jnp.zeros((ch, ch), F32)
    for at in range(0, frames, step_frames):
        total = total + mm_tn(
            feat[at : at + step_frames].reshape(rows, ch),
            cots[at : at + step_frames].reshape(rows, ch),
        )
    out_ref[LAYERS * TAPS] = total * scale
    total = jnp.zeros((ch, ch), F32)
    for seg in range(segs):
        key = feat[seg * seg_frames + key_ref[seg]]
        total = total + sum(mm_tn(key, part) for part in three_parts(seg_cot[seg]))
    out_ref[LAYERS * TAPS + 1] = total * scale


def exchange(blocks):
    return lax.all_to_all(blocks, AXES, split_axis=0, concat_axis=0, tiled=True)


def reduce_everywhere(parts, devices):
    count, ch, _ = parts.shape
    pieces = exchange(parts.reshape(devices, count * ch // devices, ch))
    mine = jnp.sum(pieces.astype(F32), axis=0).astype(BF16)
    return exchange(jnp.broadcast_to(mine, pieces.shape)).reshape(count, ch, ch).astype(F32)


def local(
    frames_in, spatial_weight, temporal_weight, uniting_weight, key_index, dilation, cotangent
):
    held, rows, cols, ch = frames_in.shape
    assert held == 1
    pixels = rows * cols
    devices = lax.axis_size("seg") * lax.axis_size("grp")
    frames = held * devices
    block = pixels // devices
    split = cols // block
    wide = round_up(cols + 1, 16)
    high = round_up(block, 16)
    rows_step = next(n for n in (4, 2, 1) if rows % n == 0)
    step_frames = max(n for n in range(1, frames + 1) if frames % n == 0 and n * high <= 512)
    scale = float((frames * pixels) ** -0.5)

    send, space_slope = call(
        functools.partial(spatial_fwd_kernel, rows_step),
        [((rows, 2, cols, ch), BF16), ((rows, wide, ch), F32)],
        [pltpu.VMEM((rows + 2, wide, ch), BF16)],
        2 * 9 * pixels * ch * ch,
        pixels * ch * 12,
        0,
        (frames_in[0], spatial_weight, cotangent[0]),
    )
    send = send.reshape(rows, 2, split, block, ch).swapaxes(1, 2).reshape(devices, 2, block, ch)
    got = exchange(send)

    padded = ((frames + 2 * HALO, high, ch), BF16)
    whole = (frames, high, ch)
    send, a0, a1, feat, cots, g0, g1, seg_cot = call(
        functools.partial(temporal_kernel, step_frames),
        [
            ((frames, 2, block, ch), BF16),
            padded,
            padded,
            (whole, BF16),
            (whole, BF16),
            padded,
            padded,
            ((key_index.shape[0], high, ch), F32),
        ],
        [pltpu.VMEM(whole, F32)] * 3,
        2 * 22 * frames * block * ch * ch,
        frames * block * ch * 18,
        2,
        (dilation, key_index, got, temporal_weight, uniting_weight),
    )
    got = exchange(send)
    (time_grads,) = call(
        functools.partial(temporal_wgrad_kernel, step_frames, scale),
        [((LAYERS * TAPS + 2, ch, ch), F32)],
        [],
        2 * 12 * frames * block * ch * ch,
        frames * block * ch * 14,
        2,
        (dilation, key_index, a0, a1, feat, g0, g1, cots, seg_cot),
    )
    (x_cat,) = call(
        functools.partial(columns_kernel, rows_step),
        [((rows * wide, 3 * ch), BF16)],
        [],
        0,
        pixels * ch * 8,
        0,
        (frames_in[0],),
    )
    got = got.reshape(rows, split, 2, block, ch).swapaxes(1, 2).reshape(rows, 2, cols, ch)
    gs, united, space_grads = call(
        functools.partial(spatial_wgrad_kernel, rows_step, scale),
        [((rows + 2, wide, ch), BF16), ((rows, cols, ch), BF16), ((9, ch, ch), BF16)],
        [],
        2 * 9 * pixels * ch * ch,
        pixels * ch * 18,
        0,
        (got, space_slope, x_cat),
    )
    (back,) = call(
        functools.partial(spatial_back_kernel, rows_step),
        [((rows, cols, ch), BF16)],
        [],
        2 * 9 * pixels * ch * ch,
        pixels * ch * 4,
        0,
        (spatial_weight, gs),
    )
    time_grads = lax.psum(time_grads, AXES)
    return (
        united[None],
        back[None],
        reduce_everywhere(space_grads, devices),
        time_grads[: LAYERS * TAPS].reshape(LAYERS, TAPS, ch, ch),
        time_grads[LAYERS * TAPS :],
    )


def solution(mesh):
    frame_spec = P(AXES, None, None, None)
    return jax.shard_map(
        local,
        mesh=mesh,
        in_specs=(frame_spec, P(), P(), P(), P(), P(), frame_spec),
        out_specs=(frame_spec, frame_spec, P(), P(), P()),
        check_vma=False,
    )
```

```python
import functools

import jax
import jax.numpy as jnp
from jax import lax
from jax.experimental import pallas as pl
from jax.experimental.pallas import tpu as pltpu
from jax.sharding import PartitionSpec as P

LAYERS = 2
TAPS = 5
DMAX = 8
HALO = 2 * DMAX
AXES = ("seg", "grp")
BF16 = jnp.bfloat16
F32 = jnp.float32
VMEM_LIMIT = 32 * 1024 * 1024


def round_up(value, step):
    return -(-value // step) * step


def silu_parts(value):
    sigma = 0.5 * jnp.tanh(0.5 * value) + 0.5
    act = value * sigma
    return act, sigma + act * (1.0 - sigma)


def mm(left, right):
    return jnp.dot(left, right, preferred_element_type=F32)


def mm_nt(left, right):
    return lax.dot_general(left, right, (((1,), (1,)), ((), ())), preferred_element_type=F32)


def mm_tn(left, right):
    return lax.dot_general(left, right, (((0,), (0,)), ((), ())), preferred_element_type=F32)


def three_parts(value):
    high = value.astype(BF16)
    rest = value - high.astype(F32)
    middle = rest.astype(BF16)
    return high, middle, (rest - middle.astype(F32)).astype(BF16)


VMEM = pl.BlockSpec(memory_space=pltpu.VMEM)
SMEM = pl.BlockSpec(memory_space=pltpu.SMEM)
ANY = pl.BlockSpec(memory_space=pl.ANY)


def call(kernel, outs, scratch, flops, moved, args):
    return pl.pallas_call(
        kernel,
        out_shape=[jax.ShapeDtypeStruct(shape, kind) for shape, kind, _ in outs],
        in_specs=[spec for _, spec in args],
        out_specs=[spec for _, _, spec in outs],
        scratch_shapes=scratch,
        compiler_params=pltpu.CompilerParams(vmem_limit_bytes=VMEM_LIMIT),
        cost_estimate=pl.CostEstimate(flops=flops, bytes_accessed=moved, transcendentals=0),
    )(*[value for value, _ in args])


def roll_rows(value, shift):
    return pltpu.roll(value, shift % value.shape[0], 0)


def spatial_fwd_kernel(
    rows_step, x_hbm, w_ref, cot_hbm, send_ref, slope_hbm, x_in, xs, slopes, in_sems, cot_sem, out_sems
):
    rows, cols, ch = x_in.shape
    wide = xs.shape[1]
    steps = rows // rows_step

    def part(step):
        return pl.ds(step * rows_step, rows_step)

    loads = [
        pltpu.make_async_copy(x_hbm.at[part(n)], x_in.at[part(n)], in_sems.at[n]) for n in range(steps)
    ]
    stores = [
        pltpu.make_async_copy(slopes.at[part(n)], slope_hbm.at[part(n)], out_sems.at[n])
        for n in range(steps)
    ]
    for load in loads:
        load.start()
    cot_copy = pltpu.make_async_copy(cot_hbm, send_ref.at[:, 1], cot_sem.at[0])
    cot_copy.start()
    xs[0] = jnp.zeros((wide, ch), BF16)
    xs[rows + 1] = jnp.zeros((wide, ch), BF16)
    weight = jnp.concatenate(
        [jnp.concatenate([w_ref[3 * a + b] for b in range(3)], axis=1) for a in range(3)], axis=0
    )
    flat = rows_step * wide

    def bring(step):
        loads[step].wait()
        at = step * rows_step
        xs[1 + at : 1 + at + rows_step] = jnp.zeros((rows_step, wide, ch), BF16)
        xs[1 + at : 1 + at + rows_step, :cols, :] = x_in[at : at + rows_step]

    bring(0)
    for step in range(steps):
        if step + 1 < steps:
            bring(step + 1)
        at = step * rows_step
        left = jnp.concatenate(
            [xs[at + a : at + a + rows_step].reshape(flat, ch) for a in range(3)], axis=1
        )
        y = mm(left, weight)
        pre = y[:, ch : 2 * ch] + roll_rows(y[:, :ch], 1) + roll_rows(y[:, 2 * ch :], -1)
        act, slope = silu_parts(pre)
        send_ref[at : at + rows_step, 0] = act.astype(BF16).reshape(rows_step, wide, ch)[:, :cols]
        slopes[at : at + rows_step] = slope.reshape(rows_step, wide, ch)
        stores[step].start()
    cot_copy.wait()
    for store in stores:
        store.wait()


def hand_out(here_ref, total_ref, pieces):
    for peer, piece in enumerate(pieces):
        piece[...] = total_ref[jnp.bitwise_xor(here_ref[1], peer)].astype(piece.dtype)


def columns_kernel(rows_step, x_ref, cat_ref):
    rows, cols, ch = x_ref.shape
    wide = cat_ref.shape[0] // rows
    flat = rows_step * wide
    pad = jnp.zeros((rows_step, wide - cols, ch), F32)
    for at in range(0, rows, rows_step):
        x = jnp.concatenate([x_ref[at : at + rows_step].astype(F32), pad], axis=1).reshape(flat, ch)
        x_cat = jnp.concatenate([roll_rows(x, 1), x, roll_rows(x, -1)], axis=1)
        cat_ref[at * wide : at * wide + flat] = x_cat.astype(BF16)


def taps_up(gs, at, rows_step):
    wide, ch = gs.shape[1:]
    return jnp.concatenate(
        [gs[at + 2 - a : at + 2 - a + rows_step].reshape(rows_step * wide, ch) for a in range(3)],
        axis=1,
    )


def spatial_wgrad_kernel(
    rows_step, scale, here_ref, got_ref, slope_ref, cat_ref, gs, *rest
):
    pieces, total_ref = rest[:-1], rest[-1]
    rows, cols, ch = got_ref.shape
    wide = gs.shape[1]
    gs[0] = jnp.zeros((wide, ch), BF16)
    gs[rows + 1] = jnp.zeros((wide, ch), BF16)
    for at in range(0, rows, rows_step):
        gs[1 + at : 1 + at + rows_step] = jnp.zeros((rows_step, wide, ch), BF16)
        gs[1 + at : 1 + at + rows_step, :cols, :] = (
            got_ref[at : at + rows_step].astype(F32) * slope_ref[at : at + rows_step, :cols, :]
        ).astype(BF16)
    flat = rows_step * wide
    total = jnp.zeros((3 * ch, 3 * ch), F32)
    for at in range(0, rows, rows_step):
        total = total + mm_tn(cat_ref[at * wide : at * wide + flat], taps_up(gs, at, rows_step))
    total_ref[...] = (
        jnp.concatenate(
            [
                total[b * ch : (b + 1) * ch, a * ch : (a + 1) * ch]
                for a in range(3)
                for b in range(3)
            ],
            axis=0,
        )
        * scale
    ).reshape(total_ref.shape)
    hand_out(here_ref, total_ref, pieces)


def spatial_back_kernel(rows_step, w_ref, gs, back_ref):
    rows, cols, ch = back_ref.shape
    wide = gs.shape[1]
    weight = jnp.concatenate(
        [
            jnp.concatenate([w_ref[3 * a + b].astype(F32).T.astype(BF16) for b in range(3)], axis=1)
            for a in range(3)
        ],
        axis=0,
    )
    for at in range(0, rows, rows_step):
        y = mm(taps_up(gs, at, rows_step), weight)
        back = y[:, ch : 2 * ch] + roll_rows(y[:, :ch], -1) + roll_rows(y[:, 2 * ch :], 1)
        back_ref[at : at + rows_step] = back.astype(BF16).reshape(rows_step, wide, ch)[:, :cols]


def clear_halo(pad_ref, frames):
    zeros = jnp.zeros((HALO,) + pad_ref.shape[1:], pad_ref.dtype)
    pad_ref[:HALO] = zeros
    pad_ref[HALO + frames :] = zeros


def taps_of(pad_ref, at, count, step_size, sign):
    high, ch = pad_ref.shape[1:]
    pieces = [
        pad_ref[pl.ds(HALO + at + sign * (k - 2) * step_size, count)].reshape(count * high, ch)
        for k in range(TAPS)
    ]
    return jnp.concatenate(pieces, axis=1)


def temporal_kernel(
    step_frames, dil_ref, key_ref, got_ref, tw_ref, uw_ref,
    grad_ref, united_ref, a1_hbm, feat_hbm, g1_hbm, g0_hbm,
    a0, a1, feat, cots, g0, g1, slope0, slope1, grad_feat, sems,
):
    frames, _, block, ch = got_ref.shape
    high = feat.shape[1]
    segs = key_ref.shape[0]
    seg_frames = frames // segs
    inside = pl.ds(HALO, frames)
    copies = [
        pltpu.make_async_copy(source, target, sems.at[n])
        for n, (source, target) in enumerate(
            (
                (a1.at[inside], a1_hbm),
                (feat, feat_hbm),
                (g1.at[inside], g1_hbm),
                (g0.at[inside], g0_hbm),
            )
        )
    ]
    for ref in (a0, a1, g0, g1):
        clear_halo(ref, frames)
    a0[HALO : HALO + frames] = jnp.zeros((frames, high, ch), BF16)
    a0[HALO : HALO + frames, :block, :] = got_ref[:, 0]
    cots[...] = jnp.zeros(cots.shape, cots.dtype)
    cots[:, :block, :] = got_ref[:, 1]
    for layer, (source, target, slopes) in enumerate(((a0, a1, slope0), (a1, feat, slope1))):
        step_size = dil_ref[layer]
        weight = jnp.concatenate([tw_ref[layer, k] for k in range(TAPS)], axis=0)
        first = HALO if layer == 0 else 0
        for at in range(0, frames, step_frames):
            pre = mm(taps_of(source, at, step_frames, step_size, 1), weight)
            act, slope = silu_parts(pre)
            target[first + at : first + at + step_frames] = act.astype(BF16).reshape(
                step_frames, high, ch
            )
            slopes[at : at + step_frames] = slope.reshape(step_frames, high, ch)
        copies[layer].start()
    for seg in range(segs):
        low, top = seg * seg_frames, (seg + 1) * seg_frames
        here = low + key_ref[seg]
        key_part = mm(feat[here], uw_ref[1])
        main = mm(feat[low:top].reshape(seg_frames * high, ch), uw_ref[0]).reshape(
            seg_frames, high, ch
        )
        united_ref[low:top] = (main + key_part[None]).astype(BF16)[:, :block]
        mine = cots[low:top]
        total = jnp.sum(mine.astype(F32), axis=0)
        grad_feat[low:top] = mm_nt(mine.reshape(seg_frames * high, ch), uw_ref[0]).reshape(
            seg_frames, high, ch
        )
        key_term = sum(mm_nt(part, uw_ref[1]) for part in three_parts(total))
        grad_feat[here] = grad_feat[here] + key_term
        g1[HALO + low : HALO + top] = (grad_feat[low:top] * slope1[low:top]).astype(BF16)
    for layer, source in ((1, g1), (0, g0)):
        copies[3 - layer].start()
        step_size = dil_ref[layer]
        weight = jnp.concatenate(
            [tw_ref[layer, k].astype(F32).T.astype(BF16) for k in range(TAPS)], axis=0
        )
        for at in range(0, frames, step_frames):
            grad = mm(taps_of(source, at, step_frames, step_size, -1), weight).reshape(
                step_frames, high, ch
            )
            if layer == 1:
                g0[HALO + at : HALO + at + step_frames] = (
                    grad * slope0[at : at + step_frames]
                ).astype(BF16)
            else:
                grad_ref[at : at + step_frames] = grad.astype(BF16)[:, :block]
    for copy in copies:
        copy.wait()


def temporal_wgrad_kernel(
    step_frames, scale, here_ref, dil_ref, key_ref, got_ref, a1_ref, feat, g0, g1, *rest
):
    pieces, (a0, a1, cots, total_ref) = rest[:-4], rest[-4:]
    frames, high, ch = feat.shape
    block = got_ref.shape[2]
    segs = key_ref.shape[0]
    seg_frames = frames // segs
    rows = step_frames * high
    clear_halo(a0, frames)
    clear_halo(a1, frames)
    a0[HALO : HALO + frames] = jnp.zeros((frames, high, ch), BF16)
    a0[HALO : HALO + frames, :block, :] = got_ref[:, 0]
    a1[HALO : HALO + frames] = a1_ref[...]
    cots[...] = jnp.zeros(cots.shape, cots.dtype)
    cots[:, :block, :] = got_ref[:, 1]
    totals = []
    for layer, acts, grads in ((0, a0, g0), (1, a1, g1)):
        total = jnp.zeros((TAPS * ch, ch), F32)
        for at in range(0, frames, step_frames):
            total = total + mm_tn(
                taps_of(acts, at, step_frames, dil_ref[layer], 1),
                grads[at : at + step_frames].reshape(rows, ch),
            )
        totals.append(total)
    total = jnp.zeros((ch, ch), F32)
    for at in range(0, frames, step_frames):
        total = total + mm_tn(
            feat[at : at + step_frames].reshape(rows, ch),
            cots[at : at + step_frames].reshape(rows, ch),
        )
    keyed = jnp.zeros((ch, ch), F32)
    for seg in range(segs):
        low, top = seg * seg_frames, (seg + 1) * seg_frames
        key = feat[low + key_ref[seg]]
        seg_cot = jnp.sum(cots[low:top].astype(F32), axis=0)
        keyed = keyed + sum(mm_tn(key, part) for part in three_parts(seg_cot))
    peers = len(pieces)
    split = LAYERS * TAPS * ch // peers
    total_ref[:, :split] = (jnp.concatenate(totals, axis=0) * scale).reshape(peers, split, ch)
    total_ref[:, split:] = (jnp.concatenate([total, keyed], axis=0) * scale).reshape(
        peers, 2 * ch // peers, ch
    )
    hand_out(here_ref, total_ref, pieces)


def sum_kernel(*refs):
    refs[-1][...] = sum(ref[...].astype(F32) for ref in refs[:-1]).astype(refs[-1].dtype)


def join_kernel(first_ref, *refs):
    out_ref = refs[-1]
    split = first_ref.shape[0]
    out_ref[:split] = first_ref[...]
    out_ref[split:] = sum(ref[...].astype(F32) for ref in refs[:-1]).astype(out_ref.dtype)


def deal_kernel(here_ref, *refs):
    pieces, outs = refs[:-3], refs[-3:]
    for peer, piece in enumerate(pieces):
        place = jnp.bitwise_xor(here_ref[1], peer)
        at = 0
        for out_ref in outs:
            count = out_ref.shape[1]
            out_ref[place] = piece[at : at + count].astype(F32)
            at += count


def exchange(blocks):
    return lax.all_to_all(blocks, AXES, split_axis=0, concat_axis=0, tiled=True)


def flip(value, peer):
    size = lax.axis_size("grp")
    return lax.ppermute(value, "grp", [(i, i ^ peer) for i in range(size)])


def turn_by(value, turn):
    size = lax.axis_size("seg")
    return lax.ppermute(value, "seg", [(i, (i + turn) % size) for i in range(size)])


def sum_of(parts):
    shape = parts[0].shape
    return call(
        sum_kernel, [(shape, BF16, VMEM)], [], 0, len(parts) * 2 * shape[0] * shape[1],
        [(part, VMEM) for part in parts],
    )[0]


def reduce_in_grp(pieces):
    return sum_of([flip(piece, peer) if peer else piece for peer, piece in enumerate(pieces)])


def all_turns(value):
    return [turn_by(value, turn) if turn else value for turn in range(lax.axis_size("seg"))]


def local(
    frames_in, spatial_weight, temporal_weight, uniting_weight, key_index, dilation, cotangent
):
    held, rows, cols, ch = frames_in.shape
    assert held == 1
    pixels = rows * cols
    peers = lax.axis_size("grp")
    devices = lax.axis_size("seg") * peers
    frames = held * devices
    block = pixels // devices
    split = cols // block
    wide = round_up(cols + 1, 16)
    high = round_up(block, 16)
    rows_step = next(n for n in (4, 2, 1) if rows % n == 0)
    steps = rows // rows_step
    step_frames = max(n for n in range(1, frames + 1) if frames % n == 0 and n * high <= 512)
    scale = float((frames * pixels) ** -0.5)
    here = jnp.stack([lax.axis_index("seg"), lax.axis_index("grp")]).astype(jnp.int32)
    space_rows, time_rows, unite_rows = (n * ch // peers for n in (9, LAYERS * TAPS, 2))

    send, space_slope = call(
        functools.partial(spatial_fwd_kernel, rows_step),
        [((rows, 2, cols, ch), BF16, VMEM), ((rows, wide, ch), F32, ANY)],
        [
            pltpu.VMEM((rows, cols, ch), BF16),
            pltpu.VMEM((rows + 2, wide, ch), BF16),
            pltpu.VMEM((rows, wide, ch), F32),
            pltpu.SemaphoreType.DMA((steps,)),
            pltpu.SemaphoreType.DMA((1,)),
            pltpu.SemaphoreType.DMA((steps,)),
        ],
        2 * 9 * pixels * ch * ch,
        pixels * ch * 12,
        [(frames_in[0], ANY), (spatial_weight, VMEM), (cotangent[0], ANY)],
    )
    send = send.reshape(rows, 2, split, block, ch).swapaxes(1, 2).reshape(devices, 2, block, ch)
    got = exchange(send)

    padded = (frames + 2 * HALO, high, ch)
    whole = (frames, high, ch)
    grad_send, united_send, a1, feat, g1, g0 = call(
        functools.partial(temporal_kernel, step_frames),
        [((frames, block, ch), BF16, VMEM)] * 2 + [(whole, BF16, ANY)] * 4,
        [
            pltpu.VMEM(padded, BF16),
            pltpu.VMEM(padded, BF16),
            pltpu.VMEM(whole, BF16),
            pltpu.VMEM(whole, BF16),
            pltpu.VMEM(padded, BF16),
            pltpu.VMEM(padded, BF16),
            pltpu.VMEM(whole, F32),
            pltpu.VMEM(whole, F32),
            pltpu.VMEM(whole, F32),
            pltpu.SemaphoreType.DMA((4,)),
        ],
        2 * 22 * frames * block * ch * ch,
        frames * block * ch * 18,
        [
            (dilation, SMEM), (key_index, SMEM), (got, VMEM),
            (temporal_weight, VMEM), (uniting_weight, VMEM),
        ],
    )
    grad_time = exchange(grad_send).reshape(rows, cols, ch)
    time_pieces = call(
        functools.partial(temporal_wgrad_kernel, step_frames, scale),
        [((time_rows + unite_rows, ch), BF16, VMEM)] * peers,
        [
            pltpu.VMEM(padded, BF16),
            pltpu.VMEM(padded, BF16),
            pltpu.VMEM(whole, BF16),
            pltpu.VMEM((peers, time_rows + unite_rows, ch), F32),
        ],
        2 * 12 * frames * block * ch * ch,
        frames * block * ch * 14,
        [
            (here, SMEM), (dilation, SMEM), (key_index, SMEM), (got, VMEM),
            (a1, VMEM), (feat, VMEM), (g0, VMEM), (g1, VMEM),
        ],
    )
    time_sum = sum_of(all_turns(reduce_in_grp(time_pieces)))
    (x_cat,) = call(
        functools.partial(columns_kernel, rows_step),
        [((rows * wide, 3 * ch), BF16, VMEM)],
        [],
        0,
        pixels * ch * 8,
        [(frames_in[0], VMEM)],
    )
    gs, *space_pieces = call(
        functools.partial(spatial_wgrad_kernel, rows_step, scale),
        [((rows + 2, wide, ch), BF16, VMEM)] + [((space_rows, ch), BF16, VMEM)] * peers,
        [pltpu.VMEM((peers, space_rows, ch), F32)],
        2 * 9 * pixels * ch * ch,
        pixels * ch * 18,
        [(here, SMEM), (grad_time, VMEM), (space_slope, VMEM), (x_cat, VMEM)],
    )
    united_send, space_pieces[0] = lax.optimization_barrier((united_send, space_pieces[0]))
    united = exchange(united_send)
    (back,) = call(
        functools.partial(spatial_back_kernel, rows_step),
        [((rows, cols, ch), BF16, VMEM)],
        [],
        2 * 9 * pixels * ch * ch,
        pixels * ch * 4,
        [(spatial_weight, VMEM), (gs, VMEM)],
    )
    space_parts = all_turns(reduce_in_grp(space_pieces))
    (piece,) = call(
        join_kernel,
        [((time_rows + unite_rows + space_rows, ch), BF16, VMEM)],
        [],
        0,
        10 * space_rows * ch,
        [(time_sum, VMEM)] + [(part, VMEM) for part in space_parts],
    )
    grads = call(
        deal_kernel,
        [((peers, count, ch), F32, VMEM) for count in (time_rows, unite_rows, space_rows)],
        [],
        0,
        6 * 21 * ch * ch,
        [(here, SMEM)] + [(flip(piece, peer) if peer else piece, VMEM) for peer in range(peers)],
    )
    return (
        united.reshape(frames_in.shape),
        back[None],
        grads[2].reshape(9, ch, ch),
        grads[0].reshape(LAYERS, TAPS, ch, ch),
        grads[1].reshape(2, ch, ch),
    )


def solution(mesh):
    frame_spec = P(AXES, None, None, None)
    return jax.shard_map(
        local,
        mesh=mesh,
        in_specs=(frame_spec, P(), P(), P(), P(), P(), frame_spec),
        out_specs=(frame_spec, frame_spec, P(), P(), P()),
        check_vma=False,
    )
```

```python
import functools

import jax
import jax.numpy as jnp
from jax import lax
from jax.experimental import pallas as pl
from jax.experimental.pallas import tpu as pltpu
from jax.sharding import PartitionSpec as P

LAYERS = 2
TAPS = 5
DMAX = 8
HALO = 2 * DMAX
AXES = ("seg", "grp")
BF16 = jnp.bfloat16
F32 = jnp.float32
BIG_VMEM = 60 * 1024 * 1024
SMALL_VMEM = 16 * 1024 * 1024


def round_up(value, step):
    return -(-value // step) * step


def silu_parts(value):
    sigma = 0.5 * jnp.tanh(0.5 * value) + 0.5
    act = value * sigma
    return act, sigma + act * (1.0 - sigma)


def mm(left, right):
    return jnp.dot(left, right, preferred_element_type=F32)


def mm_nt(left, right):
    return lax.dot_general(left, right, (((1,), (1,)), ((), ())), preferred_element_type=F32)


def mm_tn(left, right):
    return lax.dot_general(left, right, (((0,), (0,)), ((), ())), preferred_element_type=F32)


def three_parts(value):
    high = value.astype(BF16)
    rest = value - high.astype(F32)
    middle = rest.astype(BF16)
    return high, middle, (rest - middle.astype(F32)).astype(BF16)


VMEM = pl.BlockSpec(memory_space=pltpu.VMEM)
SMEM = pl.BlockSpec(memory_space=pltpu.SMEM)
HBM = pl.BlockSpec(memory_space=pltpu.HBM)


def call(kernel, outs, scratch, flops, moved, args, vmem=BIG_VMEM):
    return pl.pallas_call(
        kernel,
        out_shape=[jax.ShapeDtypeStruct(shape, kind) for shape, kind, _ in outs],
        in_specs=[spec for _, spec in args],
        out_specs=[spec for _, _, spec in outs],
        scratch_shapes=scratch,
        compiler_params=pltpu.CompilerParams(vmem_limit_bytes=vmem),
        cost_estimate=pl.CostEstimate(flops=flops, bytes_accessed=moved, transcendentals=0),
    )(*[value for value, _ in args])


def roll_rows(value, shift):
    return pltpu.roll(value, shift % value.shape[0], 0)


def spatial_fwd_kernel(
    rows_step, x_hbm, w_ref, cot_hbm, send_hbm, slope_hbm,
    x_in, xs, acts, slopes, in_sems, cot_sem, act_sems, out_sems,
):
    rows, cols, ch = x_in.shape
    wide = xs.shape[1]
    steps = rows // rows_step

    def part(step):
        return pl.ds(step * rows_step, rows_step)

    loads = [
        pltpu.make_async_copy(x_hbm.at[part(n)], x_in.at[part(n)], in_sems.at[n]) for n in range(steps)
    ]
    stores = [
        (
            pltpu.make_async_copy(acts.at[part(n)], send_hbm.at[part(n), 0], act_sems.at[n]),
            pltpu.make_async_copy(slopes.at[part(n)], slope_hbm.at[part(n)], out_sems.at[n]),
        )
        for n in range(steps)
    ]
    for load in loads:
        load.start()
    cot_copy = pltpu.make_async_copy(cot_hbm, send_hbm.at[:, 1], cot_sem.at[0])
    cot_copy.start()
    xs[0] = jnp.zeros((wide, ch), BF16)
    xs[rows + 1] = jnp.zeros((wide, ch), BF16)
    weight = jnp.concatenate(
        [jnp.concatenate([w_ref[3 * a + b] for b in range(3)], axis=1) for a in range(3)], axis=0
    )
    flat = rows_step * wide

    def bring(step):
        loads[step].wait()
        at = step * rows_step
        xs[1 + at : 1 + at + rows_step] = jnp.zeros((rows_step, wide, ch), BF16)
        xs[1 + at : 1 + at + rows_step, :cols, :] = x_in[at : at + rows_step]

    bring(0)
    for step in range(steps):
        if step + 1 < steps:
            bring(step + 1)
        at = step * rows_step
        left = jnp.concatenate(
            [xs[at + a : at + a + rows_step].reshape(flat, ch) for a in range(3)], axis=1
        )
        y = mm(left, weight)
        pre = y[:, ch : 2 * ch] + roll_rows(y[:, :ch], 1) + roll_rows(y[:, 2 * ch :], -1)
        act, slope = silu_parts(pre)
        acts[at : at + rows_step] = act.astype(BF16).reshape(rows_step, wide, ch)[:, :cols]
        slopes[at : at + rows_step] = slope.reshape(rows_step, wide, ch)
        for store in stores[step]:
            store.start()
    cot_copy.wait()
    for pair in stores:
        for store in pair:
            store.wait()


def hand_out(here_ref, total_ref, pieces):
    for peer, piece in enumerate(pieces):
        piece[...] = total_ref[jnp.bitwise_xor(here_ref[1], peer)].astype(piece.dtype)


def columns_kernel(rows_step, x_ref, cat_ref):
    rows, cols, ch = x_ref.shape
    wide = cat_ref.shape[0] // rows
    flat = rows_step * wide
    pad = jnp.zeros((rows_step, wide - cols, ch), F32)
    for at in range(0, rows, rows_step):
        x = jnp.concatenate([x_ref[at : at + rows_step].astype(F32), pad], axis=1).reshape(flat, ch)
        x_cat = jnp.concatenate([roll_rows(x, 1), x, roll_rows(x, -1)], axis=1)
        cat_ref[at * wide : at * wide + flat] = x_cat.astype(BF16)


def taps_up(gs, at, rows_step):
    wide, ch = gs.shape[1:]
    return jnp.concatenate(
        [gs[at + 2 - a : at + 2 - a + rows_step].reshape(rows_step * wide, ch) for a in range(3)],
        axis=1,
    )


def spatial_wgrad_kernel(
    rows_step, scale, here_ref, got_hbm, slope_hbm, cat_hbm, gs_hbm, *rest
):
    pieces = rest[:-9]
    got, slopes, gs, cat_ref, total_ref, got_sems, slope_sems, cat_sems, gs_sems = rest[-9:]
    rows, cols, ch = got.shape
    wide = gs.shape[1]
    steps = rows // rows_step
    flat = rows_step * wide

    def part(step, first=0):
        return pl.ds(first + step * rows_step, rows_step)

    loads = [
        (
            pltpu.make_async_copy(got_hbm.at[part(n)], got.at[part(n)], got_sems.at[n]),
            pltpu.make_async_copy(slope_hbm.at[part(n)], slopes.at[part(n)], slope_sems.at[n]),
            pltpu.make_async_copy(
                cat_hbm.at[pl.ds(n * flat, flat)], cat_ref.at[pl.ds(n * flat, flat)], cat_sems.at[n]
            ),
        )
        for n in range(steps)
    ]
    for pair in loads:
        for load in pair:
            load.start()
    stores = [
        pltpu.make_async_copy(gs.at[part(n, 1)], gs_hbm.at[part(n)], gs_sems.at[n])
        for n in range(steps)
    ]
    gs[0] = jnp.zeros((wide, ch), BF16)
    gs[rows + 1] = jnp.zeros((wide, ch), BF16)

    def bring(step):
        for load in loads[step]:
            load.wait()
        at = step * rows_step
        gs[1 + at : 1 + at + rows_step] = jnp.zeros((rows_step, wide, ch), BF16)
        gs[1 + at : 1 + at + rows_step, :cols, :] = (
            got[at : at + rows_step].astype(F32) * slopes[at : at + rows_step, :cols, :]
        ).astype(BF16)
        stores[step].start()

    total = jnp.zeros((3 * ch, 3 * ch), F32)
    bring(0)
    for step in range(steps):
        if step + 1 < steps:
            bring(step + 1)
        at = step * rows_step
        total = total + mm_tn(cat_ref[at * wide : at * wide + flat], taps_up(gs, at, rows_step))
    total_ref[...] = (
        jnp.concatenate(
            [
                total[b * ch : (b + 1) * ch, a * ch : (a + 1) * ch]
                for a in range(3)
                for b in range(3)
            ],
            axis=0,
        )
        * scale
    ).reshape(total_ref.shape)
    hand_out(here_ref, total_ref, pieces)
    for store in stores:
        store.wait()


def spatial_back_kernel(rows_step, w_ref, gs_hbm, back_hbm, gs, back_ref, sem, out_sems):
    rows, cols, ch = back_ref.shape
    stores = [
        pltpu.make_async_copy(
            back_ref.at[pl.ds(at, rows_step)], back_hbm.at[pl.ds(at, rows_step)], out_sems.at[n]
        )
        for n, at in enumerate(range(0, rows, rows_step))
    ]
    wide = gs.shape[1]
    load = pltpu.make_async_copy(gs_hbm, gs.at[pl.ds(1, rows)], sem.at[0])
    load.start()
    gs[0] = jnp.zeros((wide, ch), BF16)
    gs[rows + 1] = jnp.zeros((wide, ch), BF16)
    weight = jnp.concatenate(
        [
            jnp.concatenate([w_ref[3 * a + b].astype(F32).T.astype(BF16) for b in range(3)], axis=1)
            for a in range(3)
        ],
        axis=0,
    )
    load.wait()
    for n, at in enumerate(range(0, rows, rows_step)):
        y = mm(taps_up(gs, at, rows_step), weight)
        back = y[:, ch : 2 * ch] + roll_rows(y[:, :ch], -1) + roll_rows(y[:, 2 * ch :], 1)
        back_ref[at : at + rows_step] = back.astype(BF16).reshape(rows_step, wide, ch)[:, :cols]
        stores[n].start()
    for store in stores:
        store.wait()


def clear_halo(pad_ref, frames):
    zeros = jnp.zeros((HALO,) + pad_ref.shape[1:], pad_ref.dtype)
    pad_ref[:HALO] = zeros
    pad_ref[HALO + frames :] = zeros


def taps_of(pad_ref, at, count, step_size, sign):
    high, ch = pad_ref.shape[1:]
    pieces = [
        pad_ref[pl.ds(HALO + at + sign * (k - 2) * step_size, count)].reshape(count * high, ch)
        for k in range(TAPS)
    ]
    return jnp.concatenate(pieces, axis=1)


def temporal_kernel(
    step_frames, dil_ref, key_ref, got_hbm, tw_ref, uw_ref,
    grad_hbm, united_hbm, a0_hbm, cots_hbm, a1_hbm, feat_hbm, g1_hbm, g0_hbm,
    a0, a1, feat, cots, g0, g1, slope0, slope1, grad_feat, united_ref, act_ref, cot_ref, grad_ref,
    sems, in_sems, out_sems,
):
    frames, block, ch = act_ref.shape
    high = feat.shape[1]
    loads = [
        pltpu.make_async_copy(got_hbm.at[:, n], ref, in_sems.at[n])
        for n, ref in enumerate((act_ref, cot_ref))
    ]
    for load in loads:
        load.start()
    stores = [
        pltpu.make_async_copy(
            grad_ref.at[pl.ds(at, step_frames)], grad_hbm.at[pl.ds(at, step_frames)], out_sems.at[n]
        )
        for n, at in enumerate(range(0, frames, step_frames))
    ]
    segs = key_ref.shape[0]
    seg_frames = frames // segs
    inside = pl.ds(HALO, frames)
    copies = [
        pltpu.make_async_copy(source, target, sems.at[n])
        for n, (source, target) in enumerate(
            (
                (a1.at[inside], a1_hbm),
                (feat, feat_hbm),
                (g1.at[inside], g1_hbm),
                (g0.at[inside], g0_hbm),
                (a0.at[inside], a0_hbm),
                (cots, cots_hbm),
                (united_ref, united_hbm),
            )
        )
    ]
    for ref in (a0, a1, g0, g1):
        clear_halo(ref, frames)
    a0[HALO : HALO + frames] = jnp.zeros((frames, high, ch), BF16)
    cots[...] = jnp.zeros(cots.shape, cots.dtype)
    loads[0].wait()
    a0[HALO : HALO + frames, :block, :] = act_ref[...]
    copies[4].start()
    for layer, (source, target, slopes) in enumerate(((a0, a1, slope0), (a1, feat, slope1))):
        step_size = dil_ref[layer]
        weight = jnp.concatenate([tw_ref[layer, k] for k in range(TAPS)], axis=0)
        first = HALO if layer == 0 else 0
        for at in range(0, frames, step_frames):
            pre = mm(taps_of(source, at, step_frames, step_size, 1), weight)
            act, slope = silu_parts(pre)
            target[first + at : first + at + step_frames] = act.astype(BF16).reshape(
                step_frames, high, ch
            )
            slopes[at : at + step_frames] = slope.reshape(step_frames, high, ch)
        copies[layer].start()
    loads[1].wait()
    cots[:, :block, :] = cot_ref[...]
    copies[5].start()
    for seg in range(segs):
        low, top = seg * seg_frames, (seg + 1) * seg_frames
        here = low + key_ref[seg]
        key_part = mm(feat[here], uw_ref[1])
        main = mm(feat[low:top].reshape(seg_frames * high, ch), uw_ref[0]).reshape(
            seg_frames, high, ch
        )
        united_ref[low:top] = (main + key_part[None]).astype(BF16)[:, :block]
        mine = cots[low:top]
        total = jnp.sum(mine.astype(F32), axis=0)
        grad_feat[low:top] = mm_nt(mine.reshape(seg_frames * high, ch), uw_ref[0]).reshape(
            seg_frames, high, ch
        )
        key_term = sum(mm_nt(part, uw_ref[1]) for part in three_parts(total))
        grad_feat[here] = grad_feat[here] + key_term
        g1[HALO + low : HALO + top] = (grad_feat[low:top] * slope1[low:top]).astype(BF16)
    copies[6].start()
    for layer, source in ((1, g1), (0, g0)):
        copies[3 - layer].start()
        step_size = dil_ref[layer]
        weight = jnp.concatenate(
            [tw_ref[layer, k].astype(F32).T.astype(BF16) for k in range(TAPS)], axis=0
        )
        for n, at in enumerate(range(0, frames, step_frames)):
            grad = mm(taps_of(source, at, step_frames, step_size, -1), weight).reshape(
                step_frames, high, ch
            )
            if layer == 1:
                g0[HALO + at : HALO + at + step_frames] = (
                    grad * slope0[at : at + step_frames]
                ).astype(BF16)
            else:
                grad_ref[at : at + step_frames] = grad.astype(BF16)[:, :block]
                stores[n].start()
    for copy in copies + stores:
        copy.wait()


def temporal_wgrad_kernel(
    step_frames, scale, here_ref, dil_ref, key_ref,
    a0_hbm, g0_hbm, a1_hbm, g1_hbm, feat_hbm, cots_hbm, *rest
):
    pieces, (a0, g0, a1, g1, feat, cots, total_ref, sems) = rest[:-8], rest[-8:]
    frames, high, ch = feat.shape
    segs = key_ref.shape[0]
    seg_frames = frames // segs
    rows = step_frames * high
    inside = pl.ds(HALO, frames)
    copies = [
        pltpu.make_async_copy(source, target, sems.at[n])
        for n, (source, target) in enumerate(
            (
                (a0_hbm, a0.at[inside]),
                (g0_hbm, g0),
                (a1_hbm, a1.at[inside]),
                (g1_hbm, g1),
                (feat_hbm, feat),
                (cots_hbm, cots),
            )
        )
    ]
    for copy in copies:
        copy.start()
    clear_halo(a0, frames)
    clear_halo(a1, frames)
    totals = []
    for layer, acts, grads in ((0, a0, g0), (1, a1, g1)):
        copies[2 * layer].wait()
        copies[2 * layer + 1].wait()
        total = jnp.zeros((TAPS * ch, ch), F32)
        for at in range(0, frames, step_frames):
            total = total + mm_tn(
                taps_of(acts, at, step_frames, dil_ref[layer], 1),
                grads[at : at + step_frames].reshape(rows, ch),
            )
        totals.append(total)
    copies[4].wait()
    copies[5].wait()
    total = jnp.zeros((ch, ch), F32)
    for at in range(0, frames, step_frames):
        total = total + mm_tn(
            feat[at : at + step_frames].reshape(rows, ch),
            cots[at : at + step_frames].reshape(rows, ch),
        )
    keyed = jnp.zeros((ch, ch), F32)
    for seg in range(segs):
        low, top = seg * seg_frames, (seg + 1) * seg_frames
        key = feat[low + key_ref[seg]]
        seg_cot = jnp.sum(cots[low:top].astype(F32), axis=0)
        keyed = keyed + sum(mm_tn(key, part) for part in three_parts(seg_cot))
    peers = len(pieces)
    split = LAYERS * TAPS * ch // peers
    total_ref[:, :split] = (jnp.concatenate(totals, axis=0) * scale).reshape(peers, split, ch)
    total_ref[:, split:] = (jnp.concatenate([total, keyed], axis=0) * scale).reshape(
        peers, 2 * ch // peers, ch
    )
    hand_out(here_ref, total_ref, pieces)


def sum_kernel(*refs):
    refs[-1][...] = sum(ref[...].astype(F32) for ref in refs[:-1]).astype(refs[-1].dtype)


def join_kernel(first_ref, *refs):
    out_ref = refs[-1]
    split = first_ref.shape[0]
    out_ref[:split] = first_ref[...]
    out_ref[split:] = sum(ref[...].astype(F32) for ref in refs[:-1]).astype(out_ref.dtype)


def deal_kernel(here_ref, *refs):
    united_hbm, *pieces = refs[:-5]
    *outs, united_out, sem = refs[-5:]
    copy = pltpu.make_async_copy(united_hbm, united_out, sem.at[0])
    copy.start()
    for peer, piece in enumerate(pieces):
        place = jnp.bitwise_xor(here_ref[1], peer)
        at = 0
        for out_ref in outs:
            count = out_ref.shape[1]
            out_ref[place] = piece[at : at + count].astype(F32)
            at += count
    copy.wait()


def exchange(blocks):
    return lax.all_to_all(blocks, AXES, split_axis=0, concat_axis=0, tiled=True)


def flip(value, peer):
    size = lax.axis_size("grp")
    return lax.ppermute(value, "grp", [(i, i ^ peer) for i in range(size)])


def turn_by(value, turn):
    size = lax.axis_size("seg")
    return lax.ppermute(value, "seg", [(i, (i + turn) % size) for i in range(size)])


def sum_of(parts):
    shape = parts[0].shape
    return call(
        sum_kernel, [(shape, BF16, VMEM)], [], 0, len(parts) * 2 * shape[0] * shape[1],
        [(part, VMEM) for part in parts], SMALL_VMEM,
    )[0]


def reduce_in_grp(pieces):
    return sum_of([flip(piece, peer) if peer else piece for peer, piece in enumerate(pieces)])


def all_turns(value):
    return [turn_by(value, turn) if turn else value for turn in range(lax.axis_size("seg"))]


def local(
    frames_in, spatial_weight, temporal_weight, uniting_weight, key_index, dilation, cotangent
):
    held, rows, cols, ch = frames_in.shape
    assert held == 1
    pixels = rows * cols
    peers = lax.axis_size("grp")
    devices = lax.axis_size("seg") * peers
    frames = held * devices
    block = pixels // devices
    split = cols // block
    wide = round_up(cols + 1, 16)
    high = round_up(block, 16)
    rows_step = next(n for n in (4, 2, 1) if rows % n == 0)
    steps = rows // rows_step
    step_frames = max(n for n in range(1, frames + 1) if frames % n == 0 and n * high <= 512)
    scale = float((frames * pixels) ** -0.5)
    here = jnp.stack([lax.axis_index("seg"), lax.axis_index("grp")]).astype(jnp.int32)
    space_rows, time_rows, unite_rows = (n * ch // peers for n in (9, LAYERS * TAPS, 2))

    send, space_slope = call(
        functools.partial(spatial_fwd_kernel, rows_step),
        [((rows, 2, cols, ch), BF16, HBM), ((rows, wide, ch), F32, HBM)],
        [
            pltpu.VMEM((rows, cols, ch), BF16),
            pltpu.VMEM((rows + 2, wide, ch), BF16),
            pltpu.VMEM((rows, cols, ch), BF16),
            pltpu.VMEM((rows, wide, ch), F32),
            pltpu.SemaphoreType.DMA((steps,)),
            pltpu.SemaphoreType.DMA((1,)),
            pltpu.SemaphoreType.DMA((steps,)),
            pltpu.SemaphoreType.DMA((steps,)),
        ],
        2 * 9 * pixels * ch * ch,
        pixels * ch * 12,
        [(frames_in[0], HBM), (spatial_weight, VMEM), (cotangent[0], HBM)],
    )
    send = send.reshape(rows, 2, split, block, ch).swapaxes(1, 2).reshape(devices, 2, block, ch)
    got = exchange(send)

    padded = (frames + 2 * HALO, high, ch)
    whole = (frames, high, ch)
    grad_send, united_send, a0, cots, a1, feat, g1, g0 = call(
        functools.partial(temporal_kernel, step_frames),
        [((frames, block, ch), BF16, HBM)] * 2 + [(whole, BF16, HBM)] * 6,
        [
            pltpu.VMEM(padded, BF16),
            pltpu.VMEM(padded, BF16),
            pltpu.VMEM(whole, BF16),
            pltpu.VMEM(whole, BF16),
            pltpu.VMEM(padded, BF16),
            pltpu.VMEM(padded, BF16),
            pltpu.VMEM(whole, F32),
            pltpu.VMEM(whole, F32),
            pltpu.VMEM(whole, F32),
            pltpu.VMEM((frames, block, ch), BF16),
            pltpu.VMEM((frames, block, ch), BF16),
            pltpu.VMEM((frames, block, ch), BF16),
            pltpu.VMEM((frames, block, ch), BF16),
            pltpu.SemaphoreType.DMA((7,)),
            pltpu.SemaphoreType.DMA((2,)),
            pltpu.SemaphoreType.DMA((frames // step_frames,)),
        ],
        2 * 22 * frames * block * ch * ch,
        frames * block * ch * 18,
        [
            (dilation, SMEM), (key_index, SMEM), (got, HBM),
            (temporal_weight, VMEM), (uniting_weight, VMEM),
        ],
    )
    grad_time = exchange(grad_send).reshape(rows, cols, ch)
    time_pieces = call(
        functools.partial(temporal_wgrad_kernel, step_frames, scale),
        [((time_rows + unite_rows, ch), BF16, VMEM)] * peers,
        [
            pltpu.VMEM(padded, BF16),
            pltpu.VMEM(whole, BF16),
            pltpu.VMEM(padded, BF16),
            pltpu.VMEM(whole, BF16),
            pltpu.VMEM(whole, BF16),
            pltpu.VMEM(whole, BF16),
            pltpu.VMEM((peers, time_rows + unite_rows, ch), F32),
            pltpu.SemaphoreType.DMA((6,)),
        ],
        2 * 12 * frames * block * ch * ch,
        frames * block * ch * 14,
        [
            (here, SMEM), (dilation, SMEM), (key_index, SMEM),
            (a0, HBM), (g0, HBM), (a1, HBM), (g1, HBM), (feat, HBM), (cots, HBM),
        ],
    )
    time_sum = reduce_in_grp(time_pieces)
    time_sum, grad_time = lax.optimization_barrier((time_sum, grad_time))
    (x_cat,) = call(
        functools.partial(columns_kernel, rows_step),
        [((rows * wide, 3 * ch), BF16, VMEM)],
        [],
        0,
        pixels * ch * 8,
        [(frames_in[0], VMEM)],
    )
    gs, *space_pieces = call(
        functools.partial(spatial_wgrad_kernel, rows_step, scale),
        [((rows, wide, ch), BF16, HBM)] + [((space_rows, ch), BF16, VMEM)] * peers,
        [
            pltpu.VMEM((rows, cols, ch), BF16),
            pltpu.VMEM((rows, wide, ch), F32),
            pltpu.VMEM((rows + 2, wide, ch), BF16),
            pltpu.VMEM((rows * wide, 3 * ch), BF16),
            pltpu.VMEM((peers, space_rows, ch), F32),
        ]
        + [pltpu.SemaphoreType.DMA((steps,))] * 4,
        2 * 9 * pixels * ch * ch,
        pixels * ch * 18,
        [(here, SMEM), (grad_time, HBM), (space_slope, HBM), (x_cat, HBM)],
    )
    united_send, space_pieces[0] = lax.optimization_barrier((united_send, space_pieces[0]))
    united = exchange(united_send)
    (back,) = call(
        functools.partial(spatial_back_kernel, rows_step),
        [((rows, cols, ch), BF16, HBM)],
        [
            pltpu.VMEM((rows + 2, wide, ch), BF16),
            pltpu.VMEM((rows, cols, ch), BF16),
            pltpu.SemaphoreType.DMA((1,)),
            pltpu.SemaphoreType.DMA((steps,)),
        ],
        2 * 9 * pixels * ch * ch,
        pixels * ch * 4,
        [(spatial_weight, VMEM), (gs, HBM)],
    )
    space_parts = [flip(part, peer) if peer else part for peer, part in enumerate(space_pieces)]
    (plane,) = call(
        join_kernel,
        [((time_rows + unite_rows + space_rows, ch), BF16, VMEM)],
        [],
        0,
        2 * (peers + 10) * space_rows * ch,
        [(time_sum, VMEM)] + [(part, VMEM) for part in space_parts],
        SMALL_VMEM,
    )
    piece = sum_of(all_turns(plane))
    *grads, united = call(
        deal_kernel,
        [((peers, count, ch), F32, VMEM) for count in (time_rows, unite_rows, space_rows)]
        + [((frames, block, ch), BF16, HBM)],
        [pltpu.SemaphoreType.DMA((1,))],
        0,
        6 * 21 * ch * ch,
        [(here, SMEM), (united, HBM)]
        + [(flip(piece, peer) if peer else piece, VMEM) for peer in range(peers)],
        SMALL_VMEM,
    )
    return (
        united.reshape(frames_in.shape),
        back[None],
        grads[2].reshape(9, ch, ch),
        grads[0].reshape(LAYERS, TAPS, ch, ch),
        grads[1].reshape(2, ch, ch),
    )


def solution(mesh):
    frame_spec = P(AXES, None, None, None)
    return jax.shard_map(
        local,
        mesh=mesh,
        in_specs=(frame_spec, P(), P(), P(), P(), P(), frame_spec),
        out_specs=(frame_spec, frame_spec, P(), P(), P()),
        check_vma=False,
    )
```

```python
import functools

import jax
import jax.numpy as jnp
from jax import lax
from jax.experimental import pallas as pl
from jax.experimental.pallas import tpu as pltpu
from jax.sharding import PartitionSpec as P

LAYERS = 2
TAPS = 5
DMAX = 8
HALO = 2 * DMAX
AXES = ("seg", "grp")
BF16 = jnp.bfloat16
F32 = jnp.float32
BIG_VMEM = 60 * 1024 * 1024
MID_VMEM = 24 * 1024 * 1024
SMALL_VMEM = 16 * 1024 * 1024


def round_up(value, step):
    return -(-value // step) * step


def silu_parts(value):
    sigma = 0.5 * jnp.tanh(0.5 * value) + 0.5
    act = value * sigma
    return act, sigma + act * (1.0 - sigma)


def mm(left, right):
    return jnp.dot(left, right, preferred_element_type=F32)


def mm_nt(left, right):
    return lax.dot_general(left, right, (((1,), (1,)), ((), ())), preferred_element_type=F32)


def mm_tn(left, right):
    return lax.dot_general(left, right, (((0,), (0,)), ((), ())), preferred_element_type=F32)


def three_parts(value):
    high = value.astype(BF16)
    rest = value - high.astype(F32)
    middle = rest.astype(BF16)
    return high, middle, (rest - middle.astype(F32)).astype(BF16)


VMEM = pl.BlockSpec(memory_space=pltpu.VMEM)
SMEM = pl.BlockSpec(memory_space=pltpu.SMEM)
HBM = pl.BlockSpec(memory_space=pltpu.HBM)


def call(kernel, outs, scratch, flops, moved, args, vmem=BIG_VMEM):
    return pl.pallas_call(
        kernel,
        out_shape=[jax.ShapeDtypeStruct(shape, kind) for shape, kind, _ in outs],
        in_specs=[spec for _, spec in args],
        out_specs=[spec for _, _, spec in outs],
        scratch_shapes=scratch,
        compiler_params=pltpu.CompilerParams(vmem_limit_bytes=vmem),
        cost_estimate=pl.CostEstimate(flops=flops, bytes_accessed=moved, transcendentals=0),
    )(*[value for value, _ in args])


def roll_rows(value, shift):
    return pltpu.roll(value, shift % value.shape[0], 0)


def spatial_fwd_kernel(
    rows_step, x_hbm, w_ref, cot_hbm, send_hbm, slope_hbm,
    x_in, xs, sends, slopes, in_sems, cot_sems, send_sems, out_sems,
):
    rows, cols, ch = x_in.shape
    wide = xs.shape[1]
    steps = rows // rows_step

    def part(step):
        return pl.ds(step * rows_step, rows_step)

    loads = [
        pltpu.make_async_copy(x_hbm.at[part(n)], x_in.at[part(n)], in_sems.at[n]) for n in range(steps)
    ]
    stores = [
        (
            pltpu.make_async_copy(sends.at[part(n)], send_hbm.at[part(n)], send_sems.at[n]),
            pltpu.make_async_copy(slopes.at[part(n)], slope_hbm.at[part(n)], out_sems.at[n]),
        )
        for n in range(steps)
    ]
    cot_loads = [
        pltpu.make_async_copy(cot_hbm.at[part(n)], sends.at[part(n), 1], cot_sems.at[n])
        for n in range(steps)
    ]
    for n in range(steps):
        loads[n].start()
        cot_loads[n].start()
    xs[0] = jnp.zeros((wide, ch), BF16)
    xs[rows + 1] = jnp.zeros((wide, ch), BF16)
    weight = jnp.concatenate(
        [jnp.concatenate([w_ref[3 * a + b] for b in range(3)], axis=1) for a in range(3)], axis=0
    )
    flat = rows_step * wide

    def bring(step):
        loads[step].wait()
        at = step * rows_step
        xs[1 + at : 1 + at + rows_step] = jnp.zeros((rows_step, wide, ch), BF16)
        xs[1 + at : 1 + at + rows_step, :cols, :] = x_in[at : at + rows_step]

    bring(0)
    for step in range(steps):
        if step + 1 < steps:
            bring(step + 1)
        at = step * rows_step
        left = jnp.concatenate(
            [xs[at + a : at + a + rows_step].reshape(flat, ch) for a in range(3)], axis=1
        )
        y = mm(left, weight)
        pre = y[:, ch : 2 * ch] + roll_rows(y[:, :ch], 1) + roll_rows(y[:, 2 * ch :], -1)
        act, slope = silu_parts(pre)
        sends[at : at + rows_step, 0] = act.astype(BF16).reshape(rows_step, wide, ch)[:, :cols]
        slopes[at : at + rows_step] = slope.astype(BF16).reshape(rows_step, wide, ch)
        cot_loads[step].wait()
        for store in stores[step]:
            store.start()
    for pair in stores:
        for store in pair:
            store.wait()


def hand_out(here_ref, total_ref, pieces):
    for peer, piece in enumerate(pieces):
        piece[...] = total_ref[jnp.bitwise_xor(here_ref[1], peer)].astype(piece.dtype)


def columns_kernel(rows_step, x_ref, slope_ref, cat_ref, near_ref):
    rows, cols, ch = x_ref.shape
    wide = cat_ref.shape[1] // rows
    flat = rows_step * wide
    pad = jnp.zeros((rows_step, wide - cols, ch), F32)
    for at in range(0, rows, rows_step):
        x = jnp.concatenate([x_ref[at : at + rows_step].astype(F32), pad], axis=1).reshape(flat, ch)
        x_cat = jnp.concatenate([roll_rows(x, 1), x, roll_rows(x, -1)], axis=1)
        cat_ref[:, at * wide : at * wide + flat] = x_cat.T.astype(BF16)
    near_ref[...] = slope_ref[...]


def taps_up(gs, at, rows_step):
    wide, ch = gs.shape[1:]
    return jnp.concatenate(
        [gs[at + 2 - a : at + 2 - a + rows_step].reshape(rows_step * wide, ch) for a in range(3)],
        axis=1,
    )


def spatial_wgrad_kernel(
    rows_step, scale, here_ref, got_ref, slope_ref, cat_ref, gs, *rest
):
    pieces, total_ref = rest[:-1], rest[-1]
    rows, cols, ch = got_ref.shape
    wide = gs.shape[1]
    flat = rows_step * wide
    gs[0] = jnp.zeros((wide, ch), BF16)
    gs[rows + 1] = jnp.zeros((wide, ch), BF16)
    for at in range(0, rows, rows_step):
        gs[1 + at : 1 + at + rows_step] = jnp.zeros((rows_step, wide, ch), BF16)
        gs[1 + at : 1 + at + rows_step, :cols, :] = (
            got_ref[at : at + rows_step].astype(F32)
            * slope_ref[at : at + rows_step, :cols, :].astype(F32)
        ).astype(BF16)
    total = jnp.zeros((3 * ch, 3 * ch), F32)
    for at in range(0, rows, rows_step):
        total = total + mm(cat_ref[:, at * wide : at * wide + flat], taps_up(gs, at, rows_step))
    total_ref[...] = (
        jnp.concatenate(
            [
                total[b * ch : (b + 1) * ch, a * ch : (a + 1) * ch]
                for a in range(3)
                for b in range(3)
            ],
            axis=0,
        )
        * scale
    ).reshape(total_ref.shape)
    hand_out(here_ref, total_ref, pieces)


def spatial_back_kernel(rows_step, w_ref, gs, back_ref):
    rows, cols, ch = back_ref.shape
    wide = gs.shape[1]
    weight = jnp.concatenate(
        [
            jnp.concatenate([w_ref[3 * a + b].astype(F32).T.astype(BF16) for b in range(3)], axis=1)
            for a in range(3)
        ],
        axis=0,
    )
    for at in range(0, rows, rows_step):
        y = mm(taps_up(gs, at, rows_step), weight)
        back = y[:, ch : 2 * ch] + roll_rows(y[:, :ch], -1) + roll_rows(y[:, 2 * ch :], 1)
        back_ref[at : at + rows_step] = back.astype(BF16).reshape(rows_step, wide, ch)[:, :cols]


def clear_halo(pad_ref, frames):
    zeros = jnp.zeros((HALO,) + pad_ref.shape[1:], pad_ref.dtype)
    pad_ref[:HALO] = zeros
    pad_ref[HALO + frames :] = zeros


def taps_of(pad_ref, at, count, step_size, sign):
    high, ch = pad_ref.shape[1:]
    pieces = [
        pad_ref[pl.ds(HALO + at + sign * (k - 2) * step_size, count)].reshape(count * high, ch)
        for k in range(TAPS)
    ]
    return jnp.concatenate(pieces, axis=1)


def temporal_kernel(
    step_frames, dil_ref, key_ref, got_hbm, tw_ref, uw_ref,
    grad_hbm, united_hbm, a0_hbm, cots_hbm, a1_hbm, feat_hbm, g1_hbm, g0_hbm,
    a0, a1, feat, cots, g0, g1, slope0, slope1, grad_feat, united_ref, act_ref, cot_ref, grad_ref,
    sems, in_sems, out_sems,
):
    frames, block, ch = act_ref.shape
    high = feat.shape[1]
    loads = [
        pltpu.make_async_copy(got_hbm.at[:, n], ref, in_sems.at[n])
        for n, ref in enumerate((act_ref, cot_ref))
    ]
    for load in loads:
        load.start()
    stores = [
        pltpu.make_async_copy(
            grad_ref.at[pl.ds(at, step_frames)], grad_hbm.at[pl.ds(at, step_frames)], out_sems.at[n]
        )
        for n, at in enumerate(range(0, frames, step_frames))
    ]
    segs = key_ref.shape[0]
    seg_frames = frames // segs
    inside = pl.ds(HALO, frames)
    copies = [
        pltpu.make_async_copy(source, target, sems.at[n])
        for n, (source, target) in enumerate(
            (
                (a1.at[inside], a1_hbm),
                (feat, feat_hbm),
                (g1.at[inside], g1_hbm),
                (g0.at[inside], g0_hbm),
                (a0.at[inside], a0_hbm),
                (cots, cots_hbm),
                (united_ref, united_hbm),
            )
        )
    ]
    for ref in (a0, a1, g0, g1):
        clear_halo(ref, frames)
    a0[HALO : HALO + frames] = jnp.zeros((frames, high, ch), BF16)
    cots[...] = jnp.zeros(cots.shape, cots.dtype)
    loads[0].wait()
    a0[HALO : HALO + frames, :block, :] = act_ref[...]
    copies[4].start()
    for layer, (source, target, slopes) in enumerate(((a0, a1, slope0), (a1, feat, slope1))):
        step_size = dil_ref[layer]
        weight = jnp.concatenate([tw_ref[layer, k] for k in range(TAPS)], axis=0)
        first = HALO if layer == 0 else 0
        for at in range(0, frames, step_frames):
            pre = mm(taps_of(source, at, step_frames, step_size, 1), weight)
            act, slope = silu_parts(pre)
            target[first + at : first + at + step_frames] = act.astype(BF16).reshape(
                step_frames, high, ch
            )
            slopes[at : at + step_frames] = slope.reshape(step_frames, high, ch)
        copies[layer].start()
    loads[1].wait()
    cots[:, :block, :] = cot_ref[...]
    copies[5].start()
    for seg in range(segs):
        low, top = seg * seg_frames, (seg + 1) * seg_frames
        here = low + key_ref[seg]
        key_part = mm(feat[here], uw_ref[1])
        main = mm(feat[low:top].reshape(seg_frames * high, ch), uw_ref[0]).reshape(
            seg_frames, high, ch
        )
        united_ref[low:top] = (main + key_part[None]).astype(BF16)[:, :block]
        mine = cots[low:top]
        total = jnp.sum(mine.astype(F32), axis=0)
        grad_feat[low:top] = mm_nt(mine.reshape(seg_frames * high, ch), uw_ref[0]).reshape(
            seg_frames, high, ch
        )
        key_term = sum(mm_nt(part, uw_ref[1]) for part in three_parts(total))
        grad_feat[here] = grad_feat[here] + key_term
        g1[HALO + low : HALO + top] = (grad_feat[low:top] * slope1[low:top]).astype(BF16)
    copies[6].start()
    for layer, source in ((1, g1), (0, g0)):
        copies[3 - layer].start()
        step_size = dil_ref[layer]
        weight = jnp.concatenate(
            [tw_ref[layer, k].astype(F32).T.astype(BF16) for k in range(TAPS)], axis=0
        )
        for n, at in enumerate(range(0, frames, step_frames)):
            grad = mm(taps_of(source, at, step_frames, step_size, -1), weight).reshape(
                step_frames, high, ch
            )
            if layer == 1:
                g0[HALO + at : HALO + at + step_frames] = (
                    grad * slope0[at : at + step_frames]
                ).astype(BF16)
            else:
                grad_ref[at : at + step_frames] = grad.astype(BF16)[:, :block]
                stores[n].start()
    for copy in copies + stores:
        copy.wait()


def temporal_wgrad_kernel(
    step_frames, scale, here_ref, dil_ref, key_ref,
    a0_hbm, g0_hbm, a1_hbm, g1_hbm, feat_hbm, cots_hbm, *rest
):
    pieces, (a0, g0, a1, g1, feat, cots, total_ref, sems) = rest[:-8], rest[-8:]
    frames, high, ch = feat.shape
    segs = key_ref.shape[0]
    seg_frames = frames // segs
    rows = step_frames * high
    inside = pl.ds(HALO, frames)
    copies = [
        pltpu.make_async_copy(source, target, sems.at[n])
        for n, (source, target) in enumerate(
            (
                (a0_hbm, a0.at[inside]),
                (g0_hbm, g0),
                (a1_hbm, a1.at[inside]),
                (g1_hbm, g1),
                (feat_hbm, feat),
                (cots_hbm, cots),
            )
        )
    ]
    for copy in copies:
        copy.start()
    clear_halo(a0, frames)
    clear_halo(a1, frames)
    totals = []
    for layer, acts, grads in ((0, a0, g0), (1, a1, g1)):
        copies[2 * layer].wait()
        copies[2 * layer + 1].wait()
        total = jnp.zeros((TAPS * ch, ch), F32)
        for at in range(0, frames, step_frames):
            total = total + mm_tn(
                taps_of(acts, at, step_frames, dil_ref[layer], 1),
                grads[at : at + step_frames].reshape(rows, ch),
            )
        totals.append(total)
    copies[4].wait()
    copies[5].wait()
    total = jnp.zeros((ch, ch), F32)
    for at in range(0, frames, step_frames):
        total = total + mm_tn(
            feat[at : at + step_frames].reshape(rows, ch),
            cots[at : at + step_frames].reshape(rows, ch),
        )
    keyed = jnp.zeros((ch, ch), F32)
    for seg in range(segs):
        low, top = seg * seg_frames, (seg + 1) * seg_frames
        key = feat[low + key_ref[seg]]
        seg_cot = jnp.sum(cots[low:top].astype(F32), axis=0)
        keyed = keyed + sum(mm_tn(key, part) for part in three_parts(seg_cot))
    peers = len(pieces)
    split = LAYERS * TAPS * ch // peers
    total_ref[:, :split] = (jnp.concatenate(totals, axis=0) * scale).reshape(peers, split, ch)
    total_ref[:, split:] = (jnp.concatenate([total, keyed], axis=0) * scale).reshape(
        peers, 2 * ch // peers, ch
    )
    hand_out(here_ref, total_ref, pieces)


def sum_kernel(*refs):
    refs[-1][...] = sum(ref[...].astype(F32) for ref in refs[:-1]).astype(refs[-1].dtype)


def join_kernel(first_ref, *refs):
    out_ref = refs[-1]
    split = first_ref.shape[0]
    out_ref[:split] = first_ref[...]
    out_ref[split:] = sum(ref[...].astype(F32) for ref in refs[:-1]).astype(out_ref.dtype)


def deal_kernel(here_ref, *refs):
    united_hbm, *pieces = refs[:-5]
    *outs, united_out, sem = refs[-5:]
    copy = pltpu.make_async_copy(united_hbm, united_out, sem.at[0])
    copy.start()
    for peer, piece in enumerate(pieces):
        place = jnp.bitwise_xor(here_ref[1], peer)
        at = 0
        for out_ref in outs:
            count = out_ref.shape[1]
            out_ref[place] = piece[at : at + count].astype(F32)
            at += count
    copy.wait()


def exchange(blocks):
    return lax.all_to_all(blocks, AXES, split_axis=0, concat_axis=0, tiled=True)


def flip(value, peer):
    size = lax.axis_size("grp")
    return lax.ppermute(value, "grp", [(i, i ^ peer) for i in range(size)])


def turn_by(value, turn):
    size = lax.axis_size("seg")
    return lax.ppermute(value, "seg", [(i, (i + turn) % size) for i in range(size)])


def sum_of(parts):
    shape = parts[0].shape
    return call(
        sum_kernel, [(shape, BF16, VMEM)], [], 0, len(parts) * 2 * shape[0] * shape[1],
        [(part, VMEM) for part in parts], SMALL_VMEM,
    )[0]


def reduce_in_grp(pieces):
    return sum_of([flip(piece, peer) if peer else piece for peer, piece in enumerate(pieces)])


def all_turns(value):
    return [turn_by(value, turn) if turn else value for turn in range(lax.axis_size("seg"))]


def local(
    frames_in, spatial_weight, temporal_weight, uniting_weight, key_index, dilation, cotangent
):
    held, rows, cols, ch = frames_in.shape
    assert held == 1
    pixels = rows * cols
    peers = lax.axis_size("grp")
    devices = lax.axis_size("seg") * peers
    frames = held * devices
    block = pixels // devices
    split = cols // block
    wide = round_up(cols + 1, 16)
    high = round_up(block, 16)
    rows_step = next(n for n in (4, 2, 1) if rows % n == 0)
    steps = rows // rows_step
    step_frames = max(n for n in range(1, frames + 1) if frames % n == 0 and n * high <= 512)
    scale = float((frames * pixels) ** -0.5)
    here = jnp.stack([lax.axis_index("seg"), lax.axis_index("grp")]).astype(jnp.int32)
    space_rows, time_rows, unite_rows = (n * ch // peers for n in (9, LAYERS * TAPS, 2))

    send, space_slope = call(
        functools.partial(spatial_fwd_kernel, rows_step),
        [((rows, 2, cols, ch), BF16, HBM), ((rows, wide, ch), BF16, HBM)],
        [
            pltpu.VMEM((rows, cols, ch), BF16),
            pltpu.VMEM((rows + 2, wide, ch), BF16),
            pltpu.VMEM((rows, 2, cols, ch), BF16),
            pltpu.VMEM((rows, wide, ch), BF16),
            pltpu.SemaphoreType.DMA((steps,)),
            pltpu.SemaphoreType.DMA((steps,)),
            pltpu.SemaphoreType.DMA((steps,)),
            pltpu.SemaphoreType.DMA((steps,)),
        ],
        2 * 9 * pixels * ch * ch,
        pixels * ch * 12,
        [(frames_in[0], HBM), (spatial_weight, VMEM), (cotangent[0], HBM)],
    )
    send = send.reshape(rows, 2, split, block, ch).swapaxes(1, 2).reshape(devices, 2, block, ch)
    got = exchange(send)

    padded = (frames + 2 * HALO, high, ch)
    whole = (frames, high, ch)
    grad_send, united_send, a0, cots, a1, feat, g1, g0 = call(
        functools.partial(temporal_kernel, step_frames),
        [((frames, block, ch), BF16, HBM)] * 2 + [(whole, BF16, HBM)] * 6,
        [
            pltpu.VMEM(padded, BF16),
            pltpu.VMEM(padded, BF16),
            pltpu.VMEM(whole, BF16),
            pltpu.VMEM(whole, BF16),
            pltpu.VMEM(padded, BF16),
            pltpu.VMEM(padded, BF16),
            pltpu.VMEM(whole, F32),
            pltpu.VMEM(whole, F32),
            pltpu.VMEM(whole, F32),
            pltpu.VMEM((frames, block, ch), BF16),
            pltpu.VMEM((frames, block, ch), BF16),
            pltpu.VMEM((frames, block, ch), BF16),
            pltpu.VMEM((frames, block, ch), BF16),
            pltpu.SemaphoreType.DMA((7,)),
            pltpu.SemaphoreType.DMA((2,)),
            pltpu.SemaphoreType.DMA((frames // step_frames,)),
        ],
        2 * 22 * frames * block * ch * ch,
        frames * block * ch * 18,
        [
            (dilation, SMEM), (key_index, SMEM), (got, HBM),
            (temporal_weight, VMEM), (uniting_weight, VMEM),
        ],
    )
    grad_time = exchange(grad_send).reshape(rows, cols, ch)
    time_pieces = call(
        functools.partial(temporal_wgrad_kernel, step_frames, scale),
        [((time_rows + unite_rows, ch), BF16, VMEM)] * peers,
        [
            pltpu.VMEM(padded, BF16),
            pltpu.VMEM(whole, BF16),
            pltpu.VMEM(padded, BF16),
            pltpu.VMEM(whole, BF16),
            pltpu.VMEM(whole, BF16),
            pltpu.VMEM(whole, BF16),
            pltpu.VMEM((peers, time_rows + unite_rows, ch), F32),
            pltpu.SemaphoreType.DMA((6,)),
        ],
        2 * 12 * frames * block * ch * ch,
        frames * block * ch * 14,
        [
            (here, SMEM), (dilation, SMEM), (key_index, SMEM),
            (a0, HBM), (g0, HBM), (a1, HBM), (g1, HBM), (feat, HBM), (cots, HBM),
        ],
    )
    time_sum = reduce_in_grp(time_pieces)
    time_sum, grad_time = lax.optimization_barrier((time_sum, grad_time))
    x_cat, space_slope = call(
        functools.partial(columns_kernel, rows_step),
        [((3 * ch, rows * wide), BF16, VMEM), ((rows, wide, ch), BF16, VMEM)],
        [],
        0,
        pixels * ch * 12,
        [(frames_in[0], VMEM), (space_slope, VMEM)],
        MID_VMEM,
    )
    gs, *space_pieces = call(
        functools.partial(spatial_wgrad_kernel, rows_step, scale),
        [((rows + 2, wide, ch), BF16, VMEM)] + [((space_rows, ch), BF16, VMEM)] * peers,
        [pltpu.VMEM((peers, space_rows, ch), F32)],
        2 * 9 * pixels * ch * ch,
        pixels * ch * 18,
        [(here, SMEM), (grad_time, VMEM), (space_slope, VMEM), (x_cat, VMEM)],
        MID_VMEM,
    )
    united_send, space_pieces[0] = lax.optimization_barrier((united_send, space_pieces[0]))
    united = exchange(united_send)
    (back,) = call(
        functools.partial(spatial_back_kernel, rows_step),
        [((rows, cols, ch), BF16, VMEM)],
        [],
        2 * 9 * pixels * ch * ch,
        pixels * ch * 4,
        [(spatial_weight, VMEM), (gs, VMEM)],
        MID_VMEM,
    )
    space_pieces[0], back = lax.optimization_barrier((space_pieces[0], back))
    space_parts = [flip(part, peer) if peer else part for peer, part in enumerate(space_pieces)]
    (plane,) = call(
        join_kernel,
        [((time_rows + unite_rows + space_rows, ch), BF16, VMEM)],
        [],
        0,
        2 * (peers + 10) * space_rows * ch,
        [(time_sum, VMEM)] + [(part, VMEM) for part in space_parts],
        SMALL_VMEM,
    )
    piece = sum_of(all_turns(plane))
    *grads, united = call(
        deal_kernel,
        [((peers, count, ch), F32, VMEM) for count in (time_rows, unite_rows, space_rows)]
        + [((frames, block, ch), BF16, HBM)],
        [pltpu.SemaphoreType.DMA((1,))],
        0,
        6 * 21 * ch * ch,
        [(here, SMEM), (united, HBM)]
        + [(flip(piece, peer) if peer else piece, VMEM) for peer in range(peers)],
        SMALL_VMEM,
    )
    return (
        united.reshape(frames_in.shape),
        back[None],
        grads[2].reshape(9, ch, ch),
        grads[0].reshape(LAYERS, TAPS, ch, ch),
        grads[1].reshape(2, ch, ch),
    )


def solution(mesh):
    frame_spec = P(AXES, None, None, None)
    return jax.shard_map(
        local,
        mesh=mesh,
        in_specs=(frame_spec, P(), P(), P(), P(), P(), frame_spec),
        out_specs=(frame_spec, frame_spec, P(), P(), P()),
        check_vma=False,
    )
```

```python
import functools

import jax
import jax.numpy as jnp
from jax import lax
from jax.experimental import pallas as pl
from jax.experimental.pallas import tpu as pltpu
from jax.sharding import PartitionSpec as P

LAYERS = 2
TAPS = 5
DMAX = 8
HALO = 2 * DMAX
AXES = ("seg", "grp")
BF16 = jnp.bfloat16
F32 = jnp.float32
BIG_VMEM = 60 * 1024 * 1024
MID_VMEM = 24 * 1024 * 1024
SMALL_VMEM = 16 * 1024 * 1024


def round_up(value, step):
    return -(-value // step) * step


def silu_parts(value):
    sigma = 0.5 * jnp.tanh(0.5 * value) + 0.5
    act = value * sigma
    return act, sigma + act * (1.0 - sigma)


def mm(left, right):
    return jnp.dot(left, right, preferred_element_type=F32)


def mm_nt(left, right):
    return lax.dot_general(left, right, (((1,), (1,)), ((), ())), preferred_element_type=F32)


def mm_tn(left, right):
    return lax.dot_general(left, right, (((0,), (0,)), ((), ())), preferred_element_type=F32)


def three_parts(value):
    high = value.astype(BF16)
    rest = value - high.astype(F32)
    middle = rest.astype(BF16)
    return high, middle, (rest - middle.astype(F32)).astype(BF16)


VMEM = pl.BlockSpec(memory_space=pltpu.VMEM)
SMEM = pl.BlockSpec(memory_space=pltpu.SMEM)
HBM = pl.BlockSpec(memory_space=pltpu.HBM)


def call(kernel, outs, scratch, flops, moved, args, vmem=BIG_VMEM):
    return pl.pallas_call(
        kernel,
        out_shape=[jax.ShapeDtypeStruct(shape, kind) for shape, kind, _ in outs],
        in_specs=[spec for _, spec in args],
        out_specs=[spec for _, _, spec in outs],
        scratch_shapes=scratch,
        compiler_params=pltpu.CompilerParams(vmem_limit_bytes=vmem),
        cost_estimate=pl.CostEstimate(flops=flops, bytes_accessed=moved, transcendentals=0),
    )(*[value for value, _ in args])


def roll_rows(value, shift):
    return pltpu.roll(value, shift % value.shape[0], 0)


def spatial_pre(xs, weight, at, rows_step):
    wide, ch = xs.shape[1:]
    flat = rows_step * wide
    left = jnp.concatenate(
        [xs[at + a : at + a + rows_step].reshape(flat, ch) for a in range(3)], axis=1
    )
    y = mm(left, weight)
    return y[:, ch : 2 * ch] + roll_rows(y[:, :ch], 1) + roll_rows(y[:, 2 * ch :], -1)


def forward_weight(w_ref):
    return jnp.concatenate(
        [jnp.concatenate([w_ref[3 * a + b] for b in range(3)], axis=1) for a in range(3)], axis=0
    )


def clear_ends(ref):
    last = ref.shape[0] - 1
    ref[0] = jnp.zeros(ref.shape[1:], ref.dtype)
    ref[last] = jnp.zeros(ref.shape[1:], ref.dtype)


def put_rows(ref, at, value):
    count, cols, ch = value.shape
    ref[1 + at : 1 + at + count] = jnp.zeros((count,) + ref.shape[1:], ref.dtype)
    ref[1 + at : 1 + at + count, :cols, :] = value


def spatial_fwd_kernel(
    rows_step, x_hbm, w_ref, cot_hbm, send_hbm, x_in, xs, sends, in_sems, cot_sems, send_sems
):
    rows, cols, ch = x_in.shape
    wide = xs.shape[1]
    steps = rows // rows_step

    def part(step):
        return pl.ds(step * rows_step, rows_step)

    loads = [
        pltpu.make_async_copy(x_hbm.at[part(n)], x_in.at[part(n)], in_sems.at[n]) for n in range(steps)
    ]
    cot_loads = [
        pltpu.make_async_copy(cot_hbm.at[part(n)], sends.at[part(n), 1], cot_sems.at[n])
        for n in range(steps)
    ]
    stores = [
        pltpu.make_async_copy(sends.at[part(n)], send_hbm.at[part(n)], send_sems.at[n])
        for n in range(steps)
    ]
    for load in loads + cot_loads:
        load.start()
    clear_ends(xs)
    weight = forward_weight(w_ref)

    def bring(step):
        loads[step].wait()
        at = step * rows_step
        put_rows(xs, at, x_in[at : at + rows_step])

    bring(0)
    for step in range(steps):
        if step + 1 < steps:
            bring(step + 1)
        at = step * rows_step
        act, _ = silu_parts(spatial_pre(xs, weight, at, rows_step))
        sends[at : at + rows_step, 0] = act.astype(BF16).reshape(rows_step, wide, ch)[:, :cols]
        cot_loads[step].wait()
        stores[step].start()
    for store in stores:
        store.wait()


def spatial_slope_kernel(rows_step, x_ref, w_ref, slope_ref, xs):
    rows, cols, ch = x_ref.shape
    wide = xs.shape[1]
    clear_ends(xs)
    put_rows(xs, 0, x_ref[...])
    weight = forward_weight(w_ref)
    for at in range(0, rows, rows_step):
        _, slope = silu_parts(spatial_pre(xs, weight, at, rows_step))
        slope_ref[at : at + rows_step] = (
            slope.astype(BF16).reshape(rows_step, wide, ch)[:, :cols]
        )


def hand_out(here_ref, total_ref, pieces):
    for peer, piece in enumerate(pieces):
        piece[...] = total_ref[jnp.bitwise_xor(here_ref[1], peer)].astype(piece.dtype)


def taps_up(gs, at, rows_step):
    wide, ch = gs.shape[1:]
    return jnp.concatenate(
        [gs[at + 2 - a : at + 2 - a + rows_step].reshape(rows_step * wide, ch) for a in range(3)],
        axis=1,
    )


def fill_grads(rows_step, gs, got_ref, slope_ref):
    clear_ends(gs)
    for at in range(0, got_ref.shape[0], rows_step):
        grads = got_ref[at : at + rows_step].astype(F32)
        slopes = slope_ref[at : at + rows_step].astype(F32)
        put_rows(gs, at, (grads * slopes).astype(BF16))


def spatial_wgrad_kernel(rows_step, scale, here_ref, got_ref, slope_ref, x_ref, *rest):
    pieces, (gs, total_ref) = rest[:-2], rest[-2:]
    rows, cols, ch = got_ref.shape
    wide = gs.shape[1]
    flat = rows_step * wide
    pad = jnp.zeros((rows_step, wide - cols, ch), F32)
    fill_grads(rows_step, gs, got_ref, slope_ref)
    total = jnp.zeros((3 * ch, 3 * ch), F32)
    for at in range(0, rows, rows_step):
        x = jnp.concatenate([x_ref[at : at + rows_step].astype(F32), pad], axis=1).reshape(flat, ch)
        x_cat = jnp.concatenate([roll_rows(x, 1), x, roll_rows(x, -1)], axis=1)
        total = total + mm(x_cat.T.astype(BF16), taps_up(gs, at, rows_step))
    total_ref[...] = (
        jnp.concatenate(
            [
                total[b * ch : (b + 1) * ch, a * ch : (a + 1) * ch]
                for a in range(3)
                for b in range(3)
            ],
            axis=0,
        )
        * scale
    ).reshape(total_ref.shape)
    hand_out(here_ref, total_ref, pieces)


def spatial_back_kernel(rows_step, w_ref, got_ref, slope_ref, back_ref, gs):
    rows, cols, ch = back_ref.shape
    wide = gs.shape[1]
    weight = jnp.concatenate(
        [
            jnp.concatenate([w_ref[3 * a + b].astype(F32).T.astype(BF16) for b in range(3)], axis=1)
            for a in range(3)
        ],
        axis=0,
    )
    fill_grads(rows_step, gs, got_ref, slope_ref)
    for at in range(0, rows, rows_step):
        y = mm(taps_up(gs, at, rows_step), weight)
        back = y[:, ch : 2 * ch] + roll_rows(y[:, :ch], -1) + roll_rows(y[:, 2 * ch :], 1)
        back_ref[at : at + rows_step] = back.astype(BF16).reshape(rows_step, wide, ch)[:, :cols]


def clear_halo(pad_ref, frames):
    zeros = jnp.zeros((HALO,) + pad_ref.shape[1:], pad_ref.dtype)
    pad_ref[:HALO] = zeros
    pad_ref[HALO + frames :] = zeros


def taps_of(pad_ref, at, count, step_size, sign):
    high, ch = pad_ref.shape[1:]
    pieces = [
        pad_ref[pl.ds(HALO + at + sign * (k - 2) * step_size, count)].reshape(count * high, ch)
        for k in range(TAPS)
    ]
    return jnp.concatenate(pieces, axis=1)


def temporal_kernel(
    step_frames, dil_ref, key_ref, got_hbm, tw_ref, uw_ref,
    grad_hbm, united_hbm, a0_hbm, cots_hbm, a1_hbm, feat_hbm, g1_hbm, g0_hbm,
    a0, a1, feat, cots, g0, g1, slope0, slope1, grad_feat, united_ref, act_ref, cot_ref, grad_ref,
    sems, in_sems, out_sems,
):
    frames, block, ch = act_ref.shape
    high = feat.shape[1]
    loads = [
        pltpu.make_async_copy(got_hbm.at[:, n], ref, in_sems.at[n])
        for n, ref in enumerate((act_ref, cot_ref))
    ]
    for load in loads:
        load.start()
    stores = [
        pltpu.make_async_copy(
            grad_ref.at[pl.ds(at, step_frames)], grad_hbm.at[pl.ds(at, step_frames)], out_sems.at[n]
        )
        for n, at in enumerate(range(0, frames, step_frames))
    ]
    segs = key_ref.shape[0]
    seg_frames = frames // segs
    inside = pl.ds(HALO, frames)
    copies = [
        pltpu.make_async_copy(source, target, sems.at[n])
        for n, (source, target) in enumerate(
            (
                (a1.at[inside], a1_hbm),
                (feat, feat_hbm),
                (g1.at[inside], g1_hbm),
                (g0.at[inside], g0_hbm),
                (a0.at[inside], a0_hbm),
                (cots, cots_hbm),
                (united_ref, united_hbm),
            )
        )
    ]
    for ref in (a0, a1, g0, g1):
        clear_halo(ref, frames)
    a0[HALO : HALO + frames] = jnp.zeros((frames, high, ch), BF16)
    cots[...] = jnp.zeros(cots.shape, cots.dtype)
    loads[0].wait()
    a0[HALO : HALO + frames, :block, :] = act_ref[...]
    copies[4].start()
    for layer, (source, target, slopes) in enumerate(((a0, a1, slope0), (a1, feat, slope1))):
        step_size = dil_ref[layer]
        weight = jnp.concatenate([tw_ref[layer, k] for k in range(TAPS)], axis=0)
        first = HALO if layer == 0 else 0
        for at in range(0, frames, step_frames):
            pre = mm(taps_of(source, at, step_frames, step_size, 1), weight)
            act, slope = silu_parts(pre)
            target[first + at : first + at + step_frames] = act.astype(BF16).reshape(
                step_frames, high, ch
            )
            slopes[at : at + step_frames] = slope.reshape(step_frames, high, ch)
        copies[layer].start()
    loads[1].wait()
    cots[:, :block, :] = cot_ref[...]
    copies[5].start()
    for seg in range(segs):
        low, top = seg * seg_frames, (seg + 1) * seg_frames
        here = low + key_ref[seg]
        key_part = mm(feat[here], uw_ref[1])
        main = mm(feat[low:top].reshape(seg_frames * high, ch), uw_ref[0]).reshape(
            seg_frames, high, ch
        )
        united_ref[low:top] = (main + key_part[None]).astype(BF16)[:, :block]
        mine = cots[low:top]
        total = jnp.sum(mine.astype(F32), axis=0)
        grad_feat[low:top] = mm_nt(mine.reshape(seg_frames * high, ch), uw_ref[0]).reshape(
            seg_frames, high, ch
        )
        key_term = sum(mm_nt(part, uw_ref[1]) for part in three_parts(total))
        grad_feat[here] = grad_feat[here] + key_term
        g1[HALO + low : HALO + top] = (grad_feat[low:top] * slope1[low:top]).astype(BF16)
    copies[6].start()
    for layer, source in ((1, g1), (0, g0)):
        copies[3 - layer].start()
        step_size = dil_ref[layer]
        weight = jnp.concatenate(
            [tw_ref[layer, k].astype(F32).T.astype(BF16) for k in range(TAPS)], axis=0
        )
        for n, at in enumerate(range(0, frames, step_frames)):
            grad = mm(taps_of(source, at, step_frames, step_size, -1), weight).reshape(
                step_frames, high, ch
            )
            if layer == 1:
                g0[HALO + at : HALO + at + step_frames] = (
                    grad * slope0[at : at + step_frames]
                ).astype(BF16)
            else:
                grad_ref[at : at + step_frames] = grad.astype(BF16)[:, :block]
                stores[n].start()
    for copy in copies + stores:
        copy.wait()


def temporal_wgrad_kernel(
    step_frames, scale, here_ref, dil_ref, key_ref,
    a0_hbm, g0_hbm, a1_hbm, g1_hbm, feat_hbm, cots_hbm, *rest
):
    pieces, (a0, g0, a1, g1, feat, cots, total_ref, sems) = rest[:-8], rest[-8:]
    frames, high, ch = feat.shape
    segs = key_ref.shape[0]
    seg_frames = frames // segs
    rows = step_frames * high
    inside = pl.ds(HALO, frames)
    copies = [
        pltpu.make_async_copy(source, target, sems.at[n])
        for n, (source, target) in enumerate(
            (
                (a0_hbm, a0.at[inside]),
                (g0_hbm, g0),
                (a1_hbm, a1.at[inside]),
                (g1_hbm, g1),
                (feat_hbm, feat),
                (cots_hbm, cots),
            )
        )
    ]
    for copy in copies:
        copy.start()
    clear_halo(a0, frames)
    clear_halo(a1, frames)
    totals = []
    for layer, acts, grads in ((0, a0, g0), (1, a1, g1)):
        copies[2 * layer].wait()
        copies[2 * layer + 1].wait()
        total = jnp.zeros((TAPS * ch, ch), F32)
        for at in range(0, frames, step_frames):
            total = total + mm_tn(
                taps_of(acts, at, step_frames, dil_ref[layer], 1),
                grads[at : at + step_frames].reshape(rows, ch),
            )
        totals.append(total)
    copies[4].wait()
    copies[5].wait()
    total = jnp.zeros((ch, ch), F32)
    for at in range(0, frames, step_frames):
        total = total + mm_tn(
            feat[at : at + step_frames].reshape(rows, ch),
            cots[at : at + step_frames].reshape(rows, ch),
        )
    keyed = jnp.zeros((ch, ch), F32)
    for seg in range(segs):
        low, top = seg * seg_frames, (seg + 1) * seg_frames
        key = feat[low + key_ref[seg]]
        seg_cot = jnp.sum(cots[low:top].astype(F32), axis=0)
        keyed = keyed + sum(mm_tn(key, part) for part in three_parts(seg_cot))
    peers = len(pieces)
    split = LAYERS * TAPS * ch // peers
    total_ref[:, :split] = (jnp.concatenate(totals, axis=0) * scale).reshape(peers, split, ch)
    total_ref[:, split:] = (jnp.concatenate([total, keyed], axis=0) * scale).reshape(
        peers, 2 * ch // peers, ch
    )
    hand_out(here_ref, total_ref, pieces)


def sum_kernel(*refs):
    refs[-1][...] = sum(ref[...].astype(F32) for ref in refs[:-1]).astype(refs[-1].dtype)


def join_kernel(first_ref, *refs):
    out_ref = refs[-1]
    split = first_ref.shape[0]
    out_ref[:split] = first_ref[...]
    out_ref[split:] = sum(ref[...].astype(F32) for ref in refs[:-1]).astype(out_ref.dtype)


def deal_kernel(here_ref, *refs):
    united_hbm, *pieces = refs[:-5]
    *outs, united_out, sem = refs[-5:]
    copy = pltpu.make_async_copy(united_hbm, united_out, sem.at[0])
    copy.start()
    for peer, piece in enumerate(pieces):
        place = jnp.bitwise_xor(here_ref[1], peer)
        at = 0
        for out_ref in outs:
            count = out_ref.shape[1]
            out_ref[place] = piece[at : at + count].astype(F32)
            at += count
    copy.wait()


def exchange(blocks):
    return lax.all_to_all(blocks, AXES, split_axis=0, concat_axis=0, tiled=True)


def flip(value, peer):
    size = lax.axis_size("grp")
    return lax.ppermute(value, "grp", [(i, i ^ peer) for i in range(size)])


def turn_by(value, turn):
    size = lax.axis_size("seg")
    return lax.ppermute(value, "seg", [(i, (i + turn) % size) for i in range(size)])


def sum_of(parts):
    shape = parts[0].shape
    return call(
        sum_kernel, [(shape, BF16, VMEM)], [], 0, len(parts) * 2 * shape[0] * shape[1],
        [(part, VMEM) for part in parts], SMALL_VMEM,
    )[0]


def reduce_in_grp(pieces):
    return sum_of([flip(piece, peer) if peer else piece for peer, piece in enumerate(pieces)])


def all_turns(value):
    return [turn_by(value, turn) if turn else value for turn in range(lax.axis_size("seg"))]


def local(
    frames_in, spatial_weight, temporal_weight, uniting_weight, key_index, dilation, cotangent
):
    held, rows, cols, ch = frames_in.shape
    assert held == 1
    pixels = rows * cols
    peers = lax.axis_size("grp")
    devices = lax.axis_size("seg") * peers
    frames = held * devices
    block = pixels // devices
    split = cols // block
    wide = round_up(cols + 1, 16)
    high = round_up(block, 16)
    rows_step = next(n for n in (4, 2, 1) if rows % n == 0)
    steps = rows // rows_step
    step_frames = max(n for n in range(1, frames + 1) if frames % n == 0 and n * high <= 512)
    scale = float((frames * pixels) ** -0.5)
    here = jnp.stack([lax.axis_index("seg"), lax.axis_index("grp")]).astype(jnp.int32)
    space_rows, time_rows, unite_rows = (n * ch // peers for n in (9, LAYERS * TAPS, 2))

    (send,) = call(
        functools.partial(spatial_fwd_kernel, rows_step),
        [((rows, 2, cols, ch), BF16, HBM)],
        [
            pltpu.VMEM((rows, cols, ch), BF16),
            pltpu.VMEM((rows + 2, wide, ch), BF16),
            pltpu.VMEM((rows, 2, cols, ch), BF16),
            pltpu.SemaphoreType.DMA((steps,)),
            pltpu.SemaphoreType.DMA((steps,)),
            pltpu.SemaphoreType.DMA((steps,)),
        ],
        2 * 9 * pixels * ch * ch,
        pixels * ch * 8,
        [(frames_in[0], HBM), (spatial_weight, VMEM), (cotangent[0], HBM)],
    )
    send, frame = lax.optimization_barrier((send, frames_in[0]))
    send = send.reshape(rows, 2, split, block, ch).swapaxes(1, 2).reshape(devices, 2, block, ch)
    got = exchange(send)
    (space_slope,) = call(
        functools.partial(spatial_slope_kernel, rows_step),
        [((rows, cols, ch), BF16, VMEM)],
        [pltpu.VMEM((rows + 2, wide, ch), BF16)],
        2 * 9 * pixels * ch * ch,
        pixels * ch * 4,
        [(frame, VMEM), (spatial_weight, VMEM)],
    )
    got, space_slope = lax.optimization_barrier((got, space_slope))

    padded = (frames + 2 * HALO, high, ch)
    whole = (frames, high, ch)
    grad_send, united_send, a0, cots, a1, feat, g1, g0 = call(
        functools.partial(temporal_kernel, step_frames),
        [((frames, block, ch), BF16, HBM)] * 2 + [(whole, BF16, HBM)] * 6,
        [
            pltpu.VMEM(padded, BF16),
            pltpu.VMEM(padded, BF16),
            pltpu.VMEM(whole, BF16),
            pltpu.VMEM(whole, BF16),
            pltpu.VMEM(padded, BF16),
            pltpu.VMEM(padded, BF16),
            pltpu.VMEM(whole, F32),
            pltpu.VMEM(whole, F32),
            pltpu.VMEM(whole, F32),
            pltpu.VMEM((frames, block, ch), BF16),
            pltpu.VMEM((frames, block, ch), BF16),
            pltpu.VMEM((frames, block, ch), BF16),
            pltpu.VMEM((frames, block, ch), BF16),
            pltpu.SemaphoreType.DMA((7,)),
            pltpu.SemaphoreType.DMA((2,)),
            pltpu.SemaphoreType.DMA((frames // step_frames,)),
        ],
        2 * 22 * frames * block * ch * ch,
        frames * block * ch * 18,
        [
            (dilation, SMEM), (key_index, SMEM), (got, HBM),
            (temporal_weight, VMEM), (uniting_weight, VMEM),
        ],
    )
    grad_time = exchange(grad_send).reshape(rows, cols, ch)
    time_pieces = call(
        functools.partial(temporal_wgrad_kernel, step_frames, scale),
        [((time_rows + unite_rows, ch), BF16, VMEM)] * peers,
        [
            pltpu.VMEM(padded, BF16),
            pltpu.VMEM(whole, BF16),
            pltpu.VMEM(padded, BF16),
            pltpu.VMEM(whole, BF16),
            pltpu.VMEM(whole, BF16),
            pltpu.VMEM(whole, BF16),
            pltpu.VMEM((peers, time_rows + unite_rows, ch), F32),
            pltpu.SemaphoreType.DMA((6,)),
        ],
        2 * 12 * frames * block * ch * ch,
        frames * block * ch * 14,
        [
            (here, SMEM), (dilation, SMEM), (key_index, SMEM),
            (a0, HBM), (g0, HBM), (a1, HBM), (g1, HBM), (feat, HBM), (cots, HBM),
        ],
    )
    time_sum = reduce_in_grp(time_pieces)
    time_sum, grad_time = lax.optimization_barrier((time_sum, grad_time))
    united_send, grad_time = lax.optimization_barrier((united_send, grad_time))
    united = exchange(united_send)
    space_pieces = call(
        functools.partial(spatial_wgrad_kernel, rows_step, scale),
        [((space_rows, ch), BF16, VMEM)] * peers,
        [pltpu.VMEM((rows + 2, wide, ch), BF16), pltpu.VMEM((peers, space_rows, ch), F32)],
        2 * 9 * pixels * ch * ch,
        pixels * ch * 8,
        [(here, SMEM), (grad_time, VMEM), (space_slope, VMEM), (frame, VMEM)],
        MID_VMEM,
    )
    (back,) = call(
        functools.partial(spatial_back_kernel, rows_step),
        [((rows, cols, ch), BF16, VMEM)],
        [pltpu.VMEM((rows + 2, wide, ch), BF16)],
        2 * 9 * pixels * ch * ch,
        pixels * ch * 6,
        [(spatial_weight, VMEM), (grad_time, VMEM), (space_slope, VMEM)],
        MID_VMEM,
    )
    space_pieces = list(space_pieces)
    space_pieces[0], back = lax.optimization_barrier((space_pieces[0], back))
    space_parts = [flip(part, peer) if peer else part for peer, part in enumerate(space_pieces)]
    (plane,) = call(
        join_kernel,
        [((time_rows + unite_rows + space_rows, ch), BF16, VMEM)],
        [],
        0,
        2 * (peers + 10) * space_rows * ch,
        [(time_sum, VMEM)] + [(part, VMEM) for part in space_parts],
        SMALL_VMEM,
    )
    piece = sum_of(all_turns(plane))
    *grads, united = call(
        deal_kernel,
        [((peers, count, ch), F32, VMEM) for count in (time_rows, unite_rows, space_rows)]
        + [((frames, block, ch), BF16, HBM)],
        [pltpu.SemaphoreType.DMA((1,))],
        0,
        6 * 21 * ch * ch,
        [(here, SMEM), (united, HBM)]
        + [(flip(piece, peer) if peer else piece, VMEM) for peer in range(peers)],
        SMALL_VMEM,
    )
    return (
        united.reshape(frames_in.shape),
        back[None],
        grads[2].reshape(9, ch, ch),
        grads[0].reshape(LAYERS, TAPS, ch, ch),
        grads[1].reshape(2, ch, ch),
    )


def solution(mesh):
    frame_spec = P(AXES, None, None, None)
    return jax.shard_map(
        local,
        mesh=mesh,
        in_specs=(frame_spec, P(), P(), P(), P(), P(), frame_spec),
        out_specs=(frame_spec, frame_spec, P(), P(), P()),
        check_vma=False,
    )
```

```python
import functools

import jax
import jax.numpy as jnp
from jax import lax
from jax.experimental import pallas as pl
from jax.experimental.pallas import tpu as pltpu
from jax.sharding import PartitionSpec as P

LAYERS = 2
TAPS = 5
DMAX = 8
HALO = 2 * DMAX
AXES = ("seg", "grp")
BF16 = jnp.bfloat16
F32 = jnp.float32
BIG_VMEM = 60 * 1024 * 1024
MID_VMEM = 24 * 1024 * 1024
SMALL_VMEM = 16 * 1024 * 1024


def round_up(value, step):
    return -(-value // step) * step


def silu_parts(value):
    sigma = 0.5 * jnp.tanh(0.5 * value) + 0.5
    act = value * sigma
    return act, sigma + act * (1.0 - sigma)


def mm(left, right):
    return jnp.dot(left, right, preferred_element_type=F32)


def mm_nt(left, right):
    return lax.dot_general(left, right, (((1,), (1,)), ((), ())), preferred_element_type=F32)


def mm_tn(left, right):
    return lax.dot_general(left, right, (((0,), (0,)), ((), ())), preferred_element_type=F32)


def three_parts(value):
    high = value.astype(BF16)
    rest = value - high.astype(F32)
    middle = rest.astype(BF16)
    return high, middle, (rest - middle.astype(F32)).astype(BF16)


VMEM = pl.BlockSpec(memory_space=pltpu.VMEM)
SMEM = pl.BlockSpec(memory_space=pltpu.SMEM)
HBM = pl.BlockSpec(memory_space=pltpu.HBM)


def call(kernel, outs, scratch, flops, moved, args, vmem=BIG_VMEM):
    return pl.pallas_call(
        kernel,
        out_shape=[jax.ShapeDtypeStruct(shape, kind) for shape, kind, _ in outs],
        in_specs=[spec for _, spec in args],
        out_specs=[spec for _, _, spec in outs],
        scratch_shapes=scratch,
        compiler_params=pltpu.CompilerParams(vmem_limit_bytes=vmem),
        cost_estimate=pl.CostEstimate(flops=flops, bytes_accessed=moved, transcendentals=0),
    )(*[value for value, _ in args])


def roll_rows(value, shift):
    return pltpu.roll(value, shift % value.shape[0], 0)


def spatial_pre(xs, weight, at, rows_step):
    wide, ch = xs.shape[1:]
    flat = rows_step * wide
    left = jnp.concatenate(
        [xs[at + a : at + a + rows_step].reshape(flat, ch) for a in range(3)], axis=1
    )
    y = mm(left, weight)
    return y[:, ch : 2 * ch] + roll_rows(y[:, :ch], 1) + roll_rows(y[:, 2 * ch :], -1)


def forward_weight(w_ref):
    return jnp.concatenate(
        [jnp.concatenate([w_ref[3 * a + b] for b in range(3)], axis=1) for a in range(3)], axis=0
    )


def clear_ends(ref):
    last = ref.shape[0] - 1
    ref[0] = jnp.zeros(ref.shape[1:], ref.dtype)
    ref[last] = jnp.zeros(ref.shape[1:], ref.dtype)


def put_rows(ref, at, value):
    count, cols, ch = value.shape
    ref[1 + at : 1 + at + count] = jnp.zeros((count,) + ref.shape[1:], ref.dtype)
    ref[1 + at : 1 + at + count, :cols, :] = value


def spatial_fwd_kernel(
    rows_step, x_hbm, w_ref, cot_hbm, send_hbm, x_in, xs, sends, in_sems, cot_sems, send_sems
):
    rows, cols, ch = x_in.shape
    wide = xs.shape[1]
    steps = rows // rows_step

    def part(step):
        return pl.ds(step * rows_step, rows_step)

    loads = [
        pltpu.make_async_copy(x_hbm.at[part(n)], x_in.at[part(n)], in_sems.at[n]) for n in range(steps)
    ]
    cot_loads = [
        pltpu.make_async_copy(cot_hbm.at[part(n)], sends.at[part(n), 1], cot_sems.at[n])
        for n in range(steps)
    ]
    stores = [
        pltpu.make_async_copy(sends.at[part(n)], send_hbm.at[part(n)], send_sems.at[n])
        for n in range(steps)
    ]
    for load in loads + cot_loads:
        load.start()
    clear_ends(xs)
    weight = forward_weight(w_ref)

    def bring(step):
        loads[step].wait()
        at = step * rows_step
        put_rows(xs, at, x_in[at : at + rows_step])

    bring(0)
    for step in range(steps):
        if step + 1 < steps:
            bring(step + 1)
        at = step * rows_step
        act, _ = silu_parts(spatial_pre(xs, weight, at, rows_step))
        sends[at : at + rows_step, 0] = act.astype(BF16).reshape(rows_step, wide, ch)[:, :cols]
        cot_loads[step].wait()
        stores[step].start()
    for store in stores:
        store.wait()


def spatial_slope_kernel(rows_step, x_ref, w_ref, slope_ref, xs):
    rows, cols, ch = x_ref.shape
    wide = xs.shape[1]
    clear_ends(xs)
    put_rows(xs, 0, x_ref[...])
    weight = forward_weight(w_ref)
    for at in range(0, rows, rows_step):
        _, slope = silu_parts(spatial_pre(xs, weight, at, rows_step))
        slope_ref[at : at + rows_step] = (
            slope.astype(BF16).reshape(rows_step, wide, ch)[:, :cols]
        )


def hand_out(here_ref, total_ref, pieces):
    for peer, piece in enumerate(pieces):
        piece[...] = total_ref[jnp.bitwise_xor(here_ref[1], peer)].astype(piece.dtype)


def taps_up(gs, at, rows_step):
    wide, ch = gs.shape[1:]
    return jnp.concatenate(
        [gs[at + 2 - a : at + 2 - a + rows_step].reshape(rows_step * wide, ch) for a in range(3)],
        axis=1,
    )


def fill_grads(rows_step, gs, got_ref, slope_ref):
    clear_ends(gs)
    for at in range(0, got_ref.shape[0], rows_step):
        grads = got_ref[at : at + rows_step, 0].astype(F32)
        slopes = slope_ref[at : at + rows_step].astype(F32)
        put_rows(gs, at, (grads * slopes).astype(BF16))


def spatial_wgrad_kernel(rows_step, scale, here_ref, got_ref, slope_ref, x_ref, *rest):
    pieces, (gs, total_ref) = rest[:-2], rest[-2:]
    rows, _, cols, ch = got_ref.shape
    wide = gs.shape[1]
    flat = rows_step * wide
    pad = jnp.zeros((rows_step, wide - cols, ch), F32)
    fill_grads(rows_step, gs, got_ref, slope_ref)
    total = jnp.zeros((3 * ch, 3 * ch), F32)
    for at in range(0, rows, rows_step):
        x = jnp.concatenate([x_ref[at : at + rows_step].astype(F32), pad], axis=1).reshape(flat, ch)
        x_cat = jnp.concatenate([roll_rows(x, 1), x, roll_rows(x, -1)], axis=1)
        total = total + mm(x_cat.T.astype(BF16), taps_up(gs, at, rows_step))
    total_ref[...] = (
        jnp.concatenate(
            [
                total[b * ch : (b + 1) * ch, a * ch : (a + 1) * ch]
                for a in range(3)
                for b in range(3)
            ],
            axis=0,
        )
        * scale
    ).reshape(total_ref.shape)
    hand_out(here_ref, total_ref, pieces)


def spatial_back_kernel(rows_step, w_ref, got_ref, slope_ref, back_ref, united_ref, gs):
    rows, cols, ch = back_ref.shape
    wide = gs.shape[1]
    weight = jnp.concatenate(
        [
            jnp.concatenate([w_ref[3 * a + b].astype(F32).T.astype(BF16) for b in range(3)], axis=1)
            for a in range(3)
        ],
        axis=0,
    )
    fill_grads(rows_step, gs, got_ref, slope_ref)
    for at in range(0, rows, rows_step):
        y = mm(taps_up(gs, at, rows_step), weight)
        back = y[:, ch : 2 * ch] + roll_rows(y[:, :ch], -1) + roll_rows(y[:, 2 * ch :], 1)
        back_ref[at : at + rows_step] = back.astype(BF16).reshape(rows_step, wide, ch)[:, :cols]
    united_ref[...] = got_ref[:, 1]


def clear_halo(pad_ref, frames):
    zeros = jnp.zeros((HALO,) + pad_ref.shape[1:], pad_ref.dtype)
    pad_ref[:HALO] = zeros
    pad_ref[HALO + frames :] = zeros


def taps_of(pad_ref, at, count, step_size, sign):
    high, ch = pad_ref.shape[1:]
    pieces = [
        pad_ref[pl.ds(HALO + at + sign * (k - 2) * step_size, count)].reshape(count * high, ch)
        for k in range(TAPS)
    ]
    return jnp.concatenate(pieces, axis=1)


def temporal_kernel(
    step_frames, dil_ref, key_ref, got_hbm, tw_ref, uw_ref,
    send_hbm, a0_hbm, cots_hbm, a1_hbm, feat_hbm, g1_hbm, g0_hbm,
    a0, a1, feat, cots, g0, g1, slope0, slope1, grad_feat, united_ref, act_ref, cot_ref, grad_ref,
    sems, in_sems, out_sems,
):
    frames, block, ch = act_ref.shape
    high = feat.shape[1]
    loads = [
        pltpu.make_async_copy(got_hbm.at[:, n], ref, in_sems.at[n])
        for n, ref in enumerate((act_ref, cot_ref))
    ]
    for load in loads:
        load.start()
    stores = [
        pltpu.make_async_copy(
            grad_ref.at[pl.ds(at, step_frames)], send_hbm.at[pl.ds(at, step_frames), 0], out_sems.at[n]
        )
        for n, at in enumerate(range(0, frames, step_frames))
    ]
    segs = key_ref.shape[0]
    seg_frames = frames // segs
    inside = pl.ds(HALO, frames)
    copies = [
        pltpu.make_async_copy(source, target, sems.at[n])
        for n, (source, target) in enumerate(
            (
                (a1.at[inside], a1_hbm),
                (feat, feat_hbm),
                (g1.at[inside], g1_hbm),
                (g0.at[inside], g0_hbm),
                (a0.at[inside], a0_hbm),
                (cots, cots_hbm),
                (united_ref, send_hbm.at[:, 1]),
            )
        )
    ]
    for ref in (a0, a1, g0, g1):
        clear_halo(ref, frames)
    a0[HALO : HALO + frames] = jnp.zeros((frames, high, ch), BF16)
    cots[...] = jnp.zeros(cots.shape, cots.dtype)
    loads[0].wait()
    a0[HALO : HALO + frames, :block, :] = act_ref[...]
    copies[4].start()
    for layer, (source, target, slopes) in enumerate(((a0, a1, slope0), (a1, feat, slope1))):
        step_size = dil_ref[layer]
        weight = jnp.concatenate([tw_ref[layer, k] for k in range(TAPS)], axis=0)
        first = HALO if layer == 0 else 0
        for at in range(0, frames, step_frames):
            pre = mm(taps_of(source, at, step_frames, step_size, 1), weight)
            act, slope = silu_parts(pre)
            target[first + at : first + at + step_frames] = act.astype(BF16).reshape(
                step_frames, high, ch
            )
            slopes[at : at + step_frames] = slope.reshape(step_frames, high, ch)
        copies[layer].start()
    loads[1].wait()
    cots[:, :block, :] = cot_ref[...]
    copies[5].start()
    for seg in range(segs):
        low, top = seg * seg_frames, (seg + 1) * seg_frames
        here = low + key_ref[seg]
        key_part = mm(feat[here], uw_ref[1])
        main = mm(feat[low:top].reshape(seg_frames * high, ch), uw_ref[0]).reshape(
            seg_frames, high, ch
        )
        united_ref[low:top] = (main + key_part[None]).astype(BF16)[:, :block]
        mine = cots[low:top]
        total = jnp.sum(mine.astype(F32), axis=0)
        grad_feat[low:top] = mm_nt(mine.reshape(seg_frames * high, ch), uw_ref[0]).reshape(
            seg_frames, high, ch
        )
        key_term = sum(mm_nt(part, uw_ref[1]) for part in three_parts(total))
        grad_feat[here] = grad_feat[here] + key_term
        g1[HALO + low : HALO + top] = (grad_feat[low:top] * slope1[low:top]).astype(BF16)
    copies[6].start()
    for layer, source in ((1, g1), (0, g0)):
        copies[3 - layer].start()
        step_size = dil_ref[layer]
        weight = jnp.concatenate(
            [tw_ref[layer, k].astype(F32).T.astype(BF16) for k in range(TAPS)], axis=0
        )
        for n, at in enumerate(range(0, frames, step_frames)):
            grad = mm(taps_of(source, at, step_frames, step_size, -1), weight).reshape(
                step_frames, high, ch
            )
            if layer == 1:
                g0[HALO + at : HALO + at + step_frames] = (
                    grad * slope0[at : at + step_frames]
                ).astype(BF16)
            else:
                grad_ref[at : at + step_frames] = grad.astype(BF16)[:, :block]
                stores[n].start()
    for copy in copies + stores:
        copy.wait()


def temporal_wgrad_kernel(
    step_frames, scale, here_ref, dil_ref, key_ref,
    a0_hbm, g0_hbm, a1_hbm, g1_hbm, feat_hbm, cots_hbm, *rest
):
    pieces, (a0, g0, a1, g1, feat, cots, total_ref, sems) = rest[:-8], rest[-8:]
    frames, high, ch = feat.shape
    segs = key_ref.shape[0]
    seg_frames = frames // segs
    rows = step_frames * high
    inside = pl.ds(HALO, frames)
    copies = [
        pltpu.make_async_copy(source, target, sems.at[n])
        for n, (source, target) in enumerate(
            (
                (a0_hbm, a0.at[inside]),
                (g0_hbm, g0),
                (a1_hbm, a1.at[inside]),
                (g1_hbm, g1),
                (feat_hbm, feat),
                (cots_hbm, cots),
            )
        )
    ]
    for copy in copies:
        copy.start()
    clear_halo(a0, frames)
    clear_halo(a1, frames)
    totals = []
    for layer, acts, grads in ((0, a0, g0), (1, a1, g1)):
        copies[2 * layer].wait()
        copies[2 * layer + 1].wait()
        total = jnp.zeros((TAPS * ch, ch), F32)
        for at in range(0, frames, step_frames):
            total = total + mm_tn(
                taps_of(acts, at, step_frames, dil_ref[layer], 1),
                grads[at : at + step_frames].reshape(rows, ch),
            )
        totals.append(total)
    copies[4].wait()
    copies[5].wait()
    total = jnp.zeros((ch, ch), F32)
    for at in range(0, frames, step_frames):
        total = total + mm_tn(
            feat[at : at + step_frames].reshape(rows, ch),
            cots[at : at + step_frames].reshape(rows, ch),
        )
    keyed = jnp.zeros((ch, ch), F32)
    for seg in range(segs):
        low, top = seg * seg_frames, (seg + 1) * seg_frames
        key = feat[low + key_ref[seg]]
        seg_cot = jnp.sum(cots[low:top].astype(F32), axis=0)
        keyed = keyed + sum(mm_tn(key, part) for part in three_parts(seg_cot))
    peers = len(pieces)
    split = LAYERS * TAPS * ch // peers
    total_ref[:, :split] = (jnp.concatenate(totals, axis=0) * scale).reshape(peers, split, ch)
    total_ref[:, split:] = (jnp.concatenate([total, keyed], axis=0) * scale).reshape(
        peers, 2 * ch // peers, ch
    )
    hand_out(here_ref, total_ref, pieces)


def sum_kernel(*refs):
    refs[-1][...] = sum(ref[...].astype(F32) for ref in refs[:-1]).astype(refs[-1].dtype)


def deal_kernel(here_ref, time_ref, *refs):
    pieces, (time_out, unite_out, space_out) = refs[:-3], refs[-3:]
    split = time_out.shape[1]
    time_out[...] = time_ref[:, :split].astype(F32)
    unite_out[...] = time_ref[:, split:].astype(F32)
    for peer, piece in enumerate(pieces):
        space_out[jnp.bitwise_xor(here_ref[1], peer)] = piece[...].astype(F32)


def exchange(blocks):
    return lax.all_to_all(blocks, AXES, split_axis=0, concat_axis=0, tiled=True)


def flip(value, peer):
    size = lax.axis_size("grp")
    return lax.ppermute(value, "grp", [(i, i ^ peer) for i in range(size)])


def turn_by(value, turn):
    size = lax.axis_size("seg")
    return lax.ppermute(value, "seg", [(i, (i + turn) % size) for i in range(size)])


def sum_of(parts):
    shape = parts[0].shape
    return call(
        sum_kernel, [(shape, BF16, VMEM)], [], 0, len(parts) * 2 * shape[0] * shape[1],
        [(part, VMEM) for part in parts], SMALL_VMEM,
    )[0]


def reduce_in_grp(pieces):
    return sum_of([flip(piece, peer) if peer else piece for peer, piece in enumerate(pieces)])


def all_turns(value):
    return [turn_by(value, turn) if turn else value for turn in range(lax.axis_size("seg"))]


def local(
    frames_in, spatial_weight, temporal_weight, uniting_weight, key_index, dilation, cotangent
):
    held, rows, cols, ch = frames_in.shape
    assert held == 1
    pixels = rows * cols
    peers = lax.axis_size("grp")
    devices = lax.axis_size("seg") * peers
    frames = held * devices
    block = pixels // devices
    split = cols // block
    wide = round_up(cols + 1, 16)
    high = round_up(block, 16)
    rows_step = next(n for n in (4, 2, 1) if rows % n == 0)
    steps = rows // rows_step
    step_frames = max(n for n in range(1, frames + 1) if frames % n == 0 and n * high <= 512)
    scale = float((frames * pixels) ** -0.5)
    here = jnp.stack([lax.axis_index("seg"), lax.axis_index("grp")]).astype(jnp.int32)
    space_rows, time_rows, unite_rows = (n * ch // peers for n in (9, LAYERS * TAPS, 2))

    (send,) = call(
        functools.partial(spatial_fwd_kernel, rows_step),
        [((rows, 2, cols, ch), BF16, HBM)],
        [
            pltpu.VMEM((rows, cols, ch), BF16),
            pltpu.VMEM((rows + 2, wide, ch), BF16),
            pltpu.VMEM((rows, 2, cols, ch), BF16),
            pltpu.SemaphoreType.DMA((steps,)),
            pltpu.SemaphoreType.DMA((steps,)),
            pltpu.SemaphoreType.DMA((steps,)),
        ],
        2 * 9 * pixels * ch * ch,
        pixels * ch * 8,
        [(frames_in[0], HBM), (spatial_weight, VMEM), (cotangent[0], HBM)],
    )
    send, frame = lax.optimization_barrier((send, frames_in[0]))
    send = send.reshape(rows, 2, split, block, ch).swapaxes(1, 2).reshape(devices, 2, block, ch)
    got = exchange(send)
    (space_slope,) = call(
        functools.partial(spatial_slope_kernel, rows_step),
        [((rows, cols, ch), BF16, VMEM)],
        [pltpu.VMEM((rows + 2, wide, ch), BF16)],
        2 * 9 * pixels * ch * ch,
        pixels * ch * 4,
        [(frame, VMEM), (spatial_weight, VMEM)],
    )
    got, space_slope = lax.optimization_barrier((got, space_slope))

    padded = (frames + 2 * HALO, high, ch)
    whole = (frames, high, ch)
    send, a0, cots, a1, feat, g1, g0 = call(
        functools.partial(temporal_kernel, step_frames),
        [((frames, 2, block, ch), BF16, HBM)] + [(whole, BF16, HBM)] * 6,
        [
            pltpu.VMEM(padded, BF16),
            pltpu.VMEM(padded, BF16),
            pltpu.VMEM(whole, BF16),
            pltpu.VMEM(whole, BF16),
            pltpu.VMEM(padded, BF16),
            pltpu.VMEM(padded, BF16),
            pltpu.VMEM(whole, F32),
            pltpu.VMEM(whole, F32),
            pltpu.VMEM(whole, F32),
            pltpu.VMEM((frames, block, ch), BF16),
            pltpu.VMEM((frames, block, ch), BF16),
            pltpu.VMEM((frames, block, ch), BF16),
            pltpu.VMEM((frames, block, ch), BF16),
            pltpu.SemaphoreType.DMA((7,)),
            pltpu.SemaphoreType.DMA((2,)),
            pltpu.SemaphoreType.DMA((frames // step_frames,)),
        ],
        2 * 22 * frames * block * ch * ch,
        frames * block * ch * 18,
        [
            (dilation, SMEM), (key_index, SMEM), (got, HBM),
            (temporal_weight, VMEM), (uniting_weight, VMEM),
        ],
    )
    got = exchange(send).reshape(rows, split, 2, block, ch).swapaxes(1, 2)
    got = got.reshape(rows, 2, cols, ch)
    time_pieces = call(
        functools.partial(temporal_wgrad_kernel, step_frames, scale),
        [((time_rows + unite_rows, ch), BF16, VMEM)] * peers,
        [
            pltpu.VMEM(padded, BF16),
            pltpu.VMEM(whole, BF16),
            pltpu.VMEM(padded, BF16),
            pltpu.VMEM(whole, BF16),
            pltpu.VMEM(whole, BF16),
            pltpu.VMEM(whole, BF16),
            pltpu.VMEM((peers, time_rows + unite_rows, ch), F32),
            pltpu.SemaphoreType.DMA((6,)),
        ],
        2 * 12 * frames * block * ch * ch,
        frames * block * ch * 14,
        [
            (here, SMEM), (dilation, SMEM), (key_index, SMEM),
            (a0, HBM), (g0, HBM), (a1, HBM), (g1, HBM), (feat, HBM), (cots, HBM),
        ],
    )
    time_piece = sum_of(all_turns(reduce_in_grp(time_pieces)))
    time_grads = lax.all_gather(time_piece, "grp", axis=0)
    _, got = lax.optimization_barrier((time_piece, got))
    space_pieces = call(
        functools.partial(spatial_wgrad_kernel, rows_step, scale),
        [((space_rows, ch), BF16, VMEM)] * peers,
        [pltpu.VMEM((rows + 2, wide, ch), BF16), pltpu.VMEM((peers, space_rows, ch), F32)],
        2 * 9 * pixels * ch * ch,
        pixels * ch * 8,
        [(here, SMEM), (got, VMEM), (space_slope, VMEM), (frame, VMEM)],
        MID_VMEM,
    )
    back, united = call(
        functools.partial(spatial_back_kernel, rows_step),
        [((rows, cols, ch), BF16, VMEM)] * 2,
        [pltpu.VMEM((rows + 2, wide, ch), BF16)],
        2 * 9 * pixels * ch * ch,
        pixels * ch * 10,
        [(spatial_weight, VMEM), (got, VMEM), (space_slope, VMEM)],
        MID_VMEM,
    )
    space_pieces = list(space_pieces)
    space_pieces[0], back = lax.optimization_barrier((space_pieces[0], back))
    piece = sum_of(all_turns(reduce_in_grp(space_pieces)))
    grads = call(
        deal_kernel,
        [((peers, count, ch), F32, VMEM) for count in (time_rows, unite_rows, space_rows)],
        [],
        0,
        6 * 21 * ch * ch,
        [(here, SMEM), (time_grads, VMEM)]
        + [(flip(piece, peer) if peer else piece, VMEM) for peer in range(peers)],
        SMALL_VMEM,
    )
    return (
        united.reshape(frames_in.shape),
        back[None],
        grads[2].reshape(9, ch, ch),
        grads[0].reshape(LAYERS, TAPS, ch, ch),
        grads[1].reshape(2, ch, ch),
    )


def solution(mesh):
    frame_spec = P(AXES, None, None, None)
    return jax.shard_map(
        local,
        mesh=mesh,
        in_specs=(frame_spec, P(), P(), P(), P(), P(), frame_spec),
        out_specs=(frame_spec, frame_spec, P(), P(), P()),
        check_vma=False,
    )
```

```python
import functools

import jax
import jax.numpy as jnp
from jax import lax
from jax.experimental import pallas as pl
from jax.experimental.pallas import tpu as pltpu
from jax.sharding import PartitionSpec as P

LAYERS = 2
TAPS = 5
DMAX = 8
HALO = 2 * DMAX
AXES = ("seg", "grp")
BF16 = jnp.bfloat16
F32 = jnp.float32
BIG_VMEM = 60 * 1024 * 1024
MID_VMEM = 24 * 1024 * 1024
SMALL_VMEM = 16 * 1024 * 1024


def round_up(value, step):
    return -(-value // step) * step


def silu_parts(value):
    sigma = 0.5 * jnp.tanh(0.5 * value) + 0.5
    act = value * sigma
    return act, sigma + act * (1.0 - sigma)


def mm(left, right):
    return jnp.dot(left, right, preferred_element_type=F32)


def mm_nt(left, right):
    return lax.dot_general(left, right, (((1,), (1,)), ((), ())), preferred_element_type=F32)


def mm_tn(left, right):
    return lax.dot_general(left, right, (((0,), (0,)), ((), ())), preferred_element_type=F32)


def three_parts(value):
    high = value.astype(BF16)
    rest = value - high.astype(F32)
    middle = rest.astype(BF16)
    return high, middle, (rest - middle.astype(F32)).astype(BF16)


VMEM = pl.BlockSpec(memory_space=pltpu.VMEM)
SMEM = pl.BlockSpec(memory_space=pltpu.SMEM)
HBM = pl.BlockSpec(memory_space=pltpu.HBM)


def call(kernel, outs, scratch, flops, moved, args, vmem=BIG_VMEM):
    return pl.pallas_call(
        kernel,
        out_shape=[jax.ShapeDtypeStruct(shape, kind) for shape, kind, _ in outs],
        in_specs=[spec for _, spec in args],
        out_specs=[spec for _, _, spec in outs],
        scratch_shapes=scratch,
        compiler_params=pltpu.CompilerParams(vmem_limit_bytes=vmem),
        cost_estimate=pl.CostEstimate(flops=flops, bytes_accessed=moved, transcendentals=0),
    )(*[value for value, _ in args])


def roll_rows(value, shift):
    return pltpu.roll(value, shift % value.shape[0], 0)


def spatial_pre(xs, weight, at, rows_step):
    wide, ch = xs.shape[1:]
    flat = rows_step * wide
    left = jnp.concatenate(
        [xs[at + a : at + a + rows_step].reshape(flat, ch) for a in range(3)], axis=1
    )
    y = mm(left, weight)
    return y[:, ch : 2 * ch] + roll_rows(y[:, :ch], 1) + roll_rows(y[:, 2 * ch :], -1)


def forward_weight(w_ref):
    return jnp.concatenate(
        [jnp.concatenate([w_ref[3 * a + b] for b in range(3)], axis=1) for a in range(3)], axis=0
    )


def clear_ends(ref):
    last = ref.shape[0] - 1
    ref[0] = jnp.zeros(ref.shape[1:], ref.dtype)
    ref[last] = jnp.zeros(ref.shape[1:], ref.dtype)


def put_rows(ref, at, value):
    count, cols, ch = value.shape
    ref[1 + at : 1 + at + count] = jnp.zeros((count,) + ref.shape[1:], ref.dtype)
    ref[1 + at : 1 + at + count, :cols, :] = value


def spatial_fwd_kernel(
    rows_step, x_hbm, w_hbm, act_hbm, x_in, w_ref, xs, acts, in_sems, w_sem, out_sems
):
    rows, cols, ch = x_in.shape
    wide = xs.shape[1]
    steps = rows // rows_step

    def part(step):
        return pl.ds(step * rows_step, rows_step)

    loads = [
        pltpu.make_async_copy(x_hbm.at[part(n)], x_in.at[part(n)], in_sems.at[n]) for n in range(steps)
    ]
    stores = [
        pltpu.make_async_copy(acts.at[part(n)], act_hbm.at[part(n)], out_sems.at[n])
        for n in range(steps)
    ]
    w_load = pltpu.make_async_copy(w_hbm, w_ref, w_sem.at[0])
    w_load.start()
    for load in loads:
        load.start()
    clear_ends(xs)

    def bring(step):
        loads[step].wait()
        at = step * rows_step
        put_rows(xs, at, x_in[at : at + rows_step])

    bring(0)
    w_load.wait()
    weight = forward_weight(w_ref)
    for step in range(steps):
        if step + 1 < steps:
            bring(step + 1)
        at = step * rows_step
        act, _ = silu_parts(spatial_pre(xs, weight, at, rows_step))
        acts[at : at + rows_step] = act.astype(BF16).reshape(rows_step, wide, ch)[:, :cols]
        stores[step].start()
    for store in stores:
        store.wait()


def spatial_slope_kernel(rows_step, x_ref, w_ref, slope_ref, xs):
    rows, cols, ch = x_ref.shape
    wide = xs.shape[1]
    clear_ends(xs)
    put_rows(xs, 0, x_ref[...])
    weight = forward_weight(w_ref)
    for at in range(0, rows, rows_step):
        _, slope = silu_parts(spatial_pre(xs, weight, at, rows_step))
        slope_ref[at : at + rows_step] = (
            slope.astype(BF16).reshape(rows_step, wide, ch)[:, :cols]
        )


def hand_out(here_ref, total_ref, pieces):
    for peer, piece in enumerate(pieces):
        piece[...] = total_ref[jnp.bitwise_xor(here_ref[1], peer)].astype(piece.dtype)


def taps_up(gs, at, rows_step):
    wide, ch = gs.shape[1:]
    return jnp.concatenate(
        [gs[at + 2 - a : at + 2 - a + rows_step].reshape(rows_step * wide, ch) for a in range(3)],
        axis=1,
    )


def fill_grads(rows_step, gs, got_ref, slope_ref):
    clear_ends(gs)
    for at in range(0, got_ref.shape[0], rows_step):
        grads = got_ref[at : at + rows_step].astype(F32)
        slopes = slope_ref[at : at + rows_step].astype(F32)
        put_rows(gs, at, (grads * slopes).astype(BF16))


def spatial_wgrad_kernel(rows_step, scale, here_ref, got_ref, slope_ref, x_ref, *rest):
    pieces, (gs, total_ref) = rest[:-2], rest[-2:]
    rows, cols, ch = got_ref.shape
    wide = gs.shape[1]
    flat = rows_step * wide
    pad = jnp.zeros((rows_step, wide - cols, ch), F32)
    fill_grads(rows_step, gs, got_ref, slope_ref)
    total = jnp.zeros((3 * ch, 3 * ch), F32)
    for at in range(0, rows, rows_step):
        x = jnp.concatenate([x_ref[at : at + rows_step].astype(F32), pad], axis=1).reshape(flat, ch)
        x_cat = jnp.concatenate([roll_rows(x, 1), x, roll_rows(x, -1)], axis=1)
        total = total + mm(x_cat.T.astype(BF16), taps_up(gs, at, rows_step))
    total_ref[...] = (
        jnp.concatenate(
            [
                total[b * ch : (b + 1) * ch, a * ch : (a + 1) * ch]
                for a in range(3)
                for b in range(3)
            ],
            axis=0,
        )
        * scale
    ).reshape(total_ref.shape)
    hand_out(here_ref, total_ref, pieces)


def spatial_back_kernel(rows_step, w_ref, got_ref, slope_ref, back_ref, gs):
    rows, cols, ch = back_ref.shape
    wide = gs.shape[1]
    weight = jnp.concatenate(
        [
            jnp.concatenate([w_ref[3 * a + b].astype(F32).T.astype(BF16) for b in range(3)], axis=1)
            for a in range(3)
        ],
        axis=0,
    )
    fill_grads(rows_step, gs, got_ref, slope_ref)
    for at in range(0, rows, rows_step):
        y = mm(taps_up(gs, at, rows_step), weight)
        back = y[:, ch : 2 * ch] + roll_rows(y[:, :ch], -1) + roll_rows(y[:, 2 * ch :], 1)
        back_ref[at : at + rows_step] = back.astype(BF16).reshape(rows_step, wide, ch)[:, :cols]


def place_of(here_ref, turns, peers, turn, peer):
    return lax.rem(here_ref[0] + (turns - turn), turns) * peers + jnp.bitwise_xor(here_ref[1], peer)


def clear_halo(pad_ref, frames):
    zeros = jnp.zeros((HALO,) + pad_ref.shape[1:], pad_ref.dtype)
    pad_ref[:HALO] = zeros
    pad_ref[HALO + frames :] = zeros


def taps_of(pad_ref, at, count, step_size, sign):
    high, ch = pad_ref.shape[1:]
    pieces = [
        pad_ref[pl.ds(HALO + at + sign * (k - 2) * step_size, count)].reshape(count * high, ch)
        for k in range(TAPS)
    ]
    return jnp.concatenate(pieces, axis=1)


def temporal_kernel(
    step_frames, here_ref, dil_ref, key_ref, act_hbm, tw_hbm, uw_hbm, *rest
):
    cot_parts = rest[:-27]
    (
        grad_hbm, united_hbm, a0_hbm, cots_hbm, a1_hbm, feat_hbm, g1_hbm, g0_hbm,
        a0, a1, feat, cots, g0, g1, slope0, slope1, grad_feat, united_ref, act_ref, cot_ref, grad_ref,
        tw_ref, uw_ref, sems, in_sems, out_sems, cot_sems,
    ) = rest[len(cot_parts) :]
    frames, block, ch = act_ref.shape
    high = feat.shape[1]
    peers, turns = cot_ref.shape[:2]
    loads = [
        pltpu.make_async_copy(source, ref, in_sems.at[n])
        for n, (source, ref) in enumerate(((act_hbm, act_ref), (tw_hbm, tw_ref), (uw_hbm, uw_ref)))
    ]
    cot_loads = [
        pltpu.make_async_copy(part, cot_ref.at[n], cot_sems.at[n]) for n, part in enumerate(cot_parts)
    ]
    for load in loads + cot_loads:
        load.start()
    stores = [
        pltpu.make_async_copy(
            grad_ref.at[pl.ds(at, step_frames)], grad_hbm.at[pl.ds(at, step_frames)], out_sems.at[n]
        )
        for n, at in enumerate(range(0, frames, step_frames))
    ]
    segs = key_ref.shape[0]
    seg_frames = frames // segs
    inside = pl.ds(HALO, frames)
    copies = [
        pltpu.make_async_copy(source, target, sems.at[n])
        for n, (source, target) in enumerate(
            (
                (a1.at[inside], a1_hbm),
                (feat, feat_hbm),
                (g1.at[inside], g1_hbm),
                (g0.at[inside], g0_hbm),
                (a0.at[inside], a0_hbm),
                (cots, cots_hbm),
                (united_ref, united_hbm),
            )
        )
    ]
    for ref in (a0, a1, g0, g1):
        clear_halo(ref, frames)
    a0[HALO : HALO + frames] = jnp.zeros((frames, high, ch), BF16)
    cots[...] = jnp.zeros(cots.shape, cots.dtype)
    loads[0].wait()
    a0[HALO : HALO + frames, :block, :] = act_ref[...]
    copies[4].start()
    loads[1].wait()
    loads[2].wait()
    for layer, (source, target, slopes) in enumerate(((a0, a1, slope0), (a1, feat, slope1))):
        step_size = dil_ref[layer]
        weight = jnp.concatenate([tw_ref[layer, k] for k in range(TAPS)], axis=0)
        first = HALO if layer == 0 else 0
        for at in range(0, frames, step_frames):
            pre = mm(taps_of(source, at, step_frames, step_size, 1), weight)
            act, slope = silu_parts(pre)
            target[first + at : first + at + step_frames] = act.astype(BF16).reshape(
                step_frames, high, ch
            )
            slopes[at : at + step_frames] = slope.reshape(step_frames, high, ch)
        copies[layer].start()
    for peer in range(peers):
        cot_loads[peer].wait()
        for turn in range(turns):
            cots[place_of(here_ref, turns, peers, turn, peer), :block, :] = cot_ref[peer, turn]
    copies[5].start()
    for seg in range(segs):
        low, top = seg * seg_frames, (seg + 1) * seg_frames
        here = low + key_ref[seg]
        key_part = mm(feat[here], uw_ref[1])
        main = mm(feat[low:top].reshape(seg_frames * high, ch), uw_ref[0]).reshape(
            seg_frames, high, ch
        )
        united_ref[low:top] = (main + key_part[None]).astype(BF16)[:, :block]
        mine = cots[low:top]
        total = jnp.sum(mine.astype(F32), axis=0)
        grad_feat[low:top] = mm_nt(mine.reshape(seg_frames * high, ch), uw_ref[0]).reshape(
            seg_frames, high, ch
        )
        key_term = sum(mm_nt(part, uw_ref[1]) for part in three_parts(total))
        grad_feat[here] = grad_feat[here] + key_term
        g1[HALO + low : HALO + top] = (grad_feat[low:top] * slope1[low:top]).astype(BF16)
    copies[6].start()
    for layer, source in ((1, g1), (0, g0)):
        copies[3 - layer].start()
        step_size = dil_ref[layer]
        weight = jnp.concatenate(
            [tw_ref[layer, k].astype(F32).T.astype(BF16) for k in range(TAPS)], axis=0
        )
        for n, at in enumerate(range(0, frames, step_frames)):
            grad = mm(taps_of(source, at, step_frames, step_size, -1), weight).reshape(
                step_frames, high, ch
            )
            if layer == 1:
                g0[HALO + at : HALO + at + step_frames] = (
                    grad * slope0[at : at + step_frames]
                ).astype(BF16)
            else:
                grad_ref[at : at + step_frames] = grad.astype(BF16)[:, :block]
                stores[n].start()
    for copy in copies + stores:
        copy.wait()


def temporal_wgrad_kernel(
    step_frames, scale, here_ref, dil_ref, key_ref,
    a0_hbm, g0_hbm, a1_hbm, g1_hbm, feat_hbm, cots_hbm, *rest
):
    pieces, (a0, g0, a1, g1, feat, cots, total_ref, sems) = rest[:-8], rest[-8:]
    frames, high, ch = feat.shape
    segs = key_ref.shape[0]
    seg_frames = frames // segs
    rows = step_frames * high
    inside = pl.ds(HALO, frames)
    copies = [
        pltpu.make_async_copy(source, target, sems.at[n])
        for n, (source, target) in enumerate(
            (
                (a0_hbm, a0.at[inside]),
                (g0_hbm, g0),
                (a1_hbm, a1.at[inside]),
                (g1_hbm, g1),
                (feat_hbm, feat),
                (cots_hbm, cots),
            )
        )
    ]
    for copy in copies:
        copy.start()
    clear_halo(a0, frames)
    clear_halo(a1, frames)
    totals = []
    for layer, acts, grads in ((0, a0, g0), (1, a1, g1)):
        copies[2 * layer].wait()
        copies[2 * layer + 1].wait()
        total = jnp.zeros((TAPS * ch, ch), F32)
        for at in range(0, frames, step_frames):
            total = total + mm_tn(
                taps_of(acts, at, step_frames, dil_ref[layer], 1),
                grads[at : at + step_frames].reshape(rows, ch),
            )
        totals.append(total)
    copies[4].wait()
    copies[5].wait()
    total = jnp.zeros((ch, ch), F32)
    for at in range(0, frames, step_frames):
        total = total + mm_tn(
            feat[at : at + step_frames].reshape(rows, ch),
            cots[at : at + step_frames].reshape(rows, ch),
        )
    keyed = jnp.zeros((ch, ch), F32)
    for seg in range(segs):
        low, top = seg * seg_frames, (seg + 1) * seg_frames
        key = feat[low + key_ref[seg]]
        seg_cot = jnp.sum(cots[low:top].astype(F32), axis=0)
        keyed = keyed + sum(mm_tn(key, part) for part in three_parts(seg_cot))
    peers = len(pieces)
    split = LAYERS * TAPS * ch // peers
    total_ref[:, :split] = (jnp.concatenate(totals, axis=0) * scale).reshape(peers, split, ch)
    total_ref[:, split:] = (jnp.concatenate([total, keyed], axis=0) * scale).reshape(
        peers, 2 * ch // peers, ch
    )
    hand_out(here_ref, total_ref, pieces)


def sum_kernel(*refs):
    refs[-1][...] = sum(ref[...].astype(F32) for ref in refs[:-1]).astype(refs[-1].dtype)


def join_kernel(first_ref, *refs):
    out_ref = refs[-1]
    split = first_ref.shape[0]
    out_ref[:split] = first_ref[...]
    out_ref[split:] = sum(ref[...].astype(F32) for ref in refs[:-1]).astype(out_ref.dtype)


def deal_kernel(pieces_ref, united_hbm, *refs):
    *outs, united_out, sem = refs
    copy = pltpu.make_async_copy(united_hbm, united_out, sem.at[0])
    copy.start()
    at = 0
    for out_ref in outs:
        count = out_ref.shape[1]
        out_ref[...] = pieces_ref[:, at : at + count].astype(F32)
        at += count
    copy.wait()


def exchange(blocks):
    return lax.all_to_all(blocks, AXES, split_axis=0, concat_axis=0, tiled=True)


def flip(value, peer):
    size = lax.axis_size("grp")
    return lax.ppermute(value, "grp", [(i, i ^ peer) for i in range(size)])


def turn_by(value, turn):
    size = lax.axis_size("seg")
    return lax.ppermute(value, "seg", [(i, (i + turn) % size) for i in range(size)])


def pick(values, index):
    return lax.dynamic_index_in_dim(values, index, 0, keepdims=False)


def spread_in_seg(values):
    size = lax.axis_size("seg")
    seg = lax.axis_index("seg")
    far = []
    for turn in range(size):
        mine = pick(values, lax.rem(seg + turn, size))
        far.append(turn_by(mine, turn) if turn else mine)
    return far


def spread_in_grp(far):
    grp = lax.axis_index("grp")
    near = []
    for peer in range(lax.axis_size("grp")):
        mine = jnp.stack([pick(part, grp ^ peer) for part in far])
        near.append(flip(mine, peer) if peer else mine)
    return near


def sum_of(parts):
    shape = parts[0].shape
    return call(
        sum_kernel, [(shape, BF16, VMEM)], [], 0, len(parts) * 2 * shape[0] * shape[1],
        [(part, VMEM) for part in parts], SMALL_VMEM,
    )[0]


def reduce_in_grp(pieces):
    return sum_of([flip(piece, peer) if peer else piece for peer, piece in enumerate(pieces)])


def all_turns(value):
    return [turn_by(value, turn) if turn else value for turn in range(lax.axis_size("seg"))]


def local(
    frames_in, spatial_weight, temporal_weight, uniting_weight, key_index, dilation, cotangent
):
    held, rows, cols, ch = frames_in.shape
    assert held == 1
    pixels = rows * cols
    peers = lax.axis_size("grp")
    devices = lax.axis_size("seg") * peers
    frames = held * devices
    block = pixels // devices
    split = cols // block
    wide = round_up(cols + 1, 16)
    high = round_up(block, 16)
    rows_step = next(n for n in (4, 2, 1) if rows % n == 0)
    steps = rows // rows_step
    step_frames = max(n for n in range(1, frames + 1) if frames % n == 0 and n * high <= 512)
    scale = float((frames * pixels) ** -0.5)
    here = jnp.stack([lax.axis_index("seg"), lax.axis_index("grp")]).astype(jnp.int32)
    space_rows, time_rows, unite_rows = (n * ch // peers for n in (9, LAYERS * TAPS, 2))

    cot_far = spread_in_seg(cotangent.reshape(-1, peers, block, ch))
    (send,) = call(
        functools.partial(spatial_fwd_kernel, rows_step),
        [((rows, cols, ch), BF16, HBM)],
        [
            pltpu.VMEM((rows, cols, ch), BF16),
            pltpu.VMEM(spatial_weight.shape, BF16),
            pltpu.VMEM((rows + 2, wide, ch), BF16),
            pltpu.VMEM((rows, cols, ch), BF16),
            pltpu.SemaphoreType.DMA((steps,)),
            pltpu.SemaphoreType.DMA((1,)),
            pltpu.SemaphoreType.DMA((steps,)),
        ],
        2 * 9 * pixels * ch * ch,
        pixels * ch * 4,
        [(frames_in[0], HBM), (spatial_weight, HBM)],
    )
    send, frame, cot_far[1] = lax.optimization_barrier((send, frames_in[0], cot_far[1]))
    got = exchange(send.reshape(devices, block, ch))
    cot_near = spread_in_grp(cot_far)
    (space_slope,) = call(
        functools.partial(spatial_slope_kernel, rows_step),
        [((rows, cols, ch), BF16, VMEM)],
        [pltpu.VMEM((rows + 2, wide, ch), BF16)],
        2 * 9 * pixels * ch * ch,
        pixels * ch * 4,
        [(frame, VMEM), (spatial_weight, VMEM)],
    )
    got, space_slope = lax.optimization_barrier((got, space_slope))

    padded = (frames + 2 * HALO, high, ch)
    whole = (frames, high, ch)
    grad_send, united_send, a0, cots, a1, feat, g1, g0 = call(
        functools.partial(temporal_kernel, step_frames),
        [((frames, block, ch), BF16, HBM)] * 2 + [(whole, BF16, HBM)] * 6,
        [
            pltpu.VMEM(padded, BF16),
            pltpu.VMEM(padded, BF16),
            pltpu.VMEM(whole, BF16),
            pltpu.VMEM(whole, BF16),
            pltpu.VMEM(padded, BF16),
            pltpu.VMEM(padded, BF16),
            pltpu.VMEM(whole, F32),
            pltpu.VMEM(whole, F32),
            pltpu.VMEM(whole, F32),
            pltpu.VMEM((frames, block, ch), BF16),
            pltpu.VMEM((frames, block, ch), BF16),
            pltpu.VMEM((peers, devices // peers, block, ch), BF16),
            pltpu.VMEM((frames, block, ch), BF16),
            pltpu.VMEM(temporal_weight.shape, BF16),
            pltpu.VMEM(uniting_weight.shape, BF16),
            pltpu.SemaphoreType.DMA((7,)),
            pltpu.SemaphoreType.DMA((3,)),
            pltpu.SemaphoreType.DMA((frames // step_frames,)),
            pltpu.SemaphoreType.DMA((peers,)),
        ],
        2 * 22 * frames * block * ch * ch,
        frames * block * ch * 18,
        [
            (here, SMEM), (dilation, SMEM), (key_index, SMEM), (got, HBM),
            (temporal_weight, HBM), (uniting_weight, HBM),
        ]
        + [(part, HBM) for part in cot_near],
    )
    grad_time = exchange(grad_send).reshape(rows, cols, ch)
    time_pieces = call(
        functools.partial(temporal_wgrad_kernel, step_frames, scale),
        [((time_rows + unite_rows, ch), BF16, VMEM)] * peers,
        [
            pltpu.VMEM(padded, BF16),
            pltpu.VMEM(whole, BF16),
            pltpu.VMEM(padded, BF16),
            pltpu.VMEM(whole, BF16),
            pltpu.VMEM(whole, BF16),
            pltpu.VMEM(whole, BF16),
            pltpu.VMEM((peers, time_rows + unite_rows, ch), F32),
            pltpu.SemaphoreType.DMA((6,)),
        ],
        2 * 12 * frames * block * ch * ch,
        frames * block * ch * 14,
        [
            (here, SMEM), (dilation, SMEM), (key_index, SMEM),
            (a0, HBM), (g0, HBM), (a1, HBM), (g1, HBM), (feat, HBM), (cots, HBM),
        ],
    )
    time_sum = reduce_in_grp(time_pieces)
    time_sum, grad_time = lax.optimization_barrier((time_sum, grad_time))
    united_send, grad_time = lax.optimization_barrier((united_send, grad_time))
    united = exchange(united_send)
    space_pieces = call(
        functools.partial(spatial_wgrad_kernel, rows_step, scale),
        [((space_rows, ch), BF16, VMEM)] * peers,
        [pltpu.VMEM((rows + 2, wide, ch), BF16), pltpu.VMEM((peers, space_rows, ch), F32)],
        2 * 9 * pixels * ch * ch,
        pixels * ch * 8,
        [(here, SMEM), (grad_time, VMEM), (space_slope, VMEM), (frame, VMEM)],
        MID_VMEM,
    )
    (back,) = call(
        functools.partial(spatial_back_kernel, rows_step),
        [((rows, cols, ch), BF16, VMEM)],
        [pltpu.VMEM((rows + 2, wide, ch), BF16)],
        2 * 9 * pixels * ch * ch,
        pixels * ch * 6,
        [(spatial_weight, VMEM), (grad_time, VMEM), (space_slope, VMEM)],
        MID_VMEM,
    )
    space_pieces = list(space_pieces)
    space_pieces[0], back = lax.optimization_barrier((space_pieces[0], back))
    space_parts = [flip(part, peer) if peer else part for peer, part in enumerate(space_pieces)]
    (plane,) = call(
        join_kernel,
        [((time_rows + unite_rows + space_rows, ch), BF16, VMEM)],
        [],
        0,
        2 * (peers + 10) * space_rows * ch,
        [(time_sum, VMEM)] + [(part, VMEM) for part in space_parts],
        SMALL_VMEM,
    )
    piece = sum_of(all_turns(plane))
    *grads, united = call(
        deal_kernel,
        [((peers, count, ch), F32, VMEM) for count in (time_rows, unite_rows, space_rows)]
        + [((frames, block, ch), BF16, HBM)],
        [pltpu.SemaphoreType.DMA((1,))],
        0,
        6 * 21 * ch * ch,
        [(lax.all_gather(piece, "grp", axis=0), VMEM), (united, HBM)],
        SMALL_VMEM,
    )
    return (
        united.reshape(frames_in.shape),
        back[None],
        grads[2].reshape(9, ch, ch),
        grads[0].reshape(LAYERS, TAPS, ch, ch),
        grads[1].reshape(2, ch, ch),
    )


def solution(mesh):
    frame_spec = P(AXES, None, None, None)
    return jax.shard_map(
        local,
        mesh=mesh,
        in_specs=(frame_spec, P(), P(), P(), P(), P(), frame_spec),
        out_specs=(frame_spec, frame_spec, P(), P(), P()),
        check_vma=False,
    )
```

```python
import functools

import jax
import jax.numpy as jnp
from jax import lax
from jax.experimental import pallas as pl
from jax.experimental.pallas import tpu as pltpu
from jax.sharding import PartitionSpec as P

LAYERS = 2
TAPS = 5
DMAX = 8
HALO = 2 * DMAX
AXES = ("seg", "grp")
BF16 = jnp.bfloat16
F32 = jnp.float32
BIG_VMEM = 60 * 1024 * 1024
TIME_VMEM = 55 * 1024 * 1024
MID_VMEM = 24 * 1024 * 1024
SMALL_VMEM = 16 * 1024 * 1024


def round_up(value, step):
    return -(-value // step) * step


def silu_parts(value):
    sigma = 0.5 * jnp.tanh(0.5 * value) + 0.5
    act = value * sigma
    return act, sigma + act * (1.0 - sigma)


def mm(left, right):
    return jnp.dot(left, right, preferred_element_type=F32)


def mm_nt(left, right):
    return lax.dot_general(left, right, (((1,), (1,)), ((), ())), preferred_element_type=F32)


def mm_tn(left, right):
    return lax.dot_general(left, right, (((0,), (0,)), ((), ())), preferred_element_type=F32)


def three_parts(value):
    high = value.astype(BF16)
    rest = value - high.astype(F32)
    middle = rest.astype(BF16)
    return high, middle, (rest - middle.astype(F32)).astype(BF16)


VMEM = pl.BlockSpec(memory_space=pltpu.VMEM)
SMEM = pl.BlockSpec(memory_space=pltpu.SMEM)
HBM = pl.BlockSpec(memory_space=pltpu.HBM)


def call(kernel, outs, scratch, flops, moved, args, vmem=BIG_VMEM):
    return pl.pallas_call(
        kernel,
        out_shape=[jax.ShapeDtypeStruct(shape, kind) for shape, kind, _ in outs],
        in_specs=[spec for _, spec in args],
        out_specs=[spec for _, _, spec in outs],
        scratch_shapes=scratch,
        compiler_params=pltpu.CompilerParams(vmem_limit_bytes=vmem),
        cost_estimate=pl.CostEstimate(flops=flops, bytes_accessed=moved, transcendentals=0),
    )(*[value for value, _ in args])


def roll_rows(value, shift):
    return pltpu.roll(value, shift % value.shape[0], 0)


def spatial_pre(xs, weight, at, rows_step):
    wide, ch = xs.shape[1:]
    flat = rows_step * wide
    left = jnp.concatenate(
        [xs[at + a : at + a + rows_step].reshape(flat, ch) for a in range(3)], axis=1
    )
    y = mm(left, weight)
    return y[:, ch : 2 * ch] + roll_rows(y[:, :ch], 1) + roll_rows(y[:, 2 * ch :], -1)


def forward_weight(w_ref):
    return jnp.concatenate(
        [jnp.concatenate([w_ref[3 * a + b] for b in range(3)], axis=1) for a in range(3)], axis=0
    )


def clear_ends(ref):
    last = ref.shape[0] - 1
    ref[0] = jnp.zeros(ref.shape[1:], ref.dtype)
    ref[last] = jnp.zeros(ref.shape[1:], ref.dtype)


def put_rows(ref, at, value):
    count, cols, ch = value.shape
    ref[1 + at : 1 + at + count] = jnp.zeros((count,) + ref.shape[1:], ref.dtype)
    ref[1 + at : 1 + at + count, :cols, :] = value


def spatial_fwd_kernel(
    rows_step, x_hbm, w_hbm, cot_hbm, send_hbm,
    x_in, w_ref, xs, sends, in_sems, w_sem, cot_sems, send_sems,
):
    rows, cols, ch = x_in.shape
    wide = xs.shape[1]
    steps = rows // rows_step

    def part(step):
        return pl.ds(step * rows_step, rows_step)

    loads = [
        pltpu.make_async_copy(x_hbm.at[part(n)], x_in.at[part(n)], in_sems.at[n]) for n in range(steps)
    ]
    cot_loads = [
        pltpu.make_async_copy(cot_hbm.at[part(n)], sends.at[part(n), 1], cot_sems.at[n])
        for n in range(steps)
    ]
    stores = [
        pltpu.make_async_copy(sends.at[part(n)], send_hbm.at[part(n)], send_sems.at[n])
        for n in range(steps)
    ]
    w_load = pltpu.make_async_copy(w_hbm, w_ref, w_sem.at[0])
    for load in [loads[0], w_load] + loads[1:] + cot_loads:
        load.start()
    clear_ends(xs)

    def bring(step):
        loads[step].wait()
        at = step * rows_step
        put_rows(xs, at, x_in[at : at + rows_step])

    bring(0)
    w_load.wait()
    weight = forward_weight(w_ref)
    for step in range(steps):
        if step + 1 < steps:
            bring(step + 1)
        at = step * rows_step
        act, _ = silu_parts(spatial_pre(xs, weight, at, rows_step))
        sends[at : at + rows_step, 0] = act.astype(BF16).reshape(rows_step, wide, ch)[:, :cols]
        cot_loads[step].wait()
        stores[step].start()
    for store in stores:
        store.wait()


def spatial_slope_kernel(rows_step, x_ref, w_ref, slope_ref, xs):
    rows, cols, ch = x_ref.shape
    wide = xs.shape[1]
    clear_ends(xs)
    put_rows(xs, 0, x_ref[...])
    weight = forward_weight(w_ref)
    for at in range(0, rows, rows_step):
        _, slope = silu_parts(spatial_pre(xs, weight, at, rows_step))
        slope_ref[at : at + rows_step] = (
            slope.astype(BF16).reshape(rows_step, wide, ch)[:, :cols]
        )


def hand_out(here_ref, total_ref, pieces):
    for peer, piece in enumerate(pieces):
        piece[...] = total_ref[jnp.bitwise_xor(here_ref[1], peer)].astype(piece.dtype)


def taps_up(gs, at, rows_step):
    wide, ch = gs.shape[1:]
    return jnp.concatenate(
        [gs[at + 2 - a : at + 2 - a + rows_step].reshape(rows_step * wide, ch) for a in range(3)],
        axis=1,
    )


def fill_grads(rows_step, gs, got_ref, slope_ref):
    clear_ends(gs)
    for at in range(0, got_ref.shape[0], rows_step):
        grads = got_ref[at : at + rows_step].astype(F32)
        slopes = slope_ref[at : at + rows_step].astype(F32)
        put_rows(gs, at, (grads * slopes).astype(BF16))


def spatial_wgrad_kernel(rows_step, scale, here_ref, got_ref, slope_ref, x_ref, *rest):
    pieces, (gs, total_ref) = rest[:-2], rest[-2:]
    rows, cols, ch = got_ref.shape
    wide = gs.shape[1]
    flat = rows_step * wide
    pad = jnp.zeros((rows_step, wide - cols, ch), F32)
    fill_grads(rows_step, gs, got_ref, slope_ref)
    total = jnp.zeros((3 * ch, 3 * ch), F32)
    for at in range(0, rows, rows_step):
        x = jnp.concatenate([x_ref[at : at + rows_step].astype(F32), pad], axis=1).reshape(flat, ch)
        x_cat = jnp.concatenate([roll_rows(x, 1), x, roll_rows(x, -1)], axis=1)
        total = total + mm(x_cat.T.astype(BF16), taps_up(gs, at, rows_step))
    total_ref[...] = (
        jnp.concatenate(
            [
                total[b * ch : (b + 1) * ch, a * ch : (a + 1) * ch]
                for a in range(3)
                for b in range(3)
            ],
            axis=0,
        )
        * scale
    ).reshape(total_ref.shape)
    hand_out(here_ref, total_ref, pieces)


def spatial_back_kernel(rows_step, w_ref, got_ref, slope_ref, back_ref, gs):
    rows, cols, ch = back_ref.shape
    wide = gs.shape[1]
    weight = jnp.concatenate(
        [
            jnp.concatenate([w_ref[3 * a + b].astype(F32).T.astype(BF16) for b in range(3)], axis=1)
            for a in range(3)
        ],
        axis=0,
    )
    fill_grads(rows_step, gs, got_ref, slope_ref)
    for at in range(0, rows, rows_step):
        y = mm(taps_up(gs, at, rows_step), weight)
        back = y[:, ch : 2 * ch] + roll_rows(y[:, :ch], -1) + roll_rows(y[:, 2 * ch :], 1)
        back_ref[at : at + rows_step] = back.astype(BF16).reshape(rows_step, wide, ch)[:, :cols]


def clear_halo(pad_ref, frames):
    zeros = jnp.zeros((HALO,) + pad_ref.shape[1:], pad_ref.dtype)
    pad_ref[:HALO] = zeros
    pad_ref[HALO + frames :] = zeros


def taps_of(pad_ref, at, count, step_size, sign):
    high, ch = pad_ref.shape[1:]
    pieces = [
        pad_ref[pl.ds(HALO + at + sign * (k - 2) * step_size, count)].reshape(count * high, ch)
        for k in range(TAPS)
    ]
    return jnp.concatenate(pieces, axis=1)


def temporal_kernel(
    step_frames, dil_ref, key_ref, got_ref, tw_hbm, uw_hbm,
    grad_hbm, united_hbm, kept_hbm,
    a0, a1, feat, cots, g0, g1, slope0, slope1, united_ref, grad_ref, tw_ref, uw_ref,
    sems, in_sems, out_sems,
):
    frames, _, block, ch = got_ref.shape
    high = feat.shape[1]
    loads = [
        pltpu.make_async_copy(source, ref, in_sems.at[n])
        for n, (source, ref) in enumerate(((tw_hbm, tw_ref), (uw_hbm, uw_ref)))
    ]
    for load in loads:
        load.start()
    stores = [
        pltpu.make_async_copy(
            grad_ref.at[pl.ds(at, step_frames)], grad_hbm.at[pl.ds(at, step_frames)], out_sems.at[n]
        )
        for n, at in enumerate(range(0, frames, step_frames))
    ]
    segs = key_ref.shape[0]
    seg_frames = frames // segs
    inside = pl.ds(HALO, frames)
    copies = [
        pltpu.make_async_copy(source, target, sems.at[n])
        for n, (source, target) in enumerate(
            (
                (a1.at[inside], kept_hbm.at[0]),
                (feat, kept_hbm.at[1]),
                (g1.at[inside], kept_hbm.at[2]),
                (g0.at[inside], kept_hbm.at[3]),
                (a0.at[inside], kept_hbm.at[4]),
                (cots, kept_hbm.at[5]),
                (united_ref, united_hbm),
            )
        )
    ]
    for ref in (a0, a1, g0, g1):
        clear_halo(ref, frames)
    a0[HALO : HALO + frames] = jnp.zeros((frames, high, ch), BF16)
    cots[...] = jnp.zeros(cots.shape, cots.dtype)
    a0[HALO : HALO + frames, :block, :] = got_ref[:, 0]
    copies[4].start()
    for load in loads:
        load.wait()
    for layer, (source, target, slopes) in enumerate(((a0, a1, slope0), (a1, feat, slope1))):
        step_size = dil_ref[layer]
        weight = jnp.concatenate([tw_ref[layer, k] for k in range(TAPS)], axis=0)
        first = HALO if layer == 0 else 0
        for at in range(0, frames, step_frames):
            pre = mm(taps_of(source, at, step_frames, step_size, 1), weight)
            act, slope = silu_parts(pre)
            target[first + at : first + at + step_frames] = act.astype(BF16).reshape(
                step_frames, high, ch
            )
            slopes[at : at + step_frames] = slope.reshape(step_frames, high, ch)
        copies[layer].start()
    cots[:, :block, :] = got_ref[:, 1]
    copies[5].start()
    for seg in range(segs):
        low, top = seg * seg_frames, (seg + 1) * seg_frames
        here = low + key_ref[seg]
        key_part = mm(feat[here], uw_ref[1])
        main = mm(feat[low:top].reshape(seg_frames * high, ch), uw_ref[0]).reshape(
            seg_frames, high, ch
        )
        united_ref[low:top] = (main + key_part[None]).astype(BF16)[:, :block]
        mine = cots[low:top]
        total = jnp.sum(mine.astype(F32), axis=0)
        key_term = sum(mm_nt(part, uw_ref[1]) for part in three_parts(total))
        grad_feat = mm_nt(mine.reshape(seg_frames * high, ch), uw_ref[0]).reshape(
            seg_frames, high, ch
        )
        for n in range(seg_frames):
            grad = grad_feat[n] + jnp.where(key_ref[seg] == n, key_term, 0.0)
            g1[HALO + low + n] = (grad * slope1[low + n]).astype(BF16)
    copies[6].start()
    for layer, source in ((1, g1), (0, g0)):
        copies[3 - layer].start()
        step_size = dil_ref[layer]
        weight = jnp.concatenate(
            [tw_ref[layer, k].astype(F32).T.astype(BF16) for k in range(TAPS)], axis=0
        )
        for n, at in enumerate(range(0, frames, step_frames)):
            grad = mm(taps_of(source, at, step_frames, step_size, -1), weight).reshape(
                step_frames, high, ch
            )
            if layer == 1:
                g0[HALO + at : HALO + at + step_frames] = (
                    grad * slope0[at : at + step_frames]
                ).astype(BF16)
            else:
                grad_ref[at : at + step_frames] = grad.astype(BF16)[:, :block]
                stores[n].start()
    for copy in copies + stores:
        copy.wait()


def temporal_wgrad_kernel(
    step_frames, scale, here_ref, dil_ref, key_ref,
    kept_hbm, *rest
):
    pieces, (a0, g0, a1, g1, feat, cots, total_ref, sems) = rest[:-8], rest[-8:]
    frames, high, ch = feat.shape
    segs = key_ref.shape[0]
    seg_frames = frames // segs
    rows = step_frames * high
    inside = pl.ds(HALO, frames)
    copies = [
        pltpu.make_async_copy(source, target, sems.at[n])
        for n, (source, target) in enumerate(
            (
                (kept_hbm.at[4], a0.at[inside]),
                (kept_hbm.at[3], g0),
                (kept_hbm.at[0], a1.at[inside]),
                (kept_hbm.at[2], g1),
                (kept_hbm.at[1], feat),
                (kept_hbm.at[5], cots),
            )
        )
    ]
    for copy in copies:
        copy.start()
    clear_halo(a0, frames)
    clear_halo(a1, frames)
    totals = []
    for layer, acts, grads in ((0, a0, g0), (1, a1, g1)):
        copies[2 * layer].wait()
        copies[2 * layer + 1].wait()
        total = jnp.zeros((TAPS * ch, ch), F32)
        for at in range(0, frames, step_frames):
            total = total + mm_tn(
                taps_of(acts, at, step_frames, dil_ref[layer], 1),
                grads[at : at + step_frames].reshape(rows, ch),
            )
        totals.append(total)
    copies[4].wait()
    copies[5].wait()
    total = jnp.zeros((ch, ch), F32)
    for at in range(0, frames, step_frames):
        total = total + mm_tn(
            feat[at : at + step_frames].reshape(rows, ch),
            cots[at : at + step_frames].reshape(rows, ch),
        )
    keyed = jnp.zeros((ch, ch), F32)
    for seg in range(segs):
        low, top = seg * seg_frames, (seg + 1) * seg_frames
        key = feat[low + key_ref[seg]]
        seg_cot = jnp.sum(cots[low:top].astype(F32), axis=0)
        keyed = keyed + sum(mm_tn(key, part) for part in three_parts(seg_cot))
    peers = len(pieces)
    split = LAYERS * TAPS * ch // peers
    total_ref[:, :split] = (jnp.concatenate(totals, axis=0) * scale).reshape(peers, split, ch)
    total_ref[:, split:] = (jnp.concatenate([total, keyed], axis=0) * scale).reshape(
        peers, 2 * ch // peers, ch
    )
    hand_out(here_ref, total_ref, pieces)


def copy_kernel(from_ref, to_ref):
    to_ref[...] = from_ref[...]


def sum_kernel(*refs):
    refs[-1][...] = sum(ref[...].astype(F32) for ref in refs[:-1]).astype(refs[-1].dtype)


def join_kernel(first_ref, *refs):
    out_ref = refs[-1]
    split = first_ref.shape[0]
    out_ref[:split] = first_ref[...]
    out_ref[split:] = sum(ref[...].astype(F32) for ref in refs[:-1]).astype(out_ref.dtype)


def deal_kernel(pieces_ref, united_hbm, *refs):
    *outs, united_out, sem = refs
    copy = pltpu.make_async_copy(united_hbm, united_out, sem.at[0])
    copy.start()
    at = 0
    for out_ref in outs:
        count = out_ref.shape[1]
        out_ref[...] = pieces_ref[:, at : at + count].astype(F32)
        at += count
    copy.wait()


def exchange(blocks):
    return lax.all_to_all(blocks, AXES, split_axis=0, concat_axis=0, tiled=True)


def flip(value, peer):
    size = lax.axis_size("grp")
    return lax.ppermute(value, "grp", [(i, i ^ peer) for i in range(size)])


def turn_by(value, turn):
    size = lax.axis_size("seg")
    return lax.ppermute(value, "seg", [(i, (i + turn) % size) for i in range(size)])


def sum_of(parts):
    shape = parts[0].shape
    return call(
        sum_kernel, [(shape, BF16, VMEM)], [], 0, len(parts) * 2 * shape[0] * shape[1],
        [(part, VMEM) for part in parts], SMALL_VMEM,
    )[0]


def reduce_in_grp(pieces):
    return sum_of([flip(piece, peer) if peer else piece for peer, piece in enumerate(pieces)])


def all_turns(value):
    return [turn_by(value, turn) if turn else value for turn in range(lax.axis_size("seg"))]


def local(
    frames_in, spatial_weight, temporal_weight, uniting_weight, key_index, dilation, cotangent
):
    held, rows, cols, ch = frames_in.shape
    assert held == 1
    pixels = rows * cols
    peers = lax.axis_size("grp")
    devices = lax.axis_size("seg") * peers
    frames = held * devices
    block = pixels // devices
    split = cols // block
    wide = round_up(cols + 1, 16)
    high = round_up(block, 16)
    rows_step = next(n for n in (4, 2, 1) if rows % n == 0)
    steps = rows // rows_step
    step_frames, narrow_step = (
        max(n for n in range(1, frames + 1) if frames % n == 0 and n * high <= most)
        for most in (512, 256)
    )
    scale = float((frames * pixels) ** -0.5)
    here = jnp.stack([lax.axis_index("seg"), lax.axis_index("grp")]).astype(jnp.int32)
    space_rows, time_rows, unite_rows = (n * ch // peers for n in (9, LAYERS * TAPS, 2))

    (send,) = call(
        functools.partial(spatial_fwd_kernel, rows_step),
        [((rows, 2, cols, ch), BF16, HBM)],
        [
            pltpu.VMEM((rows, cols, ch), BF16),
            pltpu.VMEM(spatial_weight.shape, BF16),
            pltpu.VMEM((rows + 2, wide, ch), BF16),
            pltpu.VMEM((rows, 2, cols, ch), BF16),
            pltpu.SemaphoreType.DMA((steps,)),
            pltpu.SemaphoreType.DMA((1,)),
            pltpu.SemaphoreType.DMA((steps,)),
            pltpu.SemaphoreType.DMA((steps,)),
        ],
        2 * 9 * pixels * ch * ch,
        pixels * ch * 8,
        [(frames_in[0], HBM), (spatial_weight, HBM), (cotangent[0], HBM)],
    )
    send, frame = lax.optimization_barrier((send, frames_in[0]))
    send = send.reshape(rows, 2, split, block, ch).swapaxes(1, 2).reshape(devices, 2, block, ch)
    got = exchange(send)
    (space_slope,) = call(
        functools.partial(spatial_slope_kernel, rows_step),
        [((rows, cols, ch), BF16, VMEM)],
        [pltpu.VMEM((rows + 2, wide, ch), BF16)],
        2 * 9 * pixels * ch * ch,
        pixels * ch * 4,
        [(frame, VMEM), (spatial_weight, VMEM)],
    )
    got, space_slope = lax.optimization_barrier((got, space_slope))

    padded = (frames + 2 * HALO, high, ch)
    whole = (frames, high, ch)
    grad_send, united_send, kept = call(
        functools.partial(temporal_kernel, narrow_step),
        [((frames, block, ch), BF16, HBM)] * 2 + [((6,) + whole, BF16, HBM)],
        [
            pltpu.VMEM(padded, BF16),
            pltpu.VMEM(padded, BF16),
            pltpu.VMEM(whole, BF16),
            pltpu.VMEM(whole, BF16),
            pltpu.VMEM(padded, BF16),
            pltpu.VMEM(padded, BF16),
            pltpu.VMEM(whole, F32),
            pltpu.VMEM(whole, F32),
            pltpu.VMEM((frames, block, ch), BF16),
            pltpu.VMEM((frames, block, ch), BF16),
            pltpu.VMEM(temporal_weight.shape, BF16),
            pltpu.VMEM(uniting_weight.shape, BF16),
            pltpu.SemaphoreType.DMA((7,)),
            pltpu.SemaphoreType.DMA((2,)),
            pltpu.SemaphoreType.DMA((frames // narrow_step,)),
        ],
        2 * 22 * frames * block * ch * ch,
        frames * block * ch * 18,
        [
            (dilation, SMEM), (key_index, SMEM), (got, VMEM),
            (temporal_weight, HBM), (uniting_weight, HBM),
        ],
        TIME_VMEM,
    )
    grad_time = exchange(grad_send).reshape(rows, cols, ch)
    time_pieces = call(
        functools.partial(temporal_wgrad_kernel, step_frames, scale),
        [((time_rows + unite_rows, ch), BF16, VMEM)] * peers,
        [
            pltpu.VMEM(padded, BF16),
            pltpu.VMEM(whole, BF16),
            pltpu.VMEM(padded, BF16),
            pltpu.VMEM(whole, BF16),
            pltpu.VMEM(whole, BF16),
            pltpu.VMEM(whole, BF16),
            pltpu.VMEM((peers, time_rows + unite_rows, ch), F32),
            pltpu.SemaphoreType.DMA((6,)),
        ],
        2 * 12 * frames * block * ch * ch,
        frames * block * ch * 14,
        [
            (here, SMEM), (dilation, SMEM), (key_index, SMEM),
            (kept, HBM),
        ],
    )
    (space_slope,) = call(
        copy_kernel,
        [((rows, cols, ch), BF16, VMEM)],
        [],
        0,
        pixels * ch * 4,
        [(space_slope, VMEM)],
        MID_VMEM,
    )
    time_sum = reduce_in_grp(time_pieces)
    time_sum, space_slope, grad_time = lax.optimization_barrier((time_sum, space_slope, grad_time))
    united_send, grad_time = lax.optimization_barrier((united_send, grad_time))
    united = exchange(united_send)
    space_pieces = call(
        functools.partial(spatial_wgrad_kernel, rows_step, scale),
        [((space_rows, ch), BF16, VMEM)] * peers,
        [pltpu.VMEM((rows + 2, wide, ch), BF16), pltpu.VMEM((peers, space_rows, ch), F32)],
        2 * 9 * pixels * ch * ch,
        pixels * ch * 8,
        [(here, SMEM), (grad_time, VMEM), (space_slope, VMEM), (frame, VMEM)],
        MID_VMEM,
    )
    (back,) = call(
        functools.partial(spatial_back_kernel, rows_step),
        [((rows, cols, ch), BF16, VMEM)],
        [pltpu.VMEM((rows + 2, wide, ch), BF16)],
        2 * 9 * pixels * ch * ch,
        pixels * ch * 6,
        [(spatial_weight, VMEM), (grad_time, VMEM), (space_slope, VMEM)],
        MID_VMEM,
    )
    space_pieces = list(space_pieces)
    space_pieces[0], back = lax.optimization_barrier((space_pieces[0], back))
    space_parts = [flip(part, peer) if peer else part for peer, part in enumerate(space_pieces)]
    (plane,) = call(
        join_kernel,
        [((time_rows + unite_rows + space_rows, ch), BF16, VMEM)],
        [],
        0,
        2 * (peers + 10) * space_rows * ch,
        [(time_sum, VMEM)] + [(part, VMEM) for part in space_parts],
        SMALL_VMEM,
    )
    piece = sum_of(all_turns(plane))
    *grads, united = call(
        deal_kernel,
        [((peers, count, ch), F32, VMEM) for count in (time_rows, unite_rows, space_rows)]
        + [((frames, block, ch), BF16, HBM)],
        [pltpu.SemaphoreType.DMA((1,))],
        0,
        6 * 21 * ch * ch,
        [(lax.all_gather(piece, "grp", axis=0), VMEM), (united, HBM)],
        SMALL_VMEM,
    )
    return (
        united.reshape(frames_in.shape),
        back[None],
        grads[2].reshape(9, ch, ch),
        grads[0].reshape(LAYERS, TAPS, ch, ch),
        grads[1].reshape(2, ch, ch),
    )


def solution(mesh):
    frame_spec = P(AXES, None, None, None)
    return jax.shard_map(
        local,
        mesh=mesh,
        in_specs=(frame_spec, P(), P(), P(), P(), P(), frame_spec),
        out_specs=(frame_spec, frame_spec, P(), P(), P()),
        check_vma=False,
    )
```

```python
import functools

import jax
import jax.numpy as jnp
from jax import lax
from jax.experimental import pallas as pl
from jax.experimental.pallas import tpu as pltpu
from jax.sharding import PartitionSpec as P

LAYERS = 2
TAPS = 5
DMAX = 8
HALO = 2 * DMAX
AXES = ("seg", "grp")
BF16 = jnp.bfloat16
F32 = jnp.float32
BIG_VMEM = 60 * 1024 * 1024
MID_VMEM = 40 * 1024 * 1024
SPARE = 28
SMALL_VMEM = 16 * 1024 * 1024


def round_up(value, step):
    return -(-value // step) * step


def silu_parts(value):
    sigma = 0.5 * jnp.tanh(0.5 * value) + 0.5
    act = value * sigma
    return act, sigma + act * (1.0 - sigma)


def mm(left, right):
    return jnp.dot(left, right, preferred_element_type=F32)


def mm_nt(left, right):
    return lax.dot_general(left, right, (((1,), (1,)), ((), ())), preferred_element_type=F32)


def mm_tn(left, right):
    return lax.dot_general(left, right, (((0,), (0,)), ((), ())), preferred_element_type=F32)


def three_parts(value):
    high = value.astype(BF16)
    rest = value - high.astype(F32)
    middle = rest.astype(BF16)
    return high, middle, (rest - middle.astype(F32)).astype(BF16)


VMEM = pl.BlockSpec(memory_space=pltpu.VMEM)
SMEM = pl.BlockSpec(memory_space=pltpu.SMEM)
HBM = pl.BlockSpec(memory_space=pltpu.HBM)


def call(kernel, outs, scratch, flops, moved, args, vmem=BIG_VMEM):
    return pl.pallas_call(
        kernel,
        out_shape=[jax.ShapeDtypeStruct(shape, kind) for shape, kind, _ in outs],
        in_specs=[spec for _, spec in args],
        out_specs=[spec for _, _, spec in outs],
        scratch_shapes=scratch,
        compiler_params=pltpu.CompilerParams(vmem_limit_bytes=vmem),
        cost_estimate=pl.CostEstimate(flops=flops, bytes_accessed=moved, transcendentals=0),
    )(*[value for value, _ in args])


def roll_rows(value, shift):
    return pltpu.roll(value, shift % value.shape[0], 0)


def spatial_pre(xs, weight, at, rows_step):
    wide, ch = xs.shape[1:]
    flat = rows_step * wide
    left = jnp.concatenate(
        [xs[at + a : at + a + rows_step].reshape(flat, ch) for a in range(3)], axis=1
    )
    y = mm(left, weight)
    return y[:, ch : 2 * ch] + roll_rows(y[:, :ch], 1) + roll_rows(y[:, 2 * ch :], -1)


def forward_weight(w_ref):
    return jnp.concatenate(
        [jnp.concatenate([w_ref[3 * a + b] for b in range(3)], axis=1) for a in range(3)], axis=0
    )


def clear_ends(ref):
    last = ref.shape[0] - 1
    ref[0] = jnp.zeros(ref.shape[1:], ref.dtype)
    ref[last] = jnp.zeros(ref.shape[1:], ref.dtype)


def put_rows(ref, at, value):
    count, cols, ch = value.shape
    ref[1 + at : 1 + at + count, cols:, :] = jnp.zeros((count, ref.shape[1] - cols, ch), ref.dtype)
    ref[1 + at : 1 + at + count, :cols, :] = value


def spatial_fwd_kernel(
    rows_step, x_hbm, w_hbm, cot_hbm, send_hbm,
    x_in, w_ref, xs, sends, in_sems, w_sem, cot_sem, send_sems,
):
    rows, cols, ch = x_in.shape
    wide = xs.shape[1]
    parts = in_sems.shape[0]
    many = rows // parts

    def part(n):
        return pl.ds(n * many, many)

    loads = [
        pltpu.make_async_copy(x_hbm.at[part(n)], x_in.at[part(n)], in_sems.at[n]) for n in range(parts)
    ]
    stores = [
        pltpu.make_async_copy(sends.at[part(n)], send_hbm.at[part(n)], send_sems.at[n])
        for n in range(parts)
    ]
    w_load = pltpu.make_async_copy(w_hbm, w_ref, w_sem.at[0])
    cot_load = pltpu.make_async_copy(cot_hbm, sends.at[:, 1], cot_sem.at[0])
    for load in [loads[0], w_load] + loads[1:] + [cot_load]:
        load.start()
    clear_ends(xs)

    def bring(n):
        loads[n].wait()
        put_rows(xs, n * many, x_in[n * many : (n + 1) * many])

    bring(0)
    w_load.wait()
    weight = forward_weight(w_ref)
    for n in range(parts):
        if n + 1 < parts:
            bring(n + 1)
        for at in range(n * many, (n + 1) * many, rows_step):
            act, _ = silu_parts(spatial_pre(xs, weight, at, rows_step))
            sends[at : at + rows_step, 0] = act.astype(BF16).reshape(rows_step, wide, ch)[:, :cols]
        if n == 0:
            cot_load.wait()
        stores[n].start()
    for store in stores:
        store.wait()


def spatial_slope_kernel(rows_step, x_ref, w_ref, slope_hbm, xs, slopes, sem):
    rows, cols, ch = x_ref.shape
    wide = xs.shape[1]
    clear_ends(xs)
    put_rows(xs, 0, x_ref[...])
    weight = forward_weight(w_ref)
    for at in range(0, rows, rows_step):
        _, slope = silu_parts(spatial_pre(xs, weight, at, rows_step))
        slopes[at : at + rows_step] = slope.astype(BF16).reshape(rows_step, wide, ch)[:, :cols]
    store = pltpu.make_async_copy(slopes, slope_hbm.at[0], sem.at[0])
    store.start()
    store.wait()


def hand_out(here_ref, total_ref, pieces):
    for peer, piece in enumerate(pieces):
        piece[...] = total_ref[jnp.bitwise_xor(here_ref[1], peer)].astype(piece.dtype)


def taps_up(gs, at, rows_step):
    wide, ch = gs.shape[1:]
    return jnp.concatenate(
        [gs[at + 2 - a : at + 2 - a + rows_step].reshape(rows_step * wide, ch) for a in range(3)],
        axis=1,
    )


def fill_grads(rows_step, gs, got_ref, slope_ref):
    clear_ends(gs)
    for at in range(0, got_ref.shape[0], rows_step):
        grads = got_ref[at : at + rows_step].astype(F32)
        slopes = slope_ref[at : at + rows_step].astype(F32)
        put_rows(gs, at, (grads * slopes).astype(BF16))


def spatial_wgrad_kernel(rows_step, scale, here_ref, got_ref, slope_hbm, x_ref, *rest):
    pieces, (gs, slopes, cat_ref, total_ref, sem) = rest[:-5], rest[-5:]
    rows, cols, ch = got_ref.shape
    wide = gs.shape[1]
    flat = rows_step * wide
    load = pltpu.make_async_copy(slope_hbm.at[0], slopes, sem.at[0])
    load.start()
    pad = jnp.zeros((rows_step, wide - cols, ch), F32)
    for at in range(0, rows, rows_step):
        x = jnp.concatenate([x_ref[at : at + rows_step].astype(F32), pad], axis=1).reshape(flat, ch)
        x_cat = jnp.concatenate([roll_rows(x, 1), x, roll_rows(x, -1)], axis=1)
        cat_ref[:, at * wide : at * wide + flat] = x_cat.T.astype(BF16)
    load.wait()
    fill_grads(rows_step, gs, got_ref, slopes)
    total = jnp.zeros((3 * ch, 3 * ch), F32)
    for at in range(0, rows, rows_step):
        total = total + mm(cat_ref[:, at * wide : at * wide + flat], taps_up(gs, at, rows_step))
    total_ref[...] = (
        jnp.concatenate(
            [
                total[b * ch : (b + 1) * ch, a * ch : (a + 1) * ch]
                for a in range(3)
                for b in range(3)
            ],
            axis=0,
        )
        * scale
    ).reshape(total_ref.shape)
    hand_out(here_ref, total_ref, pieces)


def spatial_back_kernel(rows_step, w_ref, got_ref, slope_hbm, back_ref, gs, slopes, sem):
    rows, cols, ch = back_ref.shape
    wide = gs.shape[1]
    load = pltpu.make_async_copy(slope_hbm.at[0], slopes, sem.at[0])
    load.start()
    weight = jnp.concatenate(
        [
            jnp.concatenate([w_ref[3 * a + b].astype(F32).T.astype(BF16) for b in range(3)], axis=1)
            for a in range(3)
        ],
        axis=0,
    )
    load.wait()
    fill_grads(rows_step, gs, got_ref, slopes)
    for at in range(0, rows, rows_step):
        y = mm(taps_up(gs, at, rows_step), weight)
        back = y[:, ch : 2 * ch] + roll_rows(y[:, :ch], -1) + roll_rows(y[:, 2 * ch :], 1)
        back_ref[at : at + rows_step] = back.astype(BF16).reshape(rows_step, wide, ch)[:, :cols]


def clear_halo(pad_ref, frames):
    zeros = jnp.zeros((HALO,) + pad_ref.shape[1:], pad_ref.dtype)
    pad_ref[:HALO] = zeros
    pad_ref[HALO + frames :] = zeros


def taps_of(pad_ref, at, count, step_size, sign):
    high, ch = pad_ref.shape[1:]
    pieces = [
        pad_ref[pl.ds(HALO + at + sign * (k - 2) * step_size, count)].reshape(count * high, ch)
        for k in range(TAPS)
    ]
    return jnp.concatenate(pieces, axis=1)


def temporal_kernel(
    step_frames, dil_ref, key_ref, got_ref, tw_hbm, uw_hbm,
    grad_hbm, kept_hbm, united_hbm,
    a0, a1, feat, cots, g0, g1, slope0, slope1, united_ref, grad_ref, tw_ref, uw_ref,
    sems, in_sems, out_sems,
):
    frames, _, block, ch = got_ref.shape
    high = feat.shape[1]
    loads = [
        pltpu.make_async_copy(source, ref, in_sems.at[n])
        for n, (source, ref) in enumerate(((tw_hbm, tw_ref), (uw_hbm, uw_ref)))
    ]
    for load in loads:
        load.start()
    stores = [
        pltpu.make_async_copy(
            grad_ref.at[pl.ds(at, step_frames)], grad_hbm.at[pl.ds(at, step_frames)], out_sems.at[n]
        )
        for n, at in enumerate(range(0, frames, step_frames))
    ]
    segs = key_ref.shape[0]
    seg_frames = frames // segs
    inside = pl.ds(HALO, frames)
    copies = [
        pltpu.make_async_copy(source, target, sems.at[n])
        for n, (source, target) in enumerate(
            (
                (a1.at[inside], kept_hbm.at[0]),
                (feat, kept_hbm.at[1]),
                (g1.at[inside], kept_hbm.at[2]),
                (g0.at[inside], kept_hbm.at[3]),
                (a0.at[inside], kept_hbm.at[4]),
                (cots, kept_hbm.at[5]),
                (united_ref, united_hbm.at[0]),
            )
        )
    ]
    for ref in (a0, a1, g0, g1):
        clear_halo(ref, frames)
    if high > block:
        pad = jnp.zeros((frames, high - block, ch), BF16)
        a0[HALO : HALO + frames, block:, :] = pad
        cots[:, block:, :] = pad
    a0[HALO : HALO + frames, :block, :] = got_ref[:, 0]
    copies[4].start()
    for load in loads:
        load.wait()
    for layer, (source, target, slopes) in enumerate(((a0, a1, slope0), (a1, feat, slope1))):
        step_size = dil_ref[layer]
        weight = jnp.concatenate([tw_ref[layer, k] for k in range(TAPS)], axis=0)
        first = HALO if layer == 0 else 0
        for at in range(0, frames, step_frames):
            pre = mm(taps_of(source, at, step_frames, step_size, 1), weight)
            act, slope = silu_parts(pre)
            target[first + at : first + at + step_frames] = act.astype(BF16).reshape(
                step_frames, high, ch
            )
            slopes[at : at + step_frames] = slope.reshape(step_frames, high, ch)
        copies[layer].start()
    cots[:, :block, :] = got_ref[:, 1]
    copies[5].start()
    for seg in range(segs):
        low, top = seg * seg_frames, (seg + 1) * seg_frames
        here = low + key_ref[seg]
        key_part = mm(feat[here], uw_ref[1])
        main = mm(feat[low:top].reshape(seg_frames * high, ch), uw_ref[0]).reshape(
            seg_frames, high, ch
        )
        united_ref[low:top] = (main + key_part[None]).astype(BF16)[:, :block]
        mine = cots[low:top]
        total = jnp.sum(mine.astype(F32), axis=0)
        key_term = sum(mm_nt(part, uw_ref[1]) for part in three_parts(total))
        grad_feat = mm_nt(mine.reshape(seg_frames * high, ch), uw_ref[0]).reshape(
            seg_frames, high, ch
        )
        for n in range(seg_frames):
            grad = grad_feat[n] + jnp.where(key_ref[seg] == n, key_term, 0.0)
            g1[HALO + low + n] = (grad * slope1[low + n]).astype(BF16)
    copies[6].start()
    for layer, source in ((1, g1), (0, g0)):
        copies[3 - layer].start()
        step_size = dil_ref[layer]
        weight = jnp.concatenate(
            [tw_ref[layer, k].astype(F32).T.astype(BF16) for k in range(TAPS)], axis=0
        )
        for n, at in enumerate(range(0, frames, step_frames)):
            grad = mm(taps_of(source, at, step_frames, step_size, -1), weight).reshape(
                step_frames, high, ch
            )
            if layer == 1:
                g0[HALO + at : HALO + at + step_frames] = (
                    grad * slope0[at : at + step_frames]
                ).astype(BF16)
            else:
                grad_ref[at : at + step_frames] = grad.astype(BF16)[:, :block]
                stores[n].start()
    for copy in copies + stores:
        copy.wait()


def temporal_wgrad_kernel(
    step_frames, scale, here_ref, dil_ref, key_ref,
    kept_hbm, united_kept, united_hbm, *rest
):
    pieces, (a0, g0, a1, g1, feat, cots, united, total_ref, sems) = rest[:-9], rest[-9:]
    frames, high, ch = feat.shape
    segs = key_ref.shape[0]
    seg_frames = frames // segs
    rows = step_frames * high
    inside = pl.ds(HALO, frames)
    copies = [
        pltpu.make_async_copy(source, target, sems.at[n])
        for n, (source, target) in enumerate(
            (
                (kept_hbm.at[4], a0.at[inside]),
                (kept_hbm.at[3], g0),
                (kept_hbm.at[0], a1.at[inside]),
                (kept_hbm.at[2], g1),
                (kept_hbm.at[1], feat),
                (kept_hbm.at[5], cots),
                (united_kept.at[0], united),
            )
        )
    ]
    for copy in copies:
        copy.start()
    clear_halo(a0, frames)
    clear_halo(a1, frames)
    totals = []
    for layer, acts, grads in ((0, a0, g0), (1, a1, g1)):
        copies[2 * layer].wait()
        copies[2 * layer + 1].wait()
        total = jnp.zeros((TAPS * ch, ch), F32)
        for at in range(0, frames, step_frames):
            total = total + mm_tn(
                taps_of(acts, at, step_frames, dil_ref[layer], 1),
                grads[at : at + step_frames].reshape(rows, ch),
            )
        totals.append(total)
    for copy in copies[4:]:
        copy.wait()
    united_copy = pltpu.make_async_copy(united, united_hbm, sems.at[len(copies)])
    united_copy.start()
    total = jnp.zeros((ch, ch), F32)
    for at in range(0, frames, step_frames):
        total = total + mm_tn(
            feat[at : at + step_frames].reshape(rows, ch),
            cots[at : at + step_frames].reshape(rows, ch),
        )
    keyed = jnp.zeros((ch, ch), F32)
    for seg in range(segs):
        low, top = seg * seg_frames, (seg + 1) * seg_frames
        key = feat[low + key_ref[seg]]
        seg_cot = jnp.sum(cots[low:top].astype(F32), axis=0)
        keyed = keyed + sum(mm_tn(key, part) for part in three_parts(seg_cot))
    peers = len(pieces)
    split = LAYERS * TAPS * ch // peers
    total_ref[:, :split] = (jnp.concatenate(totals, axis=0) * scale).reshape(peers, split, ch)
    total_ref[:, split:] = (jnp.concatenate([total, keyed], axis=0) * scale).reshape(
        peers, 2 * ch // peers, ch
    )
    hand_out(here_ref, total_ref, pieces)
    united_copy.wait()


def sum_kernel(*refs):
    refs[-1][...] = sum(ref[...].astype(F32) for ref in refs[:-1]).astype(refs[-1].dtype)


def join_kernel(first_ref, *refs):
    out_ref = refs[-1]
    split = first_ref.shape[0]
    out_ref[:split] = first_ref[...]
    out_ref[split:] = sum(ref[...].astype(F32) for ref in refs[:-1]).astype(out_ref.dtype)


def deal_kernel(pieces_ref, united_hbm, *refs):
    outs_hbm, united_out, outs, sems = refs[:3], refs[3], refs[4:7], refs[7]
    copies = [pltpu.make_async_copy(united_hbm, united_out, sems.at[3])]
    copies[0].start()
    at = 0
    for n, out_ref in enumerate(outs):
        count = out_ref.shape[1]
        out_ref[...] = pieces_ref[:, at : at + count].astype(F32)
        copies.append(pltpu.make_async_copy(out_ref, outs_hbm[n], sems.at[n]))
        copies[-1].start()
        at += count
    for copy in copies:
        copy.wait()


def exchange(blocks):
    return lax.all_to_all(blocks, AXES, split_axis=0, concat_axis=0, tiled=True)


def flip(value, peer):
    size = lax.axis_size("grp")
    return lax.ppermute(value, "grp", [(i, i ^ peer) for i in range(size)])


def turn_by(value, turn):
    size = lax.axis_size("seg")
    return lax.ppermute(value, "seg", [(i, (i + turn) % size) for i in range(size)])


def sum_of(parts):
    shape = parts[0].shape
    return call(
        sum_kernel, [(shape, BF16, VMEM)], [], 0, len(parts) * 2 * shape[0] * shape[1],
        [(part, VMEM) for part in parts], SMALL_VMEM,
    )[0]


def reduce_in_grp(pieces):
    return sum_of([flip(piece, peer) if peer else piece for peer, piece in enumerate(pieces)])


def all_turns(value):
    return [turn_by(value, turn) if turn else value for turn in range(lax.axis_size("seg"))]


def local(
    frames_in, spatial_weight, temporal_weight, uniting_weight, key_index, dilation, cotangent
):
    held, rows, cols, ch = frames_in.shape
    assert held == 1
    pixels = rows * cols
    peers = lax.axis_size("grp")
    devices = lax.axis_size("seg") * peers
    frames = held * devices
    block = pixels // devices
    split = cols // block
    wide = round_up(cols + 1, 16)
    high = round_up(block, 16)
    rows_step = next(n for n in (4, 2, 1) if rows % n == 0)
    parts = next(n for n in (4, 2, 1) if rows % (n * rows_step) == 0)
    step_frames, narrow_step = (
        max(n for n in range(1, frames + 1) if frames % n == 0 and n * high <= most)
        for most in (512, 256)
    )
    scale = float((frames * pixels) ** -0.5)
    here = jnp.stack([lax.axis_index("seg"), lax.axis_index("grp")]).astype(jnp.int32)
    space_rows, time_rows, unite_rows = (n * ch // peers for n in (9, LAYERS * TAPS, 2))

    (send,) = call(
        functools.partial(spatial_fwd_kernel, rows_step),
        [((rows, 2, cols, ch), BF16, HBM)],
        [
            pltpu.VMEM((rows, cols, ch), BF16),
            pltpu.VMEM(spatial_weight.shape, BF16),
            pltpu.VMEM((rows + 2, wide, ch), BF16),
            pltpu.VMEM((rows, 2, cols, ch), BF16),
            pltpu.SemaphoreType.DMA((parts,)),
            pltpu.SemaphoreType.DMA((1,)),
            pltpu.SemaphoreType.DMA((1,)),
            pltpu.SemaphoreType.DMA((parts,)),
        ],
        2 * 9 * pixels * ch * ch,
        pixels * ch * 8,
        [(frames_in[0], HBM), (spatial_weight, HBM), (cotangent[0], HBM)],
    )
    send, frame = lax.optimization_barrier((send, frames_in[0]))
    send = send.reshape(rows, 2, split, block, ch).swapaxes(1, 2).reshape(devices, 2, block, ch)
    got = exchange(send)
    (space_slope,) = call(
        functools.partial(spatial_slope_kernel, rows_step),
        [((SPARE, rows, cols, ch), BF16, HBM)],
        [
            pltpu.VMEM((rows + 2, wide, ch), BF16),
            pltpu.VMEM((rows, cols, ch), BF16),
            pltpu.SemaphoreType.DMA((1,)),
        ],
        2 * 9 * pixels * ch * ch,
        pixels * ch * 4,
        [(frame, VMEM), (spatial_weight, VMEM)],
    )
    got, space_slope = lax.optimization_barrier((got, space_slope))

    padded = (frames + 2 * HALO, high, ch)
    whole = (frames, high, ch)
    grad_send, kept, united_kept = call(
        functools.partial(temporal_kernel, narrow_step),
        [
            ((frames, block, ch), BF16, HBM),
            ((SPARE,) + whole, BF16, HBM),
            ((SPARE, frames, block, ch), BF16, HBM),
        ],
        [
            pltpu.VMEM(padded, BF16),
            pltpu.VMEM(padded, BF16),
            pltpu.VMEM(whole, BF16),
            pltpu.VMEM(whole, BF16),
            pltpu.VMEM(padded, BF16),
            pltpu.VMEM(padded, BF16),
            pltpu.VMEM(whole, F32),
            pltpu.VMEM(whole, F32),
            pltpu.VMEM((frames, block, ch), BF16),
            pltpu.VMEM((frames, block, ch), BF16),
            pltpu.VMEM(temporal_weight.shape, BF16),
            pltpu.VMEM(uniting_weight.shape, BF16),
            pltpu.SemaphoreType.DMA((7,)),
            pltpu.SemaphoreType.DMA((2,)),
            pltpu.SemaphoreType.DMA((frames // narrow_step,)),
        ],
        2 * 22 * frames * block * ch * ch,
        frames * block * ch * 18,
        [
            (dilation, SMEM), (key_index, SMEM), (got, VMEM),
            (temporal_weight, HBM), (uniting_weight, HBM),
        ],
        MID_VMEM,
    )
    grad_time = exchange(grad_send).reshape(rows, cols, ch)
    united_send, *time_pieces = call(
        functools.partial(temporal_wgrad_kernel, step_frames, scale),
        [((frames, block, ch), BF16, HBM)]
        + [((time_rows + unite_rows, ch), BF16, VMEM)] * peers,
        [
            pltpu.VMEM(padded, BF16),
            pltpu.VMEM(whole, BF16),
            pltpu.VMEM(padded, BF16),
            pltpu.VMEM(whole, BF16),
            pltpu.VMEM(whole, BF16),
            pltpu.VMEM(whole, BF16),
            pltpu.VMEM((frames, block, ch), BF16),
            pltpu.VMEM((peers, time_rows + unite_rows, ch), F32),
            pltpu.SemaphoreType.DMA((8,)),
        ],
        2 * 12 * frames * block * ch * ch,
        frames * block * ch * 14,
        [
            (here, SMEM), (dilation, SMEM), (key_index, SMEM),
            (kept, HBM), (united_kept, HBM),
        ],
    )
    time_sum = reduce_in_grp(time_pieces)
    time_sum, grad_time = lax.optimization_barrier((time_sum, grad_time))
    united_send, grad_time = lax.optimization_barrier((united_send, grad_time))
    united = exchange(united_send)
    space_pieces = call(
        functools.partial(spatial_wgrad_kernel, rows_step, scale),
        [((space_rows, ch), BF16, VMEM)] * peers,
        [
            pltpu.VMEM((rows + 2, wide, ch), BF16),
            pltpu.VMEM((rows, cols, ch), BF16),
            pltpu.VMEM((3 * ch, rows * wide), BF16),
            pltpu.VMEM((peers, space_rows, ch), F32),
            pltpu.SemaphoreType.DMA((1,)),
        ],
        2 * 9 * pixels * ch * ch,
        pixels * ch * 8,
        [(here, SMEM), (grad_time, VMEM), (space_slope, HBM), (frame, VMEM)],
        MID_VMEM,
    )
    (back,) = call(
        functools.partial(spatial_back_kernel, rows_step),
        [((rows, cols, ch), BF16, VMEM)],
        [
            pltpu.VMEM((rows + 2, wide, ch), BF16),
            pltpu.VMEM((rows, cols, ch), BF16),
            pltpu.SemaphoreType.DMA((1,)),
        ],
        2 * 9 * pixels * ch * ch,
        pixels * ch * 6,
        [(spatial_weight, VMEM), (grad_time, VMEM), (space_slope, HBM)],
        MID_VMEM,
    )
    space_parts = [flip(part, peer) if peer else part for peer, part in enumerate(space_pieces)]
    (plane,) = call(
        join_kernel,
        [((time_rows + unite_rows + space_rows, ch), BF16, VMEM)],
        [],
        0,
        2 * (peers + 10) * space_rows * ch,
        [(time_sum, VMEM)] + [(part, VMEM) for part in space_parts],
        SMALL_VMEM,
    )
    turned = all_turns(plane)
    turned[0], back = lax.optimization_barrier((turned[0], back))
    piece = sum_of(turned)
    *grads, united = call(
        deal_kernel,
        [((peers, count, ch), F32, HBM) for count in (time_rows, unite_rows, space_rows)]
        + [((frames, block, ch), BF16, HBM)],
        [pltpu.VMEM((peers, count, ch), F32) for count in (time_rows, unite_rows, space_rows)]
        + [pltpu.SemaphoreType.DMA((4,))],
        0,
        6 * 21 * ch * ch,
        [(lax.all_gather(piece, "grp", axis=0), VMEM), (united, HBM)],
        SMALL_VMEM,
    )
    return (
        united.reshape(frames_in.shape),
        back[None],
        grads[2].reshape(9, ch, ch),
        grads[0].reshape(LAYERS, TAPS, ch, ch),
        grads[1].reshape(2, ch, ch),
    )


def solution(mesh):
    frame_spec = P(AXES, None, None, None)
    return jax.shard_map(
        local,
        mesh=mesh,
        in_specs=(frame_spec, P(), P(), P(), P(), P(), frame_spec),
        out_specs=(frame_spec, frame_spec, P(), P(), P()),
        check_vma=False,
    )
```

```python
import functools

import jax
import jax.numpy as jnp
from jax import lax
from jax.experimental import pallas as pl
from jax.experimental.pallas import tpu as pltpu
from jax.sharding import PartitionSpec as P

LAYERS = 2
TAPS = 5
DMAX = 8
HALO = 2 * DMAX
AXES = ("seg", "grp")
BF16 = jnp.bfloat16
F32 = jnp.float32
BIG_VMEM = 60 * 1024 * 1024
MID_VMEM = 40 * 1024 * 1024
SPARE = 28
SMALL_VMEM = 16 * 1024 * 1024


def round_up(value, step):
    return -(-value // step) * step


def silu_parts(value):
    sigma = 0.5 * jnp.tanh(0.5 * value) + 0.5
    act = value * sigma
    return act, sigma + act * (1.0 - sigma)


def mm(left, right):
    return jnp.dot(left, right, preferred_element_type=F32)


def mm_nt(left, right):
    return lax.dot_general(left, right, (((1,), (1,)), ((), ())), preferred_element_type=F32)


def mm_tn(left, right):
    return lax.dot_general(left, right, (((0,), (0,)), ((), ())), preferred_element_type=F32)


def three_parts(value):
    high = value.astype(BF16)
    rest = value - high.astype(F32)
    middle = rest.astype(BF16)
    return high, middle, (rest - middle.astype(F32)).astype(BF16)


VMEM = pl.BlockSpec(memory_space=pltpu.VMEM)
SMEM = pl.BlockSpec(memory_space=pltpu.SMEM)
HBM = pl.BlockSpec(memory_space=pltpu.HBM)


def call(kernel, outs, scratch, flops, moved, args, vmem=BIG_VMEM):
    return pl.pallas_call(
        kernel,
        out_shape=[jax.ShapeDtypeStruct(shape, kind) for shape, kind, _ in outs],
        in_specs=[spec for _, spec in args],
        out_specs=[spec for _, _, spec in outs],
        scratch_shapes=scratch,
        compiler_params=pltpu.CompilerParams(vmem_limit_bytes=vmem),
        cost_estimate=pl.CostEstimate(flops=flops, bytes_accessed=moved, transcendentals=0),
    )(*[value for value, _ in args])


def roll_rows(value, shift):
    return pltpu.roll(value, shift % value.shape[0], 0)


def spatial_pre(xs, weight, at, rows_step):
    wide, ch = xs.shape[1:]
    flat = rows_step * wide
    left = jnp.concatenate(
        [xs[at + a : at + a + rows_step].reshape(flat, ch) for a in range(3)], axis=1
    )
    y = mm(left, weight)
    return y[:, ch : 2 * ch] + roll_rows(y[:, :ch], 1) + roll_rows(y[:, 2 * ch :], -1)


def forward_weight(w_ref):
    return jnp.concatenate(
        [jnp.concatenate([w_ref[3 * a + b] for b in range(3)], axis=1) for a in range(3)], axis=0
    )


def clear_ends(ref):
    last = ref.shape[0] - 1
    ref[0] = jnp.zeros(ref.shape[1:], ref.dtype)
    ref[last] = jnp.zeros(ref.shape[1:], ref.dtype)


def put_rows(ref, at, value):
    count, cols, ch = value.shape
    ref[1 + at : 1 + at + count, cols:, :] = jnp.zeros((count, ref.shape[1] - cols, ch), ref.dtype)
    ref[1 + at : 1 + at + count, :cols, :] = value


def spatial_fwd_kernel(
    rows_step, x_hbm, w_hbm, cot_hbm, send_hbm,
    x_in, w_ref, xs, sends, in_sems, w_sem, cot_sem, send_sems,
):
    rows, cols, ch = x_in.shape
    wide = xs.shape[1]
    parts = in_sems.shape[0]
    many = rows // parts

    def part(n):
        return pl.ds(n * many, many)

    loads = [
        pltpu.make_async_copy(x_hbm.at[part(n)], x_in.at[part(n)], in_sems.at[n]) for n in range(parts)
    ]
    stores = [
        pltpu.make_async_copy(sends.at[part(n)], send_hbm.at[part(n)], send_sems.at[n])
        for n in range(parts)
    ]
    w_load = pltpu.make_async_copy(w_hbm, w_ref, w_sem.at[0])
    cot_load = pltpu.make_async_copy(cot_hbm, sends.at[:, 1], cot_sem.at[0])
    for load in [loads[0], w_load] + loads[1:] + [cot_load]:
        load.start()
    clear_ends(xs)

    def bring(n):
        loads[n].wait()
        put_rows(xs, n * many, x_in[n * many : (n + 1) * many])

    bring(0)
    w_load.wait()
    weight = forward_weight(w_ref)
    for n in range(parts):
        if n + 1 < parts:
            bring(n + 1)
        for at in range(n * many, (n + 1) * many, rows_step):
            act, _ = silu_parts(spatial_pre(xs, weight, at, rows_step))
            sends[at : at + rows_step, 0] = act.astype(BF16).reshape(rows_step, wide, ch)[:, :cols]
        if n == 0:
            cot_load.wait()
        stores[n].start()
    for store in stores:
        store.wait()


def spatial_slope_kernel(rows_step, x_ref, w_ref, slope_hbm, xs, slopes, sem):
    rows, cols, ch = x_ref.shape
    wide = xs.shape[1]
    clear_ends(xs)
    put_rows(xs, 0, x_ref[...])
    weight = forward_weight(w_ref)
    for at in range(0, rows, rows_step):
        _, slope = silu_parts(spatial_pre(xs, weight, at, rows_step))
        slopes[at : at + rows_step] = slope.astype(BF16).reshape(rows_step, wide, ch)[:, :cols]
    store = pltpu.make_async_copy(slopes, slope_hbm.at[0], sem.at[0])
    store.start()
    store.wait()


def hand_out(here_ref, total_ref, pieces):
    for peer, piece in enumerate(pieces):
        piece[...] = total_ref[jnp.bitwise_xor(here_ref[1], peer)].astype(piece.dtype)


def taps_up(gs, at, rows_step):
    wide, ch = gs.shape[1:]
    return jnp.concatenate(
        [gs[at + 2 - a : at + 2 - a + rows_step].reshape(rows_step * wide, ch) for a in range(3)],
        axis=1,
    )


def fill_grads(rows_step, gs, got_ref, slope_ref):
    clear_ends(gs)
    for at in range(0, got_ref.shape[0], rows_step):
        grads = got_ref[at : at + rows_step].astype(F32)
        slopes = slope_ref[at : at + rows_step].astype(F32)
        put_rows(gs, at, (grads * slopes).astype(BF16))


def spatial_wgrad_kernel(rows_step, scale, here_ref, got_ref, slope_hbm, x_ref, *rest):
    pieces, (gs, slopes, cat_ref, total_ref, sem) = rest[:-5], rest[-5:]
    rows, cols, ch = got_ref.shape
    wide = gs.shape[1]
    flat = rows_step * wide
    load = pltpu.make_async_copy(slope_hbm.at[0], slopes, sem.at[0])
    load.start()
    pad = jnp.zeros((rows_step, wide - cols, ch), F32)

    def columns(at):
        x = jnp.concatenate([x_ref[at : at + rows_step].astype(F32), pad], axis=1).reshape(flat, ch)
        x_cat = jnp.concatenate([roll_rows(x, 1), x, roll_rows(x, -1)], axis=1)
        return x_cat.T.astype(BF16)

    early = cat_ref.shape[1] // flat
    for n in range(early):
        cat_ref[:, n * flat : (n + 1) * flat] = columns(n * rows_step)
    load.wait()
    fill_grads(rows_step, gs, got_ref, slopes)
    total = jnp.zeros((3 * ch, 3 * ch), F32)
    for n, at in enumerate(range(0, rows, rows_step)):
        cat = cat_ref[:, n * flat : (n + 1) * flat] if n < early else columns(at)
        total = total + mm(cat, taps_up(gs, at, rows_step))
    total_ref[...] = (
        jnp.concatenate(
            [
                total[b * ch : (b + 1) * ch, a * ch : (a + 1) * ch]
                for a in range(3)
                for b in range(3)
            ],
            axis=0,
        )
        * scale
    ).reshape(total_ref.shape)
    hand_out(here_ref, total_ref, pieces)


def spatial_back_kernel(rows_step, w_ref, got_ref, slope_hbm, back_ref, gs, slopes, sem):
    rows, cols, ch = back_ref.shape
    wide = gs.shape[1]
    load = pltpu.make_async_copy(slope_hbm.at[0], slopes, sem.at[0])
    load.start()
    weight = jnp.concatenate(
        [
            jnp.concatenate([w_ref[3 * a + b].astype(F32).T.astype(BF16) for b in range(3)], axis=1)
            for a in range(3)
        ],
        axis=0,
    )
    load.wait()
    fill_grads(rows_step, gs, got_ref, slopes)
    for at in range(0, rows, rows_step):
        y = mm(taps_up(gs, at, rows_step), weight)
        back = y[:, ch : 2 * ch] + roll_rows(y[:, :ch], -1) + roll_rows(y[:, 2 * ch :], 1)
        back_ref[at : at + rows_step] = back.astype(BF16).reshape(rows_step, wide, ch)[:, :cols]


def clear_halo(pad_ref, frames):
    zeros = jnp.zeros((HALO,) + pad_ref.shape[1:], pad_ref.dtype)
    pad_ref[:HALO] = zeros
    pad_ref[HALO + frames :] = zeros


def taps_of(pad_ref, at, count, step_size, sign):
    high, ch = pad_ref.shape[1:]
    pieces = [
        pad_ref[pl.ds(HALO + at + sign * (k - 2) * step_size, count)].reshape(count * high, ch)
        for k in range(TAPS)
    ]
    return jnp.concatenate(pieces, axis=1)


def temporal_kernel(
    step_frames, dil_ref, key_ref, got_ref, tw_ref, uw_ref,
    grad_hbm, kept_hbm, united_hbm,
    a0, a1, feat, cots, g0, g1, slope0, slope1, united_ref, grad_ref, sems, out_sems,
):
    frames, _, block, ch = got_ref.shape
    high = feat.shape[1]
    stores = [
        pltpu.make_async_copy(
            grad_ref.at[pl.ds(at, step_frames)], grad_hbm.at[pl.ds(at, step_frames)], out_sems.at[n]
        )
        for n, at in enumerate(range(0, frames, step_frames))
    ]
    segs = key_ref.shape[0]
    seg_frames = frames // segs
    inside = pl.ds(HALO, frames)
    copies = [
        pltpu.make_async_copy(source, target, sems.at[n])
        for n, (source, target) in enumerate(
            (
                (a1.at[inside], kept_hbm.at[0]),
                (feat, kept_hbm.at[1]),
                (g1.at[inside], kept_hbm.at[2]),
                (g0.at[inside], kept_hbm.at[3]),
                (united_ref, united_hbm),
            )
        )
    ]
    for ref in (a0, a1, g0, g1):
        clear_halo(ref, frames)
    if high > block:
        pad = jnp.zeros((frames, high - block, ch), BF16)
        a0[HALO : HALO + frames, block:, :] = pad
        cots[:, block:, :] = pad
    a0[HALO : HALO + frames, :block, :] = got_ref[:, 0]
    for layer, (source, target, slopes) in enumerate(((a0, a1, slope0), (a1, feat, slope1))):
        step_size = dil_ref[layer]
        weight = jnp.concatenate([tw_ref[layer, k] for k in range(TAPS)], axis=0)
        first = HALO if layer == 0 else 0
        for at in range(0, frames, step_frames):
            pre = mm(taps_of(source, at, step_frames, step_size, 1), weight)
            act, slope = silu_parts(pre)
            target[first + at : first + at + step_frames] = act.astype(BF16).reshape(
                step_frames, high, ch
            )
            slopes[at : at + step_frames] = slope.reshape(step_frames, high, ch)
        copies[layer].start()
    cots[:, :block, :] = got_ref[:, 1]
    for seg in range(segs):
        low, top = seg * seg_frames, (seg + 1) * seg_frames
        here = low + key_ref[seg]
        key_part = mm(feat[here], uw_ref[1])
        main = mm(feat[low:top].reshape(seg_frames * high, ch), uw_ref[0]).reshape(
            seg_frames, high, ch
        )
        united_ref[low:top] = (main + key_part[None]).astype(BF16)[:, :block]
        mine = cots[low:top]
        total = jnp.sum(mine.astype(F32), axis=0)
        key_term = sum(mm_nt(part, uw_ref[1]) for part in three_parts(total))
        grad_feat = mm_nt(mine.reshape(seg_frames * high, ch), uw_ref[0]).reshape(
            seg_frames, high, ch
        )
        for n in range(seg_frames):
            grad = grad_feat[n] + jnp.where(key_ref[seg] == n, key_term, 0.0)
            g1[HALO + low + n] = (grad * slope1[low + n]).astype(BF16)
    copies[4].start()
    for layer, source in ((1, g1), (0, g0)):
        copies[3 - layer].start()
        step_size = dil_ref[layer]
        weight = jnp.concatenate(
            [tw_ref[layer, k].astype(F32).T.astype(BF16) for k in range(TAPS)], axis=0
        )
        for n, at in enumerate(range(0, frames, step_frames)):
            grad = mm(taps_of(source, at, step_frames, step_size, -1), weight).reshape(
                step_frames, high, ch
            )
            if layer == 1:
                g0[HALO + at : HALO + at + step_frames] = (
                    grad * slope0[at : at + step_frames]
                ).astype(BF16)
            else:
                grad_ref[at : at + step_frames] = grad.astype(BF16)[:, :block]
                stores[n].start()
    for copy in copies + stores:
        copy.wait()


def temporal_wgrad_kernel(
    step_frames, scale, here_ref, dil_ref, key_ref, got_ref, kept_hbm, *rest
):
    pieces, (a0, g0, a1, g1, feat, cots, total_ref, sems) = rest[:-8], rest[-8:]
    frames, high, ch = feat.shape
    block = got_ref.shape[2]
    segs = key_ref.shape[0]
    seg_frames = frames // segs
    rows = step_frames * high
    inside = pl.ds(HALO, frames)
    copies = [
        pltpu.make_async_copy(kept_hbm.at[n], target, sems.at[n])
        for n, target in ((3, g0), (0, a1.at[inside]), (2, g1), (1, feat))
    ]
    for copy in copies:
        copy.start()
    clear_halo(a0, frames)
    clear_halo(a1, frames)
    if high > block:
        pad = jnp.zeros((frames, high - block, ch), BF16)
        a0[HALO : HALO + frames, block:, :] = pad
        cots[:, block:, :] = pad
    a0[HALO : HALO + frames, :block, :] = got_ref[:, 0]
    cots[:, :block, :] = got_ref[:, 1]
    totals = []
    for layer, acts, grads in ((0, a0, g0), (1, a1, g1)):
        for copy in copies[1:3] if layer else copies[:1]:
            copy.wait()
        total = jnp.zeros((TAPS * ch, ch), F32)
        for at in range(0, frames, step_frames):
            total = total + mm_tn(
                taps_of(acts, at, step_frames, dil_ref[layer], 1),
                grads[at : at + step_frames].reshape(rows, ch),
            )
        totals.append(total)
    copies[3].wait()
    total = jnp.zeros((ch, ch), F32)
    for at in range(0, frames, step_frames):
        total = total + mm_tn(
            feat[at : at + step_frames].reshape(rows, ch),
            cots[at : at + step_frames].reshape(rows, ch),
        )
    keyed = jnp.zeros((ch, ch), F32)
    for seg in range(segs):
        low, top = seg * seg_frames, (seg + 1) * seg_frames
        key = feat[low + key_ref[seg]]
        seg_cot = jnp.sum(cots[low:top].astype(F32), axis=0)
        keyed = keyed + sum(mm_tn(key, part) for part in three_parts(seg_cot))
    peers = len(pieces)
    split = LAYERS * TAPS * ch // peers
    total_ref[:, :split] = (jnp.concatenate(totals, axis=0) * scale).reshape(peers, split, ch)
    total_ref[:, split:] = (jnp.concatenate([total, keyed], axis=0) * scale).reshape(
        peers, 2 * ch // peers, ch
    )
    hand_out(here_ref, total_ref, pieces)


def sum_kernel(*refs):
    refs[-1][...] = sum(ref[...].astype(F32) for ref in refs[:-1]).astype(refs[-1].dtype)


def join_kernel(*refs):
    *parts, out_ref = refs
    half = len(parts) // 2
    split = parts[0].shape[0]
    out_ref[:split] = sum(ref[...].astype(F32) for ref in parts[:half]).astype(out_ref.dtype)
    out_ref[split:] = sum(ref[...].astype(F32) for ref in parts[half:]).astype(out_ref.dtype)


def deal_kernel(pieces_ref, united_hbm, *refs):
    outs_hbm, united_out, outs, sems = refs[:3], refs[3], refs[4:7], refs[7]
    copies = [pltpu.make_async_copy(united_hbm, united_out, sems.at[3])]
    copies[0].start()
    at = 0
    for n, out_ref in enumerate(outs):
        count = out_ref.shape[1]
        out_ref[...] = pieces_ref[:, at : at + count].astype(F32)
        copies.append(pltpu.make_async_copy(out_ref, outs_hbm[n], sems.at[n]))
        copies[-1].start()
        at += count
    for copy in copies:
        copy.wait()


def exchange(blocks):
    return lax.all_to_all(blocks, AXES, split_axis=0, concat_axis=0, tiled=True)


def flip(value, peer):
    size = lax.axis_size("grp")
    return lax.ppermute(value, "grp", [(i, i ^ peer) for i in range(size)])


def turn_by(value, turn):
    size = lax.axis_size("seg")
    return lax.ppermute(value, "seg", [(i, (i + turn) % size) for i in range(size)])


def sum_of(parts):
    shape = parts[0].shape
    return call(
        sum_kernel, [(shape, BF16, VMEM)], [], 0, len(parts) * 2 * shape[0] * shape[1],
        [(part, VMEM) for part in parts], SMALL_VMEM,
    )[0]


def reduce_in_grp(pieces):
    return sum_of([flip(piece, peer) if peer else piece for peer, piece in enumerate(pieces)])


def all_turns(value):
    return [turn_by(value, turn) if turn else value for turn in range(lax.axis_size("seg"))]


def local(
    frames_in, spatial_weight, temporal_weight, uniting_weight, key_index, dilation, cotangent
):
    held, rows, cols, ch = frames_in.shape
    assert held == 1
    pixels = rows * cols
    peers = lax.axis_size("grp")
    devices = lax.axis_size("seg") * peers
    frames = held * devices
    block = pixels // devices
    split = cols // block
    wide = round_up(cols + 1, 16)
    high = round_up(block, 16)
    rows_step = next(n for n in (4, 2, 1) if rows % n == 0)
    steps = rows // rows_step
    parts = next(n for n in (4, 2, 1) if rows % (n * rows_step) == 0)
    step_frames = max(n for n in range(1, frames + 1) if frames % n == 0 and n * high <= 512)
    scale = float((frames * pixels) ** -0.5)
    here = jnp.stack([lax.axis_index("seg"), lax.axis_index("grp")]).astype(jnp.int32)
    space_rows, time_rows, unite_rows = (n * ch // peers for n in (9, LAYERS * TAPS, 2))

    (send,) = call(
        functools.partial(spatial_fwd_kernel, rows_step),
        [((rows, 2, cols, ch), BF16, HBM)],
        [
            pltpu.VMEM((rows, cols, ch), BF16),
            pltpu.VMEM(spatial_weight.shape, BF16),
            pltpu.VMEM((rows + 2, wide, ch), BF16),
            pltpu.VMEM((rows, 2, cols, ch), BF16),
            pltpu.SemaphoreType.DMA((parts,)),
            pltpu.SemaphoreType.DMA((1,)),
            pltpu.SemaphoreType.DMA((1,)),
            pltpu.SemaphoreType.DMA((parts,)),
        ],
        2 * 9 * pixels * ch * ch,
        pixels * ch * 8,
        [(frames_in[0], HBM), (spatial_weight, HBM), (cotangent[0], HBM)],
    )
    send, frame = lax.optimization_barrier((send, frames_in[0]))
    send = send.reshape(rows, 2, split, block, ch).swapaxes(1, 2).reshape(devices, 2, block, ch)
    got = exchange(send)
    (space_slope,) = call(
        functools.partial(spatial_slope_kernel, rows_step),
        [((SPARE, rows, cols, ch), BF16, HBM)],
        [
            pltpu.VMEM((rows + 2, wide, ch), BF16),
            pltpu.VMEM((rows, cols, ch), BF16),
            pltpu.SemaphoreType.DMA((1,)),
        ],
        2 * 9 * pixels * ch * ch,
        pixels * ch * 4,
        [(frame, VMEM), (spatial_weight, VMEM)],
    )
    got, space_slope = lax.optimization_barrier((got, space_slope))

    padded = (frames + 2 * HALO, high, ch)
    whole = (frames, high, ch)
    grad_send, kept, united_send = call(
        functools.partial(temporal_kernel, step_frames),
        [
            ((frames, block, ch), BF16, HBM),
            ((SPARE,) + whole, BF16, HBM),
            ((frames, block, ch), BF16, HBM),
        ],
        [
            pltpu.VMEM(padded, BF16),
            pltpu.VMEM(padded, BF16),
            pltpu.VMEM(whole, BF16),
            pltpu.VMEM(whole, BF16),
            pltpu.VMEM(padded, BF16),
            pltpu.VMEM(padded, BF16),
            pltpu.VMEM(whole, F32),
            pltpu.VMEM(whole, F32),
            pltpu.VMEM((frames, block, ch), BF16),
            pltpu.VMEM((frames, block, ch), BF16),
            pltpu.SemaphoreType.DMA((5,)),
            pltpu.SemaphoreType.DMA((frames // step_frames,)),
        ],
        2 * 22 * frames * block * ch * ch,
        frames * block * ch * 18,
        [
            (dilation, SMEM), (key_index, SMEM), (got, VMEM),
            (temporal_weight, VMEM), (uniting_weight, VMEM),
        ],
        MID_VMEM,
    )
    grad_time = exchange(grad_send).reshape(rows, cols, ch)
    time_pieces = call(
        functools.partial(temporal_wgrad_kernel, step_frames, scale),
        [((time_rows + unite_rows, ch), BF16, VMEM)] * peers,
        [
            pltpu.VMEM(padded, BF16),
            pltpu.VMEM(whole, BF16),
            pltpu.VMEM(padded, BF16),
            pltpu.VMEM(whole, BF16),
            pltpu.VMEM(whole, BF16),
            pltpu.VMEM(whole, BF16),
            pltpu.VMEM((peers, time_rows + unite_rows, ch), F32),
            pltpu.SemaphoreType.DMA((4,)),
        ],
        2 * 12 * frames * block * ch * ch,
        frames * block * ch * 14,
        [
            (here, SMEM), (dilation, SMEM), (key_index, SMEM), (got, VMEM), (kept, HBM),
        ],
        MID_VMEM,
    )
    time_turned = all_turns(reduce_in_grp(time_pieces))
    united_send, grad_time = lax.optimization_barrier((united_send, grad_time))
    united = exchange(united_send)
    *time_turned, grad_time = lax.optimization_barrier((*time_turned, grad_time))
    space_pieces = call(
        functools.partial(spatial_wgrad_kernel, rows_step, scale),
        [((space_rows, ch), BF16, VMEM)] * peers,
        [
            pltpu.VMEM((rows + 2, wide, ch), BF16),
            pltpu.VMEM((rows, cols, ch), BF16),
            pltpu.VMEM((3 * ch, min(3, steps) * rows_step * wide), BF16),
            pltpu.VMEM((peers, space_rows, ch), F32),
            pltpu.SemaphoreType.DMA((1,)),
        ],
        2 * 9 * pixels * ch * ch,
        pixels * ch * 8,
        [(here, SMEM), (grad_time, VMEM), (space_slope, HBM), (frame, VMEM)],
        MID_VMEM,
    )
    (back,) = call(
        functools.partial(spatial_back_kernel, rows_step),
        [((rows, cols, ch), BF16, VMEM)],
        [
            pltpu.VMEM((rows + 2, wide, ch), BF16),
            pltpu.VMEM((rows, cols, ch), BF16),
            pltpu.SemaphoreType.DMA((1,)),
        ],
        2 * 9 * pixels * ch * ch,
        pixels * ch * 6,
        [(spatial_weight, VMEM), (grad_time, VMEM), (space_slope, HBM)],
        MID_VMEM,
    )
    turned = all_turns(reduce_in_grp(space_pieces))
    turned[0], back = lax.optimization_barrier((turned[0], back))
    (piece,) = call(
        join_kernel,
        [((time_rows + unite_rows + space_rows, ch), BF16, VMEM)],
        [],
        0,
        2 * 4 * 21 * ch * ch,
        [(part, VMEM) for part in time_turned + turned],
        SMALL_VMEM,
    )
    *grads, united = call(
        deal_kernel,
        [((peers, count, ch), F32, HBM) for count in (time_rows, unite_rows, space_rows)]
        + [((frames, block, ch), BF16, HBM)],
        [pltpu.VMEM((peers, count, ch), F32) for count in (time_rows, unite_rows, space_rows)]
        + [pltpu.SemaphoreType.DMA((4,))],
        0,
        6 * 21 * ch * ch,
        [(lax.all_gather(piece, "grp", axis=0), VMEM), (united, HBM)],
        SMALL_VMEM,
    )
    return (
        united.reshape(frames_in.shape),
        back[None],
        grads[2].reshape(9, ch, ch),
        grads[0].reshape(LAYERS, TAPS, ch, ch),
        grads[1].reshape(2, ch, ch),
    )


def solution(mesh):
    frame_spec = P(AXES, None, None, None)
    return jax.shard_map(
        local,
        mesh=mesh,
        in_specs=(frame_spec, P(), P(), P(), P(), P(), frame_spec),
        out_specs=(frame_spec, frame_spec, P(), P(), P()),
        check_vma=False,
    )
```

```python
import functools

import jax
import jax.numpy as jnp
from jax import lax
from jax.experimental import pallas as pl
from jax.experimental.pallas import tpu as pltpu
from jax.sharding import PartitionSpec as P

LAYERS = 2
TAPS = 5
DMAX = 8
HALO = 2 * DMAX
AXES = ("seg", "grp")
BF16 = jnp.bfloat16
F32 = jnp.float32
BIG_VMEM = 60 * 1024 * 1024
MID_VMEM = 40 * 1024 * 1024
SPARE = 28
SMALL_VMEM = 16 * 1024 * 1024


def round_up(value, step):
    return -(-value // step) * step


def silu_parts(value):
    sigma = 0.5 * jnp.tanh(0.5 * value) + 0.5
    act = value * sigma
    return act, sigma + act * (1.0 - sigma)


def mm(left, right):
    return jnp.dot(left, right, preferred_element_type=F32)


def mm_nt(left, right):
    return lax.dot_general(left, right, (((1,), (1,)), ((), ())), preferred_element_type=F32)


def mm_tn(left, right):
    return lax.dot_general(left, right, (((0,), (0,)), ((), ())), preferred_element_type=F32)


def three_parts(value):
    high = value.astype(BF16)
    rest = value - high.astype(F32)
    middle = rest.astype(BF16)
    return high, middle, (rest - middle.astype(F32)).astype(BF16)


VMEM = pl.BlockSpec(memory_space=pltpu.VMEM)
SMEM = pl.BlockSpec(memory_space=pltpu.SMEM)
HBM = pl.BlockSpec(memory_space=pltpu.HBM)


def call(kernel, outs, scratch, flops, moved, args, vmem=BIG_VMEM):
    return pl.pallas_call(
        kernel,
        out_shape=[jax.ShapeDtypeStruct(shape, kind) for shape, kind, _ in outs],
        in_specs=[spec for _, spec in args],
        out_specs=[spec for _, _, spec in outs],
        scratch_shapes=scratch,
        compiler_params=pltpu.CompilerParams(vmem_limit_bytes=vmem),
        cost_estimate=pl.CostEstimate(flops=flops, bytes_accessed=moved, transcendentals=0),
    )(*[value for value, _ in args])


def roll_rows(value, shift):
    return pltpu.roll(value, shift % value.shape[0], 0)


def spatial_pre(xs, weight, at, rows_step):
    wide, ch = xs.shape[1:]
    flat = rows_step * wide
    left = jnp.concatenate(
        [xs[at + a : at + a + rows_step].reshape(flat, ch) for a in range(3)], axis=1
    )
    y = mm(left, weight)
    return y[:, ch : 2 * ch] + roll_rows(y[:, :ch], 1) + roll_rows(y[:, 2 * ch :], -1)


def forward_weight(w_ref):
    return jnp.concatenate(
        [jnp.concatenate([w_ref[3 * a + b] for b in range(3)], axis=1) for a in range(3)], axis=0
    )


def clear_ends(ref):
    last = ref.shape[0] - 1
    ref[0] = jnp.zeros(ref.shape[1:], ref.dtype)
    ref[last] = jnp.zeros(ref.shape[1:], ref.dtype)


def put_rows(ref, at, value):
    count, cols, ch = value.shape
    ref[1 + at : 1 + at + count, cols:, :] = jnp.zeros((count, ref.shape[1] - cols, ch), ref.dtype)
    ref[1 + at : 1 + at + count, :cols, :] = value


def spatial_fwd_kernel(
    rows_step, x_hbm, w_hbm, cot_hbm, send_hbm,
    x_in, w_ref, xs, sends, in_sems, w_sem, cot_sem, send_sems,
):
    rows, cols, ch = x_in.shape
    wide = xs.shape[1]
    parts = in_sems.shape[0]
    many = rows // parts

    def part(n):
        return pl.ds(n * many, many)

    loads = [
        pltpu.make_async_copy(x_hbm.at[part(n)], x_in.at[part(n)], in_sems.at[n]) for n in range(parts)
    ]
    stores = [
        pltpu.make_async_copy(sends.at[part(n)], send_hbm.at[part(n)], send_sems.at[n])
        for n in range(parts)
    ]
    w_load = pltpu.make_async_copy(w_hbm, w_ref, w_sem.at[0])
    cot_load = pltpu.make_async_copy(cot_hbm, sends.at[:, 1], cot_sem.at[0])
    for load in [loads[0], w_load] + loads[1:] + [cot_load]:
        load.start()
    clear_ends(xs)

    def bring(n):
        loads[n].wait()
        put_rows(xs, n * many, x_in[n * many : (n + 1) * many])

    bring(0)
    w_load.wait()
    weight = forward_weight(w_ref)
    for n in range(parts):
        if n + 1 < parts:
            bring(n + 1)
        for at in range(n * many, (n + 1) * many, rows_step):
            act, _ = silu_parts(spatial_pre(xs, weight, at, rows_step))
            sends[at : at + rows_step, 0] = act.astype(BF16).reshape(rows_step, wide, ch)[:, :cols]
        if n == 0:
            cot_load.wait()
        stores[n].start()
    for store in stores:
        store.wait()


def spatial_slope_kernel(rows_step, x_ref, w_ref, slope_hbm, xs, slopes, sem):
    rows, cols, ch = x_ref.shape
    wide = xs.shape[1]
    clear_ends(xs)
    put_rows(xs, 0, x_ref[...])
    weight = forward_weight(w_ref)
    for at in range(0, rows, rows_step):
        _, slope = silu_parts(spatial_pre(xs, weight, at, rows_step))
        slopes[at : at + rows_step] = slope.astype(BF16).reshape(rows_step, wide, ch)[:, :cols]
    store = pltpu.make_async_copy(slopes, slope_hbm.at[0], sem.at[0])
    store.start()
    store.wait()


def hand_out(here_ref, total_ref, pieces):
    for peer, piece in enumerate(pieces):
        piece[...] = total_ref[jnp.bitwise_xor(here_ref[1], peer)].astype(piece.dtype)


def taps_up(gs, at, rows_step):
    wide, ch = gs.shape[1:]
    return jnp.concatenate(
        [gs[at + 2 - a : at + 2 - a + rows_step].reshape(rows_step * wide, ch) for a in range(3)],
        axis=1,
    )


def fill_grads(rows_step, gs, got_ref, slope_ref):
    clear_ends(gs)
    for at in range(0, got_ref.shape[0], rows_step):
        grads = got_ref[at : at + rows_step].astype(F32)
        slopes = slope_ref[at : at + rows_step].astype(F32)
        put_rows(gs, at, (grads * slopes).astype(BF16))


def spatial_wgrad_kernel(rows_step, scale, here_ref, got_ref, slope_hbm, x_ref, *rest):
    pieces, (gs, slopes, cat_ref, total_ref, sem) = rest[:-5], rest[-5:]
    rows, cols, ch = got_ref.shape
    wide = gs.shape[1]
    flat = rows_step * wide
    load = pltpu.make_async_copy(slope_hbm.at[0], slopes, sem.at[0])
    load.start()
    pad = jnp.zeros((rows_step, wide - cols, ch), F32)

    def columns(at):
        x = jnp.concatenate([x_ref[at : at + rows_step].astype(F32), pad], axis=1).reshape(flat, ch)
        x_cat = jnp.concatenate([roll_rows(x, 1), x, roll_rows(x, -1)], axis=1)
        return x_cat.T.astype(BF16)

    early = cat_ref.shape[1] // flat
    for n in range(early):
        cat_ref[:, n * flat : (n + 1) * flat] = columns(n * rows_step)
    load.wait()
    fill_grads(rows_step, gs, got_ref, slopes)
    total = jnp.zeros((3 * ch, 3 * ch), F32)
    for n, at in enumerate(range(0, rows, rows_step)):
        cat = cat_ref[:, n * flat : (n + 1) * flat] if n < early else columns(at)
        total = total + mm(cat, taps_up(gs, at, rows_step))
    total_ref[...] = (
        jnp.concatenate(
            [
                total[b * ch : (b + 1) * ch, a * ch : (a + 1) * ch]
                for a in range(3)
                for b in range(3)
            ],
            axis=0,
        )
        * scale
    ).reshape(total_ref.shape)
    hand_out(here_ref, total_ref, pieces)


def spatial_back_kernel(rows_step, w_ref, got_ref, slope_hbm, back_ref, gs, slopes, sem):
    rows, cols, ch = back_ref.shape
    wide = gs.shape[1]
    load = pltpu.make_async_copy(slope_hbm.at[0], slopes, sem.at[0])
    load.start()
    weight = jnp.concatenate(
        [
            jnp.concatenate([w_ref[3 * a + b].astype(F32).T.astype(BF16) for b in range(3)], axis=1)
            for a in range(3)
        ],
        axis=0,
    )
    load.wait()
    fill_grads(rows_step, gs, got_ref, slopes)
    for at in range(0, rows, rows_step):
        y = mm(taps_up(gs, at, rows_step), weight)
        back = y[:, ch : 2 * ch] + roll_rows(y[:, :ch], -1) + roll_rows(y[:, 2 * ch :], 1)
        back_ref[at : at + rows_step] = back.astype(BF16).reshape(rows_step, wide, ch)[:, :cols]


def clear_halo(pad_ref, frames):
    zeros = jnp.zeros((HALO,) + pad_ref.shape[1:], pad_ref.dtype)
    pad_ref[:HALO] = zeros
    pad_ref[HALO + frames :] = zeros


def taps_of(pad_ref, at, count, step_size, sign):
    high, ch = pad_ref.shape[1:]
    pieces = [
        pad_ref[pl.ds(HALO + at + sign * (k - 2) * step_size, count)].reshape(count * high, ch)
        for k in range(TAPS)
    ]
    return jnp.concatenate(pieces, axis=1)


def temporal_kernel(
    step_frames, dil_ref, key_ref, got_ref, tw_hbm, uw_hbm,
    grad_hbm, kept_hbm, united_hbm,
    a0, a1, feat, cots, g0, g1, slope0, slope1, united_ref, grad_ref, tw_ref, uw_ref,
    sems, in_sems, out_sems,
):
    frames, _, block, ch = got_ref.shape
    high = feat.shape[1]
    loads = [
        pltpu.make_async_copy(source, ref, in_sems.at[n])
        for n, (source, ref) in enumerate(((tw_hbm, tw_ref), (uw_hbm, uw_ref)))
    ]
    for load in loads:
        load.start()
    stores = [
        pltpu.make_async_copy(
            grad_ref.at[pl.ds(at, step_frames)], grad_hbm.at[pl.ds(at, step_frames)], out_sems.at[n]
        )
        for n, at in enumerate(range(0, frames, step_frames))
    ]
    segs = key_ref.shape[0]
    seg_frames = frames // segs
    inside = pl.ds(HALO, frames)
    copies = [
        pltpu.make_async_copy(source, target, sems.at[n])
        for n, (source, target) in enumerate(
            (
                (a1.at[inside], kept_hbm.at[0]),
                (feat, kept_hbm.at[1]),
                (g1.at[inside], kept_hbm.at[2]),
                (g0.at[inside], kept_hbm.at[3]),
                (united_ref, united_hbm),
            )
        )
    ]
    for ref in (a0, a1, g0, g1):
        clear_halo(ref, frames)
    if high > block:
        pad = jnp.zeros((frames, high - block, ch), BF16)
        a0[HALO : HALO + frames, block:, :] = pad
        cots[:, block:, :] = pad
    a0[HALO : HALO + frames, :block, :] = got_ref[:, 0]
    for load in loads:
        load.wait()
    for layer, (source, target, slopes) in enumerate(((a0, a1, slope0), (a1, feat, slope1))):
        step_size = dil_ref[layer]
        weight = jnp.concatenate([tw_ref[layer, k] for k in range(TAPS)], axis=0)
        first = HALO if layer == 0 else 0
        for at in range(0, frames, step_frames):
            pre = mm(taps_of(source, at, step_frames, step_size, 1), weight)
            act, slope = silu_parts(pre)
            target[first + at : first + at + step_frames] = act.astype(BF16).reshape(
                step_frames, high, ch
            )
            slopes[at : at + step_frames] = slope.reshape(step_frames, high, ch)
        copies[layer].start()
    cots[:, :block, :] = got_ref[:, 1]
    for seg in range(segs):
        low, top = seg * seg_frames, (seg + 1) * seg_frames
        here = low + key_ref[seg]
        key_part = mm(feat[here], uw_ref[1])
        main = mm(feat[low:top].reshape(seg_frames * high, ch), uw_ref[0]).reshape(
            seg_frames, high, ch
        )
        united_ref[low:top] = (main + key_part[None]).astype(BF16)[:, :block]
        mine = cots[low:top]
        total = jnp.sum(mine.astype(F32), axis=0)
        key_term = sum(mm_nt(part, uw_ref[1]) for part in three_parts(total))
        grad_feat = mm_nt(mine.reshape(seg_frames * high, ch), uw_ref[0]).reshape(
            seg_frames, high, ch
        )
        for n in range(seg_frames):
            grad = grad_feat[n] + jnp.where(key_ref[seg] == n, key_term, 0.0)
            g1[HALO + low + n] = (grad * slope1[low + n]).astype(BF16)
    copies[4].start()
    for layer, source in ((1, g1), (0, g0)):
        copies[3 - layer].start()
        step_size = dil_ref[layer]
        weight = jnp.concatenate(
            [tw_ref[layer, k].astype(F32).T.astype(BF16) for k in range(TAPS)], axis=0
        )
        for n, at in enumerate(range(0, frames, step_frames)):
            grad = mm(taps_of(source, at, step_frames, step_size, -1), weight).reshape(
                step_frames, high, ch
            )
            if layer == 1:
                g0[HALO + at : HALO + at + step_frames] = (
                    grad * slope0[at : at + step_frames]
                ).astype(BF16)
            else:
                grad_ref[at : at + step_frames] = grad.astype(BF16)[:, :block]
                stores[n].start()
    for copy in copies + stores:
        copy.wait()


def temporal_wgrad_kernel(
    step_frames, scale, here_ref, dil_ref, key_ref, got_ref, kept_hbm, *rest
):
    pieces, (a0, g0, a1, g1, feat, cots, total_ref, sems) = rest[:-8], rest[-8:]
    frames, high, ch = feat.shape
    block = got_ref.shape[2]
    segs = key_ref.shape[0]
    seg_frames = frames // segs
    rows = step_frames * high
    inside = pl.ds(HALO, frames)
    copies = [
        pltpu.make_async_copy(kept_hbm.at[n], target, sems.at[n])
        for n, target in ((3, g0), (0, a1.at[inside]), (2, g1), (1, feat))
    ]
    for copy in copies:
        copy.start()
    clear_halo(a0, frames)
    clear_halo(a1, frames)
    if high > block:
        pad = jnp.zeros((frames, high - block, ch), BF16)
        a0[HALO : HALO + frames, block:, :] = pad
        cots[:, block:, :] = pad
    a0[HALO : HALO + frames, :block, :] = got_ref[:, 0]
    cots[:, :block, :] = got_ref[:, 1]
    totals = []
    for layer, acts, grads in ((0, a0, g0), (1, a1, g1)):
        for copy in copies[1:3] if layer else copies[:1]:
            copy.wait()
        total = jnp.zeros((TAPS * ch, ch), F32)
        for at in range(0, frames, step_frames):
            total = total + mm_tn(
                taps_of(acts, at, step_frames, dil_ref[layer], 1),
                grads[at : at + step_frames].reshape(rows, ch),
            )
        totals.append(total)
    copies[3].wait()
    total = jnp.zeros((ch, ch), F32)
    for at in range(0, frames, step_frames):
        total = total + mm_tn(
            feat[at : at + step_frames].reshape(rows, ch),
            cots[at : at + step_frames].reshape(rows, ch),
        )
    keyed = jnp.zeros((ch, ch), F32)
    for seg in range(segs):
        low, top = seg * seg_frames, (seg + 1) * seg_frames
        key = feat[low + key_ref[seg]]
        seg_cot = jnp.sum(cots[low:top].astype(F32), axis=0)
        keyed = keyed + sum(mm_tn(key, part) for part in three_parts(seg_cot))
    peers = len(pieces)
    split = LAYERS * TAPS * ch // peers
    total_ref[:, :split] = (jnp.concatenate(totals, axis=0) * scale).reshape(peers, split, ch)
    total_ref[:, split:] = (jnp.concatenate([total, keyed], axis=0) * scale).reshape(
        peers, 2 * ch // peers, ch
    )
    hand_out(here_ref, total_ref, pieces)


def sum_kernel(*refs):
    refs[-1][...] = sum(ref[...].astype(F32) for ref in refs[:-1]).astype(refs[-1].dtype)


def join_kernel(*refs):
    *parts, out_ref = refs
    half = len(parts) // 2
    split = parts[0].shape[0]
    out_ref[:split] = sum(ref[...].astype(F32) for ref in parts[:half]).astype(out_ref.dtype)
    out_ref[split:] = sum(ref[...].astype(F32) for ref in parts[half:]).astype(out_ref.dtype)


def deal_kernel(pieces_ref, united_hbm, *refs):
    outs_hbm, united_out, outs, sems = refs[:3], refs[3], refs[4:7], refs[7]
    copies = [pltpu.make_async_copy(united_hbm, united_out, sems.at[3])]
    copies[0].start()
    at = 0
    for n, out_ref in enumerate(outs):
        count = out_ref.shape[1]
        out_ref[...] = pieces_ref[:, at : at + count].astype(F32)
        copies.append(pltpu.make_async_copy(out_ref, outs_hbm[n], sems.at[n]))
        copies[-1].start()
        at += count
    for copy in copies:
        copy.wait()


def exchange(blocks):
    return lax.all_to_all(blocks, AXES, split_axis=0, concat_axis=0, tiled=True)


def flip(value, peer):
    size = lax.axis_size("grp")
    return lax.ppermute(value, "grp", [(i, i ^ peer) for i in range(size)])


def turn_by(value, turn):
    size = lax.axis_size("seg")
    return lax.ppermute(value, "seg", [(i, (i + turn) % size) for i in range(size)])


def sum_of(parts):
    shape = parts[0].shape
    return call(
        sum_kernel, [(shape, BF16, VMEM)], [], 0, len(parts) * 2 * shape[0] * shape[1],
        [(part, VMEM) for part in parts], SMALL_VMEM,
    )[0]


def reduce_in_grp(pieces):
    return sum_of([flip(piece, peer) if peer else piece for peer, piece in enumerate(pieces)])


def all_turns(value):
    return [turn_by(value, turn) if turn else value for turn in range(lax.axis_size("seg"))]


def local(
    frames_in, spatial_weight, temporal_weight, uniting_weight, key_index, dilation, cotangent
):
    held, rows, cols, ch = frames_in.shape
    assert held == 1
    pixels = rows * cols
    peers = lax.axis_size("grp")
    devices = lax.axis_size("seg") * peers
    frames = held * devices
    block = pixels // devices
    split = cols // block
    wide = round_up(cols + 1, 16)
    high = round_up(block, 16)
    rows_step = next(n for n in (4, 2, 1) if rows % n == 0)
    steps = rows // rows_step
    parts = next(n for n in (4, 2, 1) if rows % (n * rows_step) == 0)
    step_frames, narrow_step = (
        max(n for n in range(1, frames + 1) if frames % n == 0 and n * high <= most)
        for most in (512, 256)
    )
    scale = float((frames * pixels) ** -0.5)
    here = jnp.stack([lax.axis_index("seg"), lax.axis_index("grp")]).astype(jnp.int32)
    space_rows, time_rows, unite_rows = (n * ch // peers for n in (9, LAYERS * TAPS, 2))

    (send,) = call(
        functools.partial(spatial_fwd_kernel, rows_step),
        [((rows, 2, cols, ch), BF16, HBM)],
        [
            pltpu.VMEM((rows, cols, ch), BF16),
            pltpu.VMEM(spatial_weight.shape, BF16),
            pltpu.VMEM((rows + 2, wide, ch), BF16),
            pltpu.VMEM((rows, 2, cols, ch), BF16),
            pltpu.SemaphoreType.DMA((parts,)),
            pltpu.SemaphoreType.DMA((1,)),
            pltpu.SemaphoreType.DMA((1,)),
            pltpu.SemaphoreType.DMA((parts,)),
        ],
        2 * 9 * pixels * ch * ch,
        pixels * ch * 8,
        [(frames_in[0], HBM), (spatial_weight, HBM), (cotangent[0], HBM)],
    )
    send, frame = lax.optimization_barrier((send, frames_in[0]))
    send = send.reshape(rows, 2, split, block, ch).swapaxes(1, 2).reshape(devices, 2, block, ch)
    got = exchange(send)
    (space_slope,) = call(
        functools.partial(spatial_slope_kernel, rows_step),
        [((SPARE, rows, cols, ch), BF16, HBM)],
        [
            pltpu.VMEM((rows + 2, wide, ch), BF16),
            pltpu.VMEM((rows, cols, ch), BF16),
            pltpu.SemaphoreType.DMA((1,)),
        ],
        2 * 9 * pixels * ch * ch,
        pixels * ch * 4,
        [(frame, VMEM), (spatial_weight, VMEM)],
    )
    got, space_slope = lax.optimization_barrier((got, space_slope))

    padded = (frames + 2 * HALO, high, ch)
    whole = (frames, high, ch)
    grad_send, kept, united_send = call(
        functools.partial(temporal_kernel, narrow_step),
        [
            ((frames, block, ch), BF16, HBM),
            ((SPARE,) + whole, BF16, HBM),
            ((frames, block, ch), BF16, HBM),
        ],
        [
            pltpu.VMEM(padded, BF16),
            pltpu.VMEM(padded, BF16),
            pltpu.VMEM(whole, BF16),
            pltpu.VMEM(whole, BF16),
            pltpu.VMEM(padded, BF16),
            pltpu.VMEM(padded, BF16),
            pltpu.VMEM(whole, F32),
            pltpu.VMEM(whole, F32),
            pltpu.VMEM((frames, block, ch), BF16),
            pltpu.VMEM((frames, block, ch), BF16),
            pltpu.VMEM(temporal_weight.shape, BF16),
            pltpu.VMEM(uniting_weight.shape, BF16),
            pltpu.SemaphoreType.DMA((5,)),
            pltpu.SemaphoreType.DMA((2,)),
            pltpu.SemaphoreType.DMA((frames // narrow_step,)),
        ],
        2 * 22 * frames * block * ch * ch,
        frames * block * ch * 18,
        [
            (dilation, SMEM), (key_index, SMEM), (got, VMEM),
            (temporal_weight, HBM), (uniting_weight, HBM),
        ],
        MID_VMEM,
    )
    grad_time = exchange(grad_send).reshape(rows, cols, ch)
    time_pieces = call(
        functools.partial(temporal_wgrad_kernel, step_frames, scale),
        [((time_rows + unite_rows, ch), BF16, VMEM)] * peers,
        [
            pltpu.VMEM(padded, BF16),
            pltpu.VMEM(whole, BF16),
            pltpu.VMEM(padded, BF16),
            pltpu.VMEM(whole, BF16),
            pltpu.VMEM(whole, BF16),
            pltpu.VMEM(whole, BF16),
            pltpu.VMEM((peers, time_rows + unite_rows, ch), F32),
            pltpu.SemaphoreType.DMA((4,)),
        ],
        2 * 12 * frames * block * ch * ch,
        frames * block * ch * 14,
        [
            (here, SMEM), (dilation, SMEM), (key_index, SMEM), (got, VMEM), (kept, HBM),
        ],
        MID_VMEM,
    )
    time_turned = all_turns(reduce_in_grp(time_pieces))
    *time_turned, grad_time = lax.optimization_barrier((*time_turned, grad_time))
    united_send, grad_time = lax.optimization_barrier((united_send, grad_time))
    united = exchange(united_send)
    space_pieces = call(
        functools.partial(spatial_wgrad_kernel, rows_step, scale),
        [((space_rows, ch), BF16, VMEM)] * peers,
        [
            pltpu.VMEM((rows + 2, wide, ch), BF16),
            pltpu.VMEM((rows, cols, ch), BF16),
            pltpu.VMEM((3 * ch, min(3, steps) * rows_step * wide), BF16),
            pltpu.VMEM((peers, space_rows, ch), F32),
            pltpu.SemaphoreType.DMA((1,)),
        ],
        2 * 9 * pixels * ch * ch,
        pixels * ch * 8,
        [(here, SMEM), (grad_time, VMEM), (space_slope, HBM), (frame, VMEM)],
        MID_VMEM,
    )
    (back,) = call(
        functools.partial(spatial_back_kernel, rows_step),
        [((rows, cols, ch), BF16, VMEM)],
        [
            pltpu.VMEM((rows + 2, wide, ch), BF16),
            pltpu.VMEM((rows, cols, ch), BF16),
            pltpu.SemaphoreType.DMA((1,)),
        ],
        2 * 9 * pixels * ch * ch,
        pixels * ch * 6,
        [(spatial_weight, VMEM), (grad_time, VMEM), (space_slope, HBM)],
        MID_VMEM,
    )
    turned = all_turns(reduce_in_grp(space_pieces))
    turned[0], back = lax.optimization_barrier((turned[0], back))
    (piece,) = call(
        join_kernel,
        [((time_rows + unite_rows + space_rows, ch), BF16, VMEM)],
        [],
        0,
        2 * 4 * 21 * ch * ch,
        [(part, VMEM) for part in time_turned + turned],
        SMALL_VMEM,
    )
    *grads, united = call(
        deal_kernel,
        [((peers, count, ch), F32, HBM) for count in (time_rows, unite_rows, space_rows)]
        + [((frames, block, ch), BF16, HBM)],
        [pltpu.VMEM((peers, count, ch), F32) for count in (time_rows, unite_rows, space_rows)]
        + [pltpu.SemaphoreType.DMA((4,))],
        0,
        6 * 21 * ch * ch,
        [(lax.all_gather(piece, "grp", axis=0), VMEM), (united, HBM)],
        SMALL_VMEM,
    )
    return (
        united.reshape(frames_in.shape),
        back[None],
        grads[2].reshape(9, ch, ch),
        grads[0].reshape(LAYERS, TAPS, ch, ch),
        grads[1].reshape(2, ch, ch),
    )


def solution(mesh):
    frame_spec = P(AXES, None, None, None)
    return jax.shard_map(
        local,
        mesh=mesh,
        in_specs=(frame_spec, P(), P(), P(), P(), P(), frame_spec),
        out_specs=(frame_spec, frame_spec, P(), P(), P()),
        check_vma=False,
    )
```

```python
import functools

import jax
import jax.numpy as jnp
from jax import lax
from jax.experimental import pallas as pl
from jax.experimental.pallas import tpu as pltpu
from jax.sharding import Mesh, PartitionSpec as P

LAYERS = 2
TAPS = 5
DMAX = 8
HALO = 2 * DMAX
GRP = ("chip", "core")
AXES = ("seg",) + GRP
BF16 = jnp.bfloat16
F32 = jnp.float32
BIG_VMEM = 60 * 1024 * 1024
MID_VMEM = 40 * 1024 * 1024
SPARE = 28
SMALL_VMEM = 16 * 1024 * 1024


def round_up(value, step):
    return -(-value // step) * step


def silu_parts(value):
    sigma = 0.5 * jnp.tanh(0.5 * value) + 0.5
    act = value * sigma
    return act, sigma + act * (1.0 - sigma)


def mm(left, right):
    return jnp.dot(left, right, preferred_element_type=F32)


def mm_nt(left, right):
    return lax.dot_general(left, right, (((1,), (1,)), ((), ())), preferred_element_type=F32)


def mm_tn(left, right):
    return lax.dot_general(left, right, (((0,), (0,)), ((), ())), preferred_element_type=F32)


def three_parts(value):
    high = value.astype(BF16)
    rest = value - high.astype(F32)
    middle = rest.astype(BF16)
    return high, middle, (rest - middle.astype(F32)).astype(BF16)


VMEM = pl.BlockSpec(memory_space=pltpu.VMEM)
SMEM = pl.BlockSpec(memory_space=pltpu.SMEM)
HBM = pl.BlockSpec(memory_space=pltpu.HBM)


def call(kernel, outs, scratch, flops, moved, args, vmem=BIG_VMEM):
    return pl.pallas_call(
        kernel,
        out_shape=[jax.ShapeDtypeStruct(shape, kind) for shape, kind, _ in outs],
        in_specs=[spec for _, spec in args],
        out_specs=[spec for _, _, spec in outs],
        scratch_shapes=scratch,
        compiler_params=pltpu.CompilerParams(vmem_limit_bytes=vmem),
        cost_estimate=pl.CostEstimate(flops=flops, bytes_accessed=moved, transcendentals=0),
    )(*[value for value, _ in args])


def roll_rows(value, shift):
    return pltpu.roll(value, shift % value.shape[0], 0)


def spatial_pre(xs, weight, at, rows_step):
    wide, ch = xs.shape[1:]
    flat = rows_step * wide
    left = jnp.concatenate(
        [xs[at + a : at + a + rows_step].reshape(flat, ch) for a in range(3)], axis=1
    )
    y = mm(left, weight)
    return y[:, ch : 2 * ch] + roll_rows(y[:, :ch], 1) + roll_rows(y[:, 2 * ch :], -1)


def forward_weight(w_ref):
    return jnp.concatenate(
        [jnp.concatenate([w_ref[3 * a + b] for b in range(3)], axis=1) for a in range(3)], axis=0
    )


def clear_ends(ref):
    last = ref.shape[0] - 1
    ref[0] = jnp.zeros(ref.shape[1:], ref.dtype)
    ref[last] = jnp.zeros(ref.shape[1:], ref.dtype)


def put_rows(ref, at, value):
    count, cols, ch = value.shape
    ref[1 + at : 1 + at + count, cols:, :] = jnp.zeros((count, ref.shape[1] - cols, ch), ref.dtype)
    ref[1 + at : 1 + at + count, :cols, :] = value


def spatial_fwd_kernel(
    rows_step, x_hbm, w_hbm, cot_hbm, send_hbm,
    x_in, w_ref, xs, sends, in_sems, w_sem, cot_sem, send_sems,
):
    rows, cols, ch = x_in.shape
    wide = xs.shape[1]
    parts = in_sems.shape[0]
    many = rows // parts

    def part(n):
        return pl.ds(n * many, many)

    loads = [
        pltpu.make_async_copy(x_hbm.at[part(n)], x_in.at[part(n)], in_sems.at[n]) for n in range(parts)
    ]
    stores = [
        pltpu.make_async_copy(sends.at[part(n)], send_hbm.at[part(n)], send_sems.at[n])
        for n in range(parts)
    ]
    w_load = pltpu.make_async_copy(w_hbm, w_ref, w_sem.at[0])
    cot_load = pltpu.make_async_copy(cot_hbm, sends.at[:, 1], cot_sem.at[0])
    for load in [loads[0], w_load] + loads[1:] + [cot_load]:
        load.start()
    clear_ends(xs)

    def bring(n):
        loads[n].wait()
        put_rows(xs, n * many, x_in[n * many : (n + 1) * many])

    bring(0)
    w_load.wait()
    weight = forward_weight(w_ref)
    for n in range(parts):
        if n + 1 < parts:
            bring(n + 1)
        for at in range(n * many, (n + 1) * many, rows_step):
            act, _ = silu_parts(spatial_pre(xs, weight, at, rows_step))
            sends[at : at + rows_step, 0] = act.astype(BF16).reshape(rows_step, wide, ch)[:, :cols]
        if n == 0:
            cot_load.wait()
        stores[n].start()
    for store in stores:
        store.wait()


def spatial_slope_kernel(rows_step, x_ref, w_ref, slope_hbm, xs, slopes, sem):
    rows, cols, ch = x_ref.shape
    wide = xs.shape[1]
    clear_ends(xs)
    put_rows(xs, 0, x_ref[...])
    weight = forward_weight(w_ref)
    for at in range(0, rows, rows_step):
        _, slope = silu_parts(spatial_pre(xs, weight, at, rows_step))
        slopes[at : at + rows_step] = slope.astype(BF16).reshape(rows_step, wide, ch)[:, :cols]
    store = pltpu.make_async_copy(slopes, slope_hbm.at[0], sem.at[0])
    store.start()
    store.wait()


def hand_out(here_ref, total_ref, pieces):
    for peer, piece in enumerate(pieces):
        piece[...] = total_ref[jnp.bitwise_xor(here_ref[1], peer)].astype(piece.dtype)


def taps_up(gs, at, rows_step):
    wide, ch = gs.shape[1:]
    return jnp.concatenate(
        [gs[at + 2 - a : at + 2 - a + rows_step].reshape(rows_step * wide, ch) for a in range(3)],
        axis=1,
    )


def fill_grads(rows_step, gs, got_ref, slope_ref):
    clear_ends(gs)
    for at in range(0, got_ref.shape[0], rows_step):
        grads = got_ref[at : at + rows_step].astype(F32)
        slopes = slope_ref[at : at + rows_step].astype(F32)
        put_rows(gs, at, (grads * slopes).astype(BF16))


def spatial_wgrad_kernel(rows_step, scale, here_ref, got_ref, slope_hbm, x_ref, *rest):
    pieces, (gs, slopes, cat_ref, total_ref, sem) = rest[:-5], rest[-5:]
    rows, cols, ch = got_ref.shape
    wide = gs.shape[1]
    flat = rows_step * wide
    load = pltpu.make_async_copy(slope_hbm.at[0], slopes, sem.at[0])
    load.start()
    pad = jnp.zeros((rows_step, wide - cols, ch), F32)

    def columns(at):
        x = jnp.concatenate([x_ref[at : at + rows_step].astype(F32), pad], axis=1).reshape(flat, ch)
        x_cat = jnp.concatenate([roll_rows(x, 1), x, roll_rows(x, -1)], axis=1)
        return x_cat.T.astype(BF16)

    early = cat_ref.shape[1] // flat
    for n in range(early):
        cat_ref[:, n * flat : (n + 1) * flat] = columns(n * rows_step)
    load.wait()
    fill_grads(rows_step, gs, got_ref, slopes)
    total = jnp.zeros((3 * ch, 3 * ch), F32)
    for n, at in enumerate(range(0, rows, rows_step)):
        cat = cat_ref[:, n * flat : (n + 1) * flat] if n < early else columns(at)
        total = total + mm(cat, taps_up(gs, at, rows_step))
    total_ref[...] = (
        jnp.concatenate(
            [
                total[b * ch : (b + 1) * ch, a * ch : (a + 1) * ch]
                for a in range(3)
                for b in range(3)
            ],
            axis=0,
        )
        * scale
    ).reshape(total_ref.shape)
    hand_out(here_ref, total_ref, pieces)


def spatial_back_kernel(rows_step, w_ref, got_ref, slope_hbm, back_ref, gs, slopes, sem):
    rows, cols, ch = back_ref.shape
    wide = gs.shape[1]
    load = pltpu.make_async_copy(slope_hbm.at[0], slopes, sem.at[0])
    load.start()
    weight = jnp.concatenate(
        [
            jnp.concatenate([w_ref[3 * a + b].astype(F32).T.astype(BF16) for b in range(3)], axis=1)
            for a in range(3)
        ],
        axis=0,
    )
    load.wait()
    fill_grads(rows_step, gs, got_ref, slopes)
    for at in range(0, rows, rows_step):
        y = mm(taps_up(gs, at, rows_step), weight)
        back = y[:, ch : 2 * ch] + roll_rows(y[:, :ch], -1) + roll_rows(y[:, 2 * ch :], 1)
        back_ref[at : at + rows_step] = back.astype(BF16).reshape(rows_step, wide, ch)[:, :cols]


def clear_halo(pad_ref, frames):
    zeros = jnp.zeros((HALO,) + pad_ref.shape[1:], pad_ref.dtype)
    pad_ref[:HALO] = zeros
    pad_ref[HALO + frames :] = zeros


def taps_of(pad_ref, at, count, step_size, sign):
    high, ch = pad_ref.shape[1:]
    pieces = [
        pad_ref[pl.ds(HALO + at + sign * (k - 2) * step_size, count)].reshape(count * high, ch)
        for k in range(TAPS)
    ]
    return jnp.concatenate(pieces, axis=1)


def temporal_kernel(
    step_frames, dil_ref, key_ref, got_ref, tw_hbm, uw_hbm,
    grad_hbm, kept_hbm,
    a0, a1, feat, cots, g0, g1, slope0, slope1, grad_ref, tw_ref, uw_ref,
    sems, in_sems, out_sems,
):
    frames, _, block, ch = got_ref.shape
    high = feat.shape[1]
    loads = [
        pltpu.make_async_copy(source, ref, in_sems.at[n])
        for n, (source, ref) in enumerate(((tw_hbm, tw_ref), (uw_hbm, uw_ref)))
    ]
    for load in loads:
        load.start()
    stores = [
        pltpu.make_async_copy(
            grad_ref.at[pl.ds(at, step_frames)], grad_hbm.at[pl.ds(at, step_frames)], out_sems.at[n]
        )
        for n, at in enumerate(range(0, frames, step_frames))
    ]
    segs = key_ref.shape[0]
    seg_frames = frames // segs
    inside = pl.ds(HALO, frames)
    copies = [
        pltpu.make_async_copy(source, target, sems.at[n])
        for n, (source, target) in enumerate(
            (
                (a1.at[inside], kept_hbm.at[0]),
                (feat, kept_hbm.at[1]),
                (g1.at[inside], kept_hbm.at[2]),
                (g0.at[inside], kept_hbm.at[3]),
                (a0.at[inside], kept_hbm.at[4]),
                (cots, kept_hbm.at[5]),
            )
        )
    ]
    for ref in (a0, a1, g0, g1):
        clear_halo(ref, frames)
    if high > block:
        pad = jnp.zeros((frames, high - block, ch), BF16)
        a0[HALO : HALO + frames, block:, :] = pad
        cots[:, block:, :] = pad
    a0[HALO : HALO + frames, :block, :] = got_ref[:, 0]
    copies[4].start()
    for load in loads:
        load.wait()
    for layer, (source, target, slopes) in enumerate(((a0, a1, slope0), (a1, feat, slope1))):
        step_size = dil_ref[layer]
        weight = jnp.concatenate([tw_ref[layer, k] for k in range(TAPS)], axis=0)
        first = HALO if layer == 0 else 0
        for at in range(0, frames, step_frames):
            pre = mm(taps_of(source, at, step_frames, step_size, 1), weight)
            act, slope = silu_parts(pre)
            target[first + at : first + at + step_frames] = act.astype(BF16).reshape(
                step_frames, high, ch
            )
            slopes[at : at + step_frames] = slope.reshape(step_frames, high, ch)
        copies[layer].start()
    cots[:, :block, :] = got_ref[:, 1]
    copies[5].start()
    for seg in range(segs):
        low, top = seg * seg_frames, (seg + 1) * seg_frames
        mine = cots[low:top]
        total = jnp.sum(mine.astype(F32), axis=0)
        key_term = sum(mm_nt(part, uw_ref[1]) for part in three_parts(total))
        grad_feat = mm_nt(mine.reshape(seg_frames * high, ch), uw_ref[0]).reshape(
            seg_frames, high, ch
        )
        for n in range(seg_frames):
            grad = grad_feat[n] + jnp.where(key_ref[seg] == n, key_term, 0.0)
            g1[HALO + low + n] = (grad * slope1[low + n]).astype(BF16)
    for layer, source in ((1, g1), (0, g0)):
        copies[3 - layer].start()
        step_size = dil_ref[layer]
        weight = jnp.concatenate(
            [tw_ref[layer, k].astype(F32).T.astype(BF16) for k in range(TAPS)], axis=0
        )
        for n, at in enumerate(range(0, frames, step_frames)):
            grad = mm(taps_of(source, at, step_frames, step_size, -1), weight).reshape(
                step_frames, high, ch
            )
            if layer == 1:
                g0[HALO + at : HALO + at + step_frames] = (
                    grad * slope0[at : at + step_frames]
                ).astype(BF16)
            else:
                grad_ref[at : at + step_frames] = grad.astype(BF16)[:, :block]
                stores[n].start()
    for copy in copies + stores:
        copy.wait()


def temporal_wgrad_kernel(
    step_frames, scale, here_ref, dil_ref, key_ref,
    kept_hbm, uw_ref, united_hbm, *rest
):
    pieces, (a0, g0, a1, g1, feat, cots, united, total_ref, sems) = rest[:-9], rest[-9:]
    frames, high, ch = feat.shape
    segs = key_ref.shape[0]
    seg_frames = frames // segs
    rows = step_frames * high
    inside = pl.ds(HALO, frames)
    copies = [
        pltpu.make_async_copy(source, target, sems.at[n])
        for n, (source, target) in enumerate(
            (
                (kept_hbm.at[1], feat),
                (kept_hbm.at[4], a0.at[inside]),
                (kept_hbm.at[3], g0),
                (kept_hbm.at[0], a1.at[inside]),
                (kept_hbm.at[2], g1),
                (kept_hbm.at[5], cots),
            )
        )
    ]
    for copy in copies:
        copy.start()
    clear_halo(a0, frames)
    clear_halo(a1, frames)
    copies[0].wait()
    block = united.shape[1]
    for seg in range(segs):
        low, top = seg * seg_frames, (seg + 1) * seg_frames
        key_part = mm(feat[low + key_ref[seg]], uw_ref[1])
        main = mm(feat[low:top].reshape(seg_frames * high, ch), uw_ref[0]).reshape(
            seg_frames, high, ch
        )
        united[low:top] = (main + key_part[None]).astype(BF16)[:, :block]
    united_copy = pltpu.make_async_copy(united, united_hbm, sems.at[len(copies)])
    united_copy.start()
    totals = []
    for layer, acts, grads in ((0, a0, g0), (1, a1, g1)):
        copies[2 * layer + 1].wait()
        copies[2 * layer + 2].wait()
        total = jnp.zeros((TAPS * ch, ch), F32)
        for at in range(0, frames, step_frames):
            total = total + mm_tn(
                taps_of(acts, at, step_frames, dil_ref[layer], 1),
                grads[at : at + step_frames].reshape(rows, ch),
            )
        totals.append(total)
    copies[5].wait()
    total = jnp.zeros((ch, ch), F32)
    for at in range(0, frames, step_frames):
        total = total + mm_tn(
            feat[at : at + step_frames].reshape(rows, ch),
            cots[at : at + step_frames].reshape(rows, ch),
        )
    keyed = jnp.zeros((ch, ch), F32)
    for seg in range(segs):
        low, top = seg * seg_frames, (seg + 1) * seg_frames
        key = feat[low + key_ref[seg]]
        seg_cot = jnp.sum(cots[low:top].astype(F32), axis=0)
        keyed = keyed + sum(mm_tn(key, part) for part in three_parts(seg_cot))
    peers = len(pieces)
    split = LAYERS * TAPS * ch // peers
    total_ref[:, :split] = (jnp.concatenate(totals, axis=0) * scale).reshape(peers, split, ch)
    total_ref[:, split:] = (jnp.concatenate([total, keyed], axis=0) * scale).reshape(
        peers, 2 * ch // peers, ch
    )
    hand_out(here_ref, total_ref, pieces)
    united_copy.wait()


def sum_kernel(*refs):
    refs[-1][...] = sum(ref[...].astype(F32) for ref in refs[:-1]).astype(refs[-1].dtype)


def join_kernel(first_ref, *refs):
    out_ref = refs[-1]
    split = first_ref.shape[0]
    out_ref[:split] = first_ref[...]
    out_ref[split:] = sum(ref[...].astype(F32) for ref in refs[:-1]).astype(out_ref.dtype)


def deal_kernel(pieces_ref, united_hbm, *refs):
    outs_hbm, united_out, outs, sems = refs[:3], refs[3], refs[4:7], refs[7]
    copies = [pltpu.make_async_copy(united_hbm, united_out, sems.at[3])]
    copies[0].start()
    at = 0
    for n, out_ref in enumerate(outs):
        count = out_ref.shape[1]
        out_ref[...] = pieces_ref[:, at : at + count].astype(F32)
        copies.append(pltpu.make_async_copy(out_ref, outs_hbm[n], sems.at[n]))
        copies[-1].start()
        at += count
    for copy in copies:
        copy.wait()


def exchange(blocks):
    return lax.all_to_all(blocks, AXES, split_axis=0, concat_axis=0, tiled=True)


def flip(value, peer):
    size = lax.axis_size("chip") * lax.axis_size("core")
    return lax.ppermute(value, GRP, [(i, i ^ peer) for i in range(size)])


def turn_by(value, turn):
    size = lax.axis_size("seg")
    return lax.ppermute(value, "seg", [(i, (i + turn) % size) for i in range(size)])


def sum_of(parts):
    shape = parts[0].shape
    return call(
        sum_kernel, [(shape, BF16, VMEM)], [], 0, len(parts) * 2 * shape[0] * shape[1],
        [(part, VMEM) for part in parts], SMALL_VMEM,
    )[0]


def reduce_in_grp(pieces):
    return sum_of([flip(piece, peer) if peer else piece for peer, piece in enumerate(pieces)])


def all_turns(value):
    return [turn_by(value, turn) if turn else value for turn in range(lax.axis_size("seg"))]


def local(
    frames_in, spatial_weight, temporal_weight, uniting_weight, key_index, dilation, cotangent
):
    held, rows, cols, ch = frames_in.shape
    assert held == 1
    pixels = rows * cols
    peers = lax.axis_size("chip") * lax.axis_size("core")
    devices = lax.axis_size("seg") * peers
    frames = held * devices
    block = pixels // devices
    split = cols // block
    wide = round_up(cols + 1, 16)
    high = round_up(block, 16)
    rows_step = next(n for n in (4, 2, 1) if rows % n == 0)
    steps = rows // rows_step
    parts = next(n for n in (4, 2, 1) if rows % (n * rows_step) == 0)
    step_frames, narrow_step = (
        max(n for n in range(1, frames + 1) if frames % n == 0 and n * high <= most)
        for most in (512, 256)
    )
    scale = float((frames * pixels) ** -0.5)
    here = jnp.stack([lax.axis_index("seg"), lax.axis_index(GRP)]).astype(jnp.int32)
    space_rows, time_rows, unite_rows = (n * ch // peers for n in (9, LAYERS * TAPS, 2))

    (send,) = call(
        functools.partial(spatial_fwd_kernel, rows_step),
        [((rows, 2, cols, ch), BF16, HBM)],
        [
            pltpu.VMEM((rows, cols, ch), BF16),
            pltpu.VMEM(spatial_weight.shape, BF16),
            pltpu.VMEM((rows + 2, wide, ch), BF16),
            pltpu.VMEM((rows, 2, cols, ch), BF16),
            pltpu.SemaphoreType.DMA((parts,)),
            pltpu.SemaphoreType.DMA((1,)),
            pltpu.SemaphoreType.DMA((1,)),
            pltpu.SemaphoreType.DMA((parts,)),
        ],
        2 * 9 * pixels * ch * ch,
        pixels * ch * 8,
        [(frames_in[0], HBM), (spatial_weight, HBM), (cotangent[0], HBM)],
    )
    send, frame = lax.optimization_barrier((send, frames_in[0]))
    send = send.reshape(rows, 2, split, block, ch).swapaxes(1, 2).reshape(devices, 2, block, ch)
    got = exchange(send)
    (space_slope,) = call(
        functools.partial(spatial_slope_kernel, rows_step),
        [((SPARE, rows, cols, ch), BF16, HBM)],
        [
            pltpu.VMEM((rows + 2, wide, ch), BF16),
            pltpu.VMEM((rows, cols, ch), BF16),
            pltpu.SemaphoreType.DMA((1,)),
        ],
        2 * 9 * pixels * ch * ch,
        pixels * ch * 4,
        [(frame, VMEM), (spatial_weight, VMEM)],
    )
    got, space_slope = lax.optimization_barrier((got, space_slope))

    padded = (frames + 2 * HALO, high, ch)
    whole = (frames, high, ch)
    grad_send, kept = call(
        functools.partial(temporal_kernel, narrow_step),
        [
            ((frames, block, ch), BF16, HBM),
            ((SPARE,) + whole, BF16, HBM),
        ],
        [
            pltpu.VMEM(padded, BF16),
            pltpu.VMEM(padded, BF16),
            pltpu.VMEM(whole, BF16),
            pltpu.VMEM(whole, BF16),
            pltpu.VMEM(padded, BF16),
            pltpu.VMEM(padded, BF16),
            pltpu.VMEM(whole, F32),
            pltpu.VMEM(whole, F32),
            pltpu.VMEM((frames, block, ch), BF16),
            pltpu.VMEM(temporal_weight.shape, BF16),
            pltpu.VMEM(uniting_weight.shape, BF16),
            pltpu.SemaphoreType.DMA((6,)),
            pltpu.SemaphoreType.DMA((2,)),
            pltpu.SemaphoreType.DMA((frames // narrow_step,)),
        ],
        2 * 22 * frames * block * ch * ch,
        frames * block * ch * 18,
        [
            (dilation, SMEM), (key_index, SMEM), (got, VMEM),
            (temporal_weight, HBM), (uniting_weight, HBM),
        ],
        MID_VMEM,
    )
    grad_time = exchange(grad_send).reshape(rows, cols, ch)
    united_send, *time_pieces = call(
        functools.partial(temporal_wgrad_kernel, step_frames, scale),
        [((frames, block, ch), BF16, HBM)]
        + [((time_rows + unite_rows, ch), BF16, VMEM)] * peers,
        [
            pltpu.VMEM(padded, BF16),
            pltpu.VMEM(whole, BF16),
            pltpu.VMEM(padded, BF16),
            pltpu.VMEM(whole, BF16),
            pltpu.VMEM(whole, BF16),
            pltpu.VMEM(whole, BF16),
            pltpu.VMEM((frames, block, ch), BF16),
            pltpu.VMEM((peers, time_rows + unite_rows, ch), F32),
            pltpu.SemaphoreType.DMA((7,)),
        ],
        2 * 12 * frames * block * ch * ch,
        frames * block * ch * 14,
        [
            (here, SMEM), (dilation, SMEM), (key_index, SMEM),
            (kept, HBM), (uniting_weight, VMEM),
        ],
    )
    time_sum = reduce_in_grp(time_pieces)
    time_sum, grad_time = lax.optimization_barrier((time_sum, grad_time))
    united_send, grad_time = lax.optimization_barrier((united_send, grad_time))
    united = exchange(united_send)
    space_pieces = call(
        functools.partial(spatial_wgrad_kernel, rows_step, scale),
        [((space_rows, ch), BF16, VMEM)] * peers,
        [
            pltpu.VMEM((rows + 2, wide, ch), BF16),
            pltpu.VMEM((rows, cols, ch), BF16),
            pltpu.VMEM((3 * ch, min(3, steps) * rows_step * wide), BF16),
            pltpu.VMEM((peers, space_rows, ch), F32),
            pltpu.SemaphoreType.DMA((1,)),
        ],
        2 * 9 * pixels * ch * ch,
        pixels * ch * 8,
        [(here, SMEM), (grad_time, VMEM), (space_slope, HBM), (frame, VMEM)],
        MID_VMEM,
    )
    (back,) = call(
        functools.partial(spatial_back_kernel, rows_step),
        [((rows, cols, ch), BF16, VMEM)],
        [
            pltpu.VMEM((rows + 2, wide, ch), BF16),
            pltpu.VMEM((rows, cols, ch), BF16),
            pltpu.SemaphoreType.DMA((1,)),
        ],
        2 * 9 * pixels * ch * ch,
        pixels * ch * 6,
        [(spatial_weight, VMEM), (grad_time, VMEM), (space_slope, HBM)],
        MID_VMEM,
    )
    space_parts = [flip(part, peer) if peer else part for peer, part in enumerate(space_pieces)]
    (plane,) = call(
        join_kernel,
        [((time_rows + unite_rows + space_rows, ch), BF16, VMEM)],
        [],
        0,
        2 * (peers + 10) * space_rows * ch,
        [(time_sum, VMEM)] + [(part, VMEM) for part in space_parts],
        SMALL_VMEM,
    )
    turned = all_turns(plane)
    turned[0], back = lax.optimization_barrier((turned[0], back))
    piece = sum_of(turned)
    pieces = lax.all_gather(lax.all_gather(piece, "core", axis=0), "chip", axis=0)
    *grads, united = call(
        deal_kernel,
        [((peers, count, ch), F32, HBM) for count in (time_rows, unite_rows, space_rows)]
        + [((frames, block, ch), BF16, HBM)],
        [pltpu.VMEM((peers, count, ch), F32) for count in (time_rows, unite_rows, space_rows)]
        + [pltpu.SemaphoreType.DMA((4,))],
        0,
        6 * 21 * ch * ch,
        [(pieces.reshape(peers, -1, ch), VMEM), (united, HBM)],
        SMALL_VMEM,
    )
    return (
        united.reshape(frames_in.shape),
        back[None],
        grads[2].reshape(9, ch, ch),
        grads[0].reshape(LAYERS, TAPS, ch, ch),
        grads[1].reshape(2, ch, ch),
    )


def solution(mesh):
    segs, peers = (mesh.shape[name] for name in ("seg", "grp"))
    split = Mesh(mesh.devices.reshape(segs, peers // 2, 2), AXES)
    frame_spec = P(AXES, None, None, None)
    return jax.shard_map(
        local,
        mesh=split,
        in_specs=(frame_spec, P(), P(), P(), P(), P(), frame_spec),
        out_specs=(frame_spec, frame_spec, P(), P(), P()),
        check_vma=False,
    )
```

```python
import functools

import jax
import jax.numpy as jnp
from jax import lax
from jax.experimental import pallas as pl
from jax.experimental.pallas import tpu as pltpu
from jax.sharding import PartitionSpec as P

LAYERS = 2
TAPS = 5
DMAX = 8
HALO = 2 * DMAX
AXES = ("seg", "grp")
BF16 = jnp.bfloat16
F32 = jnp.float32
BIG_VMEM = 60 * 1024 * 1024
MID_VMEM = 40 * 1024 * 1024
SPARE = 28
SMALL_VMEM = 16 * 1024 * 1024


def round_up(value, step):
    return -(-value // step) * step


def silu_parts(value):
    sigma = 0.5 * jnp.tanh(0.5 * value) + 0.5
    act = value * sigma
    return act, sigma + act * (1.0 - sigma)


def mm(left, right):
    return jnp.dot(left, right, preferred_element_type=F32)


def mm_nt(left, right):
    return lax.dot_general(left, right, (((1,), (1,)), ((), ())), preferred_element_type=F32)


def mm_tn(left, right):
    return lax.dot_general(left, right, (((0,), (0,)), ((), ())), preferred_element_type=F32)


def three_parts(value):
    high = value.astype(BF16)
    rest = value - high.astype(F32)
    middle = rest.astype(BF16)
    return high, middle, (rest - middle.astype(F32)).astype(BF16)


VMEM = pl.BlockSpec(memory_space=pltpu.VMEM)
SMEM = pl.BlockSpec(memory_space=pltpu.SMEM)
HBM = pl.BlockSpec(memory_space=pltpu.HBM)


def call(kernel, outs, scratch, flops, moved, args, vmem=BIG_VMEM):
    return pl.pallas_call(
        kernel,
        out_shape=[jax.ShapeDtypeStruct(shape, kind) for shape, kind, _ in outs],
        in_specs=[spec for _, spec in args],
        out_specs=[spec for _, _, spec in outs],
        scratch_shapes=scratch,
        compiler_params=pltpu.CompilerParams(vmem_limit_bytes=vmem),
        cost_estimate=pl.CostEstimate(flops=flops, bytes_accessed=moved, transcendentals=0),
    )(*[value for value, _ in args])


def roll_rows(value, shift):
    return pltpu.roll(value, shift % value.shape[0], 0)


def spatial_pre(xs, weight, at, rows_step):
    wide, ch = xs.shape[1:]
    flat = rows_step * wide
    left = jnp.concatenate(
        [xs[at + a : at + a + rows_step].reshape(flat, ch) for a in range(3)], axis=1
    )
    y = mm(left, weight)
    return y[:, ch : 2 * ch] + roll_rows(y[:, :ch], 1) + roll_rows(y[:, 2 * ch :], -1)


def forward_weight(w_ref):
    return jnp.concatenate(
        [jnp.concatenate([w_ref[3 * a + b] for b in range(3)], axis=1) for a in range(3)], axis=0
    )


def clear_ends(ref):
    last = ref.shape[0] - 1
    ref[0] = jnp.zeros(ref.shape[1:], ref.dtype)
    ref[last] = jnp.zeros(ref.shape[1:], ref.dtype)


def put_rows(ref, at, value):
    count, cols, ch = value.shape
    ref[1 + at : 1 + at + count, cols:, :] = jnp.zeros((count, ref.shape[1] - cols, ch), ref.dtype)
    ref[1 + at : 1 + at + count, :cols, :] = value


def spatial_fwd_kernel(
    rows_step, x_hbm, w_hbm, cot_hbm, send_hbm,
    x_in, w_ref, xs, sends, in_sems, w_sem, cot_sem, send_sems,
):
    rows, cols, ch = x_in.shape
    wide = xs.shape[1]
    parts = in_sems.shape[0]
    many = rows // parts

    def part(n):
        return pl.ds(n * many, many)

    loads = [
        pltpu.make_async_copy(x_hbm.at[part(n)], x_in.at[part(n)], in_sems.at[n]) for n in range(parts)
    ]
    stores = [
        pltpu.make_async_copy(sends.at[part(n)], send_hbm.at[part(n)], send_sems.at[n])
        for n in range(parts)
    ]
    w_load = pltpu.make_async_copy(w_hbm, w_ref, w_sem.at[0])
    cot_load = pltpu.make_async_copy(cot_hbm, sends.at[:, 1], cot_sem.at[0])
    for load in [loads[0], w_load] + loads[1:] + [cot_load]:
        load.start()
    clear_ends(xs)

    def bring(n):
        loads[n].wait()
        put_rows(xs, n * many, x_in[n * many : (n + 1) * many])

    bring(0)
    w_load.wait()
    weight = forward_weight(w_ref)
    for n in range(parts):
        if n + 1 < parts:
            bring(n + 1)
        for at in range(n * many, (n + 1) * many, rows_step):
            act, _ = silu_parts(spatial_pre(xs, weight, at, rows_step))
            sends[at : at + rows_step, 0] = act.astype(BF16).reshape(rows_step, wide, ch)[:, :cols]
        if n == 0:
            cot_load.wait()
        stores[n].start()
    for store in stores:
        store.wait()


def spatial_slope_kernel(rows_step, x_ref, w_ref, slope_hbm, xs, slopes, sem):
    rows, cols, ch = x_ref.shape
    wide = xs.shape[1]
    clear_ends(xs)
    put_rows(xs, 0, x_ref[...])
    weight = forward_weight(w_ref)
    for at in range(0, rows, rows_step):
        _, slope = silu_parts(spatial_pre(xs, weight, at, rows_step))
        slopes[at : at + rows_step] = slope.astype(BF16).reshape(rows_step, wide, ch)[:, :cols]
    store = pltpu.make_async_copy(slopes, slope_hbm.at[0], sem.at[0])
    store.start()
    store.wait()


def hand_out(here_ref, total_ref, pieces):
    for peer, piece in enumerate(pieces):
        piece[...] = total_ref[jnp.bitwise_xor(here_ref[1], peer)].astype(piece.dtype)


def taps_up(gs, at, rows_step):
    wide, ch = gs.shape[1:]
    return jnp.concatenate(
        [gs[at + 2 - a : at + 2 - a + rows_step].reshape(rows_step * wide, ch) for a in range(3)],
        axis=1,
    )


def fill_grads(rows_step, gs, got_ref, slope_ref):
    clear_ends(gs)
    for at in range(0, got_ref.shape[0], rows_step):
        grads = got_ref[at : at + rows_step].astype(F32)
        slopes = slope_ref[at : at + rows_step].astype(F32)
        put_rows(gs, at, (grads * slopes).astype(BF16))


def spatial_wgrad_kernel(rows_step, scale, here_ref, got_ref, slope_hbm, x_ref, *rest):
    pieces, (gs, slopes, cat_ref, total_ref, sem) = rest[:-5], rest[-5:]
    rows, cols, ch = got_ref.shape
    wide = gs.shape[1]
    flat = rows_step * wide
    load = pltpu.make_async_copy(slope_hbm.at[0], slopes, sem.at[0])
    load.start()
    pad = jnp.zeros((rows_step, wide - cols, ch), F32)

    def columns(at):
        x = jnp.concatenate([x_ref[at : at + rows_step].astype(F32), pad], axis=1).reshape(flat, ch)
        x_cat = jnp.concatenate([roll_rows(x, 1), x, roll_rows(x, -1)], axis=1)
        return x_cat.T.astype(BF16)

    early = cat_ref.shape[1] // flat
    for n in range(early):
        cat_ref[:, n * flat : (n + 1) * flat] = columns(n * rows_step)
    load.wait()
    fill_grads(rows_step, gs, got_ref, slopes)
    total = jnp.zeros((3 * ch, 3 * ch), F32)
    for n, at in enumerate(range(0, rows, rows_step)):
        cat = cat_ref[:, n * flat : (n + 1) * flat] if n < early else columns(at)
        total = total + mm(cat, taps_up(gs, at, rows_step))
    total_ref[...] = (
        jnp.concatenate(
            [
                total[b * ch : (b + 1) * ch, a * ch : (a + 1) * ch]
                for a in range(3)
                for b in range(3)
            ],
            axis=0,
        )
        * scale
    ).reshape(total_ref.shape)
    hand_out(here_ref, total_ref, pieces)


def spatial_back_kernel(rows_step, w_ref, got_ref, slope_hbm, back_ref, gs, slopes, sem):
    rows, cols, ch = back_ref.shape
    wide = gs.shape[1]
    load = pltpu.make_async_copy(slope_hbm.at[0], slopes, sem.at[0])
    load.start()
    weight = jnp.concatenate(
        [
            jnp.concatenate([w_ref[3 * a + b].astype(F32).T.astype(BF16) for b in range(3)], axis=1)
            for a in range(3)
        ],
        axis=0,
    )
    load.wait()
    fill_grads(rows_step, gs, got_ref, slopes)
    for at in range(0, rows, rows_step):
        y = mm(taps_up(gs, at, rows_step), weight)
        back = y[:, ch : 2 * ch] + roll_rows(y[:, :ch], -1) + roll_rows(y[:, 2 * ch :], 1)
        back_ref[at : at + rows_step] = back.astype(BF16).reshape(rows_step, wide, ch)[:, :cols]


def clear_halo(pad_ref, frames):
    zeros = jnp.zeros((HALO,) + pad_ref.shape[1:], pad_ref.dtype)
    pad_ref[:HALO] = zeros
    pad_ref[HALO + frames :] = zeros


def taps_of(pad_ref, at, count, step_size, sign):
    high, ch = pad_ref.shape[1:]
    pieces = [
        pad_ref[pl.ds(HALO + at + sign * (k - 2) * step_size, count)].reshape(count * high, ch)
        for k in range(TAPS)
    ]
    return jnp.concatenate(pieces, axis=1)


def temporal_kernel(
    step_frames, dil_ref, key_ref, got_ref, tw_hbm, uw_hbm,
    grad_hbm, kept_hbm, united_hbm,
    a0, a1, feat, cots, g0, g1, slope0, slope1, united_ref, grad_ref, tw_ref, uw_ref,
    sems, in_sems, out_sems,
):
    frames, _, block, ch = got_ref.shape
    high = feat.shape[1]
    loads = [
        pltpu.make_async_copy(source, ref, in_sems.at[n])
        for n, (source, ref) in enumerate(((tw_hbm, tw_ref), (uw_hbm, uw_ref)))
    ]
    for load in loads:
        load.start()
    stores = [
        pltpu.make_async_copy(
            grad_ref.at[pl.ds(at, step_frames)], grad_hbm.at[pl.ds(at, step_frames)], out_sems.at[n]
        )
        for n, at in enumerate(range(0, frames, step_frames))
    ]
    segs = key_ref.shape[0]
    seg_frames = frames // segs
    inside = pl.ds(HALO, frames)
    copies = [
        pltpu.make_async_copy(source, target, sems.at[n])
        for n, (source, target) in enumerate(
            (
                (a1.at[inside], kept_hbm.at[0]),
                (feat, kept_hbm.at[1]),
                (g1.at[inside], kept_hbm.at[2]),
                (g0.at[inside], kept_hbm.at[3]),
                (a0.at[inside], kept_hbm.at[4]),
                (cots, kept_hbm.at[5]),
                (united_ref, united_hbm.at[0]),
            )
        )
    ]
    for ref in (a0, a1, g0, g1):
        clear_halo(ref, frames)
    if high > block:
        pad = jnp.zeros((frames, high - block, ch), BF16)
        a0[HALO : HALO + frames, block:, :] = pad
        cots[:, block:, :] = pad
    a0[HALO : HALO + frames, :block, :] = got_ref[:, 0]
    copies[4].start()
    for load in loads:
        load.wait()
    for layer, (source, target, slopes) in enumerate(((a0, a1, slope0), (a1, feat, slope1))):
        step_size = dil_ref[layer]
        weight = jnp.concatenate([tw_ref[layer, k] for k in range(TAPS)], axis=0)
        first = HALO if layer == 0 else 0
        for at in range(0, frames, step_frames):
            pre = mm(taps_of(source, at, step_frames, step_size, 1), weight)
            act, slope = silu_parts(pre)
            target[first + at : first + at + step_frames] = act.astype(BF16).reshape(
                step_frames, high, ch
            )
            slopes[at : at + step_frames] = slope.reshape(step_frames, high, ch)
        copies[layer].start()
    cots[:, :block, :] = got_ref[:, 1]
    copies[5].start()
    keys = jnp.concatenate([feat[seg * seg_frames + key_ref[seg]] for seg in range(segs)], axis=0)
    key_parts = mm(keys, uw_ref[1]).reshape(segs, high, ch)
    totals = jnp.concatenate(
        [
            jnp.sum(cots[seg * seg_frames : (seg + 1) * seg_frames].astype(F32), axis=0)
            for seg in range(segs)
        ],
        axis=0,
    )
    key_terms = mm_nt(jnp.concatenate(three_parts(totals), axis=0), uw_ref[1])
    key_terms = jnp.sum(key_terms.reshape(3, segs, high, ch), axis=0)
    for seg in range(segs):
        low, top = seg * seg_frames, (seg + 1) * seg_frames
        main = mm(feat[low:top].reshape(seg_frames * high, ch), uw_ref[0]).reshape(
            seg_frames, high, ch
        )
        united_ref[low:top] = (main + key_parts[seg][None]).astype(BF16)[:, :block]
        grad_feat = mm_nt(cots[low:top].reshape(seg_frames * high, ch), uw_ref[0]).reshape(
            seg_frames, high, ch
        )
        for n in range(seg_frames):
            grad = grad_feat[n] + jnp.where(key_ref[seg] == n, key_terms[seg], 0.0)
            g1[HALO + low + n] = (grad * slope1[low + n]).astype(BF16)
    copies[6].start()
    for layer, source in ((1, g1), (0, g0)):
        copies[3 - layer].start()
        step_size = dil_ref[layer]
        weight = jnp.concatenate(
            [tw_ref[layer, k].astype(F32).T.astype(BF16) for k in range(TAPS)], axis=0
        )
        for n, at in enumerate(range(0, frames, step_frames)):
            grad = mm(taps_of(source, at, step_frames, step_size, -1), weight).reshape(
                step_frames, high, ch
            )
            if layer == 1:
                g0[HALO + at : HALO + at + step_frames] = (
                    grad * slope0[at : at + step_frames]
                ).astype(BF16)
            else:
                grad_ref[at : at + step_frames] = grad.astype(BF16)[:, :block]
                stores[n].start()
    for copy in copies + stores:
        copy.wait()


def temporal_wgrad_kernel(
    step_frames, scale, here_ref, dil_ref, key_ref,
    kept_hbm, united_kept, united_hbm, *rest
):
    pieces, (a0, g0, a1, g1, feat, cots, united, total_ref, sems) = rest[:-9], rest[-9:]
    frames, high, ch = feat.shape
    segs = key_ref.shape[0]
    seg_frames = frames // segs
    rows = step_frames * high
    inside = pl.ds(HALO, frames)
    copies = [
        pltpu.make_async_copy(source, target, sems.at[n])
        for n, (source, target) in enumerate(
            (
                (kept_hbm.at[4], a0.at[inside]),
                (kept_hbm.at[3], g0),
                (kept_hbm.at[0], a1.at[inside]),
                (kept_hbm.at[2], g1),
                (kept_hbm.at[1], feat),
                (kept_hbm.at[5], cots),
                (united_kept.at[0], united),
            )
        )
    ]
    for copy in copies:
        copy.start()
    clear_halo(a0, frames)
    clear_halo(a1, frames)
    totals = []
    for layer, acts, grads in ((0, a0, g0), (1, a1, g1)):
        copies[2 * layer].wait()
        copies[2 * layer + 1].wait()
        total = jnp.zeros((TAPS * ch, ch), F32)
        for at in range(0, frames, step_frames):
            total = total + mm_tn(
                taps_of(acts, at, step_frames, dil_ref[layer], 1),
                grads[at : at + step_frames].reshape(rows, ch),
            )
        totals.append(total)
    for copy in copies[4:]:
        copy.wait()
    united_copy = pltpu.make_async_copy(united, united_hbm, sems.at[len(copies)])
    united_copy.start()
    total = jnp.zeros((ch, ch), F32)
    for at in range(0, frames, step_frames):
        total = total + mm_tn(
            feat[at : at + step_frames].reshape(rows, ch),
            cots[at : at + step_frames].reshape(rows, ch),
        )
    keyed = jnp.zeros((ch, ch), F32)
    for seg in range(segs):
        low, top = seg * seg_frames, (seg + 1) * seg_frames
        key = feat[low + key_ref[seg]]
        seg_cot = jnp.sum(cots[low:top].astype(F32), axis=0)
        keyed = keyed + sum(mm_tn(key, part) for part in three_parts(seg_cot))
    peers = len(pieces)
    split = LAYERS * TAPS * ch // peers
    total_ref[:, :split] = (jnp.concatenate(totals, axis=0) * scale).reshape(peers, split, ch)
    total_ref[:, split:] = (jnp.concatenate([total, keyed], axis=0) * scale).reshape(
        peers, 2 * ch // peers, ch
    )
    hand_out(here_ref, total_ref, pieces)
    united_copy.wait()


def sum_kernel(*refs):
    refs[-1][...] = sum(ref[...].astype(F32) for ref in refs[:-1]).astype(refs[-1].dtype)


def join_kernel(first_ref, *refs):
    out_ref = refs[-1]
    split = first_ref.shape[0]
    out_ref[:split] = first_ref[...]
    out_ref[split:] = sum(ref[...].astype(F32) for ref in refs[:-1]).astype(out_ref.dtype)


def deal_kernel(pieces_ref, united_hbm, *refs):
    outs_hbm, united_out, outs, sems = refs[:3], refs[3], refs[4:7], refs[7]
    copies = [pltpu.make_async_copy(united_hbm, united_out, sems.at[3])]
    copies[0].start()
    at = 0
    for n, out_ref in enumerate(outs):
        count = out_ref.shape[1]
        out_ref[...] = pieces_ref[:, at : at + count].astype(F32)
        copies.append(pltpu.make_async_copy(out_ref, outs_hbm[n], sems.at[n]))
        copies[-1].start()
        at += count
    for copy in copies:
        copy.wait()


def exchange(blocks):
    return lax.all_to_all(blocks, AXES, split_axis=0, concat_axis=0, tiled=True)


def flip(value, peer):
    size = lax.axis_size("grp")
    return lax.ppermute(value, "grp", [(i, i ^ peer) for i in range(size)])


def turn_by(value, turn):
    size = lax.axis_size("seg")
    return lax.ppermute(value, "seg", [(i, (i + turn) % size) for i in range(size)])


def sum_of(parts):
    shape = parts[0].shape
    return call(
        sum_kernel, [(shape, BF16, VMEM)], [], 0, len(parts) * 2 * shape[0] * shape[1],
        [(part, VMEM) for part in parts], SMALL_VMEM,
    )[0]


def reduce_in_grp(pieces):
    return sum_of([flip(piece, peer) if peer else piece for peer, piece in enumerate(pieces)])


def all_turns(value):
    return [turn_by(value, turn) if turn else value for turn in range(lax.axis_size("seg"))]


def local(
    frames_in, spatial_weight, temporal_weight, uniting_weight, key_index, dilation, cotangent
):
    held, rows, cols, ch = frames_in.shape
    assert held == 1
    pixels = rows * cols
    peers = lax.axis_size("grp")
    devices = lax.axis_size("seg") * peers
    frames = held * devices
    block = pixels // devices
    split = cols // block
    wide = round_up(cols + 1, 16)
    high = round_up(block, 16)
    rows_step = next(n for n in (4, 2, 1) if rows % n == 0)
    steps = rows // rows_step
    parts = next(n for n in (4, 2, 1) if rows % (n * rows_step) == 0)
    step_frames, narrow_step = (
        max(n for n in range(1, frames + 1) if frames % n == 0 and n * high <= most)
        for most in (512, 256)
    )
    scale = float((frames * pixels) ** -0.5)
    here = jnp.stack([lax.axis_index("seg"), lax.axis_index("grp")]).astype(jnp.int32)
    space_rows, time_rows, unite_rows = (n * ch // peers for n in (9, LAYERS * TAPS, 2))

    (send,) = call(
        functools.partial(spatial_fwd_kernel, rows_step),
        [((rows, 2, cols, ch), BF16, HBM)],
        [
            pltpu.VMEM((rows, cols, ch), BF16),
            pltpu.VMEM(spatial_weight.shape, BF16),
            pltpu.VMEM((rows + 2, wide, ch), BF16),
            pltpu.VMEM((rows, 2, cols, ch), BF16),
            pltpu.SemaphoreType.DMA((parts,)),
            pltpu.SemaphoreType.DMA((1,)),
            pltpu.SemaphoreType.DMA((1,)),
            pltpu.SemaphoreType.DMA((parts,)),
        ],
        2 * 9 * pixels * ch * ch,
        pixels * ch * 8,
        [(frames_in[0], HBM), (spatial_weight, HBM), (cotangent[0], HBM)],
    )
    send, frame = lax.optimization_barrier((send, frames_in[0]))
    send = send.reshape(rows, 2, split, block, ch).swapaxes(1, 2).reshape(devices, 2, block, ch)
    got = exchange(send)
    (space_slope,) = call(
        functools.partial(spatial_slope_kernel, rows_step),
        [((SPARE, rows, cols, ch), BF16, HBM)],
        [
            pltpu.VMEM((rows + 2, wide, ch), BF16),
            pltpu.VMEM((rows, cols, ch), BF16),
            pltpu.SemaphoreType.DMA((1,)),
        ],
        2 * 9 * pixels * ch * ch,
        pixels * ch * 4,
        [(frame, VMEM), (spatial_weight, VMEM)],
    )
    got, space_slope = lax.optimization_barrier((got, space_slope))

    padded = (frames + 2 * HALO, high, ch)
    whole = (frames, high, ch)
    grad_send, kept, united_kept = call(
        functools.partial(temporal_kernel, narrow_step),
        [
            ((frames, block, ch), BF16, HBM),
            ((SPARE,) + whole, BF16, HBM),
            ((SPARE, frames, block, ch), BF16, HBM),
        ],
        [
            pltpu.VMEM(padded, BF16),
            pltpu.VMEM(padded, BF16),
            pltpu.VMEM(whole, BF16),
            pltpu.VMEM(whole, BF16),
            pltpu.VMEM(padded, BF16),
            pltpu.VMEM(padded, BF16),
            pltpu.VMEM(whole, F32),
            pltpu.VMEM(whole, F32),
            pltpu.VMEM((frames, block, ch), BF16),
            pltpu.VMEM((frames, block, ch), BF16),
            pltpu.VMEM(temporal_weight.shape, BF16),
            pltpu.VMEM(uniting_weight.shape, BF16),
            pltpu.SemaphoreType.DMA((7,)),
            pltpu.SemaphoreType.DMA((2,)),
            pltpu.SemaphoreType.DMA((frames // narrow_step,)),
        ],
        2 * 22 * frames * block * ch * ch,
        frames * block * ch * 18,
        [
            (dilation, SMEM), (key_index, SMEM), (got, VMEM),
            (temporal_weight, HBM), (uniting_weight, HBM),
        ],
        MID_VMEM,
    )
    grad_time = exchange(grad_send).reshape(rows, cols, ch)
    united_send, *time_pieces = call(
        functools.partial(temporal_wgrad_kernel, step_frames, scale),
        [((frames, block, ch), BF16, HBM)]
        + [((time_rows + unite_rows, ch), BF16, VMEM)] * peers,
        [
            pltpu.VMEM(padded, BF16),
            pltpu.VMEM(whole, BF16),
            pltpu.VMEM(padded, BF16),
            pltpu.VMEM(whole, BF16),
            pltpu.VMEM(whole, BF16),
            pltpu.VMEM(whole, BF16),
            pltpu.VMEM((frames, block, ch), BF16),
            pltpu.VMEM((peers, time_rows + unite_rows, ch), F32),
            pltpu.SemaphoreType.DMA((8,)),
        ],
        2 * 12 * frames * block * ch * ch,
        frames * block * ch * 14,
        [
            (here, SMEM), (dilation, SMEM), (key_index, SMEM),
            (kept, HBM), (united_kept, HBM),
        ],
    )
    time_sum = reduce_in_grp(time_pieces)
    time_sum, grad_time = lax.optimization_barrier((time_sum, grad_time))
    united_send, grad_time = lax.optimization_barrier((united_send, grad_time))
    united = exchange(united_send)
    space_pieces = call(
        functools.partial(spatial_wgrad_kernel, rows_step, scale),
        [((space_rows, ch), BF16, VMEM)] * peers,
        [
            pltpu.VMEM((rows + 2, wide, ch), BF16),
            pltpu.VMEM((rows, cols, ch), BF16),
            pltpu.VMEM((3 * ch, min(3, steps) * rows_step * wide), BF16),
            pltpu.VMEM((peers, space_rows, ch), F32),
            pltpu.SemaphoreType.DMA((1,)),
        ],
        2 * 9 * pixels * ch * ch,
        pixels * ch * 8,
        [(here, SMEM), (grad_time, VMEM), (space_slope, HBM), (frame, VMEM)],
        MID_VMEM,
    )
    (back,) = call(
        functools.partial(spatial_back_kernel, rows_step),
        [((rows, cols, ch), BF16, VMEM)],
        [
            pltpu.VMEM((rows + 2, wide, ch), BF16),
            pltpu.VMEM((rows, cols, ch), BF16),
            pltpu.SemaphoreType.DMA((1,)),
        ],
        2 * 9 * pixels * ch * ch,
        pixels * ch * 6,
        [(spatial_weight, VMEM), (grad_time, VMEM), (space_slope, HBM)],
        MID_VMEM,
    )
    space_parts = [flip(part, peer) if peer else part for peer, part in enumerate(space_pieces)]
    (plane,) = call(
        join_kernel,
        [((time_rows + unite_rows + space_rows, ch), BF16, VMEM)],
        [],
        0,
        2 * (peers + 10) * space_rows * ch,
        [(time_sum, VMEM)] + [(part, VMEM) for part in space_parts],
        SMALL_VMEM,
    )
    turned = all_turns(plane)
    turned[0], back = lax.optimization_barrier((turned[0], back))
    piece = sum_of(turned)
    *grads, united = call(
        deal_kernel,
        [((peers, count, ch), F32, HBM) for count in (time_rows, unite_rows, space_rows)]
        + [((frames, block, ch), BF16, HBM)],
        [pltpu.VMEM((peers, count, ch), F32) for count in (time_rows, unite_rows, space_rows)]
        + [pltpu.SemaphoreType.DMA((4,))],
        0,
        6 * 21 * ch * ch,
        [(lax.all_gather(piece, "grp", axis=0), VMEM), (united, HBM)],
        SMALL_VMEM,
    )
    return (
        united.reshape(frames_in.shape),
        back[None],
        grads[2].reshape(9, ch, ch),
        grads[0].reshape(LAYERS, TAPS, ch, ch),
        grads[1].reshape(2, ch, ch),
    )


def solution(mesh):
    frame_spec = P(AXES, None, None, None)
    return jax.shard_map(
        local,
        mesh=mesh,
        in_specs=(frame_spec, P(), P(), P(), P(), P(), frame_spec),
        out_specs=(frame_spec, frame_spec, P(), P(), P()),
        check_vma=False,
    )
```

```python
import functools

import jax
import jax.numpy as jnp
from jax import lax
from jax.experimental import pallas as pl
from jax.experimental.pallas import tpu as pltpu
from jax.sharding import PartitionSpec as P

LAYERS = 2
TAPS = 5
DMAX = 8
HALO = 2 * DMAX
AXES = ("seg", "grp")
BF16 = jnp.bfloat16
F32 = jnp.float32
BIG_VMEM = 60 * 1024 * 1024
MID_VMEM = 40 * 1024 * 1024
SPARE = 28
SMALL_VMEM = 16 * 1024 * 1024


def round_up(value, step):
    return -(-value // step) * step


def silu_parts(value):
    sigma = 0.5 * jnp.tanh(0.5 * value) + 0.5
    act = value * sigma
    return act, sigma + act * (1.0 - sigma)


def mm(left, right):
    return jnp.dot(left, right, preferred_element_type=F32)


def mm_nt(left, right):
    return lax.dot_general(left, right, (((1,), (1,)), ((), ())), preferred_element_type=F32)


def mm_tn(left, right):
    return lax.dot_general(left, right, (((0,), (0,)), ((), ())), preferred_element_type=F32)


def three_parts(value):
    high = value.astype(BF16)
    rest = value - high.astype(F32)
    middle = rest.astype(BF16)
    return high, middle, (rest - middle.astype(F32)).astype(BF16)


VMEM = pl.BlockSpec(memory_space=pltpu.VMEM)
SMEM = pl.BlockSpec(memory_space=pltpu.SMEM)
HBM = pl.BlockSpec(memory_space=pltpu.HBM)


def call(kernel, outs, scratch, flops, moved, args, vmem=BIG_VMEM):
    return pl.pallas_call(
        kernel,
        out_shape=[jax.ShapeDtypeStruct(shape, kind) for shape, kind, _ in outs],
        in_specs=[spec for _, spec in args],
        out_specs=[spec for _, _, spec in outs],
        scratch_shapes=scratch,
        compiler_params=pltpu.CompilerParams(vmem_limit_bytes=vmem),
        cost_estimate=pl.CostEstimate(flops=flops, bytes_accessed=moved, transcendentals=0),
    )(*[value for value, _ in args])


def roll_rows(value, shift):
    return pltpu.roll(value, shift % value.shape[0], 0)


def spatial_pre(xs, weight, at, rows_step):
    wide, ch = xs.shape[1:]
    flat = rows_step * wide
    left = jnp.concatenate(
        [xs[at + a : at + a + rows_step].reshape(flat, ch) for a in range(3)], axis=1
    )
    y = mm(left, weight)
    return y[:, ch : 2 * ch] + roll_rows(y[:, :ch], 1) + roll_rows(y[:, 2 * ch :], -1)


def forward_weight(w_ref):
    return jnp.concatenate(
        [jnp.concatenate([w_ref[3 * a + b] for b in range(3)], axis=1) for a in range(3)], axis=0
    )


def clear_ends(ref):
    last = ref.shape[0] - 1
    ref[0] = jnp.zeros(ref.shape[1:], ref.dtype)
    ref[last] = jnp.zeros(ref.shape[1:], ref.dtype)


def put_rows(ref, at, value):
    count, cols, ch = value.shape
    ref[1 + at : 1 + at + count, cols:, :] = jnp.zeros((count, ref.shape[1] - cols, ch), ref.dtype)
    ref[1 + at : 1 + at + count, :cols, :] = value


def spatial_fwd_kernel(
    rows_step, x_hbm, w_hbm, cot_hbm, send_hbm,
    x_in, w_ref, xs, sends, in_sems, w_sem, cot_sem, send_sems,
):
    rows, cols, ch = x_in.shape
    wide = xs.shape[1]
    parts = in_sems.shape[0]
    many = rows // parts

    def part(n):
        return pl.ds(n * many, many)

    loads = [
        pltpu.make_async_copy(x_hbm.at[part(n)], x_in.at[part(n)], in_sems.at[n]) for n in range(parts)
    ]
    stores = [
        pltpu.make_async_copy(sends.at[part(n)], send_hbm.at[part(n)], send_sems.at[n])
        for n in range(parts)
    ]
    w_load = pltpu.make_async_copy(w_hbm, w_ref, w_sem.at[0])
    cot_load = pltpu.make_async_copy(cot_hbm, sends.at[:, 1], cot_sem.at[0])
    for load in [loads[0], w_load] + loads[1:2]:
        load.start()
    clear_ends(xs)

    def bring(n):
        loads[n].wait()
        put_rows(xs, n * many, x_in[n * many : (n + 1) * many])

    bring(0)
    for load in loads[2:] + [cot_load]:
        load.start()
    w_load.wait()
    weight = forward_weight(w_ref)
    for n in range(parts):
        if n + 1 < parts:
            bring(n + 1)
        for at in range(n * many, (n + 1) * many, rows_step):
            act, _ = silu_parts(spatial_pre(xs, weight, at, rows_step))
            sends[at : at + rows_step, 0] = act.astype(BF16).reshape(rows_step, wide, ch)[:, :cols]
        if n == 0:
            cot_load.wait()
        stores[n].start()
    for store in stores:
        store.wait()


def spatial_slope_kernel(rows_step, x_ref, w_ref, slope_hbm, xs, slopes, sem):
    rows, cols, ch = x_ref.shape
    wide = xs.shape[1]
    clear_ends(xs)
    put_rows(xs, 0, x_ref[...])
    weight = forward_weight(w_ref)
    for at in range(0, rows, rows_step):
        _, slope = silu_parts(spatial_pre(xs, weight, at, rows_step))
        slopes[at : at + rows_step] = slope.astype(BF16).reshape(rows_step, wide, ch)[:, :cols]
    store = pltpu.make_async_copy(slopes, slope_hbm.at[0], sem.at[0])
    store.start()
    store.wait()


def hand_out(here_ref, total_ref, pieces):
    for peer, piece in enumerate(pieces):
        piece[...] = total_ref[jnp.bitwise_xor(here_ref[1], peer)].astype(piece.dtype)


def taps_up(gs, at, rows_step):
    wide, ch = gs.shape[1:]
    return jnp.concatenate(
        [gs[at + 2 - a : at + 2 - a + rows_step].reshape(rows_step * wide, ch) for a in range(3)],
        axis=1,
    )


def fill_grads(rows_step, gs, got_ref, slope_ref):
    clear_ends(gs)
    for at in range(0, got_ref.shape[0], rows_step):
        grads = got_ref[at : at + rows_step].astype(F32)
        slopes = slope_ref[at : at + rows_step].astype(F32)
        put_rows(gs, at, (grads * slopes).astype(BF16))


def spatial_wgrad_kernel(rows_step, scale, here_ref, got_ref, slope_hbm, x_ref, *rest):
    pieces, (gs, slopes, cat_ref, total_ref, sem) = rest[:-5], rest[-5:]
    rows, cols, ch = got_ref.shape
    wide = gs.shape[1]
    flat = rows_step * wide
    load = pltpu.make_async_copy(slope_hbm.at[0], slopes, sem.at[0])
    load.start()
    pad = jnp.zeros((rows_step, wide - cols, ch), F32)

    def columns(at):
        x = jnp.concatenate([x_ref[at : at + rows_step].astype(F32), pad], axis=1).reshape(flat, ch)
        x_cat = jnp.concatenate([roll_rows(x, 1), x, roll_rows(x, -1)], axis=1)
        return x_cat.T.astype(BF16)

    early = cat_ref.shape[1] // flat
    for n in range(early):
        cat_ref[:, n * flat : (n + 1) * flat] = columns(n * rows_step)
    load.wait()
    fill_grads(rows_step, gs, got_ref, slopes)
    total = jnp.zeros((3 * ch, 3 * ch), F32)
    for n, at in enumerate(range(0, rows, rows_step)):
        cat = cat_ref[:, n * flat : (n + 1) * flat] if n < early else columns(at)
        total = total + mm(cat, taps_up(gs, at, rows_step))
    total_ref[...] = (
        jnp.concatenate(
            [
                total[b * ch : (b + 1) * ch, a * ch : (a + 1) * ch]
                for a in range(3)
                for b in range(3)
            ],
            axis=0,
        )
        * scale
    ).reshape(total_ref.shape)
    hand_out(here_ref, total_ref, pieces)


def spatial_back_kernel(rows_step, w_ref, got_ref, slope_hbm, back_ref, gs, slopes, sem):
    rows, cols, ch = back_ref.shape
    wide = gs.shape[1]
    load = pltpu.make_async_copy(slope_hbm.at[0], slopes, sem.at[0])
    load.start()
    weight = jnp.concatenate(
        [
            jnp.concatenate([w_ref[3 * a + b].astype(F32).T.astype(BF16) for b in range(3)], axis=1)
            for a in range(3)
        ],
        axis=0,
    )
    load.wait()
    fill_grads(rows_step, gs, got_ref, slopes)
    for at in range(0, rows, rows_step):
        y = mm(taps_up(gs, at, rows_step), weight)
        back = y[:, ch : 2 * ch] + roll_rows(y[:, :ch], -1) + roll_rows(y[:, 2 * ch :], 1)
        back_ref[at : at + rows_step] = back.astype(BF16).reshape(rows_step, wide, ch)[:, :cols]


def clear_halo(pad_ref, frames):
    zeros = jnp.zeros((HALO,) + pad_ref.shape[1:], pad_ref.dtype)
    pad_ref[:HALO] = zeros
    pad_ref[HALO + frames :] = zeros


def taps_of(pad_ref, at, count, step_size, sign):
    high, ch = pad_ref.shape[1:]
    pieces = [
        pad_ref[pl.ds(HALO + at + sign * (k - 2) * step_size, count)].reshape(count * high, ch)
        for k in range(TAPS)
    ]
    return jnp.concatenate(pieces, axis=1)


def temporal_kernel(
    step_frames, dil_ref, key_ref, got_ref, tw_hbm, uw_hbm,
    grad_hbm, kept_hbm, united_hbm,
    a0, a1, feat, cots, g0, g1, slope0, slope1, united_ref, grad_ref, tw_ref, uw_ref,
    sems, in_sems, out_sems,
):
    frames, _, block, ch = got_ref.shape
    high = feat.shape[1]
    loads = [
        pltpu.make_async_copy(source, ref, in_sems.at[n])
        for n, (source, ref) in enumerate(((tw_hbm, tw_ref), (uw_hbm, uw_ref)))
    ]
    for load in loads:
        load.start()
    stores = [
        pltpu.make_async_copy(
            grad_ref.at[pl.ds(at, step_frames)], grad_hbm.at[pl.ds(at, step_frames)], out_sems.at[n]
        )
        for n, at in enumerate(range(0, frames, step_frames))
    ]
    segs = key_ref.shape[0]
    seg_frames = frames // segs
    inside = pl.ds(HALO, frames)
    copies = [
        pltpu.make_async_copy(source, target, sems.at[n])
        for n, (source, target) in enumerate(
            (
                (a1.at[inside], kept_hbm.at[0]),
                (feat, kept_hbm.at[1]),
                (g1.at[inside], kept_hbm.at[2]),
                (g0.at[inside], kept_hbm.at[3]),
                (a0.at[inside], kept_hbm.at[4]),
                (cots, kept_hbm.at[5]),
                (united_ref, united_hbm.at[0]),
            )
        )
    ]
    for ref in (a0, a1, g0, g1):
        clear_halo(ref, frames)
    if high > block:
        pad = jnp.zeros((frames, high - block, ch), BF16)
        a0[HALO : HALO + frames, block:, :] = pad
        cots[:, block:, :] = pad
    a0[HALO : HALO + frames, :block, :] = got_ref[:, 0]
    copies[4].start()
    for load in loads:
        load.wait()
    for layer, (source, target, slopes) in enumerate(((a0, a1, slope0), (a1, feat, slope1))):
        step_size = dil_ref[layer]
        weight = jnp.concatenate([tw_ref[layer, k] for k in range(TAPS)], axis=0)
        first = HALO if layer == 0 else 0
        for at in range(0, frames, step_frames):
            pre = mm(taps_of(source, at, step_frames, step_size, 1), weight)
            act, slope = silu_parts(pre)
            target[first + at : first + at + step_frames] = act.astype(BF16).reshape(
                step_frames, high, ch
            )
            slopes[at : at + step_frames] = slope.reshape(step_frames, high, ch)
        copies[layer].start()
    cots[:, :block, :] = got_ref[:, 1]
    copies[5].start()
    keys = jnp.concatenate([feat[seg * seg_frames + key_ref[seg]] for seg in range(segs)], axis=0)
    key_parts = mm(keys, uw_ref[1]).reshape(segs, high, ch)
    totals = jnp.concatenate(
        [
            jnp.sum(cots[seg * seg_frames : (seg + 1) * seg_frames].astype(F32), axis=0)
            for seg in range(segs)
        ],
        axis=0,
    )
    key_terms = mm_nt(jnp.concatenate(three_parts(totals), axis=0), uw_ref[1])
    key_terms = jnp.sum(key_terms.reshape(3, segs, high, ch), axis=0)
    for seg in range(segs):
        low, top = seg * seg_frames, (seg + 1) * seg_frames
        main = mm(feat[low:top].reshape(seg_frames * high, ch), uw_ref[0]).reshape(
            seg_frames, high, ch
        )
        united_ref[low:top] = (main + key_parts[seg][None]).astype(BF16)[:, :block]
        grad_feat = mm_nt(cots[low:top].reshape(seg_frames * high, ch), uw_ref[0]).reshape(
            seg_frames, high, ch
        )
        for n in range(seg_frames):
            grad = grad_feat[n] + jnp.where(key_ref[seg] == n, key_terms[seg], 0.0)
            g1[HALO + low + n] = (grad * slope1[low + n]).astype(BF16)
    copies[6].start()
    for layer, source in ((1, g1), (0, g0)):
        copies[3 - layer].start()
        step_size = dil_ref[layer]
        weight = jnp.concatenate(
            [tw_ref[layer, k].astype(F32).T.astype(BF16) for k in range(TAPS)], axis=0
        )
        for n, at in enumerate(range(0, frames, step_frames)):
            grad = mm(taps_of(source, at, step_frames, step_size, -1), weight).reshape(
                step_frames, high, ch
            )
            if layer == 1:
                g0[HALO + at : HALO + at + step_frames] = (
                    grad * slope0[at : at + step_frames]
                ).astype(BF16)
            else:
                grad_ref[at : at + step_frames] = grad.astype(BF16)[:, :block]
                stores[n].start()
    for copy in copies + stores:
        copy.wait()


def temporal_wgrad_kernel(
    step_frames, scale, here_ref, dil_ref, key_ref,
    kept_hbm, united_kept, united_hbm, *rest
):
    pieces, (a0, g0, a1, g1, feat, cots, united, total_ref, sems) = rest[:-9], rest[-9:]
    frames, high, ch = feat.shape
    segs = key_ref.shape[0]
    seg_frames = frames // segs
    rows = step_frames * high
    inside = pl.ds(HALO, frames)
    copies = [
        pltpu.make_async_copy(source, target, sems.at[n])
        for n, (source, target) in enumerate(
            (
                (kept_hbm.at[4], a0.at[inside]),
                (kept_hbm.at[3], g0),
                (kept_hbm.at[0], a1.at[inside]),
                (kept_hbm.at[2], g1),
                (kept_hbm.at[1], feat),
                (kept_hbm.at[5], cots),
                (united_kept.at[0], united),
            )
        )
    ]
    for copy in copies[:2]:
        copy.start()
    clear_halo(a0, frames)
    clear_halo(a1, frames)
    totals = []
    for layer, acts, grads in ((0, a0, g0), (1, a1, g1)):
        copies[2 * layer].wait()
        copies[2 * layer + 1].wait()
        for copy in copies[4:] if layer else copies[2:4]:
            copy.start()
        total = jnp.zeros((TAPS * ch, ch), F32)
        for at in range(0, frames, step_frames):
            total = total + mm_tn(
                taps_of(acts, at, step_frames, dil_ref[layer], 1),
                grads[at : at + step_frames].reshape(rows, ch),
            )
        totals.append(total)
    for copy in copies[4:]:
        copy.wait()
    united_copy = pltpu.make_async_copy(united, united_hbm, sems.at[len(copies)])
    united_copy.start()
    total = jnp.zeros((ch, ch), F32)
    for at in range(0, frames, step_frames):
        total = total + mm_tn(
            feat[at : at + step_frames].reshape(rows, ch),
            cots[at : at + step_frames].reshape(rows, ch),
        )
    keyed = jnp.zeros((ch, ch), F32)
    for seg in range(segs):
        low, top = seg * seg_frames, (seg + 1) * seg_frames
        key = feat[low + key_ref[seg]]
        seg_cot = jnp.sum(cots[low:top].astype(F32), axis=0)
        keyed = keyed + sum(mm_tn(key, part) for part in three_parts(seg_cot))
    peers = len(pieces)
    split = LAYERS * TAPS * ch // peers
    total_ref[:, :split] = (jnp.concatenate(totals, axis=0) * scale).reshape(peers, split, ch)
    total_ref[:, split:] = (jnp.concatenate([total, keyed], axis=0) * scale).reshape(
        peers, 2 * ch // peers, ch
    )
    hand_out(here_ref, total_ref, pieces)
    united_copy.wait()


def sum_kernel(*refs):
    refs[-1][...] = sum(ref[...].astype(F32) for ref in refs[:-1]).astype(refs[-1].dtype)


def join_kernel(first_ref, *refs):
    out_ref = refs[-1]
    split = first_ref.shape[0]
    out_ref[:split] = first_ref[...]
    out_ref[split:] = sum(ref[...].astype(F32) for ref in refs[:-1]).astype(out_ref.dtype)


def deal_kernel(pieces_ref, united_hbm, *refs):
    outs_hbm, united_out, outs, sems = refs[:3], refs[3], refs[4:7], refs[7]
    copies = [pltpu.make_async_copy(united_hbm, united_out, sems.at[3])]
    copies[0].start()
    at = 0
    for n, out_ref in enumerate(outs):
        count = out_ref.shape[1]
        out_ref[...] = pieces_ref[:, at : at + count].astype(F32)
        copies.append(pltpu.make_async_copy(out_ref, outs_hbm[n], sems.at[n]))
        copies[-1].start()
        at += count
    for copy in copies:
        copy.wait()


def exchange(blocks):
    return lax.all_to_all(blocks, AXES, split_axis=0, concat_axis=0, tiled=True)


def flip(value, peer):
    size = lax.axis_size("grp")
    return lax.ppermute(value, "grp", [(i, i ^ peer) for i in range(size)])


def turn_by(value, turn):
    size = lax.axis_size("seg")
    return lax.ppermute(value, "seg", [(i, (i + turn) % size) for i in range(size)])


def sum_of(parts):
    shape = parts[0].shape
    return call(
        sum_kernel, [(shape, BF16, VMEM)], [], 0, len(parts) * 2 * shape[0] * shape[1],
        [(part, VMEM) for part in parts], SMALL_VMEM,
    )[0]


def reduce_in_grp(pieces):
    return sum_of([flip(piece, peer) if peer else piece for peer, piece in enumerate(pieces)])


def all_turns(value):
    return [turn_by(value, turn) if turn else value for turn in range(lax.axis_size("seg"))]


def local(
    frames_in, spatial_weight, temporal_weight, uniting_weight, key_index, dilation, cotangent
):
    held, rows, cols, ch = frames_in.shape
    assert held == 1
    pixels = rows * cols
    peers = lax.axis_size("grp")
    devices = lax.axis_size("seg") * peers
    frames = held * devices
    block = pixels // devices
    split = cols // block
    wide = round_up(cols + 1, 16)
    high = round_up(block, 16)
    rows_step = next(n for n in (4, 2, 1) if rows % n == 0)
    steps = rows // rows_step
    parts = next(n for n in (4, 2, 1) if rows % (n * rows_step) == 0)
    step_frames, narrow_step = (
        max(n for n in range(1, frames + 1) if frames % n == 0 and n * high <= most)
        for most in (512, 256)
    )
    scale = float((frames * pixels) ** -0.5)
    here = jnp.stack([lax.axis_index("seg"), lax.axis_index("grp")]).astype(jnp.int32)
    space_rows, time_rows, unite_rows = (n * ch // peers for n in (9, LAYERS * TAPS, 2))

    (send,) = call(
        functools.partial(spatial_fwd_kernel, rows_step),
        [((rows, 2, cols, ch), BF16, HBM)],
        [
            pltpu.VMEM((rows, cols, ch), BF16),
            pltpu.VMEM(spatial_weight.shape, BF16),
            pltpu.VMEM((rows + 2, wide, ch), BF16),
            pltpu.VMEM((rows, 2, cols, ch), BF16),
            pltpu.SemaphoreType.DMA((parts,)),
            pltpu.SemaphoreType.DMA((1,)),
            pltpu.SemaphoreType.DMA((1,)),
            pltpu.SemaphoreType.DMA((parts,)),
        ],
        2 * 9 * pixels * ch * ch,
        pixels * ch * 8,
        [(frames_in[0], HBM), (spatial_weight, HBM), (cotangent[0], HBM)],
    )
    send, frame = lax.optimization_barrier((send, frames_in[0]))
    send = send.reshape(rows, 2, split, block, ch).swapaxes(1, 2).reshape(devices, 2, block, ch)
    got = exchange(send)
    (space_slope,) = call(
        functools.partial(spatial_slope_kernel, rows_step),
        [((SPARE, rows, cols, ch), BF16, HBM)],
        [
            pltpu.VMEM((rows + 2, wide, ch), BF16),
            pltpu.VMEM((rows, cols, ch), BF16),
            pltpu.SemaphoreType.DMA((1,)),
        ],
        2 * 9 * pixels * ch * ch,
        pixels * ch * 4,
        [(frame, VMEM), (spatial_weight, VMEM)],
    )
    got, space_slope = lax.optimization_barrier((got, space_slope))

    padded = (frames + 2 * HALO, high, ch)
    whole = (frames, high, ch)
    grad_send, kept, united_kept = call(
        functools.partial(temporal_kernel, narrow_step),
        [
            ((frames, block, ch), BF16, HBM),
            ((SPARE,) + whole, BF16, HBM),
            ((SPARE, frames, block, ch), BF16, HBM),
        ],
        [
            pltpu.VMEM(padded, BF16),
            pltpu.VMEM(padded, BF16),
            pltpu.VMEM(whole, BF16),
            pltpu.VMEM(whole, BF16),
            pltpu.VMEM(padded, BF16),
            pltpu.VMEM(padded, BF16),
            pltpu.VMEM(whole, F32),
            pltpu.VMEM(whole, F32),
            pltpu.VMEM((frames, block, ch), BF16),
            pltpu.VMEM((frames, block, ch), BF16),
            pltpu.VMEM(temporal_weight.shape, BF16),
            pltpu.VMEM(uniting_weight.shape, BF16),
            pltpu.SemaphoreType.DMA((7,)),
            pltpu.SemaphoreType.DMA((2,)),
            pltpu.SemaphoreType.DMA((frames // narrow_step,)),
        ],
        2 * 22 * frames * block * ch * ch,
        frames * block * ch * 18,
        [
            (dilation, SMEM), (key_index, SMEM), (got, VMEM),
            (temporal_weight, HBM), (uniting_weight, HBM),
        ],
        MID_VMEM,
    )
    grad_time = exchange(grad_send).reshape(rows, cols, ch)
    united_send, *time_pieces = call(
        functools.partial(temporal_wgrad_kernel, step_frames, scale),
        [((frames, block, ch), BF16, HBM)]
        + [((time_rows + unite_rows, ch), BF16, VMEM)] * peers,
        [
            pltpu.VMEM(padded, BF16),
            pltpu.VMEM(whole, BF16),
            pltpu.VMEM(padded, BF16),
            pltpu.VMEM(whole, BF16),
            pltpu.VMEM(whole, BF16),
            pltpu.VMEM(whole, BF16),
            pltpu.VMEM((frames, block, ch), BF16),
            pltpu.VMEM((peers, time_rows + unite_rows, ch), F32),
            pltpu.SemaphoreType.DMA((8,)),
        ],
        2 * 12 * frames * block * ch * ch,
        frames * block * ch * 14,
        [
            (here, SMEM), (dilation, SMEM), (key_index, SMEM),
            (kept, HBM), (united_kept, HBM),
        ],
    )
    time_sum = reduce_in_grp(time_pieces)
    time_sum, grad_time = lax.optimization_barrier((time_sum, grad_time))
    united_send, grad_time = lax.optimization_barrier((united_send, grad_time))
    united = exchange(united_send)
    space_pieces = call(
        functools.partial(spatial_wgrad_kernel, rows_step, scale),
        [((space_rows, ch), BF16, VMEM)] * peers,
        [
            pltpu.VMEM((rows + 2, wide, ch), BF16),
            pltpu.VMEM((rows, cols, ch), BF16),
            pltpu.VMEM((3 * ch, min(3, steps) * rows_step * wide), BF16),
            pltpu.VMEM((peers, space_rows, ch), F32),
            pltpu.SemaphoreType.DMA((1,)),
        ],
        2 * 9 * pixels * ch * ch,
        pixels * ch * 8,
        [(here, SMEM), (grad_time, VMEM), (space_slope, HBM), (frame, VMEM)],
        MID_VMEM,
    )
    (back,) = call(
        functools.partial(spatial_back_kernel, rows_step),
        [((rows, cols, ch), BF16, VMEM)],
        [
            pltpu.VMEM((rows + 2, wide, ch), BF16),
            pltpu.VMEM((rows, cols, ch), BF16),
            pltpu.SemaphoreType.DMA((1,)),
        ],
        2 * 9 * pixels * ch * ch,
        pixels * ch * 6,
        [(spatial_weight, VMEM), (grad_time, VMEM), (space_slope, HBM)],
        MID_VMEM,
    )
    space_parts = [flip(part, peer) if peer else part for peer, part in enumerate(space_pieces)]
    (plane,) = call(
        join_kernel,
        [((time_rows + unite_rows + space_rows, ch), BF16, VMEM)],
        [],
        0,
        2 * (peers + 10) * space_rows * ch,
        [(time_sum, VMEM)] + [(part, VMEM) for part in space_parts],
        SMALL_VMEM,
    )
    turned = all_turns(plane)
    turned[0], back = lax.optimization_barrier((turned[0], back))
    piece = sum_of(turned)
    *grads, united = call(
        deal_kernel,
        [((peers, count, ch), F32, HBM) for count in (time_rows, unite_rows, space_rows)]
        + [((frames, block, ch), BF16, HBM)],
        [pltpu.VMEM((peers, count, ch), F32) for count in (time_rows, unite_rows, space_rows)]
        + [pltpu.SemaphoreType.DMA((4,))],
        0,
        6 * 21 * ch * ch,
        [(lax.all_gather(piece, "grp", axis=0), VMEM), (united, HBM)],
        SMALL_VMEM,
    )
    return (
        united.reshape(frames_in.shape),
        back[None],
        grads[2].reshape(9, ch, ch),
        grads[0].reshape(LAYERS, TAPS, ch, ch),
        grads[1].reshape(2, ch, ch),
    )


def solution(mesh):
    frame_spec = P(AXES, None, None, None)
    return jax.shard_map(
        local,
        mesh=mesh,
        in_specs=(frame_spec, P(), P(), P(), P(), P(), frame_spec),
        out_specs=(frame_spec, frame_spec, P(), P(), P()),
        check_vma=False,
    )
```

```python
import functools

import jax
import jax.numpy as jnp
from jax import lax
from jax.experimental import pallas as pl
from jax.experimental.pallas import tpu as pltpu
from jax.sharding import PartitionSpec as P

LAYERS = 2
TAPS = 5
DMAX = 8
HALO = 2 * DMAX
AXES = ("seg", "grp")
BF16 = jnp.bfloat16
F32 = jnp.float32
BIG_VMEM = 60 * 1024 * 1024
MID_VMEM = 40 * 1024 * 1024
SPARE = 28
SMALL_VMEM = 16 * 1024 * 1024


def round_up(value, step):
    return -(-value // step) * step


def silu_parts(value):
    sigma = 0.5 * jnp.tanh(0.5 * value) + 0.5
    act = value * sigma
    return act, sigma + act * (1.0 - sigma)


def mm(left, right):
    return jnp.dot(left, right, preferred_element_type=F32)


def mm_nt(left, right):
    return lax.dot_general(left, right, (((1,), (1,)), ((), ())), preferred_element_type=F32)


def mm_tn(left, right):
    return lax.dot_general(left, right, (((0,), (0,)), ((), ())), preferred_element_type=F32)


def three_parts(value):
    high = value.astype(BF16)
    rest = value - high.astype(F32)
    middle = rest.astype(BF16)
    return high, middle, (rest - middle.astype(F32)).astype(BF16)


VMEM = pl.BlockSpec(memory_space=pltpu.VMEM)
SMEM = pl.BlockSpec(memory_space=pltpu.SMEM)
HBM = pl.BlockSpec(memory_space=pltpu.HBM)


def call(kernel, outs, scratch, flops, moved, args, vmem=BIG_VMEM):
    return pl.pallas_call(
        kernel,
        out_shape=[jax.ShapeDtypeStruct(shape, kind) for shape, kind, _ in outs],
        in_specs=[spec for _, spec in args],
        out_specs=[spec for _, _, spec in outs],
        scratch_shapes=scratch,
        compiler_params=pltpu.CompilerParams(vmem_limit_bytes=vmem),
        cost_estimate=pl.CostEstimate(flops=flops, bytes_accessed=moved, transcendentals=0),
    )(*[value for value, _ in args])


def roll_rows(value, shift):
    return pltpu.roll(value, shift % value.shape[0], 0)


def spatial_pre(xs, weight, at, rows_step):
    wide, ch = xs.shape[1:]
    flat = rows_step * wide
    left = jnp.concatenate(
        [xs[at + a : at + a + rows_step].reshape(flat, ch) for a in range(3)], axis=1
    )
    y = mm(left, weight)
    return y[:, ch : 2 * ch] + roll_rows(y[:, :ch], 1) + roll_rows(y[:, 2 * ch :], -1)


def forward_weight(w_ref):
    return jnp.concatenate(
        [jnp.concatenate([w_ref[3 * a + b] for b in range(3)], axis=1) for a in range(3)], axis=0
    )


def clear_ends(ref):
    last = ref.shape[0] - 1
    ref[0] = jnp.zeros(ref.shape[1:], ref.dtype)
    ref[last] = jnp.zeros(ref.shape[1:], ref.dtype)


def put_rows(ref, at, value):
    count, cols, ch = value.shape
    ref[1 + at : 1 + at + count, cols:, :] = jnp.zeros((count, ref.shape[1] - cols, ch), ref.dtype)
    ref[1 + at : 1 + at + count, :cols, :] = value


def spatial_fwd_kernel(
    rows_step, x_hbm, w_hbm, cot_hbm, send_hbm,
    x_in, w_ref, xs, sends, in_sems, w_sem, cot_sem, send_sems,
):
    rows, cols, ch = x_in.shape
    wide = xs.shape[1]
    parts = in_sems.shape[0]
    many = rows // parts

    def part(n):
        return pl.ds(n * many, many)

    loads = [
        pltpu.make_async_copy(x_hbm.at[part(n)], x_in.at[part(n)], in_sems.at[n]) for n in range(parts)
    ]
    stores = [
        pltpu.make_async_copy(sends.at[part(n)], send_hbm.at[part(n)], send_sems.at[n])
        for n in range(parts)
    ]
    w_load = pltpu.make_async_copy(w_hbm, w_ref, w_sem.at[0])
    cot_load = pltpu.make_async_copy(cot_hbm, sends.at[:, 1], cot_sem.at[0])
    for load in [loads[0], w_load] + loads[1:] + [cot_load]:
        load.start()
    clear_ends(xs)

    def bring(n):
        loads[n].wait()
        put_rows(xs, n * many, x_in[n * many : (n + 1) * many])

    bring(0)
    w_load.wait()
    weight = forward_weight(w_ref)
    for n in range(parts):
        if n + 1 < parts:
            bring(n + 1)
        for at in range(n * many, (n + 1) * many, rows_step):
            act, _ = silu_parts(spatial_pre(xs, weight, at, rows_step))
            sends[at : at + rows_step, 0] = act.astype(BF16).reshape(rows_step, wide, ch)[:, :cols]
        if n == 0:
            cot_load.wait()
        stores[n].start()
    for store in stores:
        store.wait()


def spatial_slope_kernel(rows_step, x_ref, w_ref, slope_hbm, xs, slopes, sem):
    rows, cols, ch = x_ref.shape
    wide = xs.shape[1]
    clear_ends(xs)
    put_rows(xs, 0, x_ref[...])
    weight = forward_weight(w_ref)
    for at in range(0, rows, rows_step):
        _, slope = silu_parts(spatial_pre(xs, weight, at, rows_step))
        slopes[at : at + rows_step] = slope.astype(BF16).reshape(rows_step, wide, ch)[:, :cols]
    store = pltpu.make_async_copy(slopes, slope_hbm.at[0], sem.at[0])
    store.start()
    store.wait()


def hand_out(here_ref, total_ref, pieces):
    for peer, piece in enumerate(pieces):
        piece[...] = total_ref[jnp.bitwise_xor(here_ref[1], peer)].astype(piece.dtype)


def taps_up(gs, at, rows_step):
    wide, ch = gs.shape[1:]
    return jnp.concatenate(
        [gs[at + 2 - a : at + 2 - a + rows_step].reshape(rows_step * wide, ch) for a in range(3)],
        axis=1,
    )


def fill_grads(rows_step, gs, got_ref, slope_ref):
    clear_ends(gs)
    for at in range(0, got_ref.shape[0], rows_step):
        grads = got_ref[at : at + rows_step].astype(F32)
        slopes = slope_ref[at : at + rows_step].astype(F32)
        put_rows(gs, at, (grads * slopes).astype(BF16))


def spatial_wgrad_kernel(rows_step, scale, here_ref, got_ref, slope_hbm, x_ref, *rest):
    pieces, (gs, slopes, cat_ref, total_ref, sem) = rest[:-5], rest[-5:]
    rows, cols, ch = got_ref.shape
    wide = gs.shape[1]
    flat = rows_step * wide
    load = pltpu.make_async_copy(slope_hbm.at[0], slopes, sem.at[0])
    load.start()
    pad = jnp.zeros((rows_step, wide - cols, ch), F32)

    def columns(at):
        x = jnp.concatenate([x_ref[at : at + rows_step].astype(F32), pad], axis=1).reshape(flat, ch)
        x_cat = jnp.concatenate([roll_rows(x, 1), x, roll_rows(x, -1)], axis=1)
        return x_cat.T.astype(BF16)

    early = cat_ref.shape[1] // flat
    for n in range(early):
        cat_ref[:, n * flat : (n + 1) * flat] = columns(n * rows_step)
    load.wait()
    fill_grads(rows_step, gs, got_ref, slopes)
    total = jnp.zeros((3 * ch, 3 * ch), F32)
    for n, at in enumerate(range(0, rows, rows_step)):
        cat = cat_ref[:, n * flat : (n + 1) * flat] if n < early else columns(at)
        total = total + mm(cat, taps_up(gs, at, rows_step))
    total_ref[...] = (
        jnp.concatenate(
            [
                total[b * ch : (b + 1) * ch, a * ch : (a + 1) * ch]
                for a in range(3)
                for b in range(3)
            ],
            axis=0,
        )
        * scale
    ).reshape(total_ref.shape)
    hand_out(here_ref, total_ref, pieces)


def spatial_back_kernel(rows_step, w_ref, got_ref, slope_hbm, back_ref, gs, slopes, sem):
    rows, cols, ch = back_ref.shape
    wide = gs.shape[1]
    load = pltpu.make_async_copy(slope_hbm.at[0], slopes, sem.at[0])
    load.start()
    weight = jnp.concatenate(
        [
            jnp.concatenate([w_ref[3 * a + b].astype(F32).T.astype(BF16) for b in range(3)], axis=1)
            for a in range(3)
        ],
        axis=0,
    )
    load.wait()
    fill_grads(rows_step, gs, got_ref, slopes)
    for at in range(0, rows, rows_step):
        y = mm(taps_up(gs, at, rows_step), weight)
        back = y[:, ch : 2 * ch] + roll_rows(y[:, :ch], -1) + roll_rows(y[:, 2 * ch :], 1)
        back_ref[at : at + rows_step] = back.astype(BF16).reshape(rows_step, wide, ch)[:, :cols]


def clear_halo(pad_ref, frames):
    zeros = jnp.zeros((HALO,) + pad_ref.shape[1:], pad_ref.dtype)
    pad_ref[:HALO] = zeros
    pad_ref[HALO + frames :] = zeros


def taps_of(pad_ref, at, count, step_size, sign):
    high, ch = pad_ref.shape[1:]
    pieces = [
        pad_ref[pl.ds(HALO + at + sign * (k - 2) * step_size, count)].reshape(count * high, ch)
        for k in range(TAPS)
    ]
    return jnp.concatenate(pieces, axis=1)


def temporal_kernel(
    step_frames, dil_ref, key_ref, got_ref, tw_hbm, uw_hbm,
    grad_hbm, kept_hbm, united_hbm,
    a0, a1, feat, cots, g0, g1, slope0, slope1, united_ref, grad_ref, tw_ref, uw_ref,
    sems, in_sems, out_sems,
):
    frames, _, block, ch = got_ref.shape
    high = feat.shape[1]
    loads = [
        pltpu.make_async_copy(source, ref, in_sems.at[n])
        for n, (source, ref) in enumerate(((tw_hbm, tw_ref), (uw_hbm, uw_ref)))
    ]
    for load in loads:
        load.start()
    stores = [
        pltpu.make_async_copy(
            grad_ref.at[pl.ds(at, step_frames)], grad_hbm.at[pl.ds(at, step_frames)], out_sems.at[n]
        )
        for n, at in enumerate(range(0, frames, step_frames))
    ]
    segs = key_ref.shape[0]
    seg_frames = frames // segs
    inside = pl.ds(HALO, frames)
    copies = [
        pltpu.make_async_copy(source, target, sems.at[n])
        for n, (source, target) in enumerate(
            (
                (a1.at[inside], kept_hbm.at[0]),
                (feat, kept_hbm.at[1]),
                (g1.at[inside], kept_hbm.at[2]),
                (g0.at[inside], kept_hbm.at[3]),
                (a0.at[inside], kept_hbm.at[4]),
                (cots, kept_hbm.at[5]),
                (united_ref, united_hbm.at[0]),
            )
        )
    ]
    for ref in (a0, a1, g0, g1):
        clear_halo(ref, frames)
    if high > block:
        pad = jnp.zeros((frames, high - block, ch), BF16)
        a0[HALO : HALO + frames, block:, :] = pad
        cots[:, block:, :] = pad
    a0[HALO : HALO + frames, :block, :] = got_ref[:, 0]
    copies[4].start()
    for load in loads:
        load.wait()
    for layer, (source, target, slopes) in enumerate(((a0, a1, slope0), (a1, feat, slope1))):
        step_size = dil_ref[layer]
        weight = jnp.concatenate([tw_ref[layer, k] for k in range(TAPS)], axis=0)
        first = HALO if layer == 0 else 0
        for at in range(0, frames, step_frames):
            pre = mm(taps_of(source, at, step_frames, step_size, 1), weight)
            act, slope = silu_parts(pre)
            target[first + at : first + at + step_frames] = act.astype(BF16).reshape(
                step_frames, high, ch
            )
            slopes[at : at + step_frames] = slope.reshape(step_frames, high, ch)
        copies[layer].start()
    cots[:, :block, :] = got_ref[:, 1]
    copies[5].start()
    keys = jnp.concatenate([feat[seg * seg_frames + key_ref[seg]] for seg in range(segs)], axis=0)
    key_parts = mm(keys, uw_ref[1]).reshape(segs, high, ch)
    totals = jnp.concatenate(
        [
            jnp.sum(cots[seg * seg_frames : (seg + 1) * seg_frames].astype(F32), axis=0)
            for seg in range(segs)
        ],
        axis=0,
    )
    key_terms = mm_nt(jnp.concatenate(three_parts(totals), axis=0), uw_ref[1])
    key_terms = jnp.sum(key_terms.reshape(3, segs, high, ch), axis=0)
    for seg in range(segs):
        low, top = seg * seg_frames, (seg + 1) * seg_frames
        main = mm(feat[low:top].reshape(seg_frames * high, ch), uw_ref[0]).reshape(
            seg_frames, high, ch
        )
        united_ref[low:top] = (main + key_parts[seg][None]).astype(BF16)[:, :block]
        grad_feat = mm_nt(cots[low:top].reshape(seg_frames * high, ch), uw_ref[0]).reshape(
            seg_frames, high, ch
        )
        for n in range(seg_frames):
            grad = grad_feat[n] + jnp.where(key_ref[seg] == n, key_terms[seg], 0.0)
            g1[HALO + low + n] = (grad * slope1[low + n]).astype(BF16)
    copies[6].start()
    for layer, source in ((1, g1), (0, g0)):
        copies[3 - layer].start()
        step_size = dil_ref[layer]
        weight = jnp.concatenate(
            [tw_ref[layer, k].astype(F32).T.astype(BF16) for k in range(TAPS)], axis=0
        )
        for n, at in enumerate(range(0, frames, step_frames)):
            grad = mm(taps_of(source, at, step_frames, step_size, -1), weight).reshape(
                step_frames, high, ch
            )
            if layer == 1:
                g0[HALO + at : HALO + at + step_frames] = (
                    grad * slope0[at : at + step_frames]
                ).astype(BF16)
            else:
                grad_ref[at : at + step_frames] = grad.astype(BF16)[:, :block]
                stores[n].start()
    for copy in copies + stores:
        copy.wait()


def temporal_wgrad_kernel(
    step_frames, scale, here_ref, dil_ref, key_ref,
    kept_hbm, united_kept, united_hbm, *rest
):
    pieces, (a0, g0, a1, g1, feat, cots, united, total_ref, sems) = rest[:-9], rest[-9:]
    frames, high, ch = feat.shape
    segs = key_ref.shape[0]
    seg_frames = frames // segs
    rows = step_frames * high
    inside = pl.ds(HALO, frames)
    copies = [
        pltpu.make_async_copy(source, target, sems.at[n])
        for n, (source, target) in enumerate(
            (
                (kept_hbm.at[4], a0.at[inside]),
                (kept_hbm.at[3], g0),
                (kept_hbm.at[0], a1.at[inside]),
                (kept_hbm.at[2], g1),
                (kept_hbm.at[1], feat),
                (kept_hbm.at[5], cots),
                (united_kept.at[0], united),
            )
        )
    ]
    for copy in copies:
        copy.start()
    clear_halo(a0, frames)
    clear_halo(a1, frames)
    totals = []
    for layer, acts, grads in ((0, a0, g0), (1, a1, g1)):
        copies[2 * layer].wait()
        copies[2 * layer + 1].wait()
        total = jnp.zeros((TAPS * ch, ch), F32)
        for at in range(0, frames, step_frames):
            total = total + mm_tn(
                taps_of(acts, at, step_frames, dil_ref[layer], 1),
                grads[at : at + step_frames].reshape(rows, ch),
            )
        totals.append(total)
    for copy in copies[4:]:
        copy.wait()
    united_copy = pltpu.make_async_copy(united, united_hbm, sems.at[len(copies)])
    united_copy.start()
    total = jnp.zeros((ch, ch), F32)
    for at in range(0, frames, step_frames):
        total = total + mm_tn(
            feat[at : at + step_frames].reshape(rows, ch),
            cots[at : at + step_frames].reshape(rows, ch),
        )
    keyed = jnp.zeros((ch, ch), F32)
    for seg in range(segs):
        low, top = seg * seg_frames, (seg + 1) * seg_frames
        key = feat[low + key_ref[seg]]
        seg_cot = jnp.sum(cots[low:top].astype(F32), axis=0)
        keyed = keyed + sum(mm_tn(key, part) for part in three_parts(seg_cot))
    peers = len(pieces)
    split = LAYERS * TAPS * ch // peers
    total_ref[:, :split] = (jnp.concatenate(totals, axis=0) * scale).reshape(peers, split, ch)
    total_ref[:, split:] = (jnp.concatenate([total, keyed], axis=0) * scale).reshape(
        peers, 2 * ch // peers, ch
    )
    hand_out(here_ref, total_ref, pieces)
    united_copy.wait()


def sum_kernel(*refs):
    refs[-1][...] = sum(ref[...].astype(F32) for ref in refs[:-1]).astype(refs[-1].dtype)


def join_kernel(first_ref, *refs):
    out_ref = refs[-1]
    split = first_ref.shape[0]
    out_ref[:split] = first_ref[...]
    out_ref[split:] = sum(ref[...].astype(F32) for ref in refs[:-1]).astype(out_ref.dtype)


def deal_kernel(pieces_ref, united_hbm, *refs):
    outs_hbm, united_out, outs, sems = refs[:3], refs[3], refs[4:7], refs[7]
    copies = [pltpu.make_async_copy(united_hbm, united_out, sems.at[3])]
    copies[0].start()
    at = 0
    for n, out_ref in enumerate(outs):
        count = out_ref.shape[1]
        out_ref[...] = pieces_ref[:, at : at + count].astype(F32)
        copies.append(pltpu.make_async_copy(out_ref, outs_hbm[n], sems.at[n]))
        copies[-1].start()
        at += count
    for copy in copies:
        copy.wait()


def exchange(blocks):
    return lax.all_to_all(blocks, AXES, split_axis=0, concat_axis=0, tiled=True)


def flip(value, peer):
    size = lax.axis_size("grp")
    return lax.ppermute(value, "grp", [(i, i ^ peer) for i in range(size)])


def turn_by(value, turn):
    size = lax.axis_size("seg")
    return lax.ppermute(value, "seg", [(i, (i + turn) % size) for i in range(size)])


def sum_of(parts):
    shape = parts[0].shape
    return call(
        sum_kernel, [(shape, BF16, VMEM)], [], 0, len(parts) * 2 * shape[0] * shape[1],
        [(part, VMEM) for part in parts], SMALL_VMEM,
    )[0]


def reduce_in_grp(pieces):
    return sum_of([flip(piece, peer) if peer else piece for peer, piece in enumerate(pieces)])


def all_turns(value):
    return [turn_by(value, turn) if turn else value for turn in range(lax.axis_size("seg"))]


def local(
    frames_in, spatial_weight, temporal_weight, uniting_weight, key_index, dilation, cotangent
):
    held, rows, cols, ch = frames_in.shape
    assert held == 1
    pixels = rows * cols
    peers = lax.axis_size("grp")
    devices = lax.axis_size("seg") * peers
    frames = held * devices
    block = pixels // devices
    split = cols // block
    wide = round_up(cols + 1, 16)
    high = round_up(block, 16)
    rows_step = next(n for n in (4, 2, 1) if rows % n == 0)
    steps = rows // rows_step
    parts = next(n for n in (4, 2, 1) if rows % (n * rows_step) == 0)
    step_frames, narrow_step = (
        max(n for n in range(1, frames + 1) if frames % n == 0 and n * high <= most)
        for most in (512, 128)
    )
    scale = float((frames * pixels) ** -0.5)
    here = jnp.stack([lax.axis_index("seg"), lax.axis_index("grp")]).astype(jnp.int32)
    space_rows, time_rows, unite_rows = (n * ch // peers for n in (9, LAYERS * TAPS, 2))

    (send,) = call(
        functools.partial(spatial_fwd_kernel, rows_step),
        [((rows, 2, cols, ch), BF16, HBM)],
        [
            pltpu.VMEM((rows, cols, ch), BF16),
            pltpu.VMEM(spatial_weight.shape, BF16),
            pltpu.VMEM((rows + 2, wide, ch), BF16),
            pltpu.VMEM((rows, 2, cols, ch), BF16),
            pltpu.SemaphoreType.DMA((parts,)),
            pltpu.SemaphoreType.DMA((1,)),
            pltpu.SemaphoreType.DMA((1,)),
            pltpu.SemaphoreType.DMA((parts,)),
        ],
        2 * 9 * pixels * ch * ch,
        pixels * ch * 8,
        [(frames_in[0], HBM), (spatial_weight, HBM), (cotangent[0], HBM)],
        MID_VMEM,
    )
    send, frame = lax.optimization_barrier((send, frames_in[0]))
    send = send.reshape(rows, 2, split, block, ch).swapaxes(1, 2).reshape(devices, 2, block, ch)
    got = exchange(send)
    (space_slope,) = call(
        functools.partial(spatial_slope_kernel, rows_step),
        [((SPARE, rows, cols, ch), BF16, HBM)],
        [
            pltpu.VMEM((rows + 2, wide, ch), BF16),
            pltpu.VMEM((rows, cols, ch), BF16),
            pltpu.SemaphoreType.DMA((1,)),
        ],
        2 * 9 * pixels * ch * ch,
        pixels * ch * 4,
        [(frame, VMEM), (spatial_weight, VMEM)],
    )
    got, space_slope = lax.optimization_barrier((got, space_slope))

    padded = (frames + 2 * HALO, high, ch)
    whole = (frames, high, ch)
    grad_send, kept, united_kept = call(
        functools.partial(temporal_kernel, narrow_step),
        [
            ((frames, block, ch), BF16, HBM),
            ((SPARE,) + whole, BF16, HBM),
            ((SPARE, frames, block, ch), BF16, HBM),
        ],
        [
            pltpu.VMEM(padded, BF16),
            pltpu.VMEM(padded, BF16),
            pltpu.VMEM(whole, BF16),
            pltpu.VMEM(whole, BF16),
            pltpu.VMEM(padded, BF16),
            pltpu.VMEM(padded, BF16),
            pltpu.VMEM(whole, F32),
            pltpu.VMEM(whole, F32),
            pltpu.VMEM((frames, block, ch), BF16),
            pltpu.VMEM((frames, block, ch), BF16),
            pltpu.VMEM(temporal_weight.shape, BF16),
            pltpu.VMEM(uniting_weight.shape, BF16),
            pltpu.SemaphoreType.DMA((7,)),
            pltpu.SemaphoreType.DMA((2,)),
            pltpu.SemaphoreType.DMA((frames // narrow_step,)),
        ],
        2 * 22 * frames * block * ch * ch,
        frames * block * ch * 18,
        [
            (dilation, SMEM), (key_index, SMEM), (got, VMEM),
            (temporal_weight, HBM), (uniting_weight, HBM),
        ],
        MID_VMEM,
    )
    grad_time = exchange(grad_send).reshape(rows, cols, ch)
    united_send, *time_pieces = call(
        functools.partial(temporal_wgrad_kernel, step_frames, scale),
        [((frames, block, ch), BF16, HBM)]
        + [((time_rows + unite_rows, ch), BF16, VMEM)] * peers,
        [
            pltpu.VMEM(padded, BF16),
            pltpu.VMEM(whole, BF16),
            pltpu.VMEM(padded, BF16),
            pltpu.VMEM(whole, BF16),
            pltpu.VMEM(whole, BF16),
            pltpu.VMEM(whole, BF16),
            pltpu.VMEM((frames, block, ch), BF16),
            pltpu.VMEM((peers, time_rows + unite_rows, ch), F32),
            pltpu.SemaphoreType.DMA((8,)),
        ],
        2 * 12 * frames * block * ch * ch,
        frames * block * ch * 14,
        [
            (here, SMEM), (dilation, SMEM), (key_index, SMEM),
            (kept, HBM), (united_kept, HBM),
        ],
    )
    time_sum = reduce_in_grp(time_pieces)
    time_sum, grad_time = lax.optimization_barrier((time_sum, grad_time))
    united_send, grad_time = lax.optimization_barrier((united_send, grad_time))
    united = exchange(united_send)
    space_pieces = call(
        functools.partial(spatial_wgrad_kernel, rows_step, scale),
        [((space_rows, ch), BF16, VMEM)] * peers,
        [
            pltpu.VMEM((rows + 2, wide, ch), BF16),
            pltpu.VMEM((rows, cols, ch), BF16),
            pltpu.VMEM((3 * ch, min(3, steps) * rows_step * wide), BF16),
            pltpu.VMEM((peers, space_rows, ch), F32),
            pltpu.SemaphoreType.DMA((1,)),
        ],
        2 * 9 * pixels * ch * ch,
        pixels * ch * 8,
        [(here, SMEM), (grad_time, VMEM), (space_slope, HBM), (frame, VMEM)],
        MID_VMEM,
    )
    (back,) = call(
        functools.partial(spatial_back_kernel, rows_step),
        [((rows, cols, ch), BF16, VMEM)],
        [
            pltpu.VMEM((rows + 2, wide, ch), BF16),
            pltpu.VMEM((rows, cols, ch), BF16),
            pltpu.SemaphoreType.DMA((1,)),
        ],
        2 * 9 * pixels * ch * ch,
        pixels * ch * 6,
        [(spatial_weight, VMEM), (grad_time, VMEM), (space_slope, HBM)],
        MID_VMEM,
    )
    space_parts = [flip(part, peer) if peer else part for peer, part in enumerate(space_pieces)]
    (plane,) = call(
        join_kernel,
        [((time_rows + unite_rows + space_rows, ch), BF16, VMEM)],
        [],
        0,
        2 * (peers + 10) * space_rows * ch,
        [(time_sum, VMEM)] + [(part, VMEM) for part in space_parts],
        SMALL_VMEM,
    )
    turned = all_turns(plane)
    turned[0], back = lax.optimization_barrier((turned[0], back))
    piece = sum_of(turned)
    *grads, united = call(
        deal_kernel,
        [((peers, count, ch), F32, HBM) for count in (time_rows, unite_rows, space_rows)]
        + [((frames, block, ch), BF16, HBM)],
        [pltpu.VMEM((peers, count, ch), F32) for count in (time_rows, unite_rows, space_rows)]
        + [pltpu.SemaphoreType.DMA((4,))],
        0,
        6 * 21 * ch * ch,
        [(lax.all_gather(piece, "grp", axis=0), VMEM), (united, HBM)],
        SMALL_VMEM,
    )
    return (
        united.reshape(frames_in.shape),
        back[None],
        grads[2].reshape(9, ch, ch),
        grads[0].reshape(LAYERS, TAPS, ch, ch),
        grads[1].reshape(2, ch, ch),
    )


def solution(mesh):
    frame_spec = P(AXES, None, None, None)
    return jax.shard_map(
        local,
        mesh=mesh,
        in_specs=(frame_spec, P(), P(), P(), P(), P(), frame_spec),
        out_specs=(frame_spec, frame_spec, P(), P(), P()),
        check_vma=False,
    )
```

```python
import functools

import jax
import jax.numpy as jnp
from jax import lax
from jax.experimental import pallas as pl
from jax.experimental.pallas import tpu as pltpu
from jax.sharding import PartitionSpec as P

LAYERS = 2
TAPS = 5
DMAX = 8
HALO = 2 * DMAX
AXES = ("seg", "grp")
BF16 = jnp.bfloat16
F32 = jnp.float32
BIG_VMEM = 60 * 1024 * 1024
MID_VMEM = 40 * 1024 * 1024
SPARE = 28
SMALL_VMEM = 16 * 1024 * 1024


def round_up(value, step):
    return -(-value // step) * step


def silu_parts(value):
    sigma = 0.5 * jnp.tanh(0.5 * value) + 0.5
    act = value * sigma
    return act, sigma + act * (1.0 - sigma)


def mm(left, right):
    return jnp.dot(left, right, preferred_element_type=F32)


def mm_nt(left, right):
    return lax.dot_general(left, right, (((1,), (1,)), ((), ())), preferred_element_type=F32)


def mm_tn(left, right):
    return lax.dot_general(left, right, (((0,), (0,)), ((), ())), preferred_element_type=F32)


def three_parts(value):
    high = value.astype(BF16)
    rest = value - high.astype(F32)
    middle = rest.astype(BF16)
    return high, middle, (rest - middle.astype(F32)).astype(BF16)


VMEM = pl.BlockSpec(memory_space=pltpu.VMEM)
SMEM = pl.BlockSpec(memory_space=pltpu.SMEM)
HBM = pl.BlockSpec(memory_space=pltpu.HBM)


def call(kernel, outs, scratch, flops, moved, args, vmem=BIG_VMEM):
    return pl.pallas_call(
        kernel,
        out_shape=[jax.ShapeDtypeStruct(shape, kind) for shape, kind, _ in outs],
        in_specs=[spec for _, spec in args],
        out_specs=[spec for _, _, spec in outs],
        scratch_shapes=scratch,
        compiler_params=pltpu.CompilerParams(vmem_limit_bytes=vmem),
        cost_estimate=pl.CostEstimate(flops=flops, bytes_accessed=moved, transcendentals=0),
    )(*[value for value, _ in args])


def roll_rows(value, shift):
    return pltpu.roll(value, shift % value.shape[0], 0)


def spatial_pre(xs, weight, at, rows_step):
    wide, ch = xs.shape[1:]
    flat = rows_step * wide
    left = jnp.concatenate(
        [xs[at + a : at + a + rows_step].reshape(flat, ch) for a in range(3)], axis=1
    )
    y = mm(left, weight)
    return y[:, ch : 2 * ch] + roll_rows(y[:, :ch], 1) + roll_rows(y[:, 2 * ch :], -1)


def forward_weight(w_ref):
    return jnp.concatenate(
        [jnp.concatenate([w_ref[3 * a + b] for b in range(3)], axis=1) for a in range(3)], axis=0
    )


def clear_ends(ref):
    last = ref.shape[0] - 1
    ref[0] = jnp.zeros(ref.shape[1:], ref.dtype)
    ref[last] = jnp.zeros(ref.shape[1:], ref.dtype)


def put_rows(ref, at, value):
    count, cols, ch = value.shape
    ref[1 + at : 1 + at + count, cols:, :] = jnp.zeros((count, ref.shape[1] - cols, ch), ref.dtype)
    ref[1 + at : 1 + at + count, :cols, :] = value


def spatial_fwd_kernel(
    rows_step, x_hbm, w_hbm, cot_hbm, send_hbm,
    x_in, w_ref, xs, sends, in_sems, w_sem, cot_sem, send_sems,
):
    rows, cols, ch = x_in.shape
    wide = xs.shape[1]
    parts = in_sems.shape[0]
    many = rows // parts

    def part(n):
        return pl.ds(n * many, many)

    loads = [
        pltpu.make_async_copy(x_hbm.at[part(n)], x_in.at[part(n)], in_sems.at[n]) for n in range(parts)
    ]
    stores = [
        pltpu.make_async_copy(sends.at[part(n)], send_hbm.at[part(n)], send_sems.at[n])
        for n in range(parts)
    ]
    w_load = pltpu.make_async_copy(w_hbm, w_ref, w_sem.at[0])
    cot_load = pltpu.make_async_copy(cot_hbm, sends.at[:, 1], cot_sem.at[0])
    for load in [loads[0], w_load] + loads[1:] + [cot_load]:
        load.start()
    clear_ends(xs)

    def bring(n):
        loads[n].wait()
        put_rows(xs, n * many, x_in[n * many : (n + 1) * many])

    bring(0)
    w_load.wait()
    weight = forward_weight(w_ref)
    for n in range(parts):
        if n + 1 < parts:
            bring(n + 1)
        for at in range(n * many, (n + 1) * many, rows_step):
            act, _ = silu_parts(spatial_pre(xs, weight, at, rows_step))
            sends[at : at + rows_step, 0] = act.astype(BF16).reshape(rows_step, wide, ch)[:, :cols]
        if n == 0:
            cot_load.wait()
        stores[n].start()
    for store in stores:
        store.wait()


def spatial_slope_kernel(rows_step, x_ref, w_ref, slope_hbm, xs, slopes, sem):
    rows, cols, ch = x_ref.shape
    wide = xs.shape[1]
    clear_ends(xs)
    put_rows(xs, 0, x_ref[...])
    weight = forward_weight(w_ref)
    for at in range(0, rows, rows_step):
        _, slope = silu_parts(spatial_pre(xs, weight, at, rows_step))
        slopes[at : at + rows_step] = slope.astype(BF16).reshape(rows_step, wide, ch)[:, :cols]
    store = pltpu.make_async_copy(slopes, slope_hbm.at[0], sem.at[0])
    store.start()
    store.wait()


def hand_out(here_ref, total_ref, pieces):
    for peer, piece in enumerate(pieces):
        piece[...] = total_ref[jnp.bitwise_xor(here_ref[1], peer)].astype(piece.dtype)


def taps_up(gs, at, rows_step):
    wide, ch = gs.shape[1:]
    return jnp.concatenate(
        [gs[at + 2 - a : at + 2 - a + rows_step].reshape(rows_step * wide, ch) for a in range(3)],
        axis=1,
    )


def fill_grads(rows_step, gs, got_ref, slope_ref):
    clear_ends(gs)
    for at in range(0, got_ref.shape[0], rows_step):
        grads = got_ref[at : at + rows_step].astype(F32)
        slopes = slope_ref[at : at + rows_step].astype(F32)
        put_rows(gs, at, (grads * slopes).astype(BF16))


def spatial_wgrad_kernel(rows_step, scale, here_ref, got_ref, slope_hbm, x_ref, *rest):
    pieces, (gs, slopes, cat_ref, total_ref, sem) = rest[:-5], rest[-5:]
    rows, cols, ch = got_ref.shape
    wide = gs.shape[1]
    flat = rows_step * wide
    load = pltpu.make_async_copy(slope_hbm.at[0], slopes, sem.at[0])
    load.start()
    pad = jnp.zeros((rows_step, wide - cols, ch), F32)

    def columns(at):
        x = jnp.concatenate([x_ref[at : at + rows_step].astype(F32), pad], axis=1).reshape(flat, ch)
        x_cat = jnp.concatenate([roll_rows(x, 1), x, roll_rows(x, -1)], axis=1)
        return x_cat.T.astype(BF16)

    early = cat_ref.shape[1] // flat
    for n in range(early):
        cat_ref[:, n * flat : (n + 1) * flat] = columns(n * rows_step)
    load.wait()
    fill_grads(rows_step, gs, got_ref, slopes)
    total = jnp.zeros((3 * ch, 3 * ch), F32)
    for n, at in enumerate(range(0, rows, rows_step)):
        cat = cat_ref[:, n * flat : (n + 1) * flat] if n < early else columns(at)
        total = total + mm(cat, taps_up(gs, at, rows_step))
    total_ref[...] = (
        jnp.concatenate(
            [
                total[b * ch : (b + 1) * ch, a * ch : (a + 1) * ch]
                for a in range(3)
                for b in range(3)
            ],
            axis=0,
        )
        * scale
    ).reshape(total_ref.shape)
    hand_out(here_ref, total_ref, pieces)


def spatial_back_kernel(rows_step, w_ref, got_ref, slope_hbm, back_ref, gs, slopes, sem):
    rows, cols, ch = back_ref.shape
    wide = gs.shape[1]
    load = pltpu.make_async_copy(slope_hbm.at[0], slopes, sem.at[0])
    load.start()
    weight = jnp.concatenate(
        [
            jnp.concatenate([w_ref[3 * a + b].astype(F32).T.astype(BF16) for b in range(3)], axis=1)
            for a in range(3)
        ],
        axis=0,
    )
    load.wait()
    fill_grads(rows_step, gs, got_ref, slopes)
    for at in range(0, rows, rows_step):
        y = mm(taps_up(gs, at, rows_step), weight)
        back = y[:, ch : 2 * ch] + roll_rows(y[:, :ch], -1) + roll_rows(y[:, 2 * ch :], 1)
        back_ref[at : at + rows_step] = back.astype(BF16).reshape(rows_step, wide, ch)[:, :cols]


def clear_halo(pad_ref, frames):
    zeros = jnp.zeros((HALO,) + pad_ref.shape[1:], pad_ref.dtype)
    pad_ref[:HALO] = zeros
    pad_ref[HALO + frames :] = zeros


def taps_of(pad_ref, at, count, step_size, sign):
    high, ch = pad_ref.shape[1:]
    pieces = [
        pad_ref[pl.ds(HALO + at + sign * (k - 2) * step_size, count)].reshape(count * high, ch)
        for k in range(TAPS)
    ]
    return jnp.concatenate(pieces, axis=1)


def temporal_kernel(
    step_frames, dil_ref, key_ref, got_ref, tw_hbm, uw_hbm,
    grad_hbm, kept_hbm, united_hbm,
    a0, a1, feat, cots, g0, g1, slope0, slope1, united_ref, grad_ref, tw_ref, uw_ref,
    sems, in_sems, out_sems,
):
    frames, _, block, ch = got_ref.shape
    high = feat.shape[1]
    loads = [
        pltpu.make_async_copy(source, ref, in_sems.at[n])
        for n, (source, ref) in enumerate(((tw_hbm, tw_ref), (uw_hbm, uw_ref)))
    ]
    for load in loads:
        load.start()
    stores = [
        pltpu.make_async_copy(
            grad_ref.at[pl.ds(at, step_frames)], grad_hbm.at[pl.ds(at, step_frames)], out_sems.at[n]
        )
        for n, at in enumerate(range(0, frames, step_frames))
    ]
    segs = key_ref.shape[0]
    seg_frames = frames // segs
    inside = pl.ds(HALO, frames)
    copies = [
        pltpu.make_async_copy(source, target, sems.at[n])
        for n, (source, target) in enumerate(
            (
                (a1.at[inside], kept_hbm.at[0]),
                (feat, kept_hbm.at[1]),
                (g1.at[inside], kept_hbm.at[2]),
                (g0.at[inside], kept_hbm.at[3]),
                (a0.at[inside], kept_hbm.at[4]),
                (cots, kept_hbm.at[5]),
                (united_ref, united_hbm.at[0]),
            )
        )
    ]
    for ref in (a0, a1, g0, g1):
        clear_halo(ref, frames)
    if high > block:
        pad = jnp.zeros((frames, high - block, ch), BF16)
        a0[HALO : HALO + frames, block:, :] = pad
        cots[:, block:, :] = pad
    a0[HALO : HALO + frames, :block, :] = got_ref[:, 0]
    copies[4].start()
    for load in loads:
        load.wait()
    for layer, (source, target, slopes) in enumerate(((a0, a1, slope0), (a1, feat, slope1))):
        step_size = dil_ref[layer]
        weight = jnp.concatenate([tw_ref[layer, k] for k in range(TAPS)], axis=0)
        first = HALO if layer == 0 else 0
        for at in range(0, frames, step_frames):
            pre = mm(taps_of(source, at, step_frames, step_size, 1), weight)
            act, slope = silu_parts(pre)
            target[first + at : first + at + step_frames] = act.astype(BF16).reshape(
                step_frames, high, ch
            )
            slopes[at : at + step_frames] = slope.reshape(step_frames, high, ch)
        copies[layer].start()
    cots[:, :block, :] = got_ref[:, 1]
    copies[5].start()
    keys = jnp.concatenate([feat[seg * seg_frames + key_ref[seg]] for seg in range(segs)], axis=0)
    key_parts = mm(keys, uw_ref[1]).reshape(segs, high, ch)
    totals = jnp.concatenate(
        [
            jnp.sum(cots[seg * seg_frames : (seg + 1) * seg_frames].astype(F32), axis=0)
            for seg in range(segs)
        ],
        axis=0,
    )
    key_terms = mm_nt(jnp.concatenate(three_parts(totals), axis=0), uw_ref[1])
    key_terms = jnp.sum(key_terms.reshape(3, segs, high, ch), axis=0)
    for seg in range(segs):
        low, top = seg * seg_frames, (seg + 1) * seg_frames
        main = mm(feat[low:top].reshape(seg_frames * high, ch), uw_ref[0]).reshape(
            seg_frames, high, ch
        )
        united_ref[low:top] = (main + key_parts[seg][None]).astype(BF16)[:, :block]
        grad_feat = mm_nt(cots[low:top].reshape(seg_frames * high, ch), uw_ref[0]).reshape(
            seg_frames, high, ch
        )
        for n in range(seg_frames):
            grad = grad_feat[n] + jnp.where(key_ref[seg] == n, key_terms[seg], 0.0)
            g1[HALO + low + n] = (grad * slope1[low + n]).astype(BF16)
    copies[6].start()
    for layer, source in ((1, g1), (0, g0)):
        copies[3 - layer].start()
        step_size = dil_ref[layer]
        weight = jnp.concatenate(
            [tw_ref[layer, k].astype(F32).T.astype(BF16) for k in range(TAPS)], axis=0
        )
        for n, at in enumerate(range(0, frames, step_frames)):
            grad = mm(taps_of(source, at, step_frames, step_size, -1), weight).reshape(
                step_frames, high, ch
            )
            if layer == 1:
                g0[HALO + at : HALO + at + step_frames] = (
                    grad * slope0[at : at + step_frames]
                ).astype(BF16)
            else:
                grad_ref[at : at + step_frames] = grad.astype(BF16)[:, :block]
                stores[n].start()
    for copy in copies + stores:
        copy.wait()


def temporal_wgrad_kernel(
    step_frames, scale, here_ref, dil_ref, key_ref,
    kept_hbm, united_kept, united_hbm, *rest
):
    pieces, (a0, g0, a1, g1, feat, cots, united, total_ref, sems) = rest[:-9], rest[-9:]
    frames, high, ch = feat.shape
    segs = key_ref.shape[0]
    seg_frames = frames // segs
    rows = step_frames * high
    inside = pl.ds(HALO, frames)
    copies = [
        pltpu.make_async_copy(source, target, sems.at[n])
        for n, (source, target) in enumerate(
            (
                (kept_hbm.at[4], a0.at[inside]),
                (kept_hbm.at[3], g0),
                (kept_hbm.at[0], a1.at[inside]),
                (kept_hbm.at[2], g1),
                (kept_hbm.at[1], feat),
                (kept_hbm.at[5], cots),
                (united_kept.at[0], united),
            )
        )
    ]
    for copy in copies:
        copy.start()
    clear_halo(a0, frames)
    clear_halo(a1, frames)
    totals = []
    for layer, acts, grads in ((0, a0, g0), (1, a1, g1)):
        copies[2 * layer].wait()
        copies[2 * layer + 1].wait()
        total = jnp.zeros((TAPS * ch, ch), F32)
        for at in range(0, frames, step_frames):
            total = total + mm_tn(
                taps_of(acts, at, step_frames, dil_ref[layer], 1),
                grads[at : at + step_frames].reshape(rows, ch),
            )
        totals.append(total)
    for copy in copies[4:]:
        copy.wait()
    united_copy = pltpu.make_async_copy(united, united_hbm, sems.at[len(copies)])
    united_copy.start()
    total = jnp.zeros((ch, ch), F32)
    for at in range(0, frames, step_frames):
        total = total + mm_tn(
            feat[at : at + step_frames].reshape(rows, ch),
            cots[at : at + step_frames].reshape(rows, ch),
        )
    keyed = jnp.zeros((ch, ch), F32)
    for seg in range(segs):
        low, top = seg * seg_frames, (seg + 1) * seg_frames
        key = feat[low + key_ref[seg]]
        seg_cot = jnp.sum(cots[low:top].astype(F32), axis=0)
        keyed = keyed + sum(mm_tn(key, part) for part in three_parts(seg_cot))
    peers = len(pieces)
    split = LAYERS * TAPS * ch // peers
    total_ref[:, :split] = (jnp.concatenate(totals, axis=0) * scale).reshape(peers, split, ch)
    total_ref[:, split:] = (jnp.concatenate([total, keyed], axis=0) * scale).reshape(
        peers, 2 * ch // peers, ch
    )
    hand_out(here_ref, total_ref, pieces)
    united_copy.wait()


def sum_kernel(*refs):
    refs[-1][...] = sum(ref[...].astype(F32) for ref in refs[:-1]).astype(refs[-1].dtype)


def join_kernel(first_ref, *refs):
    out_ref = refs[-1]
    split = first_ref.shape[0]
    out_ref[:split] = first_ref[...]
    out_ref[split:] = sum(ref[...].astype(F32) for ref in refs[:-1]).astype(out_ref.dtype)


def deal_kernel(pieces_ref, united_hbm, *refs):
    outs_hbm, united_out, outs, sems = refs[:3], refs[3], refs[4:7], refs[7]
    copies = [pltpu.make_async_copy(united_hbm, united_out, sems.at[3])]
    copies[0].start()
    at = 0
    for n, out_ref in enumerate(outs):
        count = out_ref.shape[1]
        out_ref[...] = pieces_ref[:, at : at + count].astype(F32)
        copies.append(pltpu.make_async_copy(out_ref, outs_hbm[n], sems.at[n]))
        copies[-1].start()
        at += count
    for copy in copies:
        copy.wait()


def exchange(blocks):
    return lax.all_to_all(blocks, AXES, split_axis=0, concat_axis=0, tiled=True)


def flip(value, peer):
    size = lax.axis_size("grp")
    return lax.ppermute(value, "grp", [(i, i ^ peer) for i in range(size)])


def meet_in_seg(value, bit):
    size = lax.axis_size("seg")
    return lax.ppermute(value, "seg", [(i, i ^ bit) for i in range(size)])


def sum_of(parts):
    shape = parts[0].shape
    return call(
        sum_kernel, [(shape, BF16, VMEM)], [], 0, len(parts) * 2 * shape[0] * shape[1],
        [(part, VMEM) for part in parts], SMALL_VMEM,
    )[0]


def reduce_in_grp(pieces):
    return sum_of([flip(piece, peer) if peer else piece for peer, piece in enumerate(pieces)])


def local(
    frames_in, spatial_weight, temporal_weight, uniting_weight, key_index, dilation, cotangent
):
    held, rows, cols, ch = frames_in.shape
    assert held == 1
    pixels = rows * cols
    peers = lax.axis_size("grp")
    segs = lax.axis_size("seg")
    devices = segs * peers
    frames = held * devices
    block = pixels // devices
    split = cols // block
    wide = round_up(cols + 1, 16)
    high = round_up(block, 16)
    rows_step = next(n for n in (4, 2, 1) if rows % n == 0)
    steps = rows // rows_step
    parts = next(n for n in (4, 2, 1) if rows % (n * rows_step) == 0)
    step_frames, narrow_step = (
        max(n for n in range(1, frames + 1) if frames % n == 0 and n * high <= most)
        for most in (512, 256)
    )
    scale = float((frames * pixels) ** -0.5)
    here = jnp.stack([lax.axis_index("seg"), lax.axis_index("grp")]).astype(jnp.int32)
    space_rows, time_rows, unite_rows = (n * ch // peers for n in (9, LAYERS * TAPS, 2))

    (send,) = call(
        functools.partial(spatial_fwd_kernel, rows_step),
        [((rows, 2, cols, ch), BF16, HBM)],
        [
            pltpu.VMEM((rows, cols, ch), BF16),
            pltpu.VMEM(spatial_weight.shape, BF16),
            pltpu.VMEM((rows + 2, wide, ch), BF16),
            pltpu.VMEM((rows, 2, cols, ch), BF16),
            pltpu.SemaphoreType.DMA((parts,)),
            pltpu.SemaphoreType.DMA((1,)),
            pltpu.SemaphoreType.DMA((1,)),
            pltpu.SemaphoreType.DMA((parts,)),
        ],
        2 * 9 * pixels * ch * ch,
        pixels * ch * 8,
        [(frames_in[0], HBM), (spatial_weight, HBM), (cotangent[0], HBM)],
    )
    send, frame = lax.optimization_barrier((send, frames_in[0]))
    send = send.reshape(rows, 2, split, block, ch).swapaxes(1, 2).reshape(devices, 2, block, ch)
    got = exchange(send)
    (space_slope,) = call(
        functools.partial(spatial_slope_kernel, rows_step),
        [((SPARE, rows, cols, ch), BF16, HBM)],
        [
            pltpu.VMEM((rows + 2, wide, ch), BF16),
            pltpu.VMEM((rows, cols, ch), BF16),
            pltpu.SemaphoreType.DMA((1,)),
        ],
        2 * 9 * pixels * ch * ch,
        pixels * ch * 4,
        [(frame, VMEM), (spatial_weight, VMEM)],
    )
    got, space_slope = lax.optimization_barrier((got, space_slope))

    padded = (frames + 2 * HALO, high, ch)
    whole = (frames, high, ch)
    grad_send, kept, united_kept = call(
        functools.partial(temporal_kernel, narrow_step),
        [
            ((frames, block, ch), BF16, HBM),
            ((SPARE,) + whole, BF16, HBM),
            ((SPARE, frames, block, ch), BF16, HBM),
        ],
        [
            pltpu.VMEM(padded, BF16),
            pltpu.VMEM(padded, BF16),
            pltpu.VMEM(whole, BF16),
            pltpu.VMEM(whole, BF16),
            pltpu.VMEM(padded, BF16),
            pltpu.VMEM(padded, BF16),
            pltpu.VMEM(whole, F32),
            pltpu.VMEM(whole, F32),
            pltpu.VMEM((frames, block, ch), BF16),
            pltpu.VMEM((frames, block, ch), BF16),
            pltpu.VMEM(temporal_weight.shape, BF16),
            pltpu.VMEM(uniting_weight.shape, BF16),
            pltpu.SemaphoreType.DMA((7,)),
            pltpu.SemaphoreType.DMA((2,)),
            pltpu.SemaphoreType.DMA((frames // narrow_step,)),
        ],
        2 * 22 * frames * block * ch * ch,
        frames * block * ch * 18,
        [
            (dilation, SMEM), (key_index, SMEM), (got, VMEM),
            (temporal_weight, HBM), (uniting_weight, HBM),
        ],
        MID_VMEM,
    )
    grad_time = exchange(grad_send).reshape(rows, cols, ch)
    united_send, *time_pieces = call(
        functools.partial(temporal_wgrad_kernel, step_frames, scale),
        [((frames, block, ch), BF16, HBM)]
        + [((time_rows + unite_rows, ch), BF16, VMEM)] * peers,
        [
            pltpu.VMEM(padded, BF16),
            pltpu.VMEM(whole, BF16),
            pltpu.VMEM(padded, BF16),
            pltpu.VMEM(whole, BF16),
            pltpu.VMEM(whole, BF16),
            pltpu.VMEM(whole, BF16),
            pltpu.VMEM((frames, block, ch), BF16),
            pltpu.VMEM((peers, time_rows + unite_rows, ch), F32),
            pltpu.SemaphoreType.DMA((8,)),
        ],
        2 * 12 * frames * block * ch * ch,
        frames * block * ch * 14,
        [
            (here, SMEM), (dilation, SMEM), (key_index, SMEM),
            (kept, HBM), (united_kept, HBM),
        ],
    )
    time_sum = reduce_in_grp(time_pieces)
    time_sum, grad_time = lax.optimization_barrier((time_sum, grad_time))
    united_send, grad_time = lax.optimization_barrier((united_send, grad_time))
    united = exchange(united_send)
    space_pieces = call(
        functools.partial(spatial_wgrad_kernel, rows_step, scale),
        [((space_rows, ch), BF16, VMEM)] * peers,
        [
            pltpu.VMEM((rows + 2, wide, ch), BF16),
            pltpu.VMEM((rows, cols, ch), BF16),
            pltpu.VMEM((3 * ch, min(3, steps) * rows_step * wide), BF16),
            pltpu.VMEM((peers, space_rows, ch), F32),
            pltpu.SemaphoreType.DMA((1,)),
        ],
        2 * 9 * pixels * ch * ch,
        pixels * ch * 8,
        [(here, SMEM), (grad_time, VMEM), (space_slope, HBM), (frame, VMEM)],
        MID_VMEM,
    )
    (back,) = call(
        functools.partial(spatial_back_kernel, rows_step),
        [((rows, cols, ch), BF16, VMEM)],
        [
            pltpu.VMEM((rows + 2, wide, ch), BF16),
            pltpu.VMEM((rows, cols, ch), BF16),
            pltpu.SemaphoreType.DMA((1,)),
        ],
        2 * 9 * pixels * ch * ch,
        pixels * ch * 6,
        [(spatial_weight, VMEM), (grad_time, VMEM), (space_slope, HBM)],
        MID_VMEM,
    )
    space_parts = [flip(part, peer) if peer else part for peer, part in enumerate(space_pieces)]
    (plane,) = call(
        join_kernel,
        [((time_rows + unite_rows + space_rows, ch), BF16, VMEM)],
        [],
        0,
        2 * (peers + 10) * space_rows * ch,
        [(time_sum, VMEM)] + [(part, VMEM) for part in space_parts],
        SMALL_VMEM,
    )
    piece = plane
    bits = [1 << n for n in range((segs - 1).bit_length())]
    for bit in bits:
        other = meet_in_seg(piece, bit)
        if bit == bits[-1]:
            other, back = lax.optimization_barrier((other, back))
        piece = sum_of([piece, other])
    *grads, united = call(
        deal_kernel,
        [((peers, count, ch), F32, HBM) for count in (time_rows, unite_rows, space_rows)]
        + [((frames, block, ch), BF16, HBM)],
        [pltpu.VMEM((peers, count, ch), F32) for count in (time_rows, unite_rows, space_rows)]
        + [pltpu.SemaphoreType.DMA((4,))],
        0,
        6 * 21 * ch * ch,
        [(lax.all_gather(piece, "grp", axis=0), VMEM), (united, HBM)],
        SMALL_VMEM,
    )
    return (
        united.reshape(frames_in.shape),
        back[None],
        grads[2].reshape(9, ch, ch),
        grads[0].reshape(LAYERS, TAPS, ch, ch),
        grads[1].reshape(2, ch, ch),
    )


def solution(mesh):
    frame_spec = P(AXES, None, None, None)
    return jax.shard_map(
        local,
        mesh=mesh,
        in_specs=(frame_spec, P(), P(), P(), P(), P(), frame_spec),
        out_specs=(frame_spec, frame_spec, P(), P(), P()),
        check_vma=False,
    )
```

```python
import functools

import jax
import jax.numpy as jnp
from jax import lax
from jax.experimental import pallas as pl
from jax.experimental.pallas import tpu as pltpu
from jax.sharding import PartitionSpec as P

LAYERS = 2
TAPS = 5
DMAX = 8
HALO = 2 * DMAX
AXES = ("seg", "grp")
BF16 = jnp.bfloat16
F32 = jnp.float32
BIG_VMEM = 60 * 1024 * 1024
MID_VMEM = 40 * 1024 * 1024
SPARE = 28
SMALL_VMEM = 16 * 1024 * 1024


def round_up(value, step):
    return -(-value // step) * step


def silu_parts(value):
    sigma = 0.5 * jnp.tanh(0.5 * value) + 0.5
    act = value * sigma
    return act, sigma + act * (1.0 - sigma)


def mm(left, right):
    return jnp.dot(left, right, preferred_element_type=F32)


def mm_nt(left, right):
    return lax.dot_general(left, right, (((1,), (1,)), ((), ())), preferred_element_type=F32)


def mm_tn(left, right):
    return lax.dot_general(left, right, (((0,), (0,)), ((), ())), preferred_element_type=F32)


def three_parts(value):
    high = value.astype(BF16)
    rest = value - high.astype(F32)
    middle = rest.astype(BF16)
    return high, middle, (rest - middle.astype(F32)).astype(BF16)


VMEM = pl.BlockSpec(memory_space=pltpu.VMEM)
SMEM = pl.BlockSpec(memory_space=pltpu.SMEM)
HBM = pl.BlockSpec(memory_space=pltpu.HBM)


def call(kernel, outs, scratch, flops, moved, args, vmem=BIG_VMEM):
    return pl.pallas_call(
        kernel,
        out_shape=[jax.ShapeDtypeStruct(shape, kind) for shape, kind, _ in outs],
        in_specs=[spec for _, spec in args],
        out_specs=[spec for _, _, spec in outs],
        scratch_shapes=scratch,
        compiler_params=pltpu.CompilerParams(vmem_limit_bytes=vmem),
        cost_estimate=pl.CostEstimate(flops=flops, bytes_accessed=moved, transcendentals=0),
    )(*[value for value, _ in args])


def roll_rows(value, shift):
    return pltpu.roll(value, shift % value.shape[0], 0)


def spatial_pre(xs, weight, at, rows_step):
    wide, ch = xs.shape[1:]
    flat = rows_step * wide
    left = jnp.concatenate(
        [xs[at + a : at + a + rows_step].reshape(flat, ch) for a in range(3)], axis=1
    )
    y = mm(left, weight)
    return y[:, ch : 2 * ch] + roll_rows(y[:, :ch], 1) + roll_rows(y[:, 2 * ch :], -1)


def forward_weight(w_ref):
    return jnp.concatenate(
        [jnp.concatenate([w_ref[3 * a + b] for b in range(3)], axis=1) for a in range(3)], axis=0
    )


def clear_ends(ref):
    last = ref.shape[0] - 1
    ref[0] = jnp.zeros(ref.shape[1:], ref.dtype)
    ref[last] = jnp.zeros(ref.shape[1:], ref.dtype)


def put_rows(ref, at, value):
    count, cols, ch = value.shape
    ref[1 + at : 1 + at + count, cols:, :] = jnp.zeros((count, ref.shape[1] - cols, ch), ref.dtype)
    ref[1 + at : 1 + at + count, :cols, :] = value


def spatial_fwd_kernel(
    rows_step, x_hbm, w_hbm, cot_hbm, send_hbm,
    x_in, w_ref, xs, sends, in_sems, w_sem, cot_sem, send_sems,
):
    rows, cols, ch = x_in.shape
    wide = xs.shape[1]
    parts = in_sems.shape[0]
    many = rows // parts

    def part(n):
        return pl.ds(n * many, many)

    loads = [
        pltpu.make_async_copy(x_hbm.at[part(n)], x_in.at[part(n)], in_sems.at[n]) for n in range(parts)
    ]
    stores = [
        pltpu.make_async_copy(sends.at[part(n)], send_hbm.at[part(n)], send_sems.at[n])
        for n in range(parts)
    ]
    w_load = pltpu.make_async_copy(w_hbm, w_ref, w_sem.at[0])
    cot_load = pltpu.make_async_copy(cot_hbm, sends.at[:, 1], cot_sem.at[0])
    for load in [loads[0], w_load] + loads[1:] + [cot_load]:
        load.start()
    clear_ends(xs)

    def bring(n):
        loads[n].wait()
        put_rows(xs, n * many, x_in[n * many : (n + 1) * many])

    bring(0)
    w_load.wait()
    weight = forward_weight(w_ref)
    for n in range(parts):
        if n + 1 < parts:
            bring(n + 1)
        for at in range(n * many, (n + 1) * many, rows_step):
            act, _ = silu_parts(spatial_pre(xs, weight, at, rows_step))
            sends[at : at + rows_step, 0] = act.astype(BF16).reshape(rows_step, wide, ch)[:, :cols]
        if n == 0:
            cot_load.wait()
        stores[n].start()
    for store in stores:
        store.wait()


def spatial_slope_kernel(rows_step, x_ref, w_ref, slope_hbm, xs, slopes, sem):
    rows, cols, ch = x_ref.shape
    wide = xs.shape[1]
    clear_ends(xs)
    put_rows(xs, 0, x_ref[...])
    weight = forward_weight(w_ref)
    for at in range(0, rows, rows_step):
        _, slope = silu_parts(spatial_pre(xs, weight, at, rows_step))
        slopes[at : at + rows_step] = slope.astype(BF16).reshape(rows_step, wide, ch)[:, :cols]
    store = pltpu.make_async_copy(slopes, slope_hbm.at[0], sem.at[0])
    store.start()
    store.wait()


def hand_out(here_ref, total_ref, pieces):
    for peer, piece in enumerate(pieces):
        piece[...] = total_ref[jnp.bitwise_xor(here_ref[1], peer)].astype(piece.dtype)


def taps_up(gs, at, rows_step):
    wide, ch = gs.shape[1:]
    return jnp.concatenate(
        [gs[at + 2 - a : at + 2 - a + rows_step].reshape(rows_step * wide, ch) for a in range(3)],
        axis=1,
    )


def fill_grads(rows_step, gs, got_ref, slope_ref):
    clear_ends(gs)
    for at in range(0, got_ref.shape[0], rows_step):
        grads = got_ref[at : at + rows_step].astype(F32)
        slopes = slope_ref[at : at + rows_step].astype(F32)
        put_rows(gs, at, (grads * slopes).astype(BF16))


def spatial_wgrad_kernel(rows_step, scale, here_ref, got_ref, slope_hbm, x_ref, *rest):
    pieces, (gs, slopes, cat_ref, total_ref, sem) = rest[:-5], rest[-5:]
    rows, cols, ch = got_ref.shape
    wide = gs.shape[1]
    flat = rows_step * wide
    load = pltpu.make_async_copy(slope_hbm.at[0], slopes, sem.at[0])
    load.start()
    pad = jnp.zeros((rows_step, wide - cols, ch), F32)

    def columns(at):
        x = jnp.concatenate([x_ref[at : at + rows_step].astype(F32), pad], axis=1).reshape(flat, ch)
        x_cat = jnp.concatenate([roll_rows(x, 1), x, roll_rows(x, -1)], axis=1)
        return x_cat.T.astype(BF16)

    early = cat_ref.shape[1] // flat
    for n in range(early):
        cat_ref[:, n * flat : (n + 1) * flat] = columns(n * rows_step)
    load.wait()
    fill_grads(rows_step, gs, got_ref, slopes)
    total = jnp.zeros((3 * ch, 3 * ch), F32)
    for n, at in enumerate(range(0, rows, rows_step)):
        cat = cat_ref[:, n * flat : (n + 1) * flat] if n < early else columns(at)
        total = total + mm(cat, taps_up(gs, at, rows_step))
    total_ref[...] = (
        jnp.concatenate(
            [
                total[b * ch : (b + 1) * ch, a * ch : (a + 1) * ch]
                for a in range(3)
                for b in range(3)
            ],
            axis=0,
        )
        * scale
    ).reshape(total_ref.shape)
    hand_out(here_ref, total_ref, pieces)


def spatial_back_kernel(rows_step, w_ref, got_ref, slope_hbm, back_ref, gs, slopes, sem):
    rows, cols, ch = back_ref.shape
    wide = gs.shape[1]
    load = pltpu.make_async_copy(slope_hbm.at[0], slopes, sem.at[0])
    load.start()
    weight = jnp.concatenate(
        [
            jnp.concatenate([w_ref[3 * a + b].astype(F32).T.astype(BF16) for b in range(3)], axis=1)
            for a in range(3)
        ],
        axis=0,
    )
    load.wait()
    fill_grads(rows_step, gs, got_ref, slopes)
    for at in range(0, rows, rows_step):
        y = mm(taps_up(gs, at, rows_step), weight)
        back = y[:, ch : 2 * ch] + roll_rows(y[:, :ch], -1) + roll_rows(y[:, 2 * ch :], 1)
        back_ref[at : at + rows_step] = back.astype(BF16).reshape(rows_step, wide, ch)[:, :cols]


def clear_halo(pad_ref, frames):
    zeros = jnp.zeros((HALO,) + pad_ref.shape[1:], pad_ref.dtype)
    pad_ref[:HALO] = zeros
    pad_ref[HALO + frames :] = zeros


def taps_of(pad_ref, at, count, step_size, sign):
    high, ch = pad_ref.shape[1:]
    pieces = [
        pad_ref[pl.ds(HALO + at + sign * (k - 2) * step_size, count)].reshape(count * high, ch)
        for k in range(TAPS)
    ]
    return jnp.concatenate(pieces, axis=1)


def temporal_kernel(
    step_frames, dil_ref, key_ref, got_ref, tw_hbm, uw_hbm,
    grad_hbm, kept_hbm, united_hbm,
    a0, a1, feat, cots, g0, g1, slope0, slope1, united_ref, grad_ref, tw_ref, uw_ref,
    sems, in_sems, out_sems,
):
    frames, _, block, ch = got_ref.shape
    high = feat.shape[1]
    loads = [
        pltpu.make_async_copy(source, ref, in_sems.at[n])
        for n, (source, ref) in enumerate(((tw_hbm, tw_ref), (uw_hbm, uw_ref)))
    ]
    for load in loads:
        load.start()
    stores = [
        pltpu.make_async_copy(
            grad_ref.at[pl.ds(at, step_frames)], grad_hbm.at[pl.ds(at, step_frames)], out_sems.at[n]
        )
        for n, at in enumerate(range(0, frames, step_frames))
    ]
    segs = key_ref.shape[0]
    seg_frames = frames // segs
    inside = pl.ds(HALO, frames)
    copies = [
        pltpu.make_async_copy(source, target, sems.at[n])
        for n, (source, target) in enumerate(
            (
                (a1.at[inside], kept_hbm.at[0]),
                (feat, kept_hbm.at[1]),
                (g1.at[inside], kept_hbm.at[2]),
                (g0.at[inside], kept_hbm.at[3]),
                (a0.at[inside], kept_hbm.at[4]),
                (cots, kept_hbm.at[5]),
                (united_ref, united_hbm.at[0]),
            )
        )
    ]
    for ref in (a0, a1, g0, g1):
        clear_halo(ref, frames)
    if high > block:
        pad = jnp.zeros((frames, high - block, ch), BF16)
        a0[HALO : HALO + frames, block:, :] = pad
        cots[:, block:, :] = pad
    a0[HALO : HALO + frames, :block, :] = got_ref[:, 0]
    copies[4].start()
    for load in loads:
        load.wait()
    for layer, (source, target, slopes) in enumerate(((a0, a1, slope0), (a1, feat, slope1))):
        step_size = dil_ref[layer]
        weight = jnp.concatenate([tw_ref[layer, k] for k in range(TAPS)], axis=0)
        first = HALO if layer == 0 else 0
        for at in range(0, frames, step_frames):
            pre = mm(taps_of(source, at, step_frames, step_size, 1), weight)
            act, slope = silu_parts(pre)
            target[first + at : first + at + step_frames] = act.astype(BF16).reshape(
                step_frames, high, ch
            )
            slopes[at : at + step_frames] = slope.reshape(step_frames, high, ch)
        copies[layer].start()
    cots[:, :block, :] = got_ref[:, 1]
    copies[5].start()
    keys = jnp.concatenate([feat[seg * seg_frames + key_ref[seg]] for seg in range(segs)], axis=0)
    key_parts = mm(keys, uw_ref[1]).reshape(segs, high, ch)
    totals = jnp.concatenate(
        [
            jnp.sum(cots[seg * seg_frames : (seg + 1) * seg_frames].astype(F32), axis=0)
            for seg in range(segs)
        ],
        axis=0,
    )
    key_terms = mm_nt(jnp.concatenate(three_parts(totals), axis=0), uw_ref[1])
    key_terms = jnp.sum(key_terms.reshape(3, segs, high, ch), axis=0)
    for seg in range(segs):
        low, top = seg * seg_frames, (seg + 1) * seg_frames
        main = mm(feat[low:top].reshape(seg_frames * high, ch), uw_ref[0]).reshape(
            seg_frames, high, ch
        )
        united_ref[low:top] = (main + key_parts[seg][None]).astype(BF16)[:, :block]
        grad_feat = mm_nt(cots[low:top].reshape(seg_frames * high, ch), uw_ref[0]).reshape(
            seg_frames, high, ch
        )
        for n in range(seg_frames):
            grad = grad_feat[n] + jnp.where(key_ref[seg] == n, key_terms[seg], 0.0)
            g1[HALO + low + n] = (grad * slope1[low + n]).astype(BF16)
    copies[6].start()
    for layer, source in ((1, g1), (0, g0)):
        copies[3 - layer].start()
        step_size = dil_ref[layer]
        weight = jnp.concatenate(
            [tw_ref[layer, k].astype(F32).T.astype(BF16) for k in range(TAPS)], axis=0
        )
        for n, at in enumerate(range(0, frames, step_frames)):
            grad = mm(taps_of(source, at, step_frames, step_size, -1), weight).reshape(
                step_frames, high, ch
            )
            if layer == 1:
                g0[HALO + at : HALO + at + step_frames] = (
                    grad * slope0[at : at + step_frames]
                ).astype(BF16)
            else:
                grad_ref[at : at + step_frames] = grad.astype(BF16)[:, :block]
                stores[n].start()
    for copy in copies + stores:
        copy.wait()


def temporal_wgrad_kernel(
    step_frames, scale, here_ref, dil_ref, key_ref,
    kept_hbm, united_kept, united_hbm, *rest
):
    pieces, (a0, g0, a1, g1, feat, cots, united, total_ref, sems) = rest[:-9], rest[-9:]
    frames, high, ch = feat.shape
    segs = key_ref.shape[0]
    seg_frames = frames // segs
    rows = step_frames * high
    inside = pl.ds(HALO, frames)
    copies = [
        pltpu.make_async_copy(source, target, sems.at[n])
        for n, (source, target) in enumerate(
            (
                (kept_hbm.at[4], a0.at[inside]),
                (kept_hbm.at[3], g0),
                (kept_hbm.at[0], a1.at[inside]),
                (kept_hbm.at[2], g1),
                (kept_hbm.at[1], feat),
                (kept_hbm.at[5], cots),
                (united_kept.at[0], united),
            )
        )
    ]
    for copy in copies:
        copy.start()
    clear_halo(a0, frames)
    clear_halo(a1, frames)
    totals = []
    for layer, acts, grads in ((0, a0, g0), (1, a1, g1)):
        copies[2 * layer].wait()
        copies[2 * layer + 1].wait()
        total = jnp.zeros((TAPS * ch, ch), F32)
        for at in range(0, frames, step_frames):
            total = total + mm_tn(
                taps_of(acts, at, step_frames, dil_ref[layer], 1),
                grads[at : at + step_frames].reshape(rows, ch),
            )
        totals.append(total)
    for copy in copies[4:]:
        copy.wait()
    united_copy = pltpu.make_async_copy(united, united_hbm, sems.at[len(copies)])
    united_copy.start()
    total = jnp.zeros((ch, ch), F32)
    for at in range(0, frames, step_frames):
        total = total + mm_tn(
            feat[at : at + step_frames].reshape(rows, ch),
            cots[at : at + step_frames].reshape(rows, ch),
        )
    keyed = jnp.zeros((ch, ch), F32)
    for seg in range(segs):
        low, top = seg * seg_frames, (seg + 1) * seg_frames
        key = feat[low + key_ref[seg]]
        seg_cot = jnp.sum(cots[low:top].astype(F32), axis=0)
        keyed = keyed + sum(mm_tn(key, part) for part in three_parts(seg_cot))
    peers = len(pieces)
    split = LAYERS * TAPS * ch // peers
    total_ref[:, :split] = (jnp.concatenate(totals, axis=0) * scale).reshape(peers, split, ch)
    total_ref[:, split:] = (jnp.concatenate([total, keyed], axis=0) * scale).reshape(
        peers, 2 * ch // peers, ch
    )
    hand_out(here_ref, total_ref, pieces)
    united_copy.wait()


def sum_kernel(*refs):
    refs[-1][...] = sum(ref[...].astype(F32) for ref in refs[:-1]).astype(refs[-1].dtype)


def join_kernel(first_ref, *refs):
    out_ref = refs[-1]
    split = first_ref.shape[0]
    out_ref[:split] = first_ref[...]
    out_ref[split:] = sum(ref[...].astype(F32) for ref in refs[:-1]).astype(out_ref.dtype)


def deal_kernel(pieces_ref, united_hbm, *refs):
    outs_hbm, united_out, outs, sems = refs[:3], refs[3], refs[4:7], refs[7]
    copies = [pltpu.make_async_copy(united_hbm, united_out, sems.at[3])]
    copies[0].start()
    at = 0
    for n, out_ref in enumerate(outs):
        count = out_ref.shape[1]
        out_ref[...] = pieces_ref[:, at : at + count].astype(F32)
        copies.append(pltpu.make_async_copy(out_ref, outs_hbm[n], sems.at[n]))
        copies[-1].start()
        at += count
    for copy in copies:
        copy.wait()


def exchange(blocks):
    return lax.all_to_all(blocks, AXES, split_axis=0, concat_axis=0, tiled=True)


def flip(value, peer):
    size = lax.axis_size("grp")
    return lax.ppermute(value, "grp", [(i, i ^ peer) for i in range(size)])


def meet_in_seg(value, bit):
    size = lax.axis_size("seg")
    return lax.ppermute(value, "seg", [(i, i ^ bit) for i in range(size)])


def sum_of(parts):
    shape = parts[0].shape
    return call(
        sum_kernel, [(shape, BF16, VMEM)], [], 0, len(parts) * 2 * shape[0] * shape[1],
        [(part, VMEM) for part in parts], SMALL_VMEM,
    )[0]


def reduce_in_grp(pieces):
    return sum_of([flip(piece, peer) if peer else piece for peer, piece in enumerate(pieces)])


def local(
    frames_in, spatial_weight, temporal_weight, uniting_weight, key_index, dilation, cotangent
):
    held, rows, cols, ch = frames_in.shape
    assert held == 1
    pixels = rows * cols
    peers = lax.axis_size("grp")
    segs = lax.axis_size("seg")
    devices = segs * peers
    frames = held * devices
    block = pixels // devices
    split = cols // block
    wide = round_up(cols + 1, 16)
    high = round_up(block, 16)
    rows_step = next(n for n in (4, 2, 1) if rows % n == 0)
    steps = rows // rows_step
    parts = next(n for n in (4, 2, 1) if rows % (n * rows_step) == 0)
    step_frames, narrow_step = (
        max(n for n in range(1, frames + 1) if frames % n == 0 and n * high <= most)
        for most in (512, 256)
    )
    scale = float((frames * pixels) ** -0.5)
    here = jnp.stack([lax.axis_index("seg"), lax.axis_index("grp")]).astype(jnp.int32)
    space_rows, time_rows, unite_rows = (n * ch // peers for n in (9, LAYERS * TAPS, 2))

    (send,) = call(
        functools.partial(spatial_fwd_kernel, rows_step),
        [((rows, 2, cols, ch), BF16, HBM)],
        [
            pltpu.VMEM((rows, cols, ch), BF16),
            pltpu.VMEM(spatial_weight.shape, BF16),
            pltpu.VMEM((rows + 2, wide, ch), BF16),
            pltpu.VMEM((rows, 2, cols, ch), BF16),
            pltpu.SemaphoreType.DMA((parts,)),
            pltpu.SemaphoreType.DMA((1,)),
            pltpu.SemaphoreType.DMA((1,)),
            pltpu.SemaphoreType.DMA((parts,)),
        ],
        2 * 9 * pixels * ch * ch,
        pixels * ch * 8,
        [(frames_in[0], HBM), (spatial_weight, HBM), (cotangent[0], HBM)],
    )
    send, frame = lax.optimization_barrier((send, frames_in[0]))
    send = send.reshape(rows, 2, split, block, ch).swapaxes(1, 2).reshape(devices, 2, block, ch)
    got = exchange(send)
    (space_slope,) = call(
        functools.partial(spatial_slope_kernel, rows_step),
        [((SPARE, rows, cols, ch), BF16, HBM)],
        [
            pltpu.VMEM((rows + 2, wide, ch), BF16),
            pltpu.VMEM((rows, cols, ch), BF16),
            pltpu.SemaphoreType.DMA((1,)),
        ],
        2 * 9 * pixels * ch * ch,
        pixels * ch * 4,
        [(frame, VMEM), (spatial_weight, VMEM)],
    )
    got, space_slope = lax.optimization_barrier((got, space_slope))

    padded = (frames + 2 * HALO, high, ch)
    whole = (frames, high, ch)
    grad_send, kept, united_kept = call(
        functools.partial(temporal_kernel, narrow_step),
        [
            ((frames, block, ch), BF16, HBM),
            ((SPARE,) + whole, BF16, HBM),
            ((SPARE, frames, block, ch), BF16, HBM),
        ],
        [
            pltpu.VMEM(padded, BF16),
            pltpu.VMEM(padded, BF16),
            pltpu.VMEM(whole, BF16),
            pltpu.VMEM(whole, BF16),
            pltpu.VMEM(padded, BF16),
            pltpu.VMEM(padded, BF16),
            pltpu.VMEM(whole, F32),
            pltpu.VMEM(whole, F32),
            pltpu.VMEM((frames, block, ch), BF16),
            pltpu.VMEM((frames, block, ch), BF16),
            pltpu.VMEM(temporal_weight.shape, BF16),
            pltpu.VMEM(uniting_weight.shape, BF16),
            pltpu.SemaphoreType.DMA((7,)),
            pltpu.SemaphoreType.DMA((2,)),
            pltpu.SemaphoreType.DMA((frames // narrow_step,)),
        ],
        2 * 22 * frames * block * ch * ch,
        frames * block * ch * 18,
        [
            (dilation, SMEM), (key_index, SMEM), (got, VMEM),
            (temporal_weight, HBM), (uniting_weight, HBM),
        ],
        MID_VMEM,
    )
    grad_time = exchange(grad_send).reshape(rows, cols, ch)
    united_send, *time_pieces = call(
        functools.partial(temporal_wgrad_kernel, step_frames, scale),
        [((frames, block, ch), BF16, HBM)]
        + [((time_rows + unite_rows, ch), BF16, VMEM)] * peers,
        [
            pltpu.VMEM(padded, BF16),
            pltpu.VMEM(whole, BF16),
            pltpu.VMEM(padded, BF16),
            pltpu.VMEM(whole, BF16),
            pltpu.VMEM(whole, BF16),
            pltpu.VMEM(whole, BF16),
            pltpu.VMEM((frames, block, ch), BF16),
            pltpu.VMEM((peers, time_rows + unite_rows, ch), F32),
            pltpu.SemaphoreType.DMA((8,)),
        ],
        2 * 12 * frames * block * ch * ch,
        frames * block * ch * 14,
        [
            (here, SMEM), (dilation, SMEM), (key_index, SMEM),
            (kept, HBM), (united_kept, HBM),
        ],
    )
    time_sum = reduce_in_grp(time_pieces)
    time_sum, grad_time = lax.optimization_barrier((time_sum, grad_time))
    united_send, grad_time = lax.optimization_barrier((united_send, grad_time))
    united = exchange(united_send)
    space_pieces = call(
        functools.partial(spatial_wgrad_kernel, rows_step, scale),
        [((space_rows, ch), BF16, VMEM)] * peers,
        [
            pltpu.VMEM((rows + 2, wide, ch), BF16),
            pltpu.VMEM((rows, cols, ch), BF16),
            pltpu.VMEM((3 * ch, min(3, steps) * rows_step * wide), BF16),
            pltpu.VMEM((peers, space_rows, ch), F32),
            pltpu.SemaphoreType.DMA((1,)),
        ],
        2 * 9 * pixels * ch * ch,
        pixels * ch * 8,
        [(here, SMEM), (grad_time, VMEM), (space_slope, HBM), (frame, VMEM)],
        MID_VMEM,
    )
    (back,) = call(
        functools.partial(spatial_back_kernel, rows_step),
        [((rows, cols, ch), BF16, VMEM)],
        [
            pltpu.VMEM((rows + 2, wide, ch), BF16),
            pltpu.VMEM((rows, cols, ch), BF16),
            pltpu.SemaphoreType.DMA((1,)),
        ],
        2 * 9 * pixels * ch * ch,
        pixels * ch * 6,
        [(spatial_weight, VMEM), (grad_time, VMEM), (space_slope, HBM)],
        MID_VMEM,
    )
    space_parts = [flip(part, peer) if peer else part for peer, part in enumerate(space_pieces)]
    (plane,) = call(
        join_kernel,
        [((time_rows + unite_rows + space_rows, ch), BF16, VMEM)],
        [],
        0,
        2 * (peers + 10) * space_rows * ch,
        [(time_sum, VMEM)] + [(part, VMEM) for part in space_parts],
        SMALL_VMEM,
    )
    piece = plane
    bits = [1 << n for n in range((segs - 1).bit_length())]
    for bit in bits:
        other = meet_in_seg(piece, bit)
        if bit == bits[0]:
            other, back = lax.optimization_barrier((other, back))
        piece = sum_of([piece, other])
    *grads, united = call(
        deal_kernel,
        [((peers, count, ch), F32, HBM) for count in (time_rows, unite_rows, space_rows)]
        + [((frames, block, ch), BF16, HBM)],
        [pltpu.VMEM((peers, count, ch), F32) for count in (time_rows, unite_rows, space_rows)]
        + [pltpu.SemaphoreType.DMA((4,))],
        0,
        6 * 21 * ch * ch,
        [(lax.all_gather(piece, "grp", axis=0), VMEM), (united, HBM)],
        SMALL_VMEM,
    )
    return (
        united.reshape(frames_in.shape),
        back[None],
        grads[2].reshape(9, ch, ch),
        grads[0].reshape(LAYERS, TAPS, ch, ch),
        grads[1].reshape(2, ch, ch),
    )


def solution(mesh):
    frame_spec = P(AXES, None, None, None)
    return jax.shard_map(
        local,
        mesh=mesh,
        in_specs=(frame_spec, P(), P(), P(), P(), P(), frame_spec),
        out_specs=(frame_spec, frame_spec, P(), P(), P()),
        check_vma=False,
    )
```

```python
import functools

import jax
import jax.numpy as jnp
from jax import lax
from jax.experimental import pallas as pl
from jax.experimental.pallas import tpu as pltpu
from jax.sharding import PartitionSpec as P

LAYERS = 2
TAPS = 5
DMAX = 8
HALO = 2 * DMAX
AXES = ("seg", "grp")
BF16 = jnp.bfloat16
F32 = jnp.float32
BIG_VMEM = 60 * 1024 * 1024
MID_VMEM = 40 * 1024 * 1024
SPARE = 28
SMALL_VMEM = 16 * 1024 * 1024


def round_up(value, step):
    return -(-value // step) * step


def silu_parts(value):
    sigma = 0.5 * jnp.tanh(0.5 * value) + 0.5
    act = value * sigma
    return act, sigma + act * (1.0 - sigma)


def mm(left, right):
    return jnp.dot(left, right, preferred_element_type=F32)


def mm_nt(left, right):
    return lax.dot_general(left, right, (((1,), (1,)), ((), ())), preferred_element_type=F32)


def mm_tn(left, right):
    return lax.dot_general(left, right, (((0,), (0,)), ((), ())), preferred_element_type=F32)


def three_parts(value):
    high = value.astype(BF16)
    rest = value - high.astype(F32)
    middle = rest.astype(BF16)
    return high, middle, (rest - middle.astype(F32)).astype(BF16)


VMEM = pl.BlockSpec(memory_space=pltpu.VMEM)
SMEM = pl.BlockSpec(memory_space=pltpu.SMEM)
HBM = pl.BlockSpec(memory_space=pltpu.HBM)


def call(kernel, outs, scratch, flops, moved, args, vmem=BIG_VMEM):
    return pl.pallas_call(
        kernel,
        out_shape=[jax.ShapeDtypeStruct(shape, kind) for shape, kind, _ in outs],
        in_specs=[spec for _, spec in args],
        out_specs=[spec for _, _, spec in outs],
        scratch_shapes=scratch,
        compiler_params=pltpu.CompilerParams(vmem_limit_bytes=vmem),
        cost_estimate=pl.CostEstimate(flops=flops, bytes_accessed=moved, transcendentals=0),
    )(*[value for value, _ in args])


def roll_rows(value, shift):
    return pltpu.roll(value, shift % value.shape[0], 0)


def spatial_pre(xs, weight, at, rows_step):
    wide, ch = xs.shape[1:]
    flat = rows_step * wide
    left = jnp.concatenate(
        [xs[at + a : at + a + rows_step].reshape(flat, ch) for a in range(3)], axis=1
    )
    y = mm(left, weight)
    return y[:, ch : 2 * ch] + roll_rows(y[:, :ch], 1) + roll_rows(y[:, 2 * ch :], -1)


def forward_weight(w_ref):
    return jnp.concatenate(
        [jnp.concatenate([w_ref[3 * a + b] for b in range(3)], axis=1) for a in range(3)], axis=0
    )


def clear_ends(ref):
    last = ref.shape[0] - 1
    ref[0] = jnp.zeros(ref.shape[1:], ref.dtype)
    ref[last] = jnp.zeros(ref.shape[1:], ref.dtype)


def put_rows(ref, at, value):
    count, cols, ch = value.shape
    ref[1 + at : 1 + at + count, cols:, :] = jnp.zeros((count, ref.shape[1] - cols, ch), ref.dtype)
    ref[1 + at : 1 + at + count, :cols, :] = value


def spatial_fwd_kernel(
    rows_step, x_hbm, w_hbm, cot_hbm, send_hbm,
    x_in, w_ref, xs, sends, in_sems, w_sem, cot_sem, send_sems,
):
    rows, cols, ch = x_in.shape
    wide = xs.shape[1]
    parts = in_sems.shape[0]
    many = rows // parts

    def part(n):
        return pl.ds(n * many, many)

    loads = [
        pltpu.make_async_copy(x_hbm.at[part(n)], x_in.at[part(n)], in_sems.at[n]) for n in range(parts)
    ]
    stores = [
        pltpu.make_async_copy(sends.at[part(n)], send_hbm.at[part(n)], send_sems.at[n])
        for n in range(parts)
    ]
    w_load = pltpu.make_async_copy(w_hbm, w_ref, w_sem.at[0])
    cot_load = pltpu.make_async_copy(cot_hbm, sends.at[:, 1], cot_sem.at[0])
    for load in [loads[0], w_load] + loads[1:] + [cot_load]:
        load.start()
    clear_ends(xs)

    def bring(n):
        loads[n].wait()
        put_rows(xs, n * many, x_in[n * many : (n + 1) * many])

    bring(0)
    w_load.wait()
    weight = forward_weight(w_ref)
    for n in range(parts):
        if n + 1 < parts:
            bring(n + 1)
        for at in range(n * many, (n + 1) * many, rows_step):
            act, _ = silu_parts(spatial_pre(xs, weight, at, rows_step))
            sends[at : at + rows_step, 0] = act.astype(BF16).reshape(rows_step, wide, ch)[:, :cols]
        if n == 0:
            cot_load.wait()
        stores[n].start()
    for store in stores:
        store.wait()


def spatial_slope_kernel(rows_step, x_ref, w_ref, slope_hbm, xs, slopes, sem):
    rows, cols, ch = x_ref.shape
    wide = xs.shape[1]
    clear_ends(xs)
    put_rows(xs, 0, x_ref[...])
    weight = forward_weight(w_ref)
    for at in range(0, rows, rows_step):
        _, slope = silu_parts(spatial_pre(xs, weight, at, rows_step))
        slopes[at : at + rows_step] = slope.astype(BF16).reshape(rows_step, wide, ch)[:, :cols]
    store = pltpu.make_async_copy(slopes, slope_hbm.at[0], sem.at[0])
    store.start()
    store.wait()


def hand_out(here_ref, total_ref, pieces):
    for peer, piece in enumerate(pieces):
        piece[...] = total_ref[jnp.bitwise_xor(here_ref[1], peer)].astype(piece.dtype)


def taps_up(gs, at, rows_step):
    wide, ch = gs.shape[1:]
    return jnp.concatenate(
        [gs[at + 2 - a : at + 2 - a + rows_step].reshape(rows_step * wide, ch) for a in range(3)],
        axis=1,
    )


def fill_grads(rows_step, gs, got_ref, slope_ref):
    clear_ends(gs)
    for at in range(0, got_ref.shape[0], rows_step):
        grads = got_ref[at : at + rows_step].astype(F32)
        slopes = slope_ref[at : at + rows_step].astype(F32)
        put_rows(gs, at, (grads * slopes).astype(BF16))


def spatial_wgrad_kernel(rows_step, scale, here_ref, got_ref, slope_hbm, x_ref, *rest):
    pieces, (gs, slopes, cat_ref, total_ref, sem) = rest[:-5], rest[-5:]
    rows, cols, ch = got_ref.shape
    wide = gs.shape[1]
    flat = rows_step * wide
    load = pltpu.make_async_copy(slope_hbm.at[0], slopes, sem.at[0])
    load.start()
    pad = jnp.zeros((rows_step, wide - cols, ch), F32)

    def columns(at):
        x = jnp.concatenate([x_ref[at : at + rows_step].astype(F32), pad], axis=1).reshape(flat, ch)
        x_cat = jnp.concatenate([roll_rows(x, 1), x, roll_rows(x, -1)], axis=1)
        return x_cat.T.astype(BF16)

    early = cat_ref.shape[1] // flat
    for n in range(early):
        cat_ref[:, n * flat : (n + 1) * flat] = columns(n * rows_step)
    load.wait()
    fill_grads(rows_step, gs, got_ref, slopes)
    total = jnp.zeros((3 * ch, 3 * ch), F32)
    for n, at in enumerate(range(0, rows, rows_step)):
        cat = cat_ref[:, n * flat : (n + 1) * flat] if n < early else columns(at)
        total = total + mm(cat, taps_up(gs, at, rows_step))
    total_ref[...] = (
        jnp.concatenate(
            [
                total[b * ch : (b + 1) * ch, a * ch : (a + 1) * ch]
                for a in range(3)
                for b in range(3)
            ],
            axis=0,
        )
        * scale
    ).reshape(total_ref.shape)
    hand_out(here_ref, total_ref, pieces)


def spatial_back_kernel(rows_step, w_ref, got_ref, slope_hbm, back_ref, gs, slopes, sem):
    rows, cols, ch = back_ref.shape
    wide = gs.shape[1]
    load = pltpu.make_async_copy(slope_hbm.at[0], slopes, sem.at[0])
    load.start()
    weight = jnp.concatenate(
        [
            jnp.concatenate([w_ref[3 * a + b].astype(F32).T.astype(BF16) for b in range(3)], axis=1)
            for a in range(3)
        ],
        axis=0,
    )
    load.wait()
    fill_grads(rows_step, gs, got_ref, slopes)
    for at in range(0, rows, rows_step):
        y = mm(taps_up(gs, at, rows_step), weight)
        back = y[:, ch : 2 * ch] + roll_rows(y[:, :ch], -1) + roll_rows(y[:, 2 * ch :], 1)
        back_ref[at : at + rows_step] = back.astype(BF16).reshape(rows_step, wide, ch)[:, :cols]


def clear_halo(pad_ref, frames):
    zeros = jnp.zeros((HALO,) + pad_ref.shape[1:], pad_ref.dtype)
    pad_ref[:HALO] = zeros
    pad_ref[HALO + frames :] = zeros


def taps_of(pad_ref, at, count, step_size, sign):
    high, ch = pad_ref.shape[1:]
    pieces = [
        pad_ref[pl.ds(HALO + at + sign * (k - 2) * step_size, count)].reshape(count * high, ch)
        for k in range(TAPS)
    ]
    return jnp.concatenate(pieces, axis=1)


def temporal_kernel(
    step_frames, dil_ref, key_ref, got_ref, tw_hbm, uw_hbm,
    grad_hbm, kept_hbm, united_hbm,
    a0, a1, feat, cots, g0, g1, slope0, slope1, united_ref, grad_ref, tw_ref, uw_ref,
    sems, in_sems, out_sems,
):
    frames, _, block, ch = got_ref.shape
    high = feat.shape[1]
    loads = [
        pltpu.make_async_copy(source, ref, in_sems.at[n])
        for n, (source, ref) in enumerate(((tw_hbm, tw_ref), (uw_hbm, uw_ref)))
    ]
    for load in loads:
        load.start()
    parts = out_sems.shape[0]
    many = frames // parts
    stores = [
        pltpu.make_async_copy(
            grad_ref.at[pl.ds(n * many, many)], grad_hbm.at[pl.ds(n * many, many)], out_sems.at[n]
        )
        for n in range(parts)
    ]
    segs = key_ref.shape[0]
    seg_frames = frames // segs
    inside = pl.ds(HALO, frames)
    copies = [
        pltpu.make_async_copy(source, target, sems.at[n])
        for n, (source, target) in enumerate(
            (
                (a1.at[inside], kept_hbm.at[0]),
                (feat, kept_hbm.at[1]),
                (g1.at[inside], kept_hbm.at[2]),
                (g0.at[inside], kept_hbm.at[3]),
                (a0.at[inside], kept_hbm.at[4]),
                (cots, kept_hbm.at[5]),
                (united_ref, united_hbm.at[0]),
            )
        )
    ]
    for ref in (a0, a1, g0, g1):
        clear_halo(ref, frames)
    if high > block:
        pad = jnp.zeros((frames, high - block, ch), BF16)
        a0[HALO : HALO + frames, block:, :] = pad
        cots[:, block:, :] = pad
    a0[HALO : HALO + frames, :block, :] = got_ref[:, 0]
    copies[4].start()
    for load in loads:
        load.wait()
    for layer, (source, target, slopes) in enumerate(((a0, a1, slope0), (a1, feat, slope1))):
        step_size = dil_ref[layer]
        weight = jnp.concatenate([tw_ref[layer, k] for k in range(TAPS)], axis=0)
        first = HALO if layer == 0 else 0
        for at in range(0, frames, step_frames):
            pre = mm(taps_of(source, at, step_frames, step_size, 1), weight)
            act, slope = silu_parts(pre)
            target[first + at : first + at + step_frames] = act.astype(BF16).reshape(
                step_frames, high, ch
            )
            slopes[at : at + step_frames] = slope.reshape(step_frames, high, ch)
        copies[layer].start()
    cots[:, :block, :] = got_ref[:, 1]
    copies[5].start()
    keys = jnp.concatenate([feat[seg * seg_frames + key_ref[seg]] for seg in range(segs)], axis=0)
    key_parts = mm(keys, uw_ref[1]).reshape(segs, high, ch)
    totals = jnp.concatenate(
        [
            jnp.sum(cots[seg * seg_frames : (seg + 1) * seg_frames].astype(F32), axis=0)
            for seg in range(segs)
        ],
        axis=0,
    )
    key_terms = mm_nt(jnp.concatenate(three_parts(totals), axis=0), uw_ref[1])
    key_terms = jnp.sum(key_terms.reshape(3, segs, high, ch), axis=0)
    for seg in range(segs):
        low, top = seg * seg_frames, (seg + 1) * seg_frames
        main = mm(feat[low:top].reshape(seg_frames * high, ch), uw_ref[0]).reshape(
            seg_frames, high, ch
        )
        united_ref[low:top] = (main + key_parts[seg][None]).astype(BF16)[:, :block]
        grad_feat = mm_nt(cots[low:top].reshape(seg_frames * high, ch), uw_ref[0]).reshape(
            seg_frames, high, ch
        )
        for n in range(seg_frames):
            grad = grad_feat[n] + jnp.where(key_ref[seg] == n, key_terms[seg], 0.0)
            g1[HALO + low + n] = (grad * slope1[low + n]).astype(BF16)
    copies[6].start()
    for layer, source in ((1, g1), (0, g0)):
        copies[3 - layer].start()
        step_size = dil_ref[layer]
        weight = jnp.concatenate(
            [tw_ref[layer, k].astype(F32).T.astype(BF16) for k in range(TAPS)], axis=0
        )
        for at in range(0, frames, step_frames):
            grad = mm(taps_of(source, at, step_frames, step_size, -1), weight).reshape(
                step_frames, high, ch
            )
            if layer == 1:
                g0[HALO + at : HALO + at + step_frames] = (
                    grad * slope0[at : at + step_frames]
                ).astype(BF16)
            else:
                grad_ref[at : at + step_frames] = grad.astype(BF16)[:, :block]
                if (at + step_frames) % many == 0:
                    stores[at // many].start()
    for copy in copies + stores:
        copy.wait()


def temporal_wgrad_kernel(
    step_frames, scale, here_ref, dil_ref, key_ref,
    kept_hbm, united_kept, united_hbm, *rest
):
    pieces, (a0, g0, a1, g1, feat, cots, united, total_ref, sems) = rest[:-9], rest[-9:]
    frames, high, ch = feat.shape
    segs = key_ref.shape[0]
    seg_frames = frames // segs
    rows = step_frames * high
    inside = pl.ds(HALO, frames)
    copies = [
        pltpu.make_async_copy(source, target, sems.at[n])
        for n, (source, target) in enumerate(
            (
                (kept_hbm.at[4], a0.at[inside]),
                (kept_hbm.at[3], g0),
                (kept_hbm.at[0], a1.at[inside]),
                (kept_hbm.at[2], g1),
                (kept_hbm.at[1], feat),
                (kept_hbm.at[5], cots),
                (united_kept.at[0], united),
            )
        )
    ]
    for copy in copies:
        copy.start()
    clear_halo(a0, frames)
    clear_halo(a1, frames)
    totals = []
    for layer, acts, grads in ((0, a0, g0), (1, a1, g1)):
        copies[2 * layer].wait()
        copies[2 * layer + 1].wait()
        total = jnp.zeros((TAPS * ch, ch), F32)
        for at in range(0, frames, step_frames):
            total = total + mm_tn(
                taps_of(acts, at, step_frames, dil_ref[layer], 1),
                grads[at : at + step_frames].reshape(rows, ch),
            )
        totals.append(total)
    for copy in copies[4:]:
        copy.wait()
    united_copy = pltpu.make_async_copy(united, united_hbm, sems.at[len(copies)])
    united_copy.start()
    total = jnp.zeros((ch, ch), F32)
    for at in range(0, frames, step_frames):
        total = total + mm_tn(
            feat[at : at + step_frames].reshape(rows, ch),
            cots[at : at + step_frames].reshape(rows, ch),
        )
    keyed = jnp.zeros((ch, ch), F32)
    for seg in range(segs):
        low, top = seg * seg_frames, (seg + 1) * seg_frames
        key = feat[low + key_ref[seg]]
        seg_cot = jnp.sum(cots[low:top].astype(F32), axis=0)
        keyed = keyed + sum(mm_tn(key, part) for part in three_parts(seg_cot))
    peers = len(pieces)
    split = LAYERS * TAPS * ch // peers
    total_ref[:, :split] = (jnp.concatenate(totals, axis=0) * scale).reshape(peers, split, ch)
    total_ref[:, split:] = (jnp.concatenate([total, keyed], axis=0) * scale).reshape(
        peers, 2 * ch // peers, ch
    )
    hand_out(here_ref, total_ref, pieces)
    united_copy.wait()


def sum_kernel(*refs):
    refs[-1][...] = sum(ref[...].astype(F32) for ref in refs[:-1]).astype(refs[-1].dtype)


def join_kernel(first_ref, *refs):
    out_ref = refs[-1]
    split = first_ref.shape[0]
    out_ref[:split] = first_ref[...]
    out_ref[split:] = sum(ref[...].astype(F32) for ref in refs[:-1]).astype(out_ref.dtype)


def deal_kernel(pieces_ref, united_hbm, *refs):
    outs_hbm, united_out, outs, sems = refs[:3], refs[3], refs[4:7], refs[7]
    copies = [pltpu.make_async_copy(united_hbm, united_out, sems.at[3])]
    copies[0].start()
    at = 0
    for n, out_ref in enumerate(outs):
        count = out_ref.shape[1]
        out_ref[...] = pieces_ref[:, at : at + count].astype(F32)
        copies.append(pltpu.make_async_copy(out_ref, outs_hbm[n], sems.at[n]))
        copies[-1].start()
        at += count
    for copy in copies:
        copy.wait()


def exchange(blocks):
    return lax.all_to_all(blocks, AXES, split_axis=0, concat_axis=0, tiled=True)


def flip(value, peer):
    size = lax.axis_size("grp")
    return lax.ppermute(value, "grp", [(i, i ^ peer) for i in range(size)])


def meet_in_seg(value, bit):
    size = lax.axis_size("seg")
    return lax.ppermute(value, "seg", [(i, i ^ bit) for i in range(size)])


def sum_of(parts):
    shape = parts[0].shape
    return call(
        sum_kernel, [(shape, BF16, VMEM)], [], 0, len(parts) * 2 * shape[0] * shape[1],
        [(part, VMEM) for part in parts], SMALL_VMEM,
    )[0]


def reduce_in_grp(pieces):
    return sum_of([flip(piece, peer) if peer else piece for peer, piece in enumerate(pieces)])


def local(
    frames_in, spatial_weight, temporal_weight, uniting_weight, key_index, dilation, cotangent
):
    held, rows, cols, ch = frames_in.shape
    assert held == 1
    pixels = rows * cols
    peers = lax.axis_size("grp")
    segs = lax.axis_size("seg")
    devices = segs * peers
    frames = held * devices
    block = pixels // devices
    split = cols // block
    wide = round_up(cols + 1, 16)
    high = round_up(block, 16)
    rows_step = next(n for n in (4, 2, 1) if rows % n == 0)
    steps = rows // rows_step
    parts = next(n for n in (4, 2, 1) if rows % (n * rows_step) == 0)
    step_frames, narrow_step = (
        max(n for n in range(1, frames + 1) if frames % n == 0 and n * high <= most)
        for most in (512, 256)
    )
    grad_parts = 4 if frames % (4 * narrow_step) == 0 else frames // narrow_step
    scale = float((frames * pixels) ** -0.5)
    here = jnp.stack([lax.axis_index("seg"), lax.axis_index("grp")]).astype(jnp.int32)
    space_rows, time_rows, unite_rows = (n * ch // peers for n in (9, LAYERS * TAPS, 2))

    (send,) = call(
        functools.partial(spatial_fwd_kernel, rows_step),
        [((rows, 2, cols, ch), BF16, HBM)],
        [
            pltpu.VMEM((rows, cols, ch), BF16),
            pltpu.VMEM(spatial_weight.shape, BF16),
            pltpu.VMEM((rows + 2, wide, ch), BF16),
            pltpu.VMEM((rows, 2, cols, ch), BF16),
            pltpu.SemaphoreType.DMA((parts,)),
            pltpu.SemaphoreType.DMA((1,)),
            pltpu.SemaphoreType.DMA((1,)),
            pltpu.SemaphoreType.DMA((parts,)),
        ],
        2 * 9 * pixels * ch * ch,
        pixels * ch * 8,
        [(frames_in[0], HBM), (spatial_weight, HBM), (cotangent[0], HBM)],
    )
    send, frame = lax.optimization_barrier((send, frames_in[0]))
    send = send.reshape(rows, 2, split, block, ch).swapaxes(1, 2).reshape(devices, 2, block, ch)
    got = exchange(send)
    (space_slope,) = call(
        functools.partial(spatial_slope_kernel, rows_step),
        [((SPARE, rows, cols, ch), BF16, HBM)],
        [
            pltpu.VMEM((rows + 2, wide, ch), BF16),
            pltpu.VMEM((rows, cols, ch), BF16),
            pltpu.SemaphoreType.DMA((1,)),
        ],
        2 * 9 * pixels * ch * ch,
        pixels * ch * 4,
        [(frame, VMEM), (spatial_weight, VMEM)],
    )
    got, space_slope = lax.optimization_barrier((got, space_slope))

    padded = (frames + 2 * HALO, high, ch)
    whole = (frames, high, ch)
    grad_send, kept, united_kept = call(
        functools.partial(temporal_kernel, narrow_step),
        [
            ((frames, block, ch), BF16, HBM),
            ((SPARE,) + whole, BF16, HBM),
            ((SPARE, frames, block, ch), BF16, HBM),
        ],
        [
            pltpu.VMEM(padded, BF16),
            pltpu.VMEM(padded, BF16),
            pltpu.VMEM(whole, BF16),
            pltpu.VMEM(whole, BF16),
            pltpu.VMEM(padded, BF16),
            pltpu.VMEM(padded, BF16),
            pltpu.VMEM(whole, F32),
            pltpu.VMEM(whole, F32),
            pltpu.VMEM((frames, block, ch), BF16),
            pltpu.VMEM((frames, block, ch), BF16),
            pltpu.VMEM(temporal_weight.shape, BF16),
            pltpu.VMEM(uniting_weight.shape, BF16),
            pltpu.SemaphoreType.DMA((7,)),
            pltpu.SemaphoreType.DMA((2,)),
            pltpu.SemaphoreType.DMA((grad_parts,)),
        ],
        2 * 22 * frames * block * ch * ch,
        frames * block * ch * 18,
        [
            (dilation, SMEM), (key_index, SMEM), (got, VMEM),
            (temporal_weight, HBM), (uniting_weight, HBM),
        ],
        MID_VMEM,
    )
    grad_time = exchange(grad_send).reshape(rows, cols, ch)
    united_send, *time_pieces = call(
        functools.partial(temporal_wgrad_kernel, step_frames, scale),
        [((frames, block, ch), BF16, HBM)]
        + [((time_rows + unite_rows, ch), BF16, VMEM)] * peers,
        [
            pltpu.VMEM(padded, BF16),
            pltpu.VMEM(whole, BF16),
            pltpu.VMEM(padded, BF16),
            pltpu.VMEM(whole, BF16),
            pltpu.VMEM(whole, BF16),
            pltpu.VMEM(whole, BF16),
            pltpu.VMEM((frames, block, ch), BF16),
            pltpu.VMEM((peers, time_rows + unite_rows, ch), F32),
            pltpu.SemaphoreType.DMA((8,)),
        ],
        2 * 12 * frames * block * ch * ch,
        frames * block * ch * 14,
        [
            (here, SMEM), (dilation, SMEM), (key_index, SMEM),
            (kept, HBM), (united_kept, HBM),
        ],
    )
    time_sum = reduce_in_grp(time_pieces)
    time_sum, grad_time = lax.optimization_barrier((time_sum, grad_time))
    united_send, grad_time = lax.optimization_barrier((united_send, grad_time))
    united = exchange(united_send)
    space_pieces = call(
        functools.partial(spatial_wgrad_kernel, rows_step, scale),
        [((space_rows, ch), BF16, VMEM)] * peers,
        [
            pltpu.VMEM((rows + 2, wide, ch), BF16),
            pltpu.VMEM((rows, cols, ch), BF16),
            pltpu.VMEM((3 * ch, min(3, steps) * rows_step * wide), BF16),
            pltpu.VMEM((peers, space_rows, ch), F32),
            pltpu.SemaphoreType.DMA((1,)),
        ],
        2 * 9 * pixels * ch * ch,
        pixels * ch * 8,
        [(here, SMEM), (grad_time, VMEM), (space_slope, HBM), (frame, VMEM)],
        MID_VMEM,
    )
    (back,) = call(
        functools.partial(spatial_back_kernel, rows_step),
        [((rows, cols, ch), BF16, VMEM)],
        [
            pltpu.VMEM((rows + 2, wide, ch), BF16),
            pltpu.VMEM((rows, cols, ch), BF16),
            pltpu.SemaphoreType.DMA((1,)),
        ],
        2 * 9 * pixels * ch * ch,
        pixels * ch * 6,
        [(spatial_weight, VMEM), (grad_time, VMEM), (space_slope, HBM)],
        MID_VMEM,
    )
    space_parts = [flip(part, peer) if peer else part for peer, part in enumerate(space_pieces)]
    (plane,) = call(
        join_kernel,
        [((time_rows + unite_rows + space_rows, ch), BF16, VMEM)],
        [],
        0,
        2 * (peers + 10) * space_rows * ch,
        [(time_sum, VMEM)] + [(part, VMEM) for part in space_parts],
        SMALL_VMEM,
    )
    piece = plane
    bits = [1 << n for n in range((segs - 1).bit_length())]
    for bit in bits:
        other = meet_in_seg(piece, bit)
        if bit == bits[-1]:
            other, back = lax.optimization_barrier((other, back))
        piece = sum_of([piece, other])
    *grads, united = call(
        deal_kernel,
        [((peers, count, ch), F32, HBM) for count in (time_rows, unite_rows, space_rows)]
        + [((frames, block, ch), BF16, HBM)],
        [pltpu.VMEM((peers, count, ch), F32) for count in (time_rows, unite_rows, space_rows)]
        + [pltpu.SemaphoreType.DMA((4,))],
        0,
        6 * 21 * ch * ch,
        [(lax.all_gather(piece, "grp", axis=0), VMEM), (united, HBM)],
        SMALL_VMEM,
    )
    return (
        united.reshape(frames_in.shape),
        back[None],
        grads[2].reshape(9, ch, ch),
        grads[0].reshape(LAYERS, TAPS, ch, ch),
        grads[1].reshape(2, ch, ch),
    )


def solution(mesh):
    frame_spec = P(AXES, None, None, None)
    return jax.shard_map(
        local,
        mesh=mesh,
        in_specs=(frame_spec, P(), P(), P(), P(), P(), frame_spec),
        out_specs=(frame_spec, frame_spec, P(), P(), P()),
        check_vma=False,
    )
```
